32 devices in a mesh: narrow: 4 (over z), wide: 8 (over y, x, core).
Axes of the slice: x: 2, y: 2, z: 4, core: 2. Of those that a mesh axis runs over, the one named last changes fastest.
Arguments:
- hidden_in: bfloat16 [8, 1024, 1024], P('narrow', 'wide'), may hold values from -6 to 6
- out_grad: bfloat16 [8, 1024, 1024], P('narrow', 'wide'), may hold values from -6 to 6
- seg_ids: int32 [8, 1024], P('narrow', 'wide'), may hold values from 0 to 5, as said below
- expert_ids: int32 [8, 1024, 8], P('narrow', 'wide'), may hold values from 0 to 31, all different within a row
- attn_gain: bfloat16 [1024], P(('narrow', 'wide')), may hold values from 0.099609375 to 1.8984375
- w_query: bfloat16 [1024, 1024], P(('narrow', 'wide')), may hold values from -0.1875 to 0.1875
- w_key: bfloat16 [1024, 512], P(('narrow', 'wide')), may hold values from -0.1875 to 0.1875
- w_value: bfloat16 [1024, 512], P(('narrow', 'wide')), may hold values from -0.1875 to 0.1875
- w_output: bfloat16 [1024, 1024], P(('narrow', 'wide')), may hold values from -1.5 to 1.5
- moe_gain: bfloat16 [1024], P(('narrow', 'wide')), may hold values from 0.099609375 to 1.8984375
- w_router: bfloat16 [1024, 32], P(('narrow', 'wide')), may hold values from -0.09375 to 0.09375
- w_gate_up: bfloat16 [32, 1024, 1024], P('wide', 'narrow'), may hold values from -0.1875 to 0.1875
- w_down: bfloat16 [32, 512, 1024], P('wide', 'narrow'), may hold values from -0.75 to 0.75
Outputs:
- block_out: bfloat16 [8, 1024, 1024], P('narrow', 'wide')
- input_grad: bfloat16 [8, 1024, 1024], P('narrow', 'wide')
- attn_gain_grad: float32 [1024], P(('narrow', 'wide'))
- w_query_grad: float32 [1024, 1024], P(('narrow', 'wide'))
- w_key_grad: float32 [1024, 512], P(('narrow', 'wide'))
- w_value_grad: float32 [1024, 512], P(('narrow', 'wide'))
- w_output_grad: float32 [1024, 1024], P(('narrow', 'wide'))
- moe_gain_grad: float32 [1024], P(('narrow', 'wide'))
- w_router_grad: float32 [1024, 32], P(('narrow', 'wide'))
- w_gate_up_grad: float32 [32, 1024, 1024], P('wide', 'narrow')
- w_down_grad: float32 [32, 512, 1024], P('wide', 'narrow')
- expert_load: int32 [32], replicated
The draws below stay inside these ranges and needn't reach their ends.
Inputs may be any that keep to these rules, and one draw needn't show every extreme that they name: `seg_ids`: along each row the document numbers never fall. `expert_ids`: the 8 experts named by one token are all different; across the tokens of a packed row an expert is named many times, and every expert is named by some token.
All inputs are finite; a program needn't handle non-finite values.
Results may differ from the reference program's by a relative error of at most 0.017.
Values may be sent and summed in bfloat16 or wider, within the bound.
A program may use at most 192 MiB of HBM per device.

```python
import math
import jax
import jax.numpy as jnp
from jax import lax

D = 1024
HEADS = 16
KV_HEADS = 8
HEAD_DIM = 64
EXPERTS = 32
TOP = 8
FF = 512
ROWS_DEV = 2
SEQ_DEV = 128
CUTS = 5
SEQ = 1024
ROWS = 8
CAP = 80
N_NARROW = 4
N_WIDE = 8


def draw_seg_ids(key, part):
    key = jax.random.fold_in(key, 17)
    free_key, early_key, late_key, pick_key = jax.random.split(key, 4)
    free_cuts = jax.random.randint(free_key, (ROWS, CUTS), 1, SEQ)
    early_cuts = jax.random.randint(early_key, (ROWS, CUTS), 1, SEQ_DEV)
    late_cuts = jax.random.randint(late_key, (ROWS, CUTS), SEQ - SEQ_DEV + 1, SEQ)
    lane_ids = jnp.arange(CUTS)
    span_cuts = jnp.where(lane_ids[None, :] < CUTS // 2, early_cuts, late_cuts)
    picked = jax.random.randint(pick_key, (ROWS // ROWS_DEV,), 0, ROWS_DEV)
    row_ids = jnp.arange(ROWS)
    spanning = row_ids % ROWS_DEV == jnp.repeat(picked, ROWS_DEV)
    cut_points = jnp.where(spanning[:, None], span_cuts, free_cuts)
    places = jnp.arange(SEQ)
    return jnp.sum((places[None, :, None] >= cut_points[:, None, :]).astype(jnp.int32), axis=-1).astype(jnp.int32)


def block_scale(key, shape, pieces, smallest, largest):
    level, own = 1.0, jax.random.fold_in(key, 6)
    for axis_at, parts in pieces:
        heights = jnp.exp(jax.random.uniform(jax.random.fold_in(own, axis_at), (parts,), jnp.float32, smallest / len(pieces), largest / len(pieces)))
        level = level * jnp.repeat(heights, shape[axis_at] // parts).reshape([-1 if axis == axis_at else 1 for axis in range(len(shape))])
    return level


def choose_distinct(rng, rows, count, top, lift):
    ranking = jax.random.permutation(jax.random.fold_in(rng, 1), count)
    pull = ranking
    for power in range(3):
        pull = pull * pull // count
    pull = pull * lift // count
    chance = jax.random.randint(jax.random.fold_in(rng, 2), (rows, count), 0, 4096) + pull
    holders = jax.random.permutation(jax.random.fold_in(rng, 3), rows)[jnp.arange(count) % rows]
    chance = jnp.where(jnp.arange(rows)[:, None] == holders[None, :], 1 << 14, chance)
    priority = chance * count + jnp.arange(count)
    return lax.top_k(priority.astype(jnp.int32), top)[1].astype(jnp.int32)


def gaussian(key, dims, deviation, limit, cuts=(), dtype=jnp.bfloat16):
    drawn = jax.random.normal(key, dims, jnp.float32) * deviation
    if len(cuts) > 0:
        drawn = block_scale(key, dims, cuts, -0.22, 0.18) * drawn
    return jnp.clip(drawn, min=-limit, max=limit).astype(dtype)


def setup_inputs(seed: int = 0) -> dict:
    key_of = jax.random.split(jax.random.key(seed), 14)
    return {
        "hidden_in": gaussian(key_of[0], (ROWS, SEQ, D), 1.0, 6.0, ((0, 4), (1, 8))),
        "out_grad": gaussian(key_of[1], (ROWS, SEQ, D), 1.0, 6.0, ((0, 4), (1, 8))),
        "seg_ids": draw_seg_ids(jax.random.fold_in(key_of[13], 71), 0),
        "expert_ids": choose_distinct(key_of[3], ROWS * SEQ, EXPERTS, TOP, 2048).reshape((ROWS, SEQ, TOP)),
        "attn_gain": jnp.clip(1.0 + 0.18 * jax.random.normal(key_of[4], (D,), jnp.float32), 0.099609375, 1.8984375).astype(jnp.bfloat16),
        "w_query": gaussian(key_of[5], (D, HEADS * HEAD_DIM), D ** -0.5, 0.1875, ((0, 32),)),
        "w_key": gaussian(key_of[6], (D, KV_HEADS * HEAD_DIM), D ** -0.5, 0.1875, ((0, 32),)),
        "w_value": gaussian(key_of[7], (D, KV_HEADS * HEAD_DIM), D ** -0.5, 0.1875, ((0, 32),)),
        "w_output": gaussian(key_of[8], (HEADS * HEAD_DIM, D), (D // 64) ** -0.5, 1.5, ((0, 32),)),
        "moe_gain": jnp.clip(1.0 + 0.18 * jax.random.normal(key_of[9], (D,), jnp.float32), 0.099609375, 1.8984375).astype(jnp.bfloat16),
        "w_router": gaussian(key_of[10], (D, EXPERTS), (4 * D) ** -0.5, 0.09375, ((0, 32),)),
        "w_gate_up": gaussian(key_of[11], (EXPERTS, D, 2 * FF), D ** -0.5, 0.1875, ((0, 8), (1, 4))),
        "w_down": gaussian(key_of[12], (EXPERTS, FF, D), (FF // 8) ** -0.5, 0.75, ((0, 8), (1, 4))),
    }


EPSILON = 1e-06
THETA = 10000.0
MASKED = -1e+30
HIGH = lax.Precision.HIGHEST

@jax.custom_vjp
def low(v):
    return lax.optimization_barrier(v.astype(jnp.bfloat16)).astype(jnp.float32)

@jax.custom_vjp
def low_back(v):
    return v

def low_keep(v):
    return (low(v), None)

def low_pass(kept, grad):
    return (grad,)

def back_keep(v):
    return (v, None)

def back_low(kept, grad):
    return (low(grad),)
low.defvjp(low_keep, low_pass)
low_back.defvjp(back_keep, back_low)

def rms_scale(values):
    return lax.rsqrt(lax.optimization_barrier(jnp.mean(values * values, axis=-1, keepdims=True)) + EPSILON)

def rope(values, cosine, sine_table):
    half_dim = HEAD_DIM // 2
    turned = jnp.concatenate([-values[..., half_dim:], values[..., :half_dim]], axis=-1)
    return values * cosine + turned * sine_table

def positions_of(seg_ids):
    starts = jax.vmap(lambda row_segs: jnp.searchsorted(row_segs, row_segs, side='left'))(seg_ids)
    places = jnp.arange(seg_ids.shape[1]).astype(jnp.int32)
    return (places[None, :] - starts.astype(jnp.int32)).astype(jnp.float32)

def attend_row(row_args):
    queries, keys_rot, values_in, row_segs = row_args
    length = row_segs.shape[0]
    block_len = math.gcd(length, 512)
    key_places = jnp.arange(length).astype(jnp.int32)
    factor = HEAD_DIM ** (-0.5)

    def one_block(block_args):
        query_block, seg_block, place_block = block_args
        scores = jnp.einsum('qgjd,kgd->gjqk', query_block, keys_rot, precision=HIGH) * factor
        scores = low_back(scores)
        allowed = (seg_block[:, None] == row_segs[None, :]) & (place_block[:, None] >= key_places[None, :])
        scores = jnp.where(allowed[None, None], scores, MASKED)
        weights = low(jnp.exp(scores - jax.nn.logsumexp(scores, axis=-1, keepdims=True)))
        return jnp.einsum('gjqk,kgd->qgjd', weights, values_in, precision=HIGH)
    block_count = length // block_len
    attended = lax.map(jax.checkpoint(one_block), (queries.reshape(block_count, block_len, KV_HEADS, 2, HEAD_DIM), row_segs.reshape(block_count, block_len), key_places.reshape(block_count, block_len)))
    return attended.reshape(length, KV_HEADS, 2, HEAD_DIM)

def to_devices(values):
    dims_in = values.shape
    reshaped = values.reshape((N_NARROW, ROWS_DEV, N_WIDE, SEQ_DEV) + dims_in[2:])
    reshaped = jnp.swapaxes(reshaped, 1, 2)
    return reshaped.reshape((N_NARROW * N_WIDE, ROWS_DEV * SEQ_DEV) + dims_in[2:])

def from_devices(values):
    dims_in = values.shape
    reshaped = values.reshape((N_NARROW, N_WIDE, ROWS_DEV, SEQ_DEV) + dims_in[2:])
    reshaped = jnp.swapaxes(reshaped, 1, 2)
    return reshaped.reshape((N_NARROW * ROWS_DEV, N_WIDE * SEQ_DEV) + dims_in[2:])

def route_tables(expert_table):
    choose = expert_table[:, :, None] == jnp.arange(EXPERTS).astype(jnp.int32)[None, None, :]
    token_hot = lax.optimization_barrier(jnp.sum(choose, axis=1)).astype(jnp.int32)
    earlier = jnp.cumsum(token_hot, axis=0) - token_hot
    places = jnp.take_along_axis(earlier, expert_table, axis=1)
    target = jnp.where(places < CAP, expert_table * CAP + places, EXPERTS * CAP).reshape(-1).astype(jnp.int32)
    pair_count = expert_table.shape[0] * TOP
    pair_of_slot = jnp.full((EXPERTS * CAP,), pair_count, jnp.int32).at[target].set(jnp.arange(pair_count).astype(jnp.int32), mode='drop')
    return (target, pair_of_slot)

def expert_device(device_args, router_w, gate_up_w, down_w):
    normed, expert_table, target, pair_of_slot = device_args
    logits = low_back(jnp.dot(normed, router_w, precision=HIGH))
    gate_vals = jax.nn.softmax(jnp.take_along_axis(logits, expert_table, axis=1), axis=-1)
    sent_rows = low_back(jnp.take(normed, pair_of_slot // TOP, axis=0, mode='fill', fill_value=0.0))
    gate_up = low_back(jnp.einsum('ecd,edf->ecf', sent_rows.reshape(EXPERTS, CAP, -1), gate_up_w, precision=HIGH))
    hidden = low(jax.nn.silu(gate_up[..., :FF]) * gate_up[..., FF:])
    output = low(low_back(jnp.einsum('ecf,efd->ecd', hidden, down_w, precision=HIGH)))
    per_pair = jnp.take(output.reshape(EXPERTS * CAP, -1), target, axis=0, mode='fill', fill_value=0.0)
    return lax.optimization_barrier(jnp.sum(gate_vals[..., None] * per_pair.reshape(normed.shape[0], TOP, -1), axis=1))

def reference(hidden_in, out_grad, seg_ids, expert_ids, attn_gain, w_query, w_key, w_value, w_output, moe_gain, w_router, w_gate_up, w_down):
    positions = positions_of(seg_ids)
    inverse = 1.0 / THETA ** (jnp.arange(HEAD_DIM // 2).astype(jnp.float32) * 2.0 / HEAD_DIM)
    angles = positions[:, :, None] * inverse[None, None, :]
    cosine = jnp.concatenate([jnp.cos(angles), jnp.cos(angles)], axis=-1)[:, :, None, :]
    sine_table = jnp.concatenate([jnp.sin(angles), jnp.sin(angles)], axis=-1)[:, :, None, :]
    ids_dev = to_devices(expert_ids)
    target, pair_of_slot = jax.vmap(route_tables)(ids_dev)
    expert_load = lax.optimization_barrier(jnp.sum(expert_ids.reshape(-1)[:, None] == jnp.arange(EXPERTS).astype(jnp.int32)[None, :], axis=0)).astype(jnp.int32)

    def forward(inputs, gain_one, query_w, key_w, value_w, output_w, gain_two, router_w, gate_up_w, down_w):
        normed_one = low(inputs * rms_scale(inputs) * gain_one)
        query_pre = low_back(jnp.einsum('rld,de->rle', normed_one, query_w, precision=HIGH))
        key_pre = low_back(jnp.einsum('rld,de->rle', normed_one, key_w, precision=HIGH))
        values_in = low(low_back(jnp.einsum('rld,de->rle', normed_one, value_w, precision=HIGH)))
        queries = low(rope(query_pre.reshape(ROWS, SEQ, HEADS, HEAD_DIM), cosine, sine_table))
        keys_rot = low(rope(key_pre.reshape(ROWS, SEQ, KV_HEADS, HEAD_DIM), cosine, sine_table))
        values_in = values_in.reshape(ROWS, SEQ, KV_HEADS, HEAD_DIM)
        attended = lax.map(jax.checkpoint(attend_row), (queries.reshape(ROWS, SEQ, KV_HEADS, 2, HEAD_DIM), keys_rot, values_in, seg_ids))
        attended = low(low_back(attended.reshape(ROWS, SEQ, HEADS * HEAD_DIM)))
        middle = inputs + low_back(jnp.einsum('rle,ed->rld', attended, output_w, precision=HIGH))
        normed_two = low(middle * rms_scale(middle) * gain_two)
        mixture = lax.map(jax.checkpoint(lambda device_args: expert_device(device_args, router_w, gate_up_w, down_w)), (to_devices(normed_two), ids_dev, target, pair_of_slot))
        return middle + from_devices(mixture)
    weights_in = [arg.astype(jnp.float32) for arg in (attn_gain, w_query, w_key, w_value, w_output, moe_gain, w_router, w_gate_up, w_down)]
    outputs, pullback = jax.vjp(forward, hidden_in.astype(jnp.float32), *weights_in)
    grads = pullback(out_grad.astype(jnp.float32))
    return (outputs.astype(jnp.bfloat16), grads[0].astype(jnp.bfloat16), grads[1], grads[2], grads[3], grads[4], grads[5], grads[6], grads[7], grads[8], grads[9], expert_load)
```

```python
import math

import jax
import jax.numpy as jnp
import numpy as np
from jax import lax
from jax.experimental import pallas as pl
from jax.experimental.pallas import tpu as pltpu
from jax.sharding import PartitionSpec as P

KV_HEADS = 8
HEAD_DIM = 64
EXPERTS = 32
TOP = 8
FF = 512
CAP = 80


EPSILON = 1e-06
THETA = 10000.0
MASKED = -1e30


def rms_scale(values):
    return lax.rsqrt(jnp.mean(values * values, axis=-1, keepdims=True) + EPSILON)


def norm_back(values, scale, gain, upstream):
    weighted = upstream * gain
    inner_mean = jnp.mean(weighted * values, axis=-1, keepdims=True)
    value_grad = weighted * scale - values * (scale * scale * scale) * inner_mean
    gain_grad = jnp.sum(upstream * values * scale, axis=0)
    return (value_grad, gain_grad)


def lane_turn(head_dim):
    lane_ids = jnp.arange(128)
    lane_local = lane_ids % head_dim
    half_dim = head_dim // 2
    same_head = lane_ids[:, None] // head_dim == lane_ids[None, :] // head_dim
    from_upper = (lane_local[None, :] < half_dim) & (
        lane_local[:, None] == lane_local[None, :] + half_dim
    )
    from_lower = (lane_local[None, :] >= half_dim) & (
        lane_local[:, None] + half_dim == lane_local[None, :]
    )
    return jnp.where(
        same_head & from_upper, -1.0, jnp.where(same_head & from_lower, 1.0, 0.0)
    ).astype(jnp.float32)


def lane_angles(positions, head_dim):
    lane_ids = jnp.arange(128) % head_dim % (head_dim // 2)
    inverse = 1.0 / THETA ** (lane_ids.astype(jnp.float32) * 2.0 / head_dim)
    return positions[..., None] * inverse


def rotate(values, cos_table, sin_table, turner):
    dims_in = values.shape
    blocks = values.reshape(dims_in[0], dims_in[1], -1, 128)
    turned = jnp.einsum("abnl,lm->abnm", blocks, turner, precision=lax.Precision.HIGHEST)
    return (blocks * cos_table[:, :, None, :] + turned * sin_table[:, :, None, :]).reshape(dims_in)


def rotate_back(grad_in, cos_table, sin_table, turner):
    dims_in = grad_in.shape
    blocks = grad_in.reshape(dims_in[0], dims_in[1], -1, 128)
    turned = jnp.einsum(
        "abnm,lm->abnl", blocks * sin_table[:, :, None, :], turner, precision=lax.Precision.HIGHEST
    )
    return (blocks * cos_table[:, :, None, :] + turned).reshape(dims_in)


def masked_scores(query_five, key_block, seg_query, seg_key, place_query, place_key, factor):
    scores = (
        jnp.einsum("abgjd,akgd->agjbk", query_five, key_block, preferred_element_type=jnp.float32)
        * factor
    )
    allowed = (seg_query[:, :, None] == seg_key[:, None, :]) & (
        place_query[:, :, None] >= place_key[:, None, :]
    )
    return jnp.where(allowed[:, None, None], scores, MASKED)


def general_device(
    hidden_in,
    out_grad,
    seg_ids,
    expert_ids,
    attn_gain,
    w_query,
    w_key,
    w_value,
    w_output,
    moe_gain,
    w_router,
    w_gate_up,
    w_down,
):
    row_count, span_len, feat_dim = hidden_in.shape
    tok_count = row_count * span_len
    factor = HEAD_DIM ** (-0.5)
    kv_width = KV_HEADS * HEAD_DIM
    gain_one, query_w, key_w, value_w, output_w, gain_two, router_w = (
        lax.all_gather(attn_gain, ("narrow", "wide"), axis=0, tiled=True),
        lax.all_gather(w_query, ("narrow", "wide"), axis=0, tiled=True),
        lax.all_gather(w_key, ("narrow", "wide"), axis=0, tiled=True),
        lax.all_gather(w_value, ("narrow", "wide"), axis=0, tiled=True),
        lax.all_gather(w_output, ("narrow", "wide"), axis=0, tiled=True),
        lax.all_gather(moe_gain, ("narrow", "wide"), axis=0, tiled=True),
        lax.all_gather(w_router, ("narrow", "wide"), axis=0, tiled=True),
    )
    gate_up_w, down_w = (
        lax.all_gather(w_gate_up, "narrow", axis=1, tiled=True),
        lax.all_gather(w_down, "narrow", axis=1, tiled=True),
    )
    segs_all = lax.all_gather(seg_ids, "wide", axis=1, tiled=True)
    seq_len = segs_all.shape[1]
    key_step = math.gcd(seq_len, 512)
    place_local = lax.axis_index("wide") * span_len + jnp.arange(span_len, dtype=jnp.int32)
    place_query = place_local[None, :]
    starts = jnp.sum((segs_all[:, None, :] < seg_ids[:, :, None]).astype(jnp.int32), axis=-1)
    positions = (place_query - starts).astype(jnp.float32)
    angles = lane_angles(positions, HEAD_DIM)
    cos_table = jnp.cos(angles)
    sin_table = jnp.sin(angles)
    turner = lane_turn(HEAD_DIM)
    inputs = hidden_in.astype(jnp.float32)
    scale_one = rms_scale(inputs)
    gain_one_f = gain_one.astype(jnp.float32)
    normed_one = (inputs * scale_one * gain_one_f).astype(jnp.bfloat16)
    query_pre = jnp.dot(normed_one, query_w, preferred_element_type=jnp.float32)
    key_pre = jnp.dot(normed_one, key_w, preferred_element_type=jnp.float32)
    value_pre = jnp.dot(normed_one, value_w, preferred_element_type=jnp.float32)
    queries = rotate(query_pre, cos_table, sin_table, turner).astype(jnp.bfloat16)
    keys_local = rotate(key_pre, cos_table, sin_table, turner).astype(jnp.bfloat16)
    values_local = value_pre.astype(jnp.bfloat16)
    key_all, value_all = (
        lax.all_gather(keys_local, "wide", axis=1, tiled=True),
        lax.all_gather(values_local, "wide", axis=1, tiled=True),
    )
    query_five = queries.reshape(row_count, span_len, KV_HEADS, 2, HEAD_DIM)

    def key_slices(key_start, length):
        key_block = lax.dynamic_slice_in_dim(key_all, key_start, length, 1).reshape(
            row_count, length, KV_HEADS, HEAD_DIM
        )
        value_block = lax.dynamic_slice_in_dim(value_all, key_start, length, 1).reshape(
            row_count, length, KV_HEADS, HEAD_DIM
        )
        seg_key = lax.dynamic_slice_in_dim(segs_all, key_start, length, 1)
        place_key = (key_start + jnp.arange(length, dtype=jnp.int32))[None, :]
        return (key_block, value_block, seg_key, place_key)

    def scores_at(key_start, length):
        key_block, value_block, seg_key, place_key = key_slices(key_start, length)
        scores = masked_scores(
            query_five, key_block, seg_ids, seg_key, place_query, place_key, factor
        )
        return (scores, key_block, value_block)

    key_starts = jnp.arange(seq_len // key_step, dtype=jnp.int32) * key_step
    stat_shape = (row_count, KV_HEADS, 2, span_len)
    five_shape = (row_count, span_len, KV_HEADS, 2, HEAD_DIM)

    def top_step(state_now, key_start):
        row_top, row_total = state_now
        scores, unused_key, unused_value = scores_at(key_start, key_step)
        new_top = jnp.maximum(row_top, jnp.max(scores, axis=-1))
        row_total = row_total * jnp.exp(row_top - new_top) + jnp.sum(
            jnp.exp(scores - new_top[..., None]), axis=-1
        )
        return ((new_top, row_total), None)

    (row_top, row_total), unused = lax.scan(
        top_step,
        (jnp.full(stat_shape, MASKED, jnp.float32), jnp.zeros(stat_shape, jnp.float32)),
        key_starts,
    )
    log_total = row_top + jnp.log(row_total)

    def out_step(summed, key_start):
        scores, unused_key, value_block = scores_at(key_start, key_step)
        weights = jnp.exp(scores - log_total[..., None]).astype(jnp.bfloat16)
        return (
            summed
            + jnp.einsum(
                "agjbk,akgd->abgjd", weights, value_block, preferred_element_type=jnp.float32
            ),
            None,
        )

    attended, unused = lax.scan(out_step, jnp.zeros(five_shape, jnp.float32), key_starts)
    attended = attended.reshape(row_count, span_len, -1).astype(jnp.bfloat16)
    middle = inputs + jnp.dot(attended, output_w, preferred_element_type=jnp.float32)
    scale_two = rms_scale(middle)
    gain_two_f = gain_two.astype(jnp.float32)
    normed_two = (middle * scale_two * gain_two_f).astype(jnp.bfloat16)
    flat_two = normed_two.reshape(tok_count, feat_dim)
    logits = jnp.dot(flat_two, router_w, preferred_element_type=jnp.float32)
    expert_table = expert_ids.reshape(tok_count, TOP)
    choose = expert_table[:, :, None] == jnp.arange(EXPERTS, dtype=jnp.int32)[None, None, :]
    chosen = jnp.sum(jnp.where(choose, logits[:, None, :], 0.0), axis=-1)
    gate_vals = jax.nn.softmax(chosen, axis=-1)
    token_hot = jnp.sum(choose.astype(jnp.int32), axis=1)
    expert_load = lax.psum(jnp.sum(token_hot, axis=0), ("narrow", "wide"))
    earlier = jnp.cumsum(token_hot, axis=0) - token_hot
    places = jnp.sum(jnp.where(choose, earlier[:, None, :], 0), axis=-1)
    pair_count = tok_count * TOP
    target = jnp.where(places < CAP, expert_table * CAP + places, EXPERTS * CAP).reshape(-1)
    pair_of_slot = (
        jnp.full((EXPERTS * CAP,), pair_count, jnp.int32)
        .at[target]
        .set(jnp.arange(pair_count, dtype=jnp.int32), mode="drop")
    )
    token_of_slot = pair_of_slot // TOP
    outgoing = jnp.take(flat_two, token_of_slot, axis=0, mode="fill", fill_value=0).reshape(
        EXPERTS, CAP, feat_dim
    )
    received = lax.all_to_all(outgoing, "wide", split_axis=0, concat_axis=1, tiled=True)
    gate_up = jnp.einsum("ecd,edf->ecf", received, gate_up_w, preferred_element_type=jnp.float32)
    gate_half = gate_up[..., :FF]
    up_half = gate_up[..., FF:]
    sigmoid_gate = jax.nn.sigmoid(gate_half)
    activated = gate_half * sigmoid_gate
    hidden_b = (activated * up_half).astype(jnp.bfloat16)
    expert_out = jnp.einsum(
        "ecf,efd->ecd", hidden_b, down_w, preferred_element_type=jnp.float32
    ).astype(jnp.bfloat16)
    returned = lax.all_to_all(expert_out, "wide", split_axis=1, concat_axis=0, tiled=True)
    per_pair = (
        jnp.take(
            returned.reshape(EXPERTS * CAP, feat_dim), target, axis=0, mode="fill", fill_value=0
        )
        .reshape(tok_count, TOP, feat_dim)
        .astype(jnp.float32)
    )
    mixture = jnp.sum(gate_vals[:, :, None] * per_pair, axis=1)
    middle_flat = middle.reshape(tok_count, feat_dim)
    block_out = (middle_flat + mixture).reshape(row_count, span_len, feat_dim).astype(jnp.bfloat16)
    grad_out = out_grad.reshape(tok_count, feat_dim).astype(jnp.float32)
    gate_grad = jnp.sum(grad_out[:, None, :] * per_pair, axis=-1)
    gate_of_slot = jnp.take(gate_vals.reshape(-1), pair_of_slot, mode="fill", fill_value=0.0)
    slot_grad = (
        (
            jnp.take(grad_out, token_of_slot, axis=0, mode="fill", fill_value=0.0)
            * gate_of_slot[:, None]
        )
        .astype(jnp.bfloat16)
        .reshape(EXPERTS, CAP, feat_dim)
    )
    grad_received = lax.all_to_all(slot_grad, "wide", split_axis=0, concat_axis=1, tiled=True)
    down_grad = jnp.einsum(
        "ecf,ecd->efd", hidden_b, grad_received, preferred_element_type=jnp.float32
    )
    hidden_grad = jnp.einsum(
        "ecd,efd->ecf", grad_received, down_w, preferred_element_type=jnp.float32
    )
    gate_half_grad = (
        hidden_grad * up_half * (sigmoid_gate * (1.0 + gate_half * (1.0 - sigmoid_gate)))
    )
    up_half_grad = hidden_grad * activated
    gate_up_grad = jnp.concatenate([gate_half_grad, up_half_grad], axis=-1).astype(jnp.bfloat16)
    gate_up_wgrad = jnp.einsum(
        "ecd,ecf->edf", received, gate_up_grad, preferred_element_type=jnp.float32
    )
    slot_input_grad = jnp.einsum(
        "ecf,edf->ecd", gate_up_grad, gate_up_w, preferred_element_type=jnp.float32
    ).astype(jnp.bfloat16)
    input_back = lax.all_to_all(slot_input_grad, "wide", split_axis=1, concat_axis=0, tiled=True)
    pair_input_grad = jnp.take(
        input_back.reshape(EXPERTS * CAP, feat_dim), target, axis=0, mode="fill", fill_value=0
    ).reshape(tok_count, TOP, feat_dim)
    gate_mean = jnp.sum(gate_vals * gate_grad, axis=-1, keepdims=True)
    chosen_grad = gate_vals * (gate_grad - gate_mean)
    logit_grad = jnp.sum(jnp.where(choose, chosen_grad[:, :, None], 0.0), axis=1).astype(
        jnp.bfloat16
    )
    router_wgrad = jnp.einsum("td,te->de", flat_two, logit_grad, preferred_element_type=jnp.float32)
    normed_two_grad = jnp.sum(pair_input_grad.astype(jnp.float32), axis=1) + jnp.einsum(
        "te,de->td", logit_grad, router_w, preferred_element_type=jnp.float32
    )
    middle_part, gain_two_grad = norm_back(
        middle_flat, scale_two.reshape(tok_count, 1), gain_two_f, normed_two_grad
    )
    middle_grad = grad_out + middle_part
    attn_grad = middle_grad.astype(jnp.bfloat16)
    output_wgrad = jnp.einsum(
        "te,td->ed", attended.reshape(tok_count, -1), attn_grad, preferred_element_type=jnp.float32
    )
    attended_grad = jnp.einsum(
        "td,ed->te", attn_grad, output_w, preferred_element_type=jnp.float32
    ).astype(jnp.bfloat16)
    grad_five = attended_grad.reshape(five_shape)

    def sum_step(summed, key_start):
        scores, unused_key, value_block = scores_at(key_start, key_step)
        weights = jnp.exp(scores - log_total[..., None])
        weight_grad = jnp.einsum(
            "abgjd,akgd->agjbk", grad_five, value_block, preferred_element_type=jnp.float32
        )
        return (summed + jnp.sum(weights * weight_grad, axis=-1), None)

    row_dot, unused = lax.scan(sum_step, jnp.zeros(stat_shape, jnp.float32), key_starts)

    def query_step(summed, key_start):
        scores, key_block, value_block = scores_at(key_start, key_step)
        weights = jnp.exp(scores - log_total[..., None])
        weight_grad = jnp.einsum(
            "abgjd,akgd->agjbk", grad_five, value_block, preferred_element_type=jnp.float32
        )
        score_grad = (weights * (weight_grad - row_dot[..., None])).astype(jnp.bfloat16)
        return (
            summed
            + jnp.einsum(
                "agjbk,akgd->abgjd", score_grad, key_block, preferred_element_type=jnp.float32
            ),
            None,
        )

    query_grad, unused = lax.scan(query_step, jnp.zeros(five_shape, jnp.float32), key_starts)
    query_grad = query_grad.reshape(row_count, span_len, -1) * factor
    term_count = span_len * lax.axis_size("wide")
    sub_len = math.gcd(term_count, 512)

    def key_piece(sub_no):
        key_start = sub_no * sub_len
        key_block, value_block, seg_key, place_key = key_slices(key_start, sub_len)
        scores = masked_scores(
            query_five, key_block, seg_ids, seg_key, place_query, place_key, factor
        )
        weights = jnp.exp(scores - log_total[..., None])
        weight_grad = jnp.einsum(
            "abgjd,akgd->agjbk", grad_five, value_block, preferred_element_type=jnp.float32
        )
        score_grad = (weights * (weight_grad - row_dot[..., None])).astype(jnp.bfloat16)
        key_part = (
            jnp.einsum(
                "agjbk,abgjd->kagd", score_grad, query_five, preferred_element_type=jnp.float32
            )
            * factor
        )
        value_part = jnp.einsum(
            "agjbk,abgjd->kagd",
            weights.astype(jnp.bfloat16),
            grad_five,
            preferred_element_type=jnp.float32,
        )
        return jnp.concatenate(
            [
                key_part.reshape(sub_len, row_count, kv_width),
                value_part.reshape(sub_len, row_count, kv_width),
            ],
            axis=-1,
        )

    pieces = lax.map(key_piece, jnp.arange(term_count // sub_len, dtype=jnp.int32))
    summed_terms = lax.psum_scatter(
        pieces.reshape(term_count, row_count, 2 * kv_width).astype(jnp.bfloat16),
        "wide",
        scatter_dimension=0,
        tiled=True,
    ).astype(jnp.float32)
    key_grad = jnp.transpose(summed_terms[:, :, :kv_width], (1, 0, 2))
    value_grad = jnp.transpose(summed_terms[:, :, kv_width:], (1, 0, 2))
    query_back = (
        rotate_back(query_grad, cos_table, sin_table, turner)
        .astype(jnp.bfloat16)
        .reshape(tok_count, -1)
    )
    key_back = (
        rotate_back(key_grad, cos_table, sin_table, turner)
        .astype(jnp.bfloat16)
        .reshape(tok_count, -1)
    )
    value_back = value_grad.astype(jnp.bfloat16).reshape(tok_count, -1)
    flat_one = normed_one.reshape(tok_count, feat_dim)
    query_wgrad = jnp.einsum("td,te->de", flat_one, query_back, preferred_element_type=jnp.float32)
    key_wgrad = jnp.einsum("td,te->de", flat_one, key_back, preferred_element_type=jnp.float32)
    value_wgrad = jnp.einsum("td,te->de", flat_one, value_back, preferred_element_type=jnp.float32)
    normed_one_grad = (
        jnp.einsum("te,de->td", query_back, query_w, preferred_element_type=jnp.float32)
        + jnp.einsum("te,de->td", key_back, key_w, preferred_element_type=jnp.float32)
        + jnp.einsum("te,de->td", value_back, value_w, preferred_element_type=jnp.float32)
    )
    input_part, gain_one_grad = norm_back(
        inputs.reshape(tok_count, feat_dim),
        scale_one.reshape(tok_count, 1),
        gain_one_f,
        normed_one_grad,
    )
    input_grad = (
        (middle_grad + input_part).reshape(row_count, span_len, feat_dim).astype(jnp.bfloat16)
    )
    gain_one_sum, query_sum, key_wsum, value_wsum, output_sum, gain_two_sum, router_sum = (
        lax.psum_scatter(gain_one_grad, ("narrow", "wide"), scatter_dimension=0, tiled=True),
        lax.psum_scatter(query_wgrad, ("narrow", "wide"), scatter_dimension=0, tiled=True),
        lax.psum_scatter(key_wgrad, ("narrow", "wide"), scatter_dimension=0, tiled=True),
        lax.psum_scatter(value_wgrad, ("narrow", "wide"), scatter_dimension=0, tiled=True),
        lax.psum_scatter(output_wgrad, ("narrow", "wide"), scatter_dimension=0, tiled=True),
        lax.psum_scatter(gain_two_grad, ("narrow", "wide"), scatter_dimension=0, tiled=True),
        lax.psum_scatter(router_wgrad, ("narrow", "wide"), scatter_dimension=0, tiled=True),
    )
    gate_up_sum, down_sum = (
        lax.psum_scatter(
            gate_up_wgrad.astype(jnp.bfloat16), "narrow", scatter_dimension=1, tiled=True
        ).astype(jnp.float32),
        lax.psum_scatter(
            down_grad.astype(jnp.bfloat16), "narrow", scatter_dimension=1, tiled=True
        ).astype(jnp.float32),
    )
    return (
        block_out,
        input_grad,
        gain_one_sum,
        query_sum,
        key_wsum,
        value_wsum,
        output_sum,
        gain_two_sum,
        router_sum,
        gate_up_sum,
        down_sum,
        expert_load,
    )


MESH = pl.DeviceIdType.MESH
F32 = jnp.float32
BF16 = jnp.bfloat16
IN_HBM = pl.BlockSpec(memory_space=pl.ANY)
IN_VMEM = pl.BlockSpec(memory_space=pltpu.VMEM)
VMEM_BYTES = 60 * 1024 * 1024
NARROW = 4
WIDE = 8
GROUP = 16
TOKENS = 256
SPAN = 128
WIDTH = 1024
SEQ = 1024
SLOTS = 80
MINE = 2
CHUNK = 4
NT = (((1,), (1,)), ((), ()))
TN = (((0,), (0,)), ((), ()))


def mm(left, right, dims=(((1,), (0,)), ((), ()))):
    return lax.dot_general(left, right, dims, preferred_element_type=F32)


class Spot:
    def __init__(self):
        self.n = lax.axis_index("narrow")
        self.w = lax.axis_index("wide")
        self.core = lax.rem(self.w, 2)
        self.x = lax.rem(lax.div(self.w, 2), 2)
        self.y = lax.div(self.w, 4)
        self.half = lax.rem(self.n, 2)
        self.me = self.n * WIDE + self.w
        self.sib = self.w + 1 - 2 * self.core
        self.xn = self.w + 2 - 4 * self.x
        self.yn = self.w + 4 - 8 * self.y
        self.diag = self.xn + 4 - 8 * self.y
        self.mate = self.n + 1 - 2 * self.half
        self.slot = self.half * WIDE + self.w

    def wide(self, to):
        return (self.n, to)

    def greet(self, count):
        barrier = pltpu.get_barrier_semaphore()
        base = self.n - self.half

        def signal(step, carry):
            if count == WIDE:
                to = (self.n, lax.rem(self.w + step, WIDE))
            elif count == GROUP:
                other = lax.rem(self.slot + step, GROUP)
                to = (base + lax.div(other, WIDE), lax.rem(other, WIDE))
            else:
                other = lax.rem(self.me + step, NARROW * WIDE)
                to = (lax.div(other, WIDE), lax.rem(other, WIDE))
            pl.semaphore_signal(barrier, inc=1, device_id=to, device_id_type=MESH)
            return carry

        lax.fori_loop(1, count, signal, 0)
        pl.semaphore_wait(barrier, count - 1)


def remote(src, dst, send_sem, recv_sem, to):
    return pltpu.make_async_remote_copy(
        src_ref=src, dst_ref=dst, send_sem=send_sem, recv_sem=recv_sem, device_id=to, device_id_type=MESH
    )


def halves(ref, which):
    return ref.at[pl.ds(which * SPAN, SPAN)]


class PlaneGather:
    COPIES = 11

    def __init__(self, spot, own, out, base, send, recv):
        self.spot, self.own, self.out, self.base = spot, own, out, base
        self.send, self.recv = send, recv
        self.started = []

    def block(self, who):
        return self.out.at[self.base + who]

    def put(self, src, dst, number, to):
        copy = remote(src, dst, self.send.at[number], self.recv.at[number], self.spot.wide(to))
        copy.start()
        self.started.append(copy)

    def got(self, dst, number):
        remote(dst, dst, self.send.at[number], self.recv.at[number], self.spot.wide(self.spot.sib)).wait_recv()

    def begin(self):
        s = self.spot
        mine = self.block(s.w)
        self.put(halves(self.own, 0), halves(mine, 0), 0, s.xn)
        self.put(halves(self.own, 1), halves(mine, 1), 2, s.yn)
        self.put(halves(self.own, 1), halves(mine, 1), 1, s.xn)
        self.put(halves(self.own, 0), halves(mine, 0), 3, s.yn)
        self.put(self.own, mine, 4, s.sib)

    def middle(self):
        s = self.spot
        from_x, from_y = self.block(s.xn), self.block(s.yn)
        self.got(halves(from_x, 0), 0)
        self.put(halves(from_x, 0), halves(from_x, 0), 5, s.yn)
        self.got(halves(from_y, 1), 2)
        self.put(halves(from_y, 1), halves(from_y, 1), 6, s.xn)

    def late(self):
        s = self.spot
        from_x, from_y = self.block(s.xn), self.block(s.yn)
        self.got(halves(from_x, 1), 1)
        self.put(from_x, from_x, 7, s.sib)
        self.got(halves(from_y, 0), 3)
        self.put(from_y, from_y, 8, s.sib)

    def last(self):
        s = self.spot
        from_d = self.block(s.diag)
        self.got(halves(from_d, 0), 5)
        self.put(halves(from_d, 0), halves(from_d, 0), 9, s.sib)
        self.got(halves(from_d, 1), 6)
        self.put(halves(from_d, 1), halves(from_d, 1), 10, s.sib)

    def finish(self):
        s = self.spot
        sib = s.sib
        sib_x = sib + 2 - 4 * s.x
        sib_y = sib + 4 - 8 * s.y
        sib_d = sib_x + 4 - 8 * s.y
        self.got(self.block(sib), 4)
        self.got(self.block(sib_x), 7)
        self.got(self.block(sib_y), 8)
        self.got(halves(self.block(sib_d), 0), 9)
        self.got(halves(self.block(sib_d), 1), 10)
        for copy in self.started:
            copy.wait_send()


def gather_kernel(x_ref, w_ref, g_ref, seg_ref, x_all, w_all, g_all, seg_all, send, recv, local, ws, wr, gs, gr, ss, sr):
    spot = Spot()
    spot.greet(NARROW * WIDE)
    own = [
        pltpu.make_async_copy(x_ref, x_all.at[spot.w], local.at[0]),
        pltpu.make_async_copy(w_ref.at[:, pl.ds(pl.multiple_of(spot.w * 256, 256), 256)], w_all.at[spot.me], local.at[1]),
        pltpu.make_async_copy(g_ref, g_all.at[spot.me], local.at[2]),
        pltpu.make_async_copy(seg_ref, seg_all.at[spot.w], local.at[3]),
    ]
    gather = PlaneGather(spot, x_ref, x_all, 0, send, recv)
    gather.begin()
    for copy in own:
        copy.start()

    def others(step):
        other = lax.rem(spot.me + step, NARROW * WIDE)
        return other, lax.div(other, WIDE), lax.rem(other, WIDE)

    def weights(step, arriving):
        other, o_n, o_w = others(step)
        source = w_ref.at[:, pl.ds(pl.multiple_of(o_w * 256, 256), 256)]
        place = other if arriving else spot.me
        return (
            remote(source, w_all.at[place], ws.at[other], wr.at[place], (o_n, o_w)),
            remote(g_ref, g_all.at[place], gs.at[other], gr.at[place], (o_n, o_w)),
        )

    def documents(step, arriving):
        other = lax.rem(spot.w + step, WIDE)
        place = other if arriving else spot.w
        return remote(seg_ref, seg_all.at[place], ss.at[other], sr.at[place], spot.wide(other))

    def start(step, carry):
        for copy in weights(step, False):
            copy.start()
        return carry

    def start_documents(step, carry):
        documents(step, False).start()
        return carry

    lax.fori_loop(1, WIDE, start_documents, 0)
    lax.fori_loop(1, NARROW * WIDE, start, 0)
    gather.middle()
    gather.late()
    gather.last()

    def wait(step, carry):
        for copy in weights(step, False):
            copy.wait_send()
        for copy in weights(step, True):
            copy.wait_recv()
        return carry

    def wait_documents(step, carry):
        documents(step, False).wait_send()
        documents(step, True).wait_recv()
        return carry

    lax.fori_loop(1, WIDE, wait_documents, 0)
    lax.fori_loop(1, NARROW * WIDE, wait, 0)
    gather.finish()
    for copy in own:
        copy.wait()


def gather_call(x_own, w_own, g_own, seg_own):
    dma = pltpu.SemaphoreType.DMA
    return pl.pallas_call(
        gather_kernel,
        name="gather_inputs",
        out_shape=(
            jax.ShapeDtypeStruct((WIDE, TOKENS, WIDTH), BF16),
            jax.ShapeDtypeStruct((NARROW * WIDE, 32, 256), BF16),
            jax.ShapeDtypeStruct((NARROW * WIDE, 8, 128), F32),
            jax.ShapeDtypeStruct((WIDE, 8, 128), jnp.int32),
        ),
        in_specs=[IN_HBM] * 4,
        out_specs=(IN_HBM,) * 4,
        scratch_shapes=[
            dma((PlaneGather.COPIES,)),
            dma((PlaneGather.COPIES,)),
            dma((4,)),
            dma((NARROW * WIDE,)),
            dma((NARROW * WIDE,)),
            dma((NARROW * WIDE,)),
            dma((NARROW * WIDE,)),
            dma((WIDE,)),
            dma((WIDE,)),
        ],
        compiler_params=pltpu.CompilerParams(collective_id=1, has_side_effects=True),
    )(x_own, w_own, g_own, seg_own)


def lane_half():
    lanes = lax.broadcasted_iota(jnp.int32, (1, 128), 1)
    return lax.rem(lanes, 64) < 32


def turn(values, first_half):
    return jnp.where(first_half, -pltpu.roll(values, 96, 1), pltpu.roll(values, 32, 1))


def turn_back(values, first_half):
    return jnp.where(first_half, pltpu.roll(values, 96, 1), -pltpu.roll(values, 32, 1))


def gather_gain(gains):
    lane = lax.broadcasted_iota(jnp.int32, (128, WIDTH), 0)
    column = lax.broadcasted_iota(jnp.int32, (128, WIDTH), 1)
    spread = (lax.rem(column, 32) == lane).astype(BF16)
    tiled = mm(gains.astype(BF16), spread)
    owner = lax.broadcasted_iota(jnp.int32, (32, WIDTH), 0)
    place = lax.broadcasted_iota(jnp.int32, (32, WIDTH), 1)
    return jnp.sum(jnp.where(lax.div(place, 32) == owner, tiled, 0.0), axis=0, keepdims=True)


def attend_kernel(x_ref, w_ref, g_ref, seg_ref, cos_ref, sin_ref, freq_ref, h1_ref, qkv_ref, lse_ref, o_ref, angle_ref, start_ref, gain_ref):
    row = pl.program_id(0)
    first_half = lane_half()
    lanes = lax.broadcasted_iota(jnp.int32, (1, 128), 1)
    weights = w_ref[...].reshape(WIDTH, 256)
    gains = g_ref[...]
    gain_one = gather_gain(gains[:, 0, :])
    gain_two = gather_gain(gains[:, 1, :])
    gain_ref[...] = jnp.concatenate([gain_one, gain_two, jnp.zeros((6, WIDTH), F32)], axis=0)
    segs = [jnp.where(row == 0, seg_ref[c, 0:1, :], seg_ref[c, 1:2, :]) for c in range(WIDE)]
    counts = []
    for doc in range(5):
        total = jnp.zeros((1, 128), F32)
        for c in range(WIDE):
            total = total + (segs[c] == doc).astype(F32)
        counts.append(jnp.sum(total, axis=1, keepdims=True))
    starts = [jnp.zeros((1, 1), F32)]
    for doc in range(5):
        starts.append(starts[-1] + counts[doc])
    start_rows = jnp.concatenate(starts + starts[:2], axis=0)
    start_angle = start_rows * freq_ref[0:1, :]
    start_cos = jnp.cos(start_angle)
    start_sin = jnp.sin(start_angle)

    for i in range(4):
        tokens = pl.ds(i * 256, 256)
        seg_cols = [
            jnp.transpose(jnp.broadcast_to(segs[2 * i + part].astype(F32), (128, 128))) for part in range(2)
        ]
        seg_col = jnp.concatenate(seg_cols, axis=0)
        start_col = jnp.zeros((256, 128), F32)
        cos_s = jnp.broadcast_to(start_cos[0:1], (256, 128))
        sin_s = jnp.broadcast_to(start_sin[0:1], (256, 128))
        for doc in range(1, 6):
            here = seg_col == float(doc)
            start_col = jnp.where(here, starts[doc], start_col)
            cos_s = jnp.where(here, start_cos[doc : doc + 1], cos_s)
            sin_s = jnp.where(here, start_sin[doc : doc + 1], sin_s)
        start_ref[0, tokens, :] = start_col
        cos_t = cos_ref[tokens, :]
        sin_t = sin_ref[tokens, :]
        cosine = cos_t * cos_s + sin_t * sin_s
        sine = sin_t * cos_s - cos_t * sin_s
        angle_ref[0, tokens, 0:128] = cosine
        angle_ref[0, tokens, 128:256] = sine
        is_key = lanes < 64
        x = x_ref[2 * i : 2 * i + 2, 0].reshape(256, WIDTH).astype(F32)
        scale = lax.rsqrt(jnp.mean(x * x, axis=1, keepdims=True) + EPSILON)
        h1 = (x * scale * gain_one).astype(BF16)
        h1_ref[0, tokens, :] = h1
        qkv = mm(h1, weights)
        q = qkv[:, 0:128]
        kv = qkv[:, 128:256]
        q = q * cosine + turn(q, first_half) * sine
        kv = jnp.where(is_key, kv * cosine + turn(kv, first_half) * sine, kv)
        q = q.astype(BF16)
        kv = kv.astype(BF16)
        qkv_ref[0, tokens, 0:128] = q
        qkv_ref[0, tokens, 128:256] = kv
        length = 256 * (i + 1)
        keys = qkv_ref[0, 0:length, 128:192]
        values = qkv_ref[0, 0:length, 192:256]
        place_key = lax.broadcasted_iota(jnp.int32, (256, length), 1).astype(F32)
        place_query = (lax.broadcasted_iota(jnp.int32, (256, length), 0) + 256 * i).astype(F32)
        allowed = (place_key <= place_query) & (place_key >= start_col[:, 0:1])
        outs, logs = [], []
        for head in range(2):
            query = q[:, 64 * head : 64 * head + 64]
            scores = jnp.where(allowed, mm(query, keys, NT) * (HEAD_DIM**-0.5), MASKED)
            top = jnp.max(scores, axis=1, keepdims=True)
            log_total = top + jnp.log(jnp.sum(jnp.exp(scores - top), axis=1, keepdims=True))
            weights_b = jnp.exp(scores - log_total).astype(BF16)
            outs.append(mm(weights_b, values))
            logs.append(log_total)
        o_ref[0, tokens, :] = jnp.concatenate(outs, axis=1).astype(BF16)
        lse_ref[0, tokens, :] = jnp.where(is_key, logs[0], logs[1])


def attend_call(x_all, w_all, g_all, seg_all, cos_table, sin_table, freq):
    def whole(shape):
        return pl.BlockSpec(shape, lambda r: (0,) * len(shape))

    def by_row(lanes):
        return pl.BlockSpec((1, SEQ, lanes), lambda r: (r, 0, 0))

    return pl.pallas_call(
        attend_kernel,
        name="attend",
        grid=(2,),
        out_shape=(
            jax.ShapeDtypeStruct((2, SEQ, WIDTH), BF16),
            jax.ShapeDtypeStruct((2, SEQ, 256), BF16),
            jax.ShapeDtypeStruct((2, SEQ, 128), F32),
            jax.ShapeDtypeStruct((2, SEQ, 128), BF16),
            jax.ShapeDtypeStruct((2, SEQ, 256), F32),
            jax.ShapeDtypeStruct((2, SEQ, 128), F32),
            jax.ShapeDtypeStruct((8, WIDTH), F32),
        ),
        in_specs=[
            pl.BlockSpec((WIDE, 1, SPAN, WIDTH), lambda r: (0, r, 0, 0)),
            whole((NARROW * WIDE, 32, 256)),
            whole((NARROW * WIDE, 8, 128)),
            whole((WIDE, 8, 128)),
            whole((SEQ, 128)),
            whole((SEQ, 128)),
            whole((8, 128)),
        ],
        out_specs=(by_row(WIDTH), by_row(256), by_row(128), by_row(128), by_row(256), by_row(128), whole((8, WIDTH))),
        compiler_params=pltpu.CompilerParams(vmem_limit_bytes=VMEM_BYTES),
    )(x_all.reshape(WIDE, 2, SPAN, WIDTH), w_all, g_all, seg_all, cos_table, sin_table, freq)


def project_kernel(
    o_ref, x_ref, w_ref, gain_ref, ids_ref,
    h2_all, table_all, mid_ref, gate_ref,
    o_full, h2_own, table_own, os, orv, s0, r0, s1, r1, ts, tr, zs, zr, local,
):
    spot = Spot()
    spot.greet(GROUP)

    def heads(step, arriving):
        other = lax.rem(spot.w + step, WIDE)
        place = other if arriving else spot.w
        return remote(
            o_ref.at[:, pl.ds(pl.multiple_of(other * SPAN, SPAN), SPAN), :],
            o_full.at[:, :, pl.ds(pl.multiple_of(place * 128, 128), 128)],
            os.at[other], orv.at[place], spot.wide(other),
        )

    def start(step, carry):
        heads(step, False).start()
        return carry

    lax.fori_loop(1, WIDE, start, 0)
    mine = pltpu.make_async_copy(
        o_ref.at[:, pl.ds(pl.multiple_of(spot.w * SPAN, SPAN), SPAN), :],
        o_full.at[:, :, pl.ds(pl.multiple_of(spot.w * 128, 128), 128)],
        local.at[0],
    )
    mine.start()

    expert = lax.broadcasted_iota(jnp.int32, (32, TOKENS), 0)
    named = jnp.zeros((32, TOKENS), F32)
    for k in range(TOP):
        named = jnp.where(expert == ids_ref[k : k + 1, :], 1.0, named)
    before = lax.broadcasted_iota(jnp.int32, (TOKENS, TOKENS), 0) < lax.broadcasted_iota(
        jnp.int32, (TOKENS, TOKENS), 1
    )
    places = mm(named.astype(BF16), before.astype(BF16))
    kept = jnp.where((named > 0.5) & (places < float(CAP)), places, -1.0)

    def wait(step, carry):
        heads(step, False).wait_send()
        heads(step, True).wait_recv()
        return carry

    lax.fori_loop(1, WIDE, wait, 0)
    mine.wait()

    attended = o_full[...].reshape(TOKENS, WIDTH)
    mid = x_ref[...].astype(F32) + mm(attended, w_ref[:, 0:WIDTH])
    mid_ref[...] = mid
    scale = lax.rsqrt(jnp.mean(mid * mid, axis=1, keepdims=True) + EPSILON)
    h2 = (mid * scale * gain_ref[1:2, :]).astype(BF16)
    h2_own[...] = h2
    first = PlaneGather(spot, h2_own, h2_all, spot.half * WIDE, s0, r0)
    first.begin()
    there = h2_all.at[spot.slot]
    mate_slot = (1 - spot.half) * WIDE + spot.w
    arriving = h2_all.at[mate_slot]
    across = remote(h2_own, there, zs.at[0], zr.at[0], (spot.mate, spot.w))
    across.start()
    keep_own = pltpu.make_async_copy(h2_own, there, local.at[1])
    keep_own.start()

    logits = jnp.transpose(mm(h2, w_ref[:, WIDTH : WIDTH + 128]))[0:32]
    chosen = jnp.where(named > 0.5, logits, MASKED)
    rise = jnp.where(named > 0.5, jnp.exp(chosen - jnp.max(chosen, axis=0, keepdims=True)), 0.0)
    gate = rise / jnp.sum(rise, axis=0, keepdims=True)
    gate_ref[0:32, :] = gate
    gate_ref[32:64, :] = named
    for owner in range(GROUP):
        table_own[owner, 0:2, :] = kept[2 * owner : 2 * owner + 2]
        table_own[owner, 2:4, :] = gate[2 * owner : 2 * owner + 2]
        table_own[owner, 4:8, :] = jnp.zeros((4, TOKENS), F32)

    def tables(step, arriving):
        other = lax.rem(spot.slot + step, GROUP)
        o_half, o_w = lax.div(other, WIDE), lax.rem(other, WIDE)
        place = other if arriving else spot.slot
        return remote(
            table_own.at[2 * o_w + o_half], table_all.at[place], ts.at[other], tr.at[place],
            (spot.n - spot.half + o_half, o_w),
        )

    def start_table(step, carry):
        tables(step, False).start()
        return carry

    lax.fori_loop(1, GROUP, start_table, 0)
    table_mine = pltpu.make_async_copy(
        table_own.at[2 * spot.w + spot.half], table_all.at[spot.slot], local.at[2]
    )
    table_mine.start()

    first.middle()
    remote(arriving, arriving, zs.at[0], zr.at[0], (spot.mate, spot.w)).wait_recv()
    second = PlaneGather(spot, arriving, h2_all, (1 - spot.half) * WIDE, s1, r1)
    second.begin()
    first.late()
    first.last()
    second.middle()
    second.late()
    second.last()

    def wait_table(step, carry):
        tables(step, False).wait_send()
        tables(step, True).wait_recv()
        return carry

    lax.fori_loop(1, GROUP, wait_table, 0)
    first.finish()
    second.finish()
    across.wait_send()
    keep_own.wait()
    table_mine.wait()


def project_call(o_heads, x_own, w_out, gain_rows, ids):
    dma = pltpu.SemaphoreType.DMA
    return pl.pallas_call(
        project_kernel,
        name="project",
        out_shape=(
            jax.ShapeDtypeStruct((GROUP, TOKENS, WIDTH), BF16),
            jax.ShapeDtypeStruct((GROUP, 8, TOKENS), F32),
            jax.ShapeDtypeStruct((TOKENS, WIDTH), F32),
            jax.ShapeDtypeStruct((64, TOKENS), F32),
        ),
        in_specs=[IN_HBM] + [IN_VMEM] * 4,
        out_specs=(IN_HBM, IN_HBM, IN_VMEM, IN_VMEM),
        scratch_shapes=[
            pltpu.VMEM((2, SPAN, WIDTH), BF16),
            pltpu.VMEM((TOKENS, WIDTH), BF16),
            pltpu.VMEM((GROUP, 8, TOKENS), F32),
            dma((WIDE,)),
            dma((WIDE,)),
            dma((PlaneGather.COPIES,)),
            dma((PlaneGather.COPIES,)),
            dma((PlaneGather.COPIES,)),
            dma((PlaneGather.COPIES,)),
            dma((GROUP,)),
            dma((GROUP,)),
            dma((1,)),
            dma((1,)),
            dma((3,)),
        ],
        compiler_params=pltpu.CompilerParams(collective_id=2, has_side_effects=True, vmem_limit_bytes=VMEM_BYTES),
    )(o_heads, x_own, w_out, gain_rows, ids)


def load_quarters(pieces, target, depth, sems, base):
    n = lax.axis_index("narrow")
    half, pair = lax.rem(n, 2), lax.div(n, 2)
    mate = n + 1 - 2 * half
    far = n + 2 - 4 * pair
    far_mate = mate + 2 - 4 * pair
    copies = []
    for number, (piece, quarter) in enumerate(zip(pieces, (n, mate, far, far_mate))):
        copies.append(
            pltpu.make_async_copy(
                piece,
                target.at[:, pl.ds(pl.multiple_of(quarter * depth, depth), depth), :],
                sems.at[base + number],
            )
        )
    return copies


def pick(table_ref, source, expert):
    slot = lax.broadcasted_iota(jnp.int32, (SLOTS, TOKENS), 0).astype(F32)
    return slot == table_ref[source, expert : expert + 1, :]


def expert_kernel(
    h2_ref, dy_ref, table_ref, gu0, gu1, gu2, gu3, d0, d1, d2, d3,
    rows_ref, da_ref, y_ref, dgate_ref, down_grad_ref,
    w_gu, w_down, down_sum, sems,
):
    step = pl.program_id(0)

    @pl.when(step == 0)
    def _():
        copies = load_quarters((gu0, gu1, gu2, gu3), w_gu, 256, sems, 0) + load_quarters(
            (d0, d1, d2, d3), w_down, 128, sems, 4
        )
        for copy in copies:
            copy.start()
        down_sum[...] = jnp.zeros_like(down_sum)
        for copy in copies:
            copy.wait()

    picks = [[], []]
    gated = [[], []]
    dgate_ref[...] = jnp.zeros_like(dgate_ref)
    for e in range(MINE):
        masks = [pick(table_ref, s, e) for s in range(CHUNK)]
        hots = [jnp.where(mask, 1.0, 0.0).astype(BF16) for mask in masks]
        picks[e] = hots
        rows = jnp.concatenate([mm(hots[s], h2_ref[s]) for s in range(CHUNK)], axis=0).astype(BF16)
        grad_rows = jnp.concatenate([mm(hots[s], dy_ref[s, 0]) for s in range(CHUNK)], axis=0)
        gates = jnp.concatenate(
            [
                jnp.sum(jnp.where(masks[s], table_ref[s, 2 + e : 3 + e, :], 0.0), axis=1, keepdims=True)
                for s in range(CHUNK)
            ],
            axis=0,
        )
        rows_ref[0, e] = rows
        g = mm(rows, w_gu[e, :, 0:FF])
        u = mm(rows, w_gu[e, :, FF : 2 * FF])
        sigmoid = 1.0 / (1.0 + jnp.exp(-g))
        active = g * sigmoid
        hidden = (active * u).astype(BF16)
        y = mm(hidden, w_down[e]).astype(BF16).astype(F32)
        slot_dgate = jnp.sum(y * grad_rows, axis=1, keepdims=True)
        for s in range(CHUNK):
            part = slot_dgate[s * SLOTS : (s + 1) * SLOTS]
            dgate_ref[s, e : e + 1, :] = jnp.sum(jnp.where(masks[s], part, 0.0), axis=0, keepdims=True)
        gated[e] = (y * gates).astype(BF16)
        dy_pair = (grad_rows * gates).astype(BF16)
        down_sum[e] += mm(hidden, dy_pair, TN)
        dhid = mm(dy_pair, w_down[e], NT)
        da_ref[0, e, :, 0:FF] = (dhid * u * (sigmoid * (1.0 + g * (1.0 - sigmoid)))).astype(BF16)
        da_ref[0, e, :, FF : 2 * FF] = (dhid * active).astype(BF16)
    for s in range(CHUNK):
        hot = jnp.concatenate([picks[e][s] for e in range(MINE)], axis=0)
        back = jnp.concatenate([gated[e][s * SLOTS : (s + 1) * SLOTS] for e in range(MINE)], axis=0)
        y_ref[s, 0] = mm(hot, back, TN).astype(BF16)

    @pl.when(step == pl.num_programs(0) - 1)
    def _():
        down_grad_ref[...] = down_sum[...].astype(BF16)


def expert_call(h2_all, dy_all, table_all, gate_up, down):
    steps = GROUP // CHUNK
    block = pl.BlockSpec((CHUNK, TOKENS, WIDTH), lambda c: (c, 0, 0))
    small = pl.BlockSpec((CHUNK, 8, TOKENS), lambda c: (c, 0, 0))
    slots = pl.BlockSpec((1, MINE, CHUNK * SLOTS, WIDTH), lambda c: (c, 0, 0, 0))
    steps_half = WIDE // CHUNK
    to_wide = pl.BlockSpec(
        (CHUNK, 1, TOKENS, WIDTH), lambda c: (lax.rem(c, steps_half), lax.div(c, steps_half), 0, 0)
    )
    flops = 2 * GROUP * SLOTS * MINE * WIDTH * FF * 7
    return pl.pallas_call(
        expert_kernel,
        name="experts",
        grid=(steps,),
        out_shape=(
            jax.ShapeDtypeStruct((steps, MINE, CHUNK * SLOTS, WIDTH), BF16),
            jax.ShapeDtypeStruct((steps, MINE, CHUNK * SLOTS, 2 * FF), BF16),
            jax.ShapeDtypeStruct((WIDE, 2, TOKENS, WIDTH), BF16),
            jax.ShapeDtypeStruct((GROUP, 8, TOKENS), F32),
            jax.ShapeDtypeStruct((MINE, FF, WIDTH), BF16),
        ),
        in_specs=[block, to_wide, small] + [IN_HBM] * 8,
        out_specs=(slots, slots, to_wide, small, pl.BlockSpec((MINE, FF, WIDTH), lambda c: (0, 0, 0))),
        scratch_shapes=[
            pltpu.VMEM((MINE, WIDTH, 2 * FF), BF16),
            pltpu.VMEM((MINE, FF, WIDTH), BF16),
            pltpu.VMEM((MINE, FF, WIDTH), F32),
            pltpu.SemaphoreType.DMA((8,)),
        ],
        compiler_params=pltpu.CompilerParams(vmem_limit_bytes=VMEM_BYTES),
        cost_estimate=pl.CostEstimate(flops=flops, bytes_accessed=40 << 20, transcendentals=1 << 20),
    )(h2_all, dy_all, table_all, *gate_up, *down)


def gate_up_grad_kernel(rows_ref, da_ref, out_ref):
    rows = rows_ref[:, 0].reshape(GROUP * SLOTS, WIDTH // 2)
    da = da_ref[:, 0].reshape(GROUP * SLOTS, 2 * FF)
    out_ref[0] = mm(rows, da, TN).astype(BF16)


def gate_up_grad_call(rows, da):
    steps = GROUP // CHUNK
    return pl.pallas_call(
        gate_up_grad_kernel,
        name="gate_up_grad",
        grid=(MINE, 2),
        out_shape=jax.ShapeDtypeStruct((MINE, WIDTH, 2 * FF), BF16),
        in_specs=[
            pl.BlockSpec((steps, 1, CHUNK * SLOTS, WIDTH // 2), lambda e, d: (0, e, 0, d)),
            pl.BlockSpec((steps, 1, CHUNK * SLOTS, 2 * FF), lambda e, d: (0, e, 0, 0)),
        ],
        out_specs=pl.BlockSpec((1, WIDTH // 2, 2 * FF), lambda e, d: (e, d, 0)),
        compiler_params=pltpu.CompilerParams(vmem_limit_bytes=VMEM_BYTES),
        cost_estimate=pl.CostEstimate(
            flops=2 * GROUP * SLOTS * MINE * WIDTH * 2 * FF, bytes_accessed=14 << 20, transcendentals=0
        ),
    )(rows, da)


def rows_grad_kernel(da_ref, table_ref, gu0, gu1, gu2, gu3, out_ref, w_gu, sems):
    step = pl.program_id(0)

    @pl.when(step == 0)
    def _():
        copies = load_quarters((gu0, gu1, gu2, gu3), w_gu, 256, sems, 0)
        for copy in copies:
            copy.start()
        for copy in copies:
            copy.wait()

    grads = [mm(da_ref[0, e], w_gu[e], NT).astype(BF16) for e in range(MINE)]
    for s in range(CHUNK):
        hot = jnp.concatenate(
            [jnp.where(pick(table_ref, s, e), 1.0, 0.0).astype(BF16) for e in range(MINE)], axis=0
        )
        back = jnp.concatenate([grads[e][s * SLOTS : (s + 1) * SLOTS] for e in range(MINE)], axis=0)
        out_ref[s] = mm(hot, back, TN).astype(BF16)


def rows_grad_call(da, table_all, gate_up):
    steps = GROUP // CHUNK
    return pl.pallas_call(
        rows_grad_kernel,
        name="rows_grad",
        grid=(steps,),
        out_shape=jax.ShapeDtypeStruct((GROUP, TOKENS, WIDTH), BF16),
        in_specs=[
            pl.BlockSpec((1, MINE, CHUNK * SLOTS, 2 * FF), lambda c: (c, 0, 0, 0)),
            pl.BlockSpec((CHUNK, 8, TOKENS), lambda c: (c, 0, 0)),
        ]
        + [IN_HBM] * 4,
        out_specs=pl.BlockSpec((CHUNK, TOKENS, WIDTH), lambda c: (c, 0, 0)),
        scratch_shapes=[pltpu.VMEM((MINE, WIDTH, 2 * FF), BF16), pltpu.SemaphoreType.DMA((4,))],
        compiler_params=pltpu.CompilerParams(vmem_limit_bytes=VMEM_BYTES),
        cost_estimate=pl.CostEstimate(
            flops=2 * GROUP * SLOTS * MINE * WIDTH * 2 * FF, bytes_accessed=20 << 20, transcendentals=0
        ),
    )(da, table_all, *gate_up)


def widen(ref_value):
    return ref_value.astype(F32)


class PlaneReduce:
    COPIES = 10

    def __init__(self, spot, part, base, acc, from_core, from_one, from_two, send, recv, local):
        self.spot, self.part, self.base = spot, part, base
        self.acc, self.from_core, self.from_one, self.from_two = acc, from_core, from_one, from_two
        self.send, self.recv, self.local = send, recv, local
        self.started = []
        s = spot
        self.q_own = 2 * s.y + s.x
        self.q_x = 2 * s.y + 1 - s.x
        self.q_y = 2 - 2 * s.y + s.x
        self.q_d = 3 - self.q_own

    def put(self, src, dst, number, to):
        copy = remote(src, dst, self.send.at[number], self.recv.at[number], self.spot.wide(to))
        copy.start()
        self.started.append(copy)

    def got(self, dst, number):
        remote(dst, dst, self.send.at[number], self.recv.at[number], self.spot.wide(self.spot.sib)).wait_recv()

    def begin(self):
        s = self.spot
        self.loads = []
        for q in range(4):
            self.put(self.part.at[self.base + 2 * q + 1 - s.core], self.from_core.at[q], q, s.sib)
            copy = pltpu.make_async_copy(self.part.at[self.base + 2 * q + s.core], self.acc.at[q], self.local.at[q])
            copy.start()
            self.loads.append(copy)

    def across_core(self):
        s = self.spot
        for q in range(4):
            self.loads[q].wait()
            self.got(self.from_core.at[q], q)
            self.acc[q] = (widen(self.acc[q]) + widen(self.from_core[q])).astype(BF16)
        self.put(halves(self.acc.at[self.q_d], 0), self.from_one.at[1], 5, s.xn)
        self.put(halves(self.acc.at[self.q_d], 1), self.from_one.at[3], 7, s.yn)
        self.put(halves(self.acc.at[self.q_x], 0), self.from_one.at[0], 4, s.xn)
        self.put(halves(self.acc.at[self.q_y], 1), self.from_one.at[2], 6, s.yn)

    def across_one(self):
        s = self.spot
        self.got(self.from_one.at[1], 5)
        upper = halves(self.acc.at[self.q_y], 0)
        upper[...] = (widen(upper[...]) + widen(self.from_one[1])).astype(BF16)
        self.put(upper, self.from_two.at[0], 8, s.yn)
        self.got(self.from_one.at[3], 7)
        lower = halves(self.acc.at[self.q_x], 1)
        lower[...] = (widen(lower[...]) + widen(self.from_one[3])).astype(BF16)
        self.put(lower, self.from_two.at[1], 9, s.xn)

    def total(self, out):
        self.got(self.from_one.at[0], 4)
        self.got(self.from_two.at[0], 8)
        own = self.acc.at[self.q_own]
        out[0:SPAN, :] = widen(own[0:SPAN, :]) + widen(self.from_one[0]) + widen(self.from_two[0])
        self.got(self.from_one.at[2], 6)
        self.got(self.from_two.at[1], 9)
        out[SPAN:TOKENS, :] = widen(own[SPAN:TOKENS, :]) + widen(self.from_one[2]) + widen(self.from_two[1])

    def finish(self):
        for copy in self.started:
            copy.wait_send()


def reduce_scratch():
    dma = pltpu.SemaphoreType.DMA
    return [
        pltpu.VMEM((2, 4, TOKENS, WIDTH), BF16),
        pltpu.VMEM((2, 4, TOKENS, WIDTH), BF16),
        pltpu.VMEM((2, 4, SPAN, WIDTH), BF16),
        pltpu.VMEM((2, 2, SPAN, WIDTH), BF16),
        pltpu.VMEM((TOKENS, WIDTH), F32),
        pltpu.VMEM((TOKENS, WIDTH), BF16),
        pltpu.VMEM((TOKENS, WIDTH), BF16),
        dma((2, PlaneReduce.COPIES)),
        dma((2, PlaneReduce.COPIES)),
        dma((2, 4)),
        dma((1,)),
        dma((1,)),
    ]


def group_reduce(spot, part, scratch):
    acc, from_core, from_one, from_two, total, mate_send, mate_recv, send, recv, local, zs, zr = scratch
    sums = []
    for which, base in ((0, (1 - spot.half) * WIDE), (1, spot.half * WIDE)):
        sums.append(
            PlaneReduce(
                spot, part, base, acc.at[which], from_core.at[which], from_one.at[which], from_two.at[which],
                send.at[which], recv.at[which], local.at[which],
            )
        )
    theirs, ours = sums
    theirs.begin()
    ours.begin()
    theirs.across_core()
    ours.across_core()
    theirs.across_one()
    theirs.total(total)
    mate_send[...] = total[...].astype(BF16)
    across = remote(mate_send, mate_recv, zs.at[0], zr.at[0], (spot.mate, spot.w))
    across.start()
    ours.across_one()
    ours.total(total)
    across.wait_recv()
    total[...] += widen(mate_recv[...])
    theirs.finish()
    ours.finish()
    across.wait_send()


def collect_kernel(
    part_ref, dgate_ref, h2_ref, mid_ref, gate_ref, w_ref, gain_ref, dy_ref,
    dattn_all, dmid_ref, small_ref,
    dgate_all, h2_own, dattn_own, ts, tr, s0, r0, local, *scratch,
):
    spot = Spot()
    spot.greet(GROUP)

    def tables(step, arriving):
        other = lax.rem(spot.slot + step, GROUP)
        o_half, o_w = lax.div(other, WIDE), lax.rem(other, WIDE)
        place = other if arriving else spot.slot
        return remote(
            dgate_ref.at[other], dgate_all.at[place], ts.at[other], tr.at[place],
            (spot.n - spot.half + o_half, o_w),
        )

    def start_table(step, carry):
        tables(step, False).start()
        return carry

    lax.fori_loop(1, GROUP, start_table, 0)
    mine = pltpu.make_async_copy(dgate_ref.at[spot.slot], dgate_all.at[spot.slot], local.at[0])
    mine.start()
    load = pltpu.make_async_copy(h2_ref.at[spot.slot], h2_own, local.at[1])
    load.start()
    group_reduce(spot, part_ref, scratch)

    def wait_table(step, carry):
        tables(step, False).wait_send()
        tables(step, True).wait_recv()
        return carry

    lax.fori_loop(1, GROUP, wait_table, 0)
    mine.wait()
    load.wait()

    total = scratch[4]
    gate = gate_ref[0:32, :]
    dgate = jnp.concatenate([dgate_all[(o % 2) * WIDE + o // 2, 0:2, :] for o in range(GROUP)], axis=0)
    dsel = gate * (dgate - jnp.sum(gate * dgate, axis=0, keepdims=True))
    dlogits = jnp.concatenate([dsel, jnp.zeros((96, TOKENS), F32)], axis=0)
    dh2 = total[...] + mm(jnp.transpose(dlogits).astype(BF16), w_ref[:, WIDTH : WIDTH + 128], NT)
    small_ref[0:32, :] = mm(dsel.astype(BF16), h2_own[...])
    mid = mid_ref[...]
    scale = lax.rsqrt(jnp.mean(mid * mid, axis=1, keepdims=True) + EPSILON)
    small_ref[32:33, :] = jnp.sum(dh2 * mid * scale, axis=0, keepdims=True)
    lane = lax.broadcasted_iota(jnp.int32, (32, WIDTH), 1)
    column = lax.broadcasted_iota(jnp.int32, (32, WIDTH), 0)
    count = jnp.sum(gate_ref[32:64, :], axis=1, keepdims=True)
    small_ref[33:34, :] = jnp.sum(jnp.where(lax.rem(lane, 128) == column, count, 0.0), axis=0, keepdims=True)
    small_ref[34:40, :] = jnp.zeros((6, WIDTH), F32)
    weighted = dh2 * gain_ref[1:2, :]
    inner = jnp.mean(weighted * mid, axis=1, keepdims=True)
    dmid = dy_ref[...].astype(F32) + weighted * scale - mid * (scale * scale * scale) * inner
    dmid_ref[...] = dmid
    dattn_own[...] = dmid.astype(BF16)
    gather = PlaneGather(spot, dattn_own, dattn_all, 0, s0, r0)
    gather.begin()
    keep = pltpu.make_async_copy(dattn_own, dattn_all.at[spot.w], local.at[0])
    keep.start()
    gather.middle()
    gather.late()
    gather.last()
    gather.finish()
    keep.wait()


def collect_call(part, dgate, h2_all, mid, gate, w_out, gain_rows, dy_own):
    dma = pltpu.SemaphoreType.DMA
    return pl.pallas_call(
        collect_kernel,
        name="collect",
        out_shape=(
            jax.ShapeDtypeStruct((WIDE, TOKENS, WIDTH), BF16),
            jax.ShapeDtypeStruct((TOKENS, WIDTH), F32),
            jax.ShapeDtypeStruct((40, WIDTH), F32),
        ),
        in_specs=[IN_HBM] * 3 + [IN_VMEM] * 5,
        out_specs=(IN_HBM, IN_VMEM, IN_VMEM),
        scratch_shapes=[
            pltpu.VMEM((GROUP, 8, TOKENS), F32),
            pltpu.VMEM((TOKENS, WIDTH), BF16),
            pltpu.VMEM((TOKENS, WIDTH), BF16),
            dma((GROUP,)),
            dma((GROUP,)),
            dma((PlaneGather.COPIES,)),
            dma((PlaneGather.COPIES,)),
            dma((2,)),
        ]
        + reduce_scratch(),
        compiler_params=pltpu.CompilerParams(collective_id=3, has_side_effects=True, vmem_limit_bytes=VMEM_BYTES),
    )(part, dgate, h2_all, mid, gate, w_out, gain_rows, dy_own)


def attend_back_kernel(
    dattn_ref, w_ref, h1_ref, qkv_ref, lse_ref, o_ref, angle_ref, start_ref,
    dqkv_ref, wgrad_ref, ograd_ref,
    do_ref, dkv_ref, wsum, osum,
):
    row = pl.program_id(0)
    first_half = lane_half()
    is_key = lax.broadcasted_iota(jnp.int32, (1, 128), 1) < 64

    @pl.when(row == 0)
    def _():
        wsum[...] = jnp.zeros_like(wsum)
        osum[...] = jnp.zeros_like(osum)

    dattn = dattn_ref[:, 0].reshape(SEQ, WIDTH)
    do_ref[...] = mm(dattn, w_ref[...], NT).astype(BF16)
    osum[...] += mm(o_ref[0], dattn, TN)
    dkv_ref[...] = jnp.zeros_like(dkv_ref)
    for i in range(4):
        tokens = pl.ds(i * 256, 256)
        length = 256 * (i + 1)
        keys = qkv_ref[0, 0:length, 128:192]
        values = qkv_ref[0, 0:length, 192:256]
        place_key = lax.broadcasted_iota(jnp.int32, (256, length), 1).astype(F32)
        place_query = (lax.broadcasted_iota(jnp.int32, (256, length), 0) + 256 * i).astype(F32)
        allowed = (place_key <= place_query) & (place_key >= start_ref[0, tokens, 0:1])
        query_grads = []
        dk = jnp.zeros((length, HEAD_DIM), F32)
        dv = jnp.zeros((length, HEAD_DIM), F32)
        for head in range(2):
            part = slice(64 * head, 64 * head + 64)
            query = qkv_ref[0, tokens, part]
            do = do_ref[tokens, part]
            log_total = lse_ref[0, tokens, 64 * head : 64 * head + 1]
            scores = jnp.where(allowed, mm(query, keys, NT) * (HEAD_DIM**-0.5), MASKED)
            weights = jnp.exp(scores - log_total)
            dp = mm(do, values, NT)
            delta = jnp.sum(weights * dp, axis=1, keepdims=True)
            ds = (weights * (dp - delta)).astype(BF16)
            query_grads.append(mm(ds, keys) * (HEAD_DIM**-0.5))
            dk = dk + mm(ds, query, TN)
            dv = dv + mm(weights.astype(BF16), do, TN)
        dkv_ref[0:length, :] += jnp.concatenate([dk * (HEAD_DIM**-0.5), dv], axis=1)
        dq = jnp.concatenate(query_grads, axis=1)
        cosine = angle_ref[0, tokens, 0:128]
        sine = angle_ref[0, tokens, 128:256]
        dqkv_ref[0, tokens, 0:128] = (dq * cosine + turn_back(dq * sine, first_half)).astype(BF16)
    for i in range(4):
        tokens = pl.ds(i * 256, 256)
        cosine = angle_ref[0, tokens, 0:128]
        sine = angle_ref[0, tokens, 128:256]
        dkv = dkv_ref[tokens, :]
        turned = dkv * cosine + turn_back(dkv * sine, first_half)
        dqkv_ref[0, tokens, 128:256] = jnp.where(is_key, turned, dkv).astype(BF16)
    wsum[...] += mm(h1_ref[0], dqkv_ref[0], TN)

    @pl.when(row == 1)
    def _():
        wgrad_ref[...] = wsum[...].astype(BF16)
        ograd_ref[...] = osum[...].astype(BF16)


def attend_back_call(dattn_all, w_rows, h1, qkv, lse, o_heads, angle, start):
    def by_row(lanes):
        return pl.BlockSpec((1, SEQ, lanes), lambda r: (r, 0, 0))

    def whole(shape):
        return pl.BlockSpec(shape, lambda r: (0,) * len(shape))

    return pl.pallas_call(
        attend_back_kernel,
        name="attend_back",
        grid=(2,),
        out_shape=(
            jax.ShapeDtypeStruct((2, SEQ, 256), BF16),
            jax.ShapeDtypeStruct((WIDTH, 256), BF16),
            jax.ShapeDtypeStruct((128, WIDTH), BF16),
        ),
        in_specs=[
            pl.BlockSpec((WIDE, 1, SPAN, WIDTH), lambda r: (0, r, 0, 0)),
            whole((128, WIDTH)),
            by_row(WIDTH),
            by_row(256),
            by_row(128),
            by_row(128),
            by_row(256),
            by_row(128),
        ],
        out_specs=(by_row(256), whole((WIDTH, 256)), whole((128, WIDTH))),
        scratch_shapes=[
            pltpu.VMEM((SEQ, 128), BF16),
            pltpu.VMEM((SEQ, 128), F32),
            pltpu.VMEM((WIDTH, 256), F32),
            pltpu.VMEM((128, WIDTH), F32),
        ],
        compiler_params=pltpu.CompilerParams(vmem_limit_bytes=VMEM_BYTES),
        cost_estimate=pl.CostEstimate(flops=8 << 30, bytes_accessed=16 << 20, transcendentals=3 << 20),
    )(dattn_all.reshape(WIDE, 2, SPAN, WIDTH), w_rows, h1, qkv, lse, o_heads, angle, start)


def finish_kernel(
    dqkv_ref, wg_ref, og_ref, small_ref, w_ref, x_ref, dmid_ref, gain_ref,
    in_grad, q_grad, k_grad, v_grad, o_grad, sums, gain_sum,
    dq_full, w_recv, o_recv, s_recv, gain_own, g_recv,
    qs, qr, ws, wr, os, orv, ss, sr, gs, gr, local,
):
    spot = Spot()
    everyone = NARROW * WIDE
    spot.greet(everyone)

    def to_plane(step, arriving):
        other = lax.rem(spot.w + step, WIDE)
        place = other if arriving else spot.w
        return remote(
            dqkv_ref.at[:, pl.ds(pl.multiple_of(other * SPAN, SPAN), SPAN), :],
            dq_full.at[:, :, pl.ds(pl.multiple_of(place * 256, 256), 256)],
            qs.at[other], qr.at[place], spot.wide(other),
        )

    def others(step):
        other = lax.rem(spot.me + step, everyone)
        return other, (lax.div(other, WIDE), lax.rem(other, WIDE))

    def rows_of(ref, owner):
        return ref.at[pl.ds(pl.multiple_of(owner * 32, 32), 32)]

    def lanes_of(ref, owner):
        return ref.at[:, pl.ds(pl.multiple_of(lax.div(owner, 4) * 128, 128), 128)]

    def to_owner(step, arriving):
        other, to = others(step)
        place = other if arriving else spot.me
        return (
            remote(rows_of(wg_ref, other), w_recv.at[place], ws.at[other], wr.at[place], to),
            remote(lanes_of(small_ref, other), s_recv.at[place], ss.at[other], sr.at[place], to),
        )

    def gain_to_owner(step, arriving):
        other, to = others(step)
        place = other if arriving else spot.me
        return remote(lanes_of(gain_own, other), g_recv.at[place], gs.at[other], gr.at[place], to)

    def start_plane(step, carry):
        to_plane(step, False).start()
        return carry

    def start_owner(step, carry):
        for copy in to_owner(step, False):
            copy.start()
        return carry

    def start_gain(step, carry):
        gain_to_owner(step, False).start()
        return carry

    lax.fori_loop(1, WIDE, start_plane, 0)
    mine = [
        pltpu.make_async_copy(
            dqkv_ref.at[:, pl.ds(pl.multiple_of(spot.w * SPAN, SPAN), SPAN), :],
            dq_full.at[:, :, pl.ds(pl.multiple_of(spot.w * 256, 256), 256)],
            local.at[0],
        ),
        pltpu.make_async_copy(rows_of(wg_ref, spot.me), w_recv.at[spot.me], local.at[1]),
        pltpu.make_async_copy(lanes_of(small_ref, spot.me), s_recv.at[spot.me], local.at[2]),
    ]
    for copy in mine:
        copy.start()

    def output_copies(act_local, act_send, act_recv):
        for i in range(4):
            owner = 4 * spot.w + i
            to = (lax.div(owner, WIDE), lax.rem(owner, WIDE))
            source = og_ref.at[pl.ds(i * 32, 32)]
            here = owner == spot.me

            @pl.when(here)
            def _():
                act_local(pltpu.make_async_copy(source, o_recv.at[spot.n], local.at[3]))

            @pl.when(jnp.logical_not(here))
            def _():
                act_send(remote(source, o_recv.at[spot.n], os.at[i], orv.at[spot.n], to))

        for plane in range(NARROW):
            giver = lax.div(spot.me, 4)
            here = (plane == spot.n) & (giver == spot.w)

            @pl.when(jnp.logical_not(here))
            def _():
                place = o_recv.at[plane]
                act_recv(remote(place, place, os.at[0], orv.at[plane], (plane, giver)))

    def nothing(copy):
        return None

    output_copies(lambda c: c.start(), lambda c: c.start(), nothing)
    lax.fori_loop(1, everyone, start_owner, 0)

    def wait_plane(step, carry):
        to_plane(step, False).wait_send()
        to_plane(step, True).wait_recv()
        return carry

    lax.fori_loop(1, WIDE, wait_plane, 0)
    mine[0].wait()
    dqkv = dq_full[...].reshape(TOKENS, 2 * WIDTH)
    dh1 = mm(dqkv, w_ref[...], NT)
    x = x_ref[...].astype(F32)
    scale = lax.rsqrt(jnp.mean(x * x, axis=1, keepdims=True) + EPSILON)
    gain_own[0:1, :] = jnp.sum(dh1 * x * scale, axis=0, keepdims=True)
    gain_own[1:8, :] = jnp.zeros((7, WIDTH), F32)
    lax.fori_loop(1, everyone, start_gain, 0)
    gain_mine = pltpu.make_async_copy(lanes_of(gain_own, spot.me), g_recv.at[spot.me], local.at[0])
    gain_mine.start()
    weighted = dh1 * gain_ref[0:1, :]
    inner = jnp.mean(weighted * x, axis=1, keepdims=True)
    in_grad[...] = (dmid_ref[...] + weighted * scale - x * (scale * scale * scale) * inner).astype(BF16)

    def wait_owner(step, carry):
        for copy in to_owner(step, False):
            copy.wait_send()
        for copy in to_owner(step, True):
            copy.wait_recv()
        return carry

    lax.fori_loop(1, everyone, wait_owner, 0)
    mine[1].wait()
    mine[2].wait()
    output_copies(lambda c: c.wait(), lambda c: c.wait_send(), lambda c: c.wait_recv())
    for w in range(WIDE):
        total = widen(w_recv[w])
        for plane in range(1, NARROW):
            total = total + widen(w_recv[plane * WIDE + w])
        q_grad[:, 128 * w : 128 * w + 128] = total[:, 0:128]
        k_grad[:, 64 * w : 64 * w + 64] = total[:, 128:192]
        v_grad[:, 64 * w : 64 * w + 64] = total[:, 192:256]
    total = widen(o_recv[0])
    for plane in range(1, NARROW):
        total = total + widen(o_recv[plane])
    o_grad[...] = total
    total = s_recv[0]
    for device in range(1, everyone):
        total = total + s_recv[device]
    sums[...] = total

    def wait_gain(step, carry):
        gain_to_owner(step, False).wait_send()
        gain_to_owner(step, True).wait_recv()
        return carry

    lax.fori_loop(1, everyone, wait_gain, 0)
    gain_mine.wait()
    total = g_recv[0]
    for device in range(1, everyone):
        total = total + g_recv[device]
    gain_sum[...] = total


def finish_call(dqkv, wgrad, ograd, small, w_full, x_own, dmid, gain_rows):
    dma = pltpu.SemaphoreType.DMA
    everyone = NARROW * WIDE
    return pl.pallas_call(
        finish_kernel,
        name="finish",
        out_shape=(
            jax.ShapeDtypeStruct((TOKENS, WIDTH), BF16),
            jax.ShapeDtypeStruct((32, WIDTH), F32),
            jax.ShapeDtypeStruct((32, WIDTH // 2), F32),
            jax.ShapeDtypeStruct((32, WIDTH // 2), F32),
            jax.ShapeDtypeStruct((32, WIDTH), F32),
            jax.ShapeDtypeStruct((40, 128), F32),
            jax.ShapeDtypeStruct((8, 128), F32),
        ),
        in_specs=[IN_HBM] * 4 + [IN_VMEM] * 4,
        out_specs=(IN_VMEM,) * 7,
        scratch_shapes=[
            pltpu.VMEM((2, SPAN, 2 * WIDTH), BF16),
            pltpu.VMEM((everyone, 32, 256), BF16),
            pltpu.VMEM((NARROW, 32, WIDTH), BF16),
            pltpu.VMEM((everyone, 40, 128), F32),
            pltpu.VMEM((8, WIDTH), F32),
            pltpu.VMEM((everyone, 8, 128), F32),
            dma((WIDE,)),
            dma((WIDE,)),
            dma((everyone,)),
            dma((everyone,)),
            dma((4,)),
            dma((NARROW,)),
            dma((everyone,)),
            dma((everyone,)),
            dma((everyone,)),
            dma((everyone,)),
            dma((4,)),
        ],
        compiler_params=pltpu.CompilerParams(collective_id=4, has_side_effects=True, vmem_limit_bytes=VMEM_BYTES),
    )(dqkv, wgrad, ograd, small, w_full, x_own, dmid, gain_rows)


def swap(values, distance):
    return lax.ppermute(values, "narrow", [(i, i ^ distance) for i in range(NARROW)])


def quarters(shard, half):
    by_pair = shard.reshape((2, MINE) + shard.shape[1:])
    own = lax.dynamic_index_in_dim(by_pair, half, 0, keepdims=False)
    other = lax.dynamic_index_in_dim(by_pair, 1 - half, 0, keepdims=False)
    return own, swap(other, 1), swap(own, 2), swap(other, 3)


def owner_sums(grad, depth, n, half):
    def rows(quarter):
        return lax.dynamic_slice_in_dim(grad, quarter * depth, depth, axis=1)

    mate = n + 1 - 2 * half
    far = n + 2 - 4 * (n // 2)
    far_mate = mate + 2 - 4 * (n // 2)
    own = rows(n)
    from_far = swap(rows(far), 2)
    from_mate = swap(rows(mate), 1)
    from_far_mate = swap(rows(far_mate), 3)
    same = own.astype(F32) + from_far.astype(F32)
    opposite = from_mate.astype(F32) + from_far_mate.astype(F32)
    is_first = half == 0
    return jnp.concatenate(
        [jnp.where(is_first, same, opposite), jnp.where(is_first, opposite, same)], axis=0
    )


def position_tables():
    freq = (1.0 / np.float32(THETA) ** (np.arange(32, dtype=np.float32) * np.float32(2.0) / np.float32(HEAD_DIM))).astype(np.float32)
    angle = np.arange(SEQ, dtype=np.float32)[:, None] * freq[None, :]
    cosine = np.tile(np.cos(angle.astype(np.float64)), (1, 4)).astype(np.float32)
    sine = np.tile(np.sin(angle.astype(np.float64)), (1, 4)).astype(np.float32)
    return cosine, sine, np.tile(freq[None, :], (8, 4)).astype(np.float32)


def fast_device(
    hidden_in, out_grad, seg_ids, expert_ids, attn_gain, w_query, w_key, w_value, w_output,
    moe_gain, w_router, w_gate_up, w_down,
):
    n = lax.axis_index("narrow")
    w = lax.axis_index("wide")
    half = n % 2
    me = n * WIDE + w
    cos_table, sin_table, freq = position_tables()

    gate_up = quarters(w_gate_up, half)
    down = quarters(w_down, half)
    out_shard = jnp.concatenate([w_output, w_router, jnp.zeros((32, 96), BF16)], axis=1)
    w_out = lax.all_gather(out_shard, ("narrow", "wide"), axis=0, tiled=True)

    x_own = hidden_in.reshape(TOKENS, WIDTH)
    dy_own = out_grad.reshape(TOKENS, WIDTH)
    w_own = jnp.concatenate(
        [w_query.reshape(32, WIDE, 128), w_key.reshape(32, WIDE, 64), w_value.reshape(32, WIDE, 64)], axis=2
    ).reshape(32, 2 * WIDTH)
    gains = jnp.concatenate([attn_gain[None], moe_gain[None]], axis=0).astype(F32)
    g_own = jnp.pad(gains, ((0, 6), (0, 96)))
    seg_own = jnp.pad(seg_ids, ((0, 6), (0, 0)))
    ids = expert_ids.reshape(TOKENS, TOP).T

    x_all, w_all, g_all, seg_all = gather_call(x_own, w_own, g_own, seg_own)
    h1, qkv, lse, o_heads, angle, start, gain_rows = attend_call(
        x_all, w_all, g_all, seg_all, cos_table, sin_table, freq
    )
    dy_mate = swap(dy_own, 1)
    dy_pair = jnp.where(half == 0, jnp.stack([dy_own, dy_mate]), jnp.stack([dy_mate, dy_own]))
    dy_all = lax.all_gather(dy_pair.reshape(2 * TOKENS, WIDTH), "wide", axis=0, tiled=True).reshape(
        WIDE, 2, TOKENS, WIDTH
    )
    w_full = lax.all_gather(w_own, ("narrow", "wide"), axis=0, tiled=True)

    h2_all, table_all, mid, gate = project_call(o_heads, x_own, w_out, gain_rows, ids)
    rows, da, y_part, dgate, down_grad = expert_call(h2_all, dy_all, table_all, gate_up, down)
    down_sum = owner_sums(down_grad, FF // NARROW, n, half)
    y_plane = lax.psum_scatter(
        y_part.reshape(WIDE * 2 * TOKENS, WIDTH), "wide", scatter_dimension=0, tiled=True
    ).reshape(2, TOKENS, WIDTH)
    y_own = lax.dynamic_index_in_dim(y_plane, half, 0, keepdims=False)
    y_mate = swap(lax.dynamic_index_in_dim(y_plane, 1 - half, 0, keepdims=False), 1)
    block_out = (mid + y_own.astype(F32) + y_mate.astype(F32)).astype(BF16)
    gate_up_grad = gate_up_grad_call(rows, da)
    gate_up_sum = owner_sums(gate_up_grad, WIDTH // NARROW, n, half)
    part = rows_grad_call(da, table_all, gate_up)
    dattn_all, dmid, small = collect_call(part, dgate, h2_all, mid, gate, w_out, gain_rows, dy_own)
    w_rows = lax.dynamic_slice(w_out, (w * 128, 0), (128, WIDTH))
    dqkv, wgrad, ograd = attend_back_call(dattn_all, w_rows, h1, qkv, lse, o_heads, angle, start)
    in_grad, q_grad, k_grad, v_grad, o_grad, sums, gain_sum = finish_call(
        dqkv, wgrad, ograd, small, w_full, x_own, dmid, gain_rows
    )
    lanes = (me % 4) * 32
    router_grad = lax.dynamic_slice(sums, (0, lanes), (32, 32)).T
    moe_gain_grad = lax.dynamic_slice(sums, (32, lanes), (1, 32)).reshape(32)
    attn_gain_grad = lax.dynamic_slice(gain_sum, (0, lanes), (1, 32)).reshape(32)
    expert_load = sums[33, 0:32].astype(jnp.int32)
    return (
        block_out.reshape(hidden_in.shape),
        in_grad.reshape(hidden_in.shape),
        attn_gain_grad,
        q_grad,
        k_grad,
        v_grad,
        o_grad,
        moe_gain_grad,
        router_grad,
        gate_up_sum,
        down_sum,
        expert_load,
    )


def solution(mesh):
    planned = mesh.shape["narrow"] == NARROW and mesh.shape["wide"] == WIDE
    return jax.shard_map(
        fast_device if planned else general_device,
        mesh=mesh,
        in_specs=(
            P("narrow", "wide", None),
            P("narrow", "wide", None),
            P("narrow", "wide"),
            P("narrow", "wide", None),
            P(("narrow", "wide")),
            P(("narrow", "wide"), None),
            P(("narrow", "wide"), None),
            P(("narrow", "wide"), None),
            P(("narrow", "wide"), None),
            P(("narrow", "wide")),
            P(("narrow", "wide"), None),
            P("wide", "narrow", None),
            P("wide", "narrow", None),
        ),
        out_specs=(
            P("narrow", "wide", None),
            P("narrow", "wide", None),
            P(("narrow", "wide")),
            P(("narrow", "wide"), None),
            P(("narrow", "wide"), None),
            P(("narrow", "wide"), None),
            P(("narrow", "wide"), None),
            P(("narrow", "wide")),
            P(("narrow", "wide"), None),
            P("wide", "narrow", None),
            P("wide", "narrow", None),
            P(),
        ),
        check_vma=False,
    )
```

```python
import math

import functools
import jax
import jax.numpy as jnp
import numpy as np
from jax import lax
from jax.experimental import pallas as pl
from jax.experimental.pallas import tpu as pltpu
from jax.sharding import PartitionSpec as P

KV_HEADS = 8
HEAD_DIM = 64
EXPERTS = 32
TOP = 8
FF = 512
CAP = 80


EPSILON = 1e-06
THETA = 10000.0
MASKED = -1e30


def rms_scale(values):
    return lax.rsqrt(jnp.mean(values * values, axis=-1, keepdims=True) + EPSILON)


def norm_back(values, scale, gain, upstream):
    weighted = upstream * gain
    inner_mean = jnp.mean(weighted * values, axis=-1, keepdims=True)
    value_grad = weighted * scale - values * (scale * scale * scale) * inner_mean
    gain_grad = jnp.sum(upstream * values * scale, axis=0)
    return (value_grad, gain_grad)


def lane_turn(head_dim):
    lane_ids = jnp.arange(128)
    lane_local = lane_ids % head_dim
    half_dim = head_dim // 2
    same_head = lane_ids[:, None] // head_dim == lane_ids[None, :] // head_dim
    from_upper = (lane_local[None, :] < half_dim) & (
        lane_local[:, None] == lane_local[None, :] + half_dim
    )
    from_lower = (lane_local[None, :] >= half_dim) & (
        lane_local[:, None] + half_dim == lane_local[None, :]
    )
    return jnp.where(
        same_head & from_upper, -1.0, jnp.where(same_head & from_lower, 1.0, 0.0)
    ).astype(jnp.float32)


def lane_angles(positions, head_dim):
    lane_ids = jnp.arange(128) % head_dim % (head_dim // 2)
    inverse = 1.0 / THETA ** (lane_ids.astype(jnp.float32) * 2.0 / head_dim)
    return positions[..., None] * inverse


def rotate(values, cos_table, sin_table, turner):
    dims_in = values.shape
    blocks = values.reshape(dims_in[0], dims_in[1], -1, 128)
    turned = jnp.einsum("abnl,lm->abnm", blocks, turner, precision=lax.Precision.HIGHEST)
    return (blocks * cos_table[:, :, None, :] + turned * sin_table[:, :, None, :]).reshape(dims_in)


def rotate_back(grad_in, cos_table, sin_table, turner):
    dims_in = grad_in.shape
    blocks = grad_in.reshape(dims_in[0], dims_in[1], -1, 128)
    turned = jnp.einsum(
        "abnm,lm->abnl", blocks * sin_table[:, :, None, :], turner, precision=lax.Precision.HIGHEST
    )
    return (blocks * cos_table[:, :, None, :] + turned).reshape(dims_in)


def masked_scores(query_five, key_block, seg_query, seg_key, place_query, place_key, factor):
    scores = (
        jnp.einsum("abgjd,akgd->agjbk", query_five, key_block, preferred_element_type=jnp.float32)
        * factor
    )
    allowed = (seg_query[:, :, None] == seg_key[:, None, :]) & (
        place_query[:, :, None] >= place_key[:, None, :]
    )
    return jnp.where(allowed[:, None, None], scores, MASKED)


def general_device(
    hidden_in,
    out_grad,
    seg_ids,
    expert_ids,
    attn_gain,
    w_query,
    w_key,
    w_value,
    w_output,
    moe_gain,
    w_router,
    w_gate_up,
    w_down,
):
    row_count, span_len, feat_dim = hidden_in.shape
    tok_count = row_count * span_len
    factor = HEAD_DIM ** (-0.5)
    kv_width = KV_HEADS * HEAD_DIM
    gain_one, query_w, key_w, value_w, output_w, gain_two, router_w = (
        lax.all_gather(attn_gain, ("narrow", "wide"), axis=0, tiled=True),
        lax.all_gather(w_query, ("narrow", "wide"), axis=0, tiled=True),
        lax.all_gather(w_key, ("narrow", "wide"), axis=0, tiled=True),
        lax.all_gather(w_value, ("narrow", "wide"), axis=0, tiled=True),
        lax.all_gather(w_output, ("narrow", "wide"), axis=0, tiled=True),
        lax.all_gather(moe_gain, ("narrow", "wide"), axis=0, tiled=True),
        lax.all_gather(w_router, ("narrow", "wide"), axis=0, tiled=True),
    )
    gate_up_w, down_w = (
        lax.all_gather(w_gate_up, "narrow", axis=1, tiled=True),
        lax.all_gather(w_down, "narrow", axis=1, tiled=True),
    )
    segs_all = lax.all_gather(seg_ids, "wide", axis=1, tiled=True)
    seq_len = segs_all.shape[1]
    key_step = math.gcd(seq_len, 512)
    place_local = lax.axis_index("wide") * span_len + jnp.arange(span_len, dtype=jnp.int32)
    place_query = place_local[None, :]
    starts = jnp.sum((segs_all[:, None, :] < seg_ids[:, :, None]).astype(jnp.int32), axis=-1)
    positions = (place_query - starts).astype(jnp.float32)
    angles = lane_angles(positions, HEAD_DIM)
    cos_table = jnp.cos(angles)
    sin_table = jnp.sin(angles)
    turner = lane_turn(HEAD_DIM)
    inputs = hidden_in.astype(jnp.float32)
    scale_one = rms_scale(inputs)
    gain_one_f = gain_one.astype(jnp.float32)
    normed_one = (inputs * scale_one * gain_one_f).astype(jnp.bfloat16)
    query_pre = jnp.dot(normed_one, query_w, preferred_element_type=jnp.float32)
    key_pre = jnp.dot(normed_one, key_w, preferred_element_type=jnp.float32)
    value_pre = jnp.dot(normed_one, value_w, preferred_element_type=jnp.float32)
    queries = rotate(query_pre, cos_table, sin_table, turner).astype(jnp.bfloat16)
    keys_local = rotate(key_pre, cos_table, sin_table, turner).astype(jnp.bfloat16)
    values_local = value_pre.astype(jnp.bfloat16)
    key_all, value_all = (
        lax.all_gather(keys_local, "wide", axis=1, tiled=True),
        lax.all_gather(values_local, "wide", axis=1, tiled=True),
    )
    query_five = queries.reshape(row_count, span_len, KV_HEADS, 2, HEAD_DIM)

    def key_slices(key_start, length):
        key_block = lax.dynamic_slice_in_dim(key_all, key_start, length, 1).reshape(
            row_count, length, KV_HEADS, HEAD_DIM
        )
        value_block = lax.dynamic_slice_in_dim(value_all, key_start, length, 1).reshape(
            row_count, length, KV_HEADS, HEAD_DIM
        )
        seg_key = lax.dynamic_slice_in_dim(segs_all, key_start, length, 1)
        place_key = (key_start + jnp.arange(length, dtype=jnp.int32))[None, :]
        return (key_block, value_block, seg_key, place_key)

    def scores_at(key_start, length):
        key_block, value_block, seg_key, place_key = key_slices(key_start, length)
        scores = masked_scores(
            query_five, key_block, seg_ids, seg_key, place_query, place_key, factor
        )
        return (scores, key_block, value_block)

    key_starts = jnp.arange(seq_len // key_step, dtype=jnp.int32) * key_step
    stat_shape = (row_count, KV_HEADS, 2, span_len)
    five_shape = (row_count, span_len, KV_HEADS, 2, HEAD_DIM)

    def top_step(state_now, key_start):
        row_top, row_total = state_now
        scores, unused_key, unused_value = scores_at(key_start, key_step)
        new_top = jnp.maximum(row_top, jnp.max(scores, axis=-1))
        row_total = row_total * jnp.exp(row_top - new_top) + jnp.sum(
            jnp.exp(scores - new_top[..., None]), axis=-1
        )
        return ((new_top, row_total), None)

    (row_top, row_total), unused = lax.scan(
        top_step,
        (jnp.full(stat_shape, MASKED, jnp.float32), jnp.zeros(stat_shape, jnp.float32)),
        key_starts,
    )
    log_total = row_top + jnp.log(row_total)

    def out_step(summed, key_start):
        scores, unused_key, value_block = scores_at(key_start, key_step)
        weights = jnp.exp(scores - log_total[..., None]).astype(jnp.bfloat16)
        return (
            summed
            + jnp.einsum(
                "agjbk,akgd->abgjd", weights, value_block, preferred_element_type=jnp.float32
            ),
            None,
        )

    attended, unused = lax.scan(out_step, jnp.zeros(five_shape, jnp.float32), key_starts)
    attended = attended.reshape(row_count, span_len, -1).astype(jnp.bfloat16)
    middle = inputs + jnp.dot(attended, output_w, preferred_element_type=jnp.float32)
    scale_two = rms_scale(middle)
    gain_two_f = gain_two.astype(jnp.float32)
    normed_two = (middle * scale_two * gain_two_f).astype(jnp.bfloat16)
    flat_two = normed_two.reshape(tok_count, feat_dim)
    logits = jnp.dot(flat_two, router_w, preferred_element_type=jnp.float32)
    expert_table = expert_ids.reshape(tok_count, TOP)
    choose = expert_table[:, :, None] == jnp.arange(EXPERTS, dtype=jnp.int32)[None, None, :]
    chosen = jnp.sum(jnp.where(choose, logits[:, None, :], 0.0), axis=-1)
    gate_vals = jax.nn.softmax(chosen, axis=-1)
    token_hot = jnp.sum(choose.astype(jnp.int32), axis=1)
    expert_load = lax.psum(jnp.sum(token_hot, axis=0), ("narrow", "wide"))
    earlier = jnp.cumsum(token_hot, axis=0) - token_hot
    places = jnp.sum(jnp.where(choose, earlier[:, None, :], 0), axis=-1)
    pair_count = tok_count * TOP
    target = jnp.where(places < CAP, expert_table * CAP + places, EXPERTS * CAP).reshape(-1)
    pair_of_slot = (
        jnp.full((EXPERTS * CAP,), pair_count, jnp.int32)
        .at[target]
        .set(jnp.arange(pair_count, dtype=jnp.int32), mode="drop")
    )
    token_of_slot = pair_of_slot // TOP
    outgoing = jnp.take(flat_two, token_of_slot, axis=0, mode="fill", fill_value=0).reshape(
        EXPERTS, CAP, feat_dim
    )
    received = lax.all_to_all(outgoing, "wide", split_axis=0, concat_axis=1, tiled=True)
    gate_up = jnp.einsum("ecd,edf->ecf", received, gate_up_w, preferred_element_type=jnp.float32)
    gate_half = gate_up[..., :FF]
    up_half = gate_up[..., FF:]
    sigmoid_gate = jax.nn.sigmoid(gate_half)
    activated = gate_half * sigmoid_gate
    hidden_b = (activated * up_half).astype(jnp.bfloat16)
    expert_out = jnp.einsum(
        "ecf,efd->ecd", hidden_b, down_w, preferred_element_type=jnp.float32
    ).astype(jnp.bfloat16)
    returned = lax.all_to_all(expert_out, "wide", split_axis=1, concat_axis=0, tiled=True)
    per_pair = (
        jnp.take(
            returned.reshape(EXPERTS * CAP, feat_dim), target, axis=0, mode="fill", fill_value=0
        )
        .reshape(tok_count, TOP, feat_dim)
        .astype(jnp.float32)
    )
    mixture = jnp.sum(gate_vals[:, :, None] * per_pair, axis=1)
    middle_flat = middle.reshape(tok_count, feat_dim)
    block_out = (middle_flat + mixture).reshape(row_count, span_len, feat_dim).astype(jnp.bfloat16)
    grad_out = out_grad.reshape(tok_count, feat_dim).astype(jnp.float32)
    gate_grad = jnp.sum(grad_out[:, None, :] * per_pair, axis=-1)
    gate_of_slot = jnp.take(gate_vals.reshape(-1), pair_of_slot, mode="fill", fill_value=0.0)
    slot_grad = (
        (
            jnp.take(grad_out, token_of_slot, axis=0, mode="fill", fill_value=0.0)
            * gate_of_slot[:, None]
        )
        .astype(jnp.bfloat16)
        .reshape(EXPERTS, CAP, feat_dim)
    )
    grad_received = lax.all_to_all(slot_grad, "wide", split_axis=0, concat_axis=1, tiled=True)
    down_grad = jnp.einsum(
        "ecf,ecd->efd", hidden_b, grad_received, preferred_element_type=jnp.float32
    )
    hidden_grad = jnp.einsum(
        "ecd,efd->ecf", grad_received, down_w, preferred_element_type=jnp.float32
    )
    gate_half_grad = (
        hidden_grad * up_half * (sigmoid_gate * (1.0 + gate_half * (1.0 - sigmoid_gate)))
    )
    up_half_grad = hidden_grad * activated
    gate_up_grad = jnp.concatenate([gate_half_grad, up_half_grad], axis=-1).astype(jnp.bfloat16)
    gate_up_wgrad = jnp.einsum(
        "ecd,ecf->edf", received, gate_up_grad, preferred_element_type=jnp.float32
    )
    slot_input_grad = jnp.einsum(
        "ecf,edf->ecd", gate_up_grad, gate_up_w, preferred_element_type=jnp.float32
    ).astype(jnp.bfloat16)
    input_back = lax.all_to_all(slot_input_grad, "wide", split_axis=1, concat_axis=0, tiled=True)
    pair_input_grad = jnp.take(
        input_back.reshape(EXPERTS * CAP, feat_dim), target, axis=0, mode="fill", fill_value=0
    ).reshape(tok_count, TOP, feat_dim)
    gate_mean = jnp.sum(gate_vals * gate_grad, axis=-1, keepdims=True)
    chosen_grad = gate_vals * (gate_grad - gate_mean)
    logit_grad = jnp.sum(jnp.where(choose, chosen_grad[:, :, None], 0.0), axis=1).astype(
        jnp.bfloat16
    )
    router_wgrad = jnp.einsum("td,te->de", flat_two, logit_grad, preferred_element_type=jnp.float32)
    normed_two_grad = jnp.sum(pair_input_grad.astype(jnp.float32), axis=1) + jnp.einsum(
        "te,de->td", logit_grad, router_w, preferred_element_type=jnp.float32
    )
    middle_part, gain_two_grad = norm_back(
        middle_flat, scale_two.reshape(tok_count, 1), gain_two_f, normed_two_grad
    )
    middle_grad = grad_out + middle_part
    attn_grad = middle_grad.astype(jnp.bfloat16)
    output_wgrad = jnp.einsum(
        "te,td->ed", attended.reshape(tok_count, -1), attn_grad, preferred_element_type=jnp.float32
    )
    attended_grad = jnp.einsum(
        "td,ed->te", attn_grad, output_w, preferred_element_type=jnp.float32
    ).astype(jnp.bfloat16)
    grad_five = attended_grad.reshape(five_shape)

    def sum_step(summed, key_start):
        scores, unused_key, value_block = scores_at(key_start, key_step)
        weights = jnp.exp(scores - log_total[..., None])
        weight_grad = jnp.einsum(
            "abgjd,akgd->agjbk", grad_five, value_block, preferred_element_type=jnp.float32
        )
        return (summed + jnp.sum(weights * weight_grad, axis=-1), None)

    row_dot, unused = lax.scan(sum_step, jnp.zeros(stat_shape, jnp.float32), key_starts)

    def query_step(summed, key_start):
        scores, key_block, value_block = scores_at(key_start, key_step)
        weights = jnp.exp(scores - log_total[..., None])
        weight_grad = jnp.einsum(
            "abgjd,akgd->agjbk", grad_five, value_block, preferred_element_type=jnp.float32
        )
        score_grad = (weights * (weight_grad - row_dot[..., None])).astype(jnp.bfloat16)
        return (
            summed
            + jnp.einsum(
                "agjbk,akgd->abgjd", score_grad, key_block, preferred_element_type=jnp.float32
            ),
            None,
        )

    query_grad, unused = lax.scan(query_step, jnp.zeros(five_shape, jnp.float32), key_starts)
    query_grad = query_grad.reshape(row_count, span_len, -1) * factor
    term_count = span_len * lax.axis_size("wide")
    sub_len = math.gcd(term_count, 512)

    def key_piece(sub_no):
        key_start = sub_no * sub_len
        key_block, value_block, seg_key, place_key = key_slices(key_start, sub_len)
        scores = masked_scores(
            query_five, key_block, seg_ids, seg_key, place_query, place_key, factor
        )
        weights = jnp.exp(scores - log_total[..., None])
        weight_grad = jnp.einsum(
            "abgjd,akgd->agjbk", grad_five, value_block, preferred_element_type=jnp.float32
        )
        score_grad = (weights * (weight_grad - row_dot[..., None])).astype(jnp.bfloat16)
        key_part = (
            jnp.einsum(
                "agjbk,abgjd->kagd", score_grad, query_five, preferred_element_type=jnp.float32
            )
            * factor
        )
        value_part = jnp.einsum(
            "agjbk,abgjd->kagd",
            weights.astype(jnp.bfloat16),
            grad_five,
            preferred_element_type=jnp.float32,
        )
        return jnp.concatenate(
            [
                key_part.reshape(sub_len, row_count, kv_width),
                value_part.reshape(sub_len, row_count, kv_width),
            ],
            axis=-1,
        )

    pieces = lax.map(key_piece, jnp.arange(term_count // sub_len, dtype=jnp.int32))
    summed_terms = lax.psum_scatter(
        pieces.reshape(term_count, row_count, 2 * kv_width).astype(jnp.bfloat16),
        "wide",
        scatter_dimension=0,
        tiled=True,
    ).astype(jnp.float32)
    key_grad = jnp.transpose(summed_terms[:, :, :kv_width], (1, 0, 2))
    value_grad = jnp.transpose(summed_terms[:, :, kv_width:], (1, 0, 2))
    query_back = (
        rotate_back(query_grad, cos_table, sin_table, turner)
        .astype(jnp.bfloat16)
        .reshape(tok_count, -1)
    )
    key_back = (
        rotate_back(key_grad, cos_table, sin_table, turner)
        .astype(jnp.bfloat16)
        .reshape(tok_count, -1)
    )
    value_back = value_grad.astype(jnp.bfloat16).reshape(tok_count, -1)
    flat_one = normed_one.reshape(tok_count, feat_dim)
    query_wgrad = jnp.einsum("td,te->de", flat_one, query_back, preferred_element_type=jnp.float32)
    key_wgrad = jnp.einsum("td,te->de", flat_one, key_back, preferred_element_type=jnp.float32)
    value_wgrad = jnp.einsum("td,te->de", flat_one, value_back, preferred_element_type=jnp.float32)
    normed_one_grad = (
        jnp.einsum("te,de->td", query_back, query_w, preferred_element_type=jnp.float32)
        + jnp.einsum("te,de->td", key_back, key_w, preferred_element_type=jnp.float32)
        + jnp.einsum("te,de->td", value_back, value_w, preferred_element_type=jnp.float32)
    )
    input_part, gain_one_grad = norm_back(
        inputs.reshape(tok_count, feat_dim),
        scale_one.reshape(tok_count, 1),
        gain_one_f,
        normed_one_grad,
    )
    input_grad = (
        (middle_grad + input_part).reshape(row_count, span_len, feat_dim).astype(jnp.bfloat16)
    )
    gain_one_sum, query_sum, key_wsum, value_wsum, output_sum, gain_two_sum, router_sum = (
        lax.psum_scatter(gain_one_grad, ("narrow", "wide"), scatter_dimension=0, tiled=True),
        lax.psum_scatter(query_wgrad, ("narrow", "wide"), scatter_dimension=0, tiled=True),
        lax.psum_scatter(key_wgrad, ("narrow", "wide"), scatter_dimension=0, tiled=True),
        lax.psum_scatter(value_wgrad, ("narrow", "wide"), scatter_dimension=0, tiled=True),
        lax.psum_scatter(output_wgrad, ("narrow", "wide"), scatter_dimension=0, tiled=True),
        lax.psum_scatter(gain_two_grad, ("narrow", "wide"), scatter_dimension=0, tiled=True),
        lax.psum_scatter(router_wgrad, ("narrow", "wide"), scatter_dimension=0, tiled=True),
    )
    gate_up_sum, down_sum = (
        lax.psum_scatter(
            gate_up_wgrad.astype(jnp.bfloat16), "narrow", scatter_dimension=1, tiled=True
        ).astype(jnp.float32),
        lax.psum_scatter(
            down_grad.astype(jnp.bfloat16), "narrow", scatter_dimension=1, tiled=True
        ).astype(jnp.float32),
    )
    return (
        block_out,
        input_grad,
        gain_one_sum,
        query_sum,
        key_wsum,
        value_wsum,
        output_sum,
        gain_two_sum,
        router_sum,
        gate_up_sum,
        down_sum,
        expert_load,
    )


MESH = pl.DeviceIdType.MESH
F32 = jnp.float32
BF16 = jnp.bfloat16
IN_HBM = pl.BlockSpec(memory_space=pl.ANY)
IN_VMEM = pl.BlockSpec(memory_space=pltpu.VMEM)
VMEM_BYTES = 60 * 1024 * 1024
NARROW = 4
WIDE = 8
GROUP = 16
TOKENS = 256
SPAN = 128
WIDTH = 1024
SEQ = 1024
SLOTS = 80
MINE = 2
CHUNK = 4
NT = (((1,), (1,)), ((), ()))
TN = (((0,), (0,)), ((), ()))


def duration(us):
    return pl.CostEstimate(flops=us * 1000000000, bytes_accessed=us * 3600000, transcendentals=0)


def mm(left, right, dims=(((1,), (0,)), ((), ()))):
    return lax.dot_general(left, right, dims, preferred_element_type=F32)


class Spot:
    def __init__(self):
        self.n = lax.axis_index("narrow")
        self.w = lax.axis_index("wide")
        self.core = lax.rem(self.w, 2)
        self.x = lax.rem(lax.div(self.w, 2), 2)
        self.y = lax.div(self.w, 4)
        self.half = lax.rem(self.n, 2)
        self.me = self.n * WIDE + self.w
        self.sib = self.w + 1 - 2 * self.core
        self.xn = self.w + 2 - 4 * self.x
        self.yn = self.w + 4 - 8 * self.y
        self.diag = self.xn + 4 - 8 * self.y
        self.mate = self.n + 1 - 2 * self.half
        self.slot = self.half * WIDE + self.w

    def wide(self, to):
        return (self.n, to)

    def greet(self, count):
        barrier = pltpu.get_barrier_semaphore()
        base = self.n - self.half

        def signal(step, carry):
            if count == WIDE:
                to = (self.n, lax.rem(self.w + step, WIDE))
            elif count == GROUP:
                other = lax.rem(self.slot + step, GROUP)
                to = (base + lax.div(other, WIDE), lax.rem(other, WIDE))
            else:
                other = lax.rem(self.me + step, NARROW * WIDE)
                to = (lax.div(other, WIDE), lax.rem(other, WIDE))
            pl.semaphore_signal(barrier, inc=1, device_id=to, device_id_type=MESH)
            return carry

        lax.fori_loop(1, count, signal, 0)
        pl.semaphore_wait(barrier, count - 1)


def remote(src, dst, send_sem, recv_sem, to):
    return pltpu.make_async_remote_copy(
        src_ref=src, dst_ref=dst, send_sem=send_sem, recv_sem=recv_sem, device_id=to, device_id_type=MESH
    )


def halves(ref, which):
    return ref.at[pl.ds(which * SPAN, SPAN)]


class PlaneGather:
    COPIES = 11

    def __init__(self, spot, source, place, send, recv):
        self.spot, self.source, self.place = spot, source, place
        self.send, self.recv = send, recv
        self.started = []

    def put(self, src, dst, number, to):
        copy = remote(src, dst, self.send.at[number], self.recv.at[number], self.spot.wide(to))
        copy.start()
        self.started.append(copy)

    def pass_on(self, who, half, number, to):
        place = self.place(who, half)
        self.put(place, place, number, to)

    def got(self, who, half, number):
        dst = self.place(who, half)
        remote(dst, dst, self.send.at[number], self.recv.at[number], self.spot.wide(self.spot.sib)).wait_recv()

    def begin(self):
        s = self.spot
        self.put(self.source(0), self.place(s.w, 0), 0, s.xn)
        self.put(self.source(1), self.place(s.w, 1), 2, s.yn)
        self.put(self.source(1), self.place(s.w, 1), 1, s.xn)
        self.put(self.source(0), self.place(s.w, 0), 3, s.yn)
        self.put(self.source(None), self.place(s.w, None), 4, s.sib)

    def middle(self):
        s = self.spot
        self.got(s.xn, 0, 0)
        self.pass_on(s.xn, 0, 5, s.yn)
        self.got(s.yn, 1, 2)
        self.pass_on(s.yn, 1, 6, s.xn)

    def late(self):
        s = self.spot
        self.got(s.xn, 1, 1)
        self.pass_on(s.xn, None, 7, s.sib)
        self.got(s.yn, 0, 3)
        self.pass_on(s.yn, None, 8, s.sib)

    def last(self):
        s = self.spot
        self.got(s.diag, 0, 5)
        self.pass_on(s.diag, 0, 9, s.sib)
        self.got(s.diag, 1, 6)
        self.pass_on(s.diag, 1, 10, s.sib)

    def finish(self):
        s = self.spot
        sib_x = s.sib + 2 - 4 * s.x
        sib_y = s.sib + 4 - 8 * s.y
        sib_d = sib_x + 4 - 8 * s.y
        self.got(s.sib, None, 4)
        self.got(sib_x, None, 7)
        self.got(sib_y, None, 8)
        self.got(sib_d, 0, 9)
        self.got(sib_d, 1, 10)
        for copy in self.started:
            copy.wait_send()


def gather_tokens(spot, own, out, base, send, recv):
    def part(ref, half):
        return ref if half is None else ref.at[pl.ds(half * SPAN, SPAN)]

    return PlaneGather(
        spot, lambda half: part(own, half), lambda who, half: part(out.at[base + who], half), send, recv
    )


def gather_kernel(
    x_ref, w_ref, g_ref, seg_ref, wo_ref, dy_ref,
    x_all, w_all, g_all, seg_all, wo_block, dy_pair,
    send, recv, local, ws, wr, gs, gr, ss, sr, zs, zr, ds, dr,
):
    spot = Spot()
    spot.greet(NARROW * WIDE)
    own = [
        pltpu.make_async_copy(x_ref, x_all.at[spot.w], local.at[0]),
        pltpu.make_async_copy(w_ref.at[:, pl.ds(pl.multiple_of(spot.w * 256, 256), 256)], w_all.at[spot.me], local.at[1]),
        pltpu.make_async_copy(g_ref, g_all.at[spot.me], local.at[2]),
        pltpu.make_async_copy(seg_ref, seg_all.at[spot.w], local.at[3]),
        pltpu.make_async_copy(wo_ref, wo_block.at[spot.n], local.at[4]),
        pltpu.make_async_copy(dy_ref, dy_pair.at[spot.half], local.at[5]),
    ]
    gather = gather_tokens(spot, x_ref, x_all, 0, send, recv)

    def others(step):
        other = lax.rem(spot.me + step, NARROW * WIDE)
        return other, lax.div(other, WIDE), lax.rem(other, WIDE)

    def weights(step, arriving):
        other, o_n, o_w = others(step)
        source = w_ref.at[:, pl.ds(pl.multiple_of(o_w * 256, 256), 256)]
        place = other if arriving else spot.me
        return (
            remote(source, w_all.at[place], ws.at[other], wr.at[place], (o_n, o_w)),
            remote(g_ref, g_all.at[place], gs.at[other], gr.at[place], (o_n, o_w)),
        )

    def documents(step, arriving):
        other = lax.rem(spot.w + step, WIDE)
        place = other if arriving else spot.w
        return remote(seg_ref, seg_all.at[place], ss.at[other], sr.at[place], spot.wide(other))

    def column(step, arriving):
        other = lax.rem(spot.n + step, NARROW)
        place = other if arriving else spot.n
        return remote(wo_ref, wo_block.at[place], zs.at[other], zr.at[place], (other, spot.w))

    def start(step, carry):
        for copy in weights(step, False):
            copy.start()
        return carry

    def start_column(step, carry):
        column(step, False).start()
        return carry

    def start_documents(step, carry):
        documents(step, False).start()
        return carry

    lax.fori_loop(1, WIDE, start_documents, 0)
    lax.fori_loop(1, NARROW * WIDE, start, 0)
    gather.begin()
    lax.fori_loop(1, NARROW, start_column, 0)
    for copy in own:
        copy.start()
    across = remote(dy_ref, dy_pair.at[spot.half], ds.at[0], dr.at[0], (spot.mate, spot.w))
    across.start()
    gather.middle()
    gather.late()
    gather.last()

    def wait(step, carry):
        for copy in weights(step, False):
            copy.wait_send()
        for copy in weights(step, True):
            copy.wait_recv()
        return carry

    def wait_column(step, carry):
        column(step, False).wait_send()
        column(step, True).wait_recv()
        return carry

    def wait_documents(step, carry):
        documents(step, False).wait_send()
        documents(step, True).wait_recv()
        return carry

    lax.fori_loop(1, WIDE, wait_documents, 0)
    lax.fori_loop(1, NARROW * WIDE, wait, 0)
    lax.fori_loop(1, NARROW, wait_column, 0)
    gather.finish()
    across.wait_send()
    arrived = dy_pair.at[1 - spot.half]
    remote(arrived, arrived, ds.at[0], dr.at[0], (spot.mate, spot.w)).wait_recv()
    for copy in own:
        copy.wait()


def gather_call(x_own, w_own, g_own, seg_own, wo_own, dy_own):
    dma = pltpu.SemaphoreType.DMA
    return pl.pallas_call(
        gather_kernel,
        name="gather_inputs",
        out_shape=(
            jax.ShapeDtypeStruct((WIDE, TOKENS, WIDTH), BF16),
            jax.ShapeDtypeStruct((NARROW * WIDE, 32, 256), BF16),
            jax.ShapeDtypeStruct((NARROW * WIDE, 8, 128), F32),
            jax.ShapeDtypeStruct((WIDE, 8, 128), jnp.int32),
            jax.ShapeDtypeStruct((NARROW, 32, WIDTH + 128), BF16),
            jax.ShapeDtypeStruct((2, TOKENS, WIDTH), BF16),
        ),
        in_specs=[IN_VMEM] * 6,
        out_specs=(IN_HBM,) * 6,
        scratch_shapes=[
            dma((PlaneGather.COPIES,)),
            dma((PlaneGather.COPIES,)),
            dma((6,)),
            dma((NARROW * WIDE,)),
            dma((NARROW * WIDE,)),
            dma((NARROW * WIDE,)),
            dma((NARROW * WIDE,)),
            dma((WIDE,)),
            dma((WIDE,)),
            dma((NARROW,)),
            dma((NARROW,)),
            dma((1,)),
            dma((1,)),
        ],
        compiler_params=pltpu.CompilerParams(collective_id=1, has_side_effects=True),
        cost_estimate=duration(1),
    )(x_own, w_own, g_own, seg_own, wo_own, dy_own)


def lane_half():
    lanes = lax.broadcasted_iota(jnp.int32, (1, 128), 1)
    return lax.rem(lanes, 64) < 32


def turn(values, first_half):
    return jnp.where(first_half, -pltpu.roll(values, 96, 1), pltpu.roll(values, 32, 1))


def turn_back(values, first_half):
    return jnp.where(first_half, pltpu.roll(values, 96, 1), -pltpu.roll(values, 32, 1))


def gather_gain(gains):
    lane = lax.broadcasted_iota(jnp.int32, (128, WIDTH), 0)
    column = lax.broadcasted_iota(jnp.int32, (128, WIDTH), 1)
    spread = (lax.rem(column, 32) == lane).astype(BF16)
    tiled = mm(gains.astype(BF16), spread)
    owner = lax.broadcasted_iota(jnp.int32, (32, WIDTH), 0)
    place = lax.broadcasted_iota(jnp.int32, (32, WIDTH), 1)
    return jnp.sum(jnp.where(lax.div(place, 32) == owner, tiled, 0.0), axis=0, keepdims=True)


class Attention:
    def __init__(self, x_ref, w_ref, seg_ref, cos_ref, sin_ref, freq_ref, gain_one, h1_ref, qkv_ref, lse_ref, o_ref, angle_ref, start_ref):
        self.x_ref, self.seg_ref, self.cos_ref, self.sin_ref = x_ref, seg_ref, cos_ref, sin_ref
        self.h1_ref, self.qkv_ref, self.lse_ref, self.o_ref = h1_ref, qkv_ref, lse_ref, o_ref
        self.angle_ref, self.start_ref = angle_ref, start_ref
        self.gain_one = gain_one
        self.w_ref = w_ref
        self.first_half = lane_half()
        self.is_key = lax.broadcasted_iota(jnp.int32, (1, 128), 1) < 64
        self.starts, self.start_cos, self.start_sin = [], [], []
        for row in range(2):
            segs = [seg_ref[c, row : row + 1, :] for c in range(WIDE)]
            starts = [jnp.zeros((1, 1), F32)]
            for doc in range(5):
                total = jnp.zeros((1, 128), F32)
                for seg in segs:
                    total = total + jnp.where(seg == doc, 1.0, 0.0)
                starts.append(starts[-1] + jnp.sum(total, axis=1, keepdims=True))
            angle = jnp.concatenate(starts + starts[:2], axis=0) * freq_ref[0:1, :]
            self.starts.append(starts)
            self.start_cos.append(jnp.cos(angle))
            self.start_sin.append(jnp.sin(angle))

    def chunk(self, row, i):
        tokens = pl.ds(i * 256, 256)
        starts, start_cos, start_sin = self.starts[row], self.start_cos[row], self.start_sin[row]
        seg_cols = []
        for part in range(2):
            seg = self.seg_ref[2 * i + part, row : row + 1, :].astype(F32)
            seg_cols.append(jnp.transpose(jnp.broadcast_to(seg, (128, 128))))
        seg_col = jnp.concatenate(seg_cols, axis=0)
        start_col = jnp.zeros((256, 128), F32)
        cos_s = jnp.broadcast_to(start_cos[0:1], (256, 128))
        sin_s = jnp.broadcast_to(start_sin[0:1], (256, 128))
        for doc in range(1, 6):
            here = seg_col == float(doc)
            start_col = jnp.where(here, starts[doc], start_col)
            cos_s = jnp.where(here, start_cos[doc : doc + 1], cos_s)
            sin_s = jnp.where(here, start_sin[doc : doc + 1], sin_s)
        self.start_ref[row, tokens, :] = start_col
        cos_t = self.cos_ref[tokens, :]
        sin_t = self.sin_ref[tokens, :]
        cosine = cos_t * cos_s + sin_t * sin_s
        sine = sin_t * cos_s - cos_t * sin_s
        self.angle_ref[row, tokens, 0:128] = cosine
        self.angle_ref[row, tokens, 128:256] = sine
        x = self.x_ref[2 * i : 2 * i + 2, row].reshape(256, WIDTH).astype(F32)
        scale = lax.rsqrt(jnp.mean(x * x, axis=1, keepdims=True) + EPSILON)
        h1 = (x * scale * self.gain_one).astype(BF16)
        self.h1_ref[row, tokens, :] = h1
        qkv = mm(h1, self.w_ref[...].reshape(WIDTH, 256))
        q = qkv[:, 0:128]
        kv = qkv[:, 128:256]
        q = (q * cosine + turn(q, self.first_half) * sine).astype(BF16)
        kv = jnp.where(self.is_key, kv * cosine + turn(kv, self.first_half) * sine, kv).astype(BF16)
        self.qkv_ref[row, tokens, 0:128] = q
        self.qkv_ref[row, tokens, 128:256] = kv
        length = 256 * (i + 1)
        keys = self.qkv_ref[row, 0:length, 128:192]
        values = self.qkv_ref[row, 0:length, 192:256]
        place_key = lax.broadcasted_iota(jnp.int32, (256, length), 1).astype(F32)
        place_query = (lax.broadcasted_iota(jnp.int32, (256, length), 0) + 256 * i).astype(F32)
        allowed = (place_key <= place_query) & (place_key >= start_col[:, 0:1])
        outs, logs = [], []
        for head in range(2):
            query = q[:, 64 * head : 64 * head + 64]
            scores = jnp.where(allowed, mm(query, keys, NT) * (HEAD_DIM**-0.5), MASKED)
            top = jnp.max(scores, axis=1, keepdims=True)
            log_total = top + jnp.log(jnp.sum(jnp.exp(scores - top), axis=1, keepdims=True))
            outs.append(mm(jnp.exp(scores - log_total).astype(BF16), values))
            logs.append(log_total)
        self.o_ref[row, tokens, :] = jnp.concatenate(outs, axis=1).astype(BF16)
        self.lse_ref[row, tokens, :] = jnp.where(self.is_key, logs[0], logs[1])


def forward_kernel(
    x_ref, w_ref, g_ref, seg_ref, cos_ref, sin_ref, freq_ref, wo_ref, ids_ref, dy_ref, wq_ref, own_piece, other_piece,
    h1_out, qkv_ref, lse_ref, o_ref, angle_ref, start_ref, gain_ref, mid_ref, gate_ref, w_all,
    h2_all, dy_all, table_all, wq_block, far_piece, mate_piece,
    h1_ref, o_full, h2_own, table_own,
    os, orv, w_send, w_recv, a_send, a_recv, b_send, b_recv, s0, r0, s1, r1, ts, tr, zs, zr, cs, cr, es, er, local,
):
    spot = Spot()
    spot.greet(NARROW * WIDE)
    mate_base = (1 - spot.half) * WIDE
    own_base = spot.half * WIDE
    mate_slot = mate_base + spot.w

    def w_source(half):
        return wo_ref if half is None else wo_ref.at[pl.ds(2 * half, 2)]

    def w_place(who, half):
        return w_all.at[:, who] if half is None else w_all.at[pl.ds(2 * half, 2), who]

    w_gather = PlaneGather(spot, w_source, w_place, w_send, w_recv)
    dy_gather = gather_tokens(spot, dy_ref.at[spot.half], dy_all, own_base, a_send, a_recv)
    mate_dy_gather = gather_tokens(spot, dy_ref.at[1 - spot.half], dy_all, mate_base, b_send, b_recv)
    w_gather.begin()
    dy_gather.begin()

    def column(step, arriving):
        other = lax.rem(spot.n + step, NARROW)
        place = other if arriving else spot.n
        return remote(wq_ref, wq_block.at[place], cs.at[other], cr.at[place], (other, spot.w))

    def start_column(step, carry):
        column(step, False).start()
        return carry

    def wait_column(step, carry):
        column(step, False).wait_send()
        column(step, True).wait_recv()
        return carry

    keep = [
        pltpu.make_async_copy(wo_ref, w_place(spot.w, None), local.at[0]),
        pltpu.make_async_copy(dy_ref.at[spot.half], dy_all.at[spot.slot], local.at[1]),
        pltpu.make_async_copy(dy_ref.at[1 - spot.half], dy_all.at[mate_slot], local.at[2]),
        pltpu.make_async_copy(wq_ref, wq_block.at[spot.n], local.at[7]),
    ]
    for copy in keep:
        copy.start()

    def heads(to, place):
        return (
            o_ref.at[:, pl.ds(to * SPAN, SPAN), :],
            o_full.at[:, :, pl.ds(pl.multiple_of(place * 128, 128), 128)],
        )

    def each_head_copy(to, act_local, act_remote):
        source, target = heads(to, spot.w)

        @pl.when(spot.w == to)
        def _():
            act_local(pltpu.make_async_copy(source, target, local.at[3]))

        @pl.when(spot.w != to)
        def _():
            act_remote(remote(source, target, os.at[to], orv.at[spot.w], spot.wide(to)))

    expert = lax.broadcasted_iota(jnp.int32, (32, TOKENS), 0)
    named = jnp.zeros((32, TOKENS), F32)
    for k in range(TOP):
        named = jnp.where(expert == ids_ref[k : k + 1, :], 1.0, named)
    before = lax.broadcasted_iota(jnp.int32, (TOKENS, TOKENS), 0) < lax.broadcasted_iota(
        jnp.int32, (TOKENS, TOKENS), 1
    )
    places = mm(named.astype(BF16), jnp.where(before, 1.0, 0.0).astype(BF16))
    kept = jnp.where((named > 0.5) & (places < float(CAP)), places, -1.0)

    gains = g_ref[...]
    gain_one = gather_gain(gains[:, 0, :])
    gain_two = gather_gain(gains[:, 1, :])
    gain_ref[...] = jnp.concatenate([gain_one, gain_two, jnp.zeros((6, WIDTH), F32)], axis=0)
    attention = Attention(
        x_ref, w_ref, seg_ref, cos_ref, sin_ref, freq_ref, gain_one,
        h1_ref, qkv_ref, lse_ref, o_ref, angle_ref, start_ref,
    )
    between = {1: [w_gather.middle], 2: [w_gather.late, dy_gather.middle], 3: [w_gather.last, dy_gather.late]}
    for i in range(4):
        for row in range(2):
            attention.chunk(row, i)
        for to in (2 * i, 2 * i + 1):
            each_head_copy(to, lambda copy: copy.start(), lambda copy: copy.start())
        for step in between.get(i, []):
            step()
    pair = lax.div(spot.n, 2)
    far = remote(own_piece, far_piece, es.at[0], er.at[0], (spot.n + 2 - 4 * pair, spot.w))
    far.start()
    near = remote(other_piece, mate_piece, es.at[1], er.at[1], (spot.mate, spot.w))
    h1_copy = pltpu.make_async_copy(h1_ref, h1_out, local.at[4])
    h1_copy.start()
    dy_gather.last()
    mate_dy_gather.begin()
    w_gather.finish()
    keep[0].wait()
    for to in range(WIDE):
        each_head_copy(to, lambda copy: copy.wait(), lambda copy: copy.wait_send())

    def wait_heads(step, carry):
        other = lax.rem(spot.w + step, WIDE)
        target = o_full.at[:, :, pl.ds(pl.multiple_of(other * 128, 128), 128)]
        remote(target, target, os.at[0], orv.at[other], spot.wide(other)).wait_recv()
        return carry

    lax.fori_loop(1, WIDE, wait_heads, 0)
    attended = o_full[...].reshape(TOKENS, WIDTH)
    x_own = x_ref[spot.w].reshape(TOKENS, WIDTH).astype(F32)
    mid = x_own + mm(attended, w_all[:, :, :, 0:WIDTH].reshape(WIDTH, WIDTH))
    mid_ref[...] = mid
    scale = lax.rsqrt(jnp.mean(mid * mid, axis=1, keepdims=True) + EPSILON)
    h2 = (mid * scale * gain_two).astype(BF16)
    h2_own[...] = h2
    across = remote(h2_own, h2_all.at[spot.slot], zs.at[0], zr.at[0], (spot.mate, spot.w))
    across.start()
    first = gather_tokens(spot, h2_own, h2_all, own_base, s0, r0)
    first.begin()
    keep_own = pltpu.make_async_copy(h2_own, h2_all.at[spot.slot], local.at[5])
    keep_own.start()

    logits = jnp.transpose(mm(h2, w_all[:, :, :, WIDTH : WIDTH + 128].reshape(WIDTH, 128)))[0:32]
    chosen = jnp.where(named > 0.5, logits, MASKED)
    rise = jnp.where(named > 0.5, jnp.exp(chosen - jnp.max(chosen, axis=0, keepdims=True)), 0.0)
    gate = rise / jnp.sum(rise, axis=0, keepdims=True)
    gate_ref[0:32, :] = gate
    gate_ref[32:64, :] = named
    for owner in range(GROUP):
        table_own[owner, 0:2, :] = kept[2 * owner : 2 * owner + 2]
        table_own[owner, 2:4, :] = gate[2 * owner : 2 * owner + 2]
        table_own[owner, 4:8, :] = jnp.zeros((4, TOKENS), F32)

    def tables(step, arriving):
        other = lax.rem(spot.slot + step, GROUP)
        o_half, o_w = lax.div(other, WIDE), lax.rem(other, WIDE)
        place = other if arriving else spot.slot
        return remote(
            table_own.at[2 * o_w + o_half], table_all.at[place], ts.at[other], tr.at[place],
            (spot.n - spot.half + o_half, o_w),
        )

    def start_table(step, carry):
        tables(step, False).start()
        return carry

    lax.fori_loop(1, GROUP, start_table, 0)
    lax.fori_loop(1, NARROW, start_column, 0)
    table_mine = pltpu.make_async_copy(
        table_own.at[2 * spot.w + spot.half], table_all.at[spot.slot], local.at[6]
    )
    table_mine.start()

    mate_dy_gather.middle()
    mate_dy_gather.late()
    first.middle()
    mate_dy_gather.last()
    first.late()
    first.last()
    arriving = h2_all.at[mate_slot]
    remote(arriving, arriving, zs.at[0], zr.at[0], (spot.mate, spot.w)).wait_recv()
    second = gather_tokens(spot, arriving, h2_all, mate_base, s1, r1)
    second.begin()
    near.start()
    second.middle()
    second.late()
    second.last()

    def wait_table(step, carry):
        tables(step, False).wait_send()
        tables(step, True).wait_recv()
        return carry

    lax.fori_loop(1, GROUP, wait_table, 0)
    lax.fori_loop(1, NARROW, wait_column, 0)
    keep[3].wait()
    dy_gather.finish()
    mate_dy_gather.finish()
    first.finish()
    second.finish()
    across.wait_send()
    keep[1].wait()
    keep[2].wait()
    keep_own.wait()
    table_mine.wait()
    h1_copy.wait()
    for copy in (far, near):
        copy.wait_send()
        copy.wait_recv()


def forward_call(x_all, w_all, g_all, seg_all, cos_table, sin_table, freq, wo_block, ids, dy_pair, w_own, own, other):
    dma = pltpu.SemaphoreType.DMA
    copies = PlaneGather.COPIES
    return pl.pallas_call(
        forward_kernel,
        name="forward",
        out_shape=(
            jax.ShapeDtypeStruct((2, SEQ, WIDTH), BF16),
            jax.ShapeDtypeStruct((2, SEQ, 256), BF16),
            jax.ShapeDtypeStruct((2, SEQ, 128), F32),
            jax.ShapeDtypeStruct((2, SEQ, 128), BF16),
            jax.ShapeDtypeStruct((2, SEQ, 256), F32),
            jax.ShapeDtypeStruct((2, SEQ, 128), F32),
            jax.ShapeDtypeStruct((8, WIDTH), F32),
            jax.ShapeDtypeStruct((TOKENS, WIDTH), F32),
            jax.ShapeDtypeStruct((64, TOKENS), F32),
            jax.ShapeDtypeStruct((NARROW, WIDE, 32, WIDTH + 128), BF16),
            jax.ShapeDtypeStruct((GROUP, TOKENS, WIDTH), BF16),
            jax.ShapeDtypeStruct((GROUP, TOKENS, WIDTH), BF16),
            jax.ShapeDtypeStruct((GROUP, 8, TOKENS), F32),
            jax.ShapeDtypeStruct((NARROW, 32, 2 * WIDTH), BF16),
            jax.ShapeDtypeStruct((384, WIDTH), BF16),
            jax.ShapeDtypeStruct((384, WIDTH), BF16),
        ),
        in_specs=[IN_VMEM] * 7 + [IN_HBM, IN_VMEM, IN_VMEM, IN_VMEM, IN_HBM, IN_HBM],
        out_specs=(IN_HBM,) + (IN_VMEM,) * 9 + (IN_HBM,) * 6,
        scratch_shapes=[
            pltpu.VMEM((2, SEQ, WIDTH), BF16),
            pltpu.VMEM((2, SPAN, WIDTH), BF16),
            pltpu.VMEM((TOKENS, WIDTH), BF16),
            pltpu.VMEM((GROUP, 8, TOKENS), F32),
            dma((WIDE,)),
            dma((WIDE,)),
        ]
        + [dma((copies,))] * 10
        + [dma((GROUP,)), dma((GROUP,)), dma((1,)), dma((1,)), dma((NARROW,)), dma((NARROW,)), dma((2,)), dma((2,)), dma((8,))],
        compiler_params=pltpu.CompilerParams(collective_id=2, has_side_effects=True, vmem_limit_bytes=VMEM_BYTES),
        cost_estimate=duration(1),
    )(x_all.reshape(WIDE, 2, SPAN, WIDTH), w_all, g_all, seg_all, cos_table, sin_table, freq, wo_block, ids, dy_pair, w_own, own, other)


def load_quarters(pieces, target, first, depth, sems, base):
    n = lax.axis_index("narrow")
    half, pair = lax.rem(n, 2), lax.div(n, 2)
    mate = n + 1 - 2 * half
    far = n + 2 - 4 * pair
    far_mate = mate + 2 - 4 * pair
    copies = []
    for number, (piece, quarter) in enumerate(zip(pieces, (n, mate, far, far_mate))):
        copies.append(
            pltpu.make_async_copy(
                piece.at[pl.ds(first, depth)],
                target.at[pl.ds(pl.multiple_of(quarter * depth, depth), depth)],
                sems.at[base + number],
            )
        )
    return copies


def pick(table_ref, source, expert):
    slot = lax.broadcasted_iota(jnp.int32, (SLOTS, TOKENS), 0).astype(F32)
    return slot == table_ref[source, expert : expert + 1, :]


def expert_kernel(e, *refs):
    if e == 0:
        h2_ref, dy_ref, table_ref, w0, w1, w2, w3 = refs[:7]
        refs = refs[7:]
    else:
        h2_ref, dy_ref, table_ref, w0, w1, w2, w3, y_before, dgate_before = refs[:9]
        refs = refs[9:]
    rows_ref, da_ref, y_ref, dgate_ref, down_grad_ref, w_gu, w_down, down_sum, sems = refs
    step = pl.program_id(0)

    @pl.when(step == 0)
    def _():
        pieces = (w0, w1, w2, w3)
        copies = load_quarters(pieces, w_gu, 0, 256, sems, 0) + load_quarters(pieces, w_down, 256, 128, sems, 4)
        for copy in copies:
            copy.start()
        down_sum[...] = jnp.zeros_like(down_sum)
        for copy in copies:
            copy.wait()

    masks = [pick(table_ref, s, e) for s in range(CHUNK)]
    hots = [jnp.where(mask, 1.0, 0.0).astype(BF16) for mask in masks]
    rows = jnp.concatenate([mm(hots[s], h2_ref[s]) for s in range(CHUNK)], axis=0).astype(BF16)
    grad_rows = jnp.concatenate([mm(hots[s], dy_ref[s]) for s in range(CHUNK)], axis=0)
    gates = jnp.concatenate(
        [
            jnp.sum(jnp.where(masks[s], table_ref[s, 2 + e : 3 + e, :], 0.0), axis=1, keepdims=True)
            for s in range(CHUNK)
        ],
        axis=0,
    )
    rows_ref[0] = rows
    g = mm(rows, w_gu[:, 0:FF])
    u = mm(rows, w_gu[:, FF : 2 * FF])
    sigmoid = 1.0 / (1.0 + jnp.exp(-g))
    active = g * sigmoid
    hidden = (active * u).astype(BF16)
    y = mm(hidden, w_down[...]).astype(BF16).astype(F32)
    slot_dgate = jnp.sum(y * grad_rows, axis=1, keepdims=True)
    if e == 0:
        dgate_ref[...] = jnp.zeros_like(dgate_ref)
    else:
        dgate_ref[...] = dgate_before[...]
    for s in range(CHUNK):
        part = slot_dgate[s * SLOTS : (s + 1) * SLOTS]
        dgate_ref[s, e : e + 1, :] = jnp.sum(jnp.where(masks[s], part, 0.0), axis=0, keepdims=True)
    gated = (y * gates).astype(BF16)
    dy_pair = (grad_rows * gates).astype(BF16)
    down_sum[...] += mm(hidden, dy_pair, TN)
    dhid = mm(dy_pair, w_down[...], NT)
    da_ref[0, :, 0:FF] = (dhid * u * (sigmoid * (1.0 + g * (1.0 - sigmoid)))).astype(BF16)
    da_ref[0, :, FF : 2 * FF] = (dhid * active).astype(BF16)
    for s in range(CHUNK):
        back = mm(hots[s], gated[s * SLOTS : (s + 1) * SLOTS], TN)
        if e == 1:
            back = back + y_before[s].astype(F32)
        y_ref[s] = back.astype(BF16)

    @pl.when(step == pl.num_programs(0) - 1)
    def _():
        down_grad_ref[...] = down_sum[...].astype(BF16)


STEPS = GROUP // CHUNK


def expert_specs():
    block = pl.BlockSpec((CHUNK, TOKENS, WIDTH), lambda c, *_: (c, 0, 0))
    small = pl.BlockSpec((CHUNK, 8, TOKENS), lambda c, *_: (c, 0, 0))
    slots = pl.BlockSpec((1, CHUNK * SLOTS, WIDTH), lambda c, *_: (c, 0, 0))
    return block, small, slots


def expert_call(e, h2_all, dy_all, table_all, pieces, before):
    block, small, slots = expert_specs()
    return pl.pallas_call(
        functools.partial(expert_kernel, e),
        name=f"expert_{e}",
        grid=(STEPS,),
        out_shape=(
            jax.ShapeDtypeStruct((STEPS, CHUNK * SLOTS, WIDTH), BF16),
            jax.ShapeDtypeStruct((STEPS, CHUNK * SLOTS, 2 * FF), BF16),
            jax.ShapeDtypeStruct((GROUP, TOKENS, WIDTH), BF16),
            jax.ShapeDtypeStruct((GROUP, 8, TOKENS), F32),
            jax.ShapeDtypeStruct((FF, WIDTH), BF16),
        ),
        in_specs=[block, block, small] + [IN_HBM] * 4 + ([block, small] if e else []),
        out_specs=(slots, slots, block, small, pl.BlockSpec((FF, WIDTH), lambda c: (0, 0))),
        scratch_shapes=[
            pltpu.VMEM((WIDTH, 2 * FF), BF16),
            pltpu.VMEM((FF, WIDTH), BF16),
            pltpu.VMEM((FF, WIDTH), F32),
            pltpu.SemaphoreType.DMA((8,)),
        ],
        compiler_params=pltpu.CompilerParams(vmem_limit_bytes=VMEM_BYTES),
        cost_estimate=duration(1),
    )(h2_all, dy_all, table_all, *pieces, *before)


def weight_grad_kernel(n_ref, rows_ref, da_ref, down_ref, own, mate, far, far_mate):
    step = pl.program_id(0)
    rows = rows_ref[...].reshape(GROUP * SLOTS, WIDTH // NARROW)
    da = da_ref[...].reshape(GROUP * SLOTS, 2 * FF)
    grad = mm(rows, da, TN).astype(BF16)
    for number, out in enumerate((own, mate, far, far_mate)):

        @pl.when(step == number)
        def _():
            out[0:256, :] = grad
            out[256:384, :] = down_ref[...]


def weight_grad_call(e, n_row, rows, da, down_grad):
    def quarter(step, n_ref):
        n = n_ref[0]
        mate = n + 1 - 2 * lax.rem(n, 2)
        far = 2 - 4 * lax.div(n, 2)
        return jnp.where(lax.rem(step, 2) == 1, mate, n) + jnp.where(step >= 2, far, 0)

    whole = pl.BlockSpec((384, WIDTH), lambda j, n_ref: (0, 0))
    return pl.pallas_call(
        weight_grad_kernel,
        name=f"weight_grad_{e}",
        grid_spec=pltpu.PrefetchScalarGridSpec(
            num_scalar_prefetch=1,
            grid=(NARROW,),
            in_specs=[
                pl.BlockSpec((STEPS, CHUNK * SLOTS, 256), lambda j, n_ref: (0, 0, quarter(j, n_ref))),
                pl.BlockSpec((STEPS, CHUNK * SLOTS, 2 * FF), lambda j, n_ref: (0, 0, 0)),
                pl.BlockSpec((128, WIDTH), lambda j, n_ref: (quarter(j, n_ref), 0)),
            ],
            out_specs=(whole,) * 4,
        ),
        out_shape=(jax.ShapeDtypeStruct((384, WIDTH), BF16),) * 4,
        compiler_params=pltpu.CompilerParams(vmem_limit_bytes=VMEM_BYTES),
        cost_estimate=duration(1),
    )(n_row, rows, da, down_grad)


def rows_grad_kernel(e, *refs):
    if e == 0:
        da_ref, table_ref, w0, w1, w2, w3, out_ref, w_gu, sems = refs
    else:
        da_ref, table_ref, w0, w1, w2, w3, before, out_ref, w_gu, sems = refs
    step = pl.program_id(0)

    @pl.when(step == 0)
    def _():
        copies = load_quarters((w0, w1, w2, w3), w_gu, 0, 256, sems, 0)
        for copy in copies:
            copy.start()
        for copy in copies:
            copy.wait()

    grads = mm(da_ref[0], w_gu[...], NT).astype(BF16)
    for s in range(CHUNK):
        hot = jnp.where(pick(table_ref, s, e), 1.0, 0.0).astype(BF16)
        back = mm(hot, grads[s * SLOTS : (s + 1) * SLOTS], TN)
        if e == 1:
            back = back + before[s].astype(F32)
        out_ref[s] = back.astype(BF16)


def rows_grad_call(e, da, table_all, pieces, before):
    block, small, slots = expert_specs()
    return pl.pallas_call(
        functools.partial(rows_grad_kernel, e),
        name=f"rows_grad_{e}",
        grid=(STEPS,),
        out_shape=jax.ShapeDtypeStruct((GROUP, TOKENS, WIDTH), BF16),
        in_specs=[slots, small] + [IN_HBM] * 4 + ([block] if e else []),
        out_specs=block,
        scratch_shapes=[pltpu.VMEM((WIDTH, 2 * FF), BF16), pltpu.SemaphoreType.DMA((4,))],
        compiler_params=pltpu.CompilerParams(vmem_limit_bytes=VMEM_BYTES),
        cost_estimate=duration(1),
    )(da, table_all, *pieces, *before)


def owner_sum_kernel(half_ref, own, mate, far, far_mate, *refs):
    gate_up_ref, down_ref = refs[-2:]
    first, second = (own, far), (mate, far_mate)
    for step, (left, right) in enumerate((first, second)):

        @pl.when(pl.program_id(0) == step)
        def _():
            total = left[...].astype(F32) + right[...].astype(F32)
            gate_up_ref[0] = total[0:256]
            down_ref[0] = total[256:384]


def owner_sum_call(e, half_row, parts, before, after):
    def place(step, half_ref):
        return (2 * lax.rem(half_ref[0] + step, 2) + e, 0, 0)

    whole = pl.BlockSpec((384, WIDTH), lambda j, half_ref: (0, 0))
    return pl.pallas_call(
        owner_sum_kernel,
        name=f"owner_sum_{e}",
        grid_spec=pltpu.PrefetchScalarGridSpec(
            num_scalar_prefetch=1,
            grid=(2,),
            in_specs=[whole] * 4 + [IN_HBM] * (len(before) + 1),
            out_specs=(pl.BlockSpec((1, 256, WIDTH), place), pl.BlockSpec((1, 128, WIDTH), place)),
        ),
        out_shape=(
            jax.ShapeDtypeStruct((4, 256, WIDTH), F32),
            jax.ShapeDtypeStruct((4, 128, WIDTH), F32),
        ),
        input_output_aliases={6: 0, 7: 1} if before else {},
        compiler_params=pltpu.CompilerParams(vmem_limit_bytes=VMEM_BYTES),
        cost_estimate=duration(1),
    )(half_row, *parts, after, *before)


def widen(ref_value):
    return ref_value.astype(F32)


class PlaneReduce:
    COPIES = 10

    def __init__(self, spot, part, buffers, send, recv, local):
        self.spot, self.part = spot, part
        self.acc, self.from_core, self.from_one, self.from_two = buffers
        self.send, self.recv, self.local = send, recv, local
        self.started = []
        s = spot
        self.q_own = 2 * s.y + s.x
        self.q_x = 2 * s.y + 1 - s.x
        self.q_y = 2 - 2 * s.y + s.x
        self.q_d = 3 - self.q_own

    def put(self, src, dst, number, to):
        copy = remote(src, dst, self.send.at[number], self.recv.at[number], self.spot.wide(to))
        copy.start()
        self.started.append(copy)

    def got(self, dst, number):
        remote(dst, dst, self.send.at[number], self.recv.at[number], self.spot.wide(self.spot.sib)).wait_recv()

    def begin(self):
        s = self.spot
        self.loads = []
        for q in range(4):
            self.put(self.part(2 * q + 1 - s.core), self.from_core.at[q], q, s.sib)
            copy = pltpu.make_async_copy(self.part(2 * q + s.core), self.acc.at[q], self.local.at[q])
            copy.start()
            self.loads.append(copy)

    def across_core(self):
        s = self.spot
        for q in range(4):
            self.loads[q].wait()
            self.got(self.from_core.at[q], q)
            self.acc[q] = (widen(self.acc[q]) + widen(self.from_core[q])).astype(BF16)
        self.put(halves(self.acc.at[self.q_d], 0), self.from_one.at[1], 5, s.xn)
        self.put(halves(self.acc.at[self.q_d], 1), self.from_one.at[3], 7, s.yn)
        self.put(halves(self.acc.at[self.q_x], 0), self.from_one.at[0], 4, s.xn)
        self.put(halves(self.acc.at[self.q_y], 1), self.from_one.at[2], 6, s.yn)

    def across_one(self):
        s = self.spot
        self.got(self.from_one.at[1], 5)
        upper = halves(self.acc.at[self.q_y], 0)
        upper[...] = (widen(upper[...]) + widen(self.from_one[1])).astype(BF16)
        self.put(upper, self.from_two.at[0], 8, s.yn)
        self.got(self.from_one.at[3], 7)
        lower = halves(self.acc.at[self.q_x], 1)
        lower[...] = (widen(lower[...]) + widen(self.from_one[3])).astype(BF16)
        self.put(lower, self.from_two.at[1], 9, s.xn)

    def total(self, out):
        self.got(self.from_one.at[0], 4)
        self.got(self.from_two.at[0], 8)
        own = self.acc.at[self.q_own]
        out[0:SPAN, :] = widen(own[0:SPAN, :]) + widen(self.from_one[0]) + widen(self.from_two[0])
        self.got(self.from_one.at[2], 6)
        self.got(self.from_two.at[1], 9)
        out[SPAN:TOKENS, :] = widen(own[SPAN:TOKENS, :]) + widen(self.from_one[2]) + widen(self.from_two[1])

    def finish(self):
        for copy in self.started:
            copy.wait_send()


def halves(ref, which):
    return ref.at[pl.ds(which * SPAN, SPAN)]


class GroupReduce:
    def __init__(self, spot, theirs, ours, scratch):
        acc, from_core, from_one, from_two, total, mate_send, mate_recv, send, recv, local, zs, zr = scratch
        self.total_ref, self.mate_send, self.mate_recv = total, mate_send, mate_recv
        parts = []
        for which, part in enumerate((theirs, ours)):
            buffers = (acc.at[which], from_core.at[which], from_one.at[which], from_two.at[which])
            parts.append(PlaneReduce(spot, part, buffers, send.at[which], recv.at[which], local.at[which]))
        self.theirs, self.ours = parts
        self.across = remote(mate_send, mate_recv, zs.at[0], zr.at[0], (spot.mate, spot.w))

    def begin(self):
        self.theirs.begin()
        self.ours.begin()

    def across_core(self):
        self.theirs.across_core()
        self.ours.across_core()

    def across_one(self):
        self.theirs.across_one()
        self.ours.across_one()

    def to_mate(self):
        self.theirs.total(self.total_ref)
        self.mate_send[...] = self.total_ref[...].astype(BF16)
        self.across.start()

    def finish(self):
        self.ours.total(self.total_ref)
        self.across.wait_recv()
        self.total_ref[...] += widen(self.mate_recv[...])
        self.theirs.finish()
        self.ours.finish()
        self.across.wait_send()


def reduce_scratch():
    dma = pltpu.SemaphoreType.DMA
    return [
        pltpu.VMEM((2, 4, TOKENS, WIDTH), BF16),
        pltpu.VMEM((2, 4, TOKENS, WIDTH), BF16),
        pltpu.VMEM((2, 4, SPAN, WIDTH), BF16),
        pltpu.VMEM((2, 2, SPAN, WIDTH), BF16),
        pltpu.VMEM((TOKENS, WIDTH), F32),
        pltpu.VMEM((TOKENS, WIDTH), BF16),
        pltpu.VMEM((TOKENS, WIDTH), BF16),
        dma((2, PlaneReduce.COPIES)),
        dma((2, PlaneReduce.COPIES)),
        dma((2, 4)),
        dma((1,)),
        dma((1,)),
    ]


REDUCE_REFS = 12


class AttentionBack:
    def __init__(self, dattn_all, w_rows, qkv_ref, lse_ref, o_ref, angle_ref, start_ref, dqkv_ref, dkv_ref, dq_ref, osum):
        self.dattn_all, self.w_rows, self.qkv, self.lse, self.o = dattn_all, w_rows, qkv_ref, lse_ref, o_ref
        self.angle, self.start = angle_ref, start_ref
        self.dqkv, self.dkv, self.dq, self.osum = dqkv_ref, dkv_ref, dq_ref, osum
        self.first_half = lane_half()
        self.is_key = lax.broadcasted_iota(jnp.int32, (1, 128), 1) < 64
        dkv_ref[...] = jnp.zeros_like(dkv_ref)
        osum[...] = jnp.zeros_like(osum)

    def stack(self, both):
        return jnp.concatenate([both[:, 0:64], both[:, 64:128]], axis=0)

    def chunk(self, row, q):
        first = pl.multiple_of(q * 256, 256)
        tokens = pl.ds(first, 256)
        dattn = self.dattn_all[pl.ds(2 * q, 2), pl.ds(row * SPAN, SPAN), :].reshape(256, WIDTH)
        outs = self.o[row, tokens, :]
        do = mm(dattn, self.w_rows[...], NT).astype(BF16)
        self.osum[...] += mm(outs, dattn, TN)
        inner = do.astype(F32) * outs.astype(F32)
        delta = jnp.concatenate(
            [
                jnp.sum(jnp.where(self.is_key, inner, 0.0), axis=1, keepdims=True),
                jnp.sum(jnp.where(self.is_key, 0.0, inner), axis=1, keepdims=True),
            ],
            axis=0,
        )
        query = self.stack(self.qkv[row, tokens, 0:128])
        do = self.stack(do)
        log_total = jnp.concatenate([self.lse[row, tokens, 0:1], self.lse[row, tokens, 64:65]], axis=0)
        start = self.start[row, tokens, 0:1]
        start = jnp.concatenate([start, start], axis=0)
        place = lax.broadcasted_iota(jnp.int32, (256, 1), 0)
        place_query = (jnp.concatenate([place, place], axis=0) + q * 256).astype(F32)
        self.dq[...] = jnp.zeros_like(self.dq)

        def key_block(block, carry):
            keys_at = pl.ds(pl.multiple_of(block * 256, 256), 256)
            keys = self.qkv[row, keys_at, 128:192]
            values = self.qkv[row, keys_at, 192:256]
            place_key = (lax.broadcasted_iota(jnp.int32, (1, 256), 1) + block * 256).astype(F32)
            allowed = (place_key <= place_query) & (place_key >= start)
            scores = jnp.where(allowed, mm(query, keys, NT) * (HEAD_DIM**-0.5), MASKED)
            weights = jnp.exp(scores - log_total)
            dp = mm(do, values, NT)
            ds = (weights * (dp - delta)).astype(BF16)
            self.dq[...] += mm(ds, keys)
            dk = mm(ds, query, TN) * (HEAD_DIM**-0.5)
            dv = mm(weights.astype(BF16), do, TN)
            self.dkv[row, keys_at, :] += jnp.concatenate([dk, dv], axis=1)
            return carry

        lax.fori_loop(0, q + 1, key_block, 0)
        dq = jnp.concatenate([self.dq[0:256], self.dq[256:512]], axis=1) * (HEAD_DIM**-0.5)
        cosine = self.angle[row, tokens, 0:128]
        sine = self.angle[row, tokens, 128:256]
        self.dqkv[row, tokens, 0:128] = (dq * cosine + turn_back(dq * sine, self.first_half)).astype(BF16)

    def keys(self, row):
        cosine = self.angle[row, :, 0:128]
        sine = self.angle[row, :, 128:256]
        dkv = self.dkv[row]
        turned = dkv * cosine + turn_back(dkv * sine, self.first_half)
        self.dqkv[row, :, 128:256] = jnp.where(self.is_key, turned, dkv).astype(BF16)


def backward_kernel(*refs):
    (
        part_ref, y_ref, dgate_ref, h2_ref, w_out_ref, w_full_ref, h1_ref, qkv_ref, lse_ref, o_ref,
        angle_ref, start_ref, x_ref, mid_ref, gate_ref, gain_ref, dy_ref,
    ) = refs[:17]
    block_out, in_grad, q_grad, k_grad, v_grad, o_grad, sums, gain_sum = refs[17:25]
    (
        dgate_all, h2_own, dattn_all, dmid_ref, small_ref, small_all, small_sum, w_router, w_rows, w_full,
        h1, qkv, lse, outs, angle, start, dqkv_ref, dkv_ref, dq_ref, osum, og_ref, wg_ref,
        dq_full, w_recv, o_recv, s_recv, gain_own, g_recv,
        ts, tr, s0, r0, bs, br, qs, qr, ws, wr, os, orv, ss, sr, gs, gr, local,
    ) = refs[25:70]
    h2_sum_refs = refs[70 : 70 + REDUCE_REFS]
    y_sum_refs = refs[70 + REDUCE_REFS :]

    spot = Spot()
    everyone = NARROW * WIDE
    spot.greet(everyone)
    base, mate_base = spot.half * WIDE, (1 - spot.half) * WIDE
    h2_sum = GroupReduce(
        spot, lambda who: part_ref.at[mate_base + who], lambda who: part_ref.at[base + who], h2_sum_refs
    )
    y_sum = GroupReduce(spot, lambda who: y_ref.at[mate_base + who], lambda who: y_ref.at[base + who], y_sum_refs)
    h2_sum.begin()

    def tables(step, arriving):
        other = lax.rem(spot.slot + step, GROUP)
        o_half, o_w = lax.div(other, WIDE), lax.rem(other, WIDE)
        place = other if arriving else spot.slot
        return remote(
            dgate_ref.at[other], dgate_all.at[place], ts.at[other], tr.at[place],
            (spot.n - spot.half + o_half, o_w),
        )

    def start_table(step, carry):
        tables(step, False).start()
        return carry

    lax.fori_loop(1, GROUP, start_table, 0)
    rows = pl.ds(pl.multiple_of(spot.w * 128, 128), 128)
    loads = [
        (dgate_ref.at[spot.slot], dgate_all.at[spot.slot]),
        (h2_ref.at[spot.slot], h2_own),
        (w_out_ref.at[:, pl.ds(WIDTH, 128)], w_router),
        (w_out_ref.at[rows, pl.ds(0, WIDTH)], w_rows),
        (qkv_ref, qkv),
        (lse_ref, lse),
        (o_ref, outs),
        (angle_ref, angle),
        (start_ref, start),
        (h1_ref, h1),
    ]
    loads = [pltpu.make_async_copy(src, dst, local.at[i]) for i, (src, dst) in enumerate(loads)]
    for copy in loads:
        copy.start()
    w_loads = [pltpu.make_async_copy(w_full_ref.at[who], w_full.at[:, who], local.at[10 + who]) for who in range(WIDE)]
    for copy in w_loads:
        copy.start()
    y_sum.begin()
    h2_sum.across_core()
    h2_sum.across_one()
    h2_sum.to_mate()
    y_sum.across_core()
    h2_sum.finish()

    def wait_table(step, carry):
        tables(step, False).wait_send()
        tables(step, True).wait_recv()
        return carry

    lax.fori_loop(1, GROUP, wait_table, 0)
    for copy in loads[:4]:
        copy.wait()

    gate = gate_ref[0:32, :]
    dgate = jnp.concatenate([dgate_all[(o % 2) * WIDE + o // 2, 0:2, :] for o in range(GROUP)], axis=0)
    dsel = gate * (dgate - jnp.sum(gate * dgate, axis=0, keepdims=True))
    dlogits = jnp.concatenate([dsel, jnp.zeros((96, TOKENS), F32)], axis=0)
    dh2 = h2_sum.total_ref[...] + mm(jnp.transpose(dlogits).astype(BF16), w_router[...], NT)
    mid = mid_ref[...]
    scale = lax.rsqrt(jnp.mean(mid * mid, axis=1, keepdims=True) + EPSILON)
    weighted = dh2 * gain_ref[1:2, :]
    inner = jnp.mean(weighted * mid, axis=1, keepdims=True)
    dmid = dy_ref[...].astype(F32) + weighted * scale - mid * (scale * scale * scale) * inner
    dmid_ref[...] = dmid
    dattn_all[spot.w] = dmid.astype(BF16)
    mine = dattn_all.at[spot.w]
    gather = PlaneGather(
        spot,
        lambda half: mine if half is None else halves(mine, half),
        lambda who, half: dattn_all.at[who] if half is None else halves(dattn_all.at[who], half),
        s0, r0,
    )
    gather.begin()
    small_ref[0:32, :] = mm(dsel.astype(BF16), h2_own[...])
    small_ref[32:33, :] = jnp.sum(dh2 * mid * scale, axis=0, keepdims=True)
    lane = lax.broadcasted_iota(jnp.int32, (32, WIDTH), 1)
    column = lax.broadcasted_iota(jnp.int32, (32, WIDTH), 0)
    count = jnp.sum(gate_ref[32:64, :], axis=1, keepdims=True)
    small_ref[33:34, :] = jnp.sum(jnp.where(lax.rem(lane, 128) == column, count, 0.0), axis=0, keepdims=True)
    small_ref[34:40, :] = jnp.zeros((6, WIDTH), F32)

    def lanes_to(step, arriving):
        other = lax.rem(spot.w + step, WIDE)
        place = other if arriving else spot.w
        return remote(
            small_ref.at[:, pl.ds(pl.multiple_of(other * 128, 128), 128)], small_all.at[place],
            bs.at[other], br.at[place], spot.wide(other),
        )

    def start_lanes(step, carry):
        lanes_to(step, False).start()
        return carry

    lax.fori_loop(1, WIDE, start_lanes, 0)
    small_all[spot.w] = small_ref[:, pl.ds(pl.multiple_of(spot.w * 128, 128), 128)]

    for copy in loads[4:9]:
        copy.wait()
    back = AttentionBack(dattn_all, w_rows, qkv, lse, outs, angle, start, dqkv_ref, dkv_ref, dq_ref, osum)
    order = h2_sum.ours
    gather.got(spot.sib, None, 4)
    back.chunk(0, order.q_own)
    gather.middle()
    back.chunk(1, order.q_own)
    gather.late()
    gather.last()
    sib_x = spot.sib + 2 - 4 * spot.x
    sib_y = spot.sib + 4 - 8 * spot.y
    gather.got(sib_x, None, 7)
    back.chunk(0, order.q_x)
    back.chunk(1, order.q_x)
    y_sum.across_one()
    gather.got(sib_y, None, 8)
    back.chunk(0, order.q_y)
    back.chunk(1, order.q_y)
    y_sum.to_mate()
    sib_d = sib_x + 4 - 8 * spot.y
    gather.got(sib_d, 0, 9)
    gather.got(sib_d, 1, 10)
    back.chunk(0, order.q_d)
    back.chunk(1, order.q_d)
    for copy in gather.started:
        copy.wait_send()
    back.keys(0)
    back.keys(1)

    def to_plane(step, arriving):
        other = lax.rem(spot.w + step, WIDE)
        place = other if arriving else spot.w
        return remote(
            dqkv_ref.at[:, pl.ds(pl.multiple_of(other * SPAN, SPAN), SPAN), :],
            dq_full.at[:, :, pl.ds(pl.multiple_of(place * 256, 256), 256)],
            qs.at[other], qr.at[place], spot.wide(other),
        )

    def others(step):
        other = lax.rem(spot.me + step, everyone)
        return other, (lax.div(other, WIDE), lax.rem(other, WIDE))

    def rows_of(ref, owner):
        return ref.at[pl.ds(pl.multiple_of(owner * 32, 32), 32)]

    def lanes_of(ref, owner):
        return ref.at[:, pl.ds(pl.multiple_of(lax.div(owner, 4) * 128, 128), 128)]

    def to_owner(step, arriving):
        other, to = others(step)
        place = other if arriving else spot.me
        return remote(rows_of(wg_ref, other), w_recv.at[place], ws.at[other], wr.at[place], to)

    def gain_to_owner(step, arriving):
        other, to = others(step)
        place = other if arriving else spot.me
        return remote(lanes_of(gain_own, other), g_recv.at[place], gs.at[other], gr.at[place], to)

    def start_plane(step, carry):
        to_plane(step, False).start()
        return carry

    def start_owner(step, carry):
        to_owner(step, False).start()
        return carry

    def start_gain(step, carry):
        gain_to_owner(step, False).start()
        return carry

    lax.fori_loop(1, WIDE, start_plane, 0)
    plane_mine = pltpu.make_async_copy(
        dqkv_ref.at[:, pl.ds(pl.multiple_of(spot.w * SPAN, SPAN), SPAN), :],
        dq_full.at[:, :, pl.ds(pl.multiple_of(spot.w * 256, 256), 256)],
        local.at[0],
    )
    plane_mine.start()

    loads[9].wait()
    wg_ref[...] = (mm(h1[0], dqkv_ref[0], TN) + mm(h1[1], dqkv_ref[1], TN)).astype(BF16)
    lax.fori_loop(1, everyone, start_owner, 0)
    owner_mine = pltpu.make_async_copy(rows_of(wg_ref, spot.me), w_recv.at[spot.me], local.at[1])
    owner_mine.start()
    og_ref[...] = osum[...].astype(BF16)

    def wait_lanes(step, carry):
        lanes_to(step, False).wait_send()
        lanes_to(step, True).wait_recv()
        return carry

    lax.fori_loop(1, WIDE, wait_lanes, 0)
    lane_total = small_all[0]
    for device in range(1, WIDE):
        lane_total = lane_total + small_all[device]
    small_sum[...] = lane_total

    def output_copies(act_local, act_send, act_recv):
        for i in range(4):
            owner = 4 * spot.w + i
            to = (lax.div(owner, WIDE), lax.rem(owner, WIDE))
            source = og_ref.at[pl.ds(i * 32, 32)]
            here = owner == spot.me

            @pl.when(here)
            def _():
                act_local(pltpu.make_async_copy(source, o_recv.at[spot.n], local.at[3]))
                act_local(pltpu.make_async_copy(small_sum, s_recv.at[spot.n], local.at[2]))

            @pl.when(jnp.logical_not(here))
            def _():
                act_send(remote(source, o_recv.at[spot.n], os.at[i], orv.at[spot.n], to))
                act_send(remote(small_sum, s_recv.at[spot.n], ss.at[i], sr.at[spot.n], to))

        for plane in range(NARROW):
            giver = lax.div(spot.me, 4)
            here = (plane == spot.n) & (giver == spot.w)

            @pl.when(jnp.logical_not(here))
            def _():
                place = o_recv.at[plane]
                act_recv(remote(place, place, os.at[0], orv.at[plane], (plane, giver)))
                small = s_recv.at[plane]
                act_recv(remote(small, small, ss.at[0], sr.at[plane], (plane, giver)))

    def nothing(copy):
        return None

    output_copies(lambda c: c.start(), lambda c: c.start(), nothing)

    def wait_plane(step, carry):
        to_plane(step, False).wait_send()
        to_plane(step, True).wait_recv()
        return carry

    lax.fori_loop(1, WIDE, wait_plane, 0)
    plane_mine.wait()
    for copy in w_loads:
        copy.wait()
    dh1 = mm(dq_full[...].reshape(TOKENS, 2 * WIDTH), w_full[...].reshape(WIDTH, 2 * WIDTH), NT)
    x = x_ref[...].astype(F32)
    scale = lax.rsqrt(jnp.mean(x * x, axis=1, keepdims=True) + EPSILON)
    gain_own[0:1, :] = jnp.sum(dh1 * x * scale, axis=0, keepdims=True)
    gain_own[1:8, :] = jnp.zeros((7, WIDTH), F32)
    lax.fori_loop(1, everyone, start_gain, 0)
    gain_mine = pltpu.make_async_copy(lanes_of(gain_own, spot.me), g_recv.at[spot.me], local.at[0])
    gain_mine.start()
    weighted = dh1 * gain_ref[0:1, :]
    inner = jnp.mean(weighted * x, axis=1, keepdims=True)
    in_grad[...] = (dmid_ref[...] + weighted * scale - x * (scale * scale * scale) * inner).astype(BF16)
    y_sum.finish()
    block_out[...] = (mid_ref[...] + y_sum.total_ref[...]).astype(BF16)

    def wait_owner(step, carry):
        to_owner(step, False).wait_send()
        to_owner(step, True).wait_recv()
        return carry

    lax.fori_loop(1, everyone, wait_owner, 0)
    owner_mine.wait()
    output_copies(lambda c: c.wait(), lambda c: c.wait_send(), lambda c: c.wait_recv())
    for w in range(WIDE):
        total = widen(w_recv[w])
        for plane in range(1, NARROW):
            total = total + widen(w_recv[plane * WIDE + w])
        q_grad[:, 128 * w : 128 * w + 128] = total[:, 0:128]
        k_grad[:, 64 * w : 64 * w + 64] = total[:, 128:192]
        v_grad[:, 64 * w : 64 * w + 64] = total[:, 192:256]
    total = widen(o_recv[0])
    for plane in range(1, NARROW):
        total = total + widen(o_recv[plane])
    o_grad[...] = total
    total = s_recv[0]
    for plane in range(1, NARROW):
        total = total + s_recv[plane]
    sums[...] = total

    def wait_gain(step, carry):
        gain_to_owner(step, False).wait_send()
        gain_to_owner(step, True).wait_recv()
        return carry

    lax.fori_loop(1, everyone, wait_gain, 0)
    gain_mine.wait()
    total = g_recv[0]
    for device in range(1, everyone):
        total = total + g_recv[device]
    gain_sum[...] = total


def backward_call(*operands):
    dma = pltpu.SemaphoreType.DMA
    vmem = pltpu.VMEM
    everyone = NARROW * WIDE
    copies = PlaneGather.COPIES
    return pl.pallas_call(
        backward_kernel,
        name="backward",
        out_shape=(
            jax.ShapeDtypeStruct((TOKENS, WIDTH), BF16),
            jax.ShapeDtypeStruct((TOKENS, WIDTH), BF16),
            jax.ShapeDtypeStruct((32, WIDTH), F32),
            jax.ShapeDtypeStruct((32, WIDTH // 2), F32),
            jax.ShapeDtypeStruct((32, WIDTH // 2), F32),
            jax.ShapeDtypeStruct((32, WIDTH), F32),
            jax.ShapeDtypeStruct((40, 128), F32),
            jax.ShapeDtypeStruct((8, 128), F32),
        ),
        in_specs=[IN_HBM] * 12 + [IN_VMEM] * 5,
        out_specs=(IN_VMEM,) * 8,
        scratch_shapes=[
            vmem((GROUP, 8, TOKENS), F32),
            vmem((TOKENS, WIDTH), BF16),
            vmem((WIDE, TOKENS, WIDTH), BF16),
            vmem((TOKENS, WIDTH), F32),
            vmem((40, WIDTH), F32),
            vmem((WIDE, 40, 128), F32),
            vmem((40, 128), F32),
            vmem((WIDTH, 128), BF16),
            vmem((128, WIDTH), BF16),
            vmem((NARROW, WIDE, 32, 2 * WIDTH), BF16),
            vmem((2, SEQ, WIDTH), BF16),
            vmem((2, SEQ, 256), BF16),
            vmem((2, SEQ, 128), F32),
            vmem((2, SEQ, 128), BF16),
            vmem((2, SEQ, 256), F32),
            vmem((2, SEQ, 128), F32),
            vmem((2, SEQ, 256), BF16),
            vmem((2, SEQ, 128), F32),
            vmem((512, HEAD_DIM), F32),
            vmem((128, WIDTH), F32),
            vmem((128, WIDTH), BF16),
            vmem((WIDTH, 256), BF16),
            vmem((2, SPAN, 2 * WIDTH), BF16),
            vmem((everyone, 32, 256), BF16),
            vmem((NARROW, 32, WIDTH), BF16),
            vmem((NARROW, 40, 128), F32),
            vmem((8, WIDTH), F32),
            vmem((everyone, 8, 128), F32),
            dma((GROUP,)),
            dma((GROUP,)),
            dma((copies,)),
            dma((copies,)),
            dma((WIDE,)),
            dma((WIDE,)),
            dma((WIDE,)),
            dma((WIDE,)),
            dma((everyone,)),
            dma((everyone,)),
            dma((4,)),
            dma((NARROW,)),
            dma((4,)),
            dma((NARROW,)),
            dma((everyone,)),
            dma((everyone,)),
            dma((18,)),
        ]
        + reduce_scratch()
        + reduce_scratch(),
        compiler_params=pltpu.CompilerParams(collective_id=3, has_side_effects=True, vmem_limit_bytes=VMEM_BYTES),
        cost_estimate=duration(1),
    )(*operands)


def swap(values, distance):
    return lax.ppermute(values, "narrow", [(i, i ^ distance) for i in range(NARROW)])


def expert_pieces(w_gate_up, w_down, e, half):
    def piece(pair):
        return jnp.concatenate(
            [
                lax.dynamic_index_in_dim(w_gate_up, 2 * pair + e, 0, keepdims=False),
                lax.dynamic_index_in_dim(w_down, 2 * pair + e, 0, keepdims=False),
            ],
            axis=0,
        )

    return piece(half), piece(1 - half)


def position_tables():
    freq = (1.0 / np.float32(THETA) ** (np.arange(32, dtype=np.float32) * np.float32(2.0) / np.float32(HEAD_DIM))).astype(np.float32)
    angle = np.arange(SEQ, dtype=np.float32)[:, None] * freq[None, :]
    cosine = np.tile(np.cos(angle.astype(np.float64)), (1, 4)).astype(np.float32)
    sine = np.tile(np.sin(angle.astype(np.float64)), (1, 4)).astype(np.float32)
    return cosine, sine, np.tile(freq[None, :], (8, 4)).astype(np.float32)


def fast_device(
    hidden_in, out_grad, seg_ids, expert_ids, attn_gain, w_query, w_key, w_value, w_output,
    moe_gain, w_router, w_gate_up, w_down,
):
    n = lax.axis_index("narrow")
    w = lax.axis_index("wide")
    half = n % 2
    me = n * WIDE + w
    cos_table, sin_table, freq = position_tables()

    wo_own = jnp.concatenate([w_output, w_router, jnp.zeros((32, 96), BF16)], axis=1)
    x_own = hidden_in.reshape(TOKENS, WIDTH)
    dy_own = out_grad.reshape(TOKENS, WIDTH)
    w_own = jnp.concatenate(
        [w_query.reshape(32, WIDE, 128), w_key.reshape(32, WIDE, 64), w_value.reshape(32, WIDE, 64)], axis=2
    ).reshape(32, 2 * WIDTH)
    gains = jnp.concatenate([attn_gain[None], moe_gain[None]], axis=0).astype(F32)
    g_own = jnp.pad(gains, ((0, 6), (0, 96)))
    seg_own = jnp.pad(seg_ids, ((0, 6), (0, 0)))
    ids = expert_ids.reshape(TOKENS, TOP).T

    x_all, w_all, g_all, seg_all, wo_block, dy_pair = gather_call(x_own, w_own, g_own, seg_own, wo_own, dy_own)
    w_gate_up, w_down, x_all, dy_pair = lax.optimization_barrier((w_gate_up, w_down, x_all, dy_pair))
    own_0, other_0 = expert_pieces(w_gate_up, w_down, 0, half)
    own_1, other_1 = expert_pieces(w_gate_up, w_down, 1, half)
    pieces_0 = (own_0, swap(other_0, 1), swap(own_0, 2), swap(other_0, 3))
    (
        h1, qkv, lse, o_heads, angle, start, gain_rows, mid, gate, w_out, h2_all, dy_all, table_all, wq_block,
        far_1, mate_1,
    ) = forward_call(
        x_all, w_all, g_all, seg_all, cos_table, sin_table, freq, wo_block, ids, dy_pair, w_own, own_1, other_1
    )
    w_out = w_out.reshape(WIDTH, WIDTH + 128)
    other_1, h2_all = lax.optimization_barrier((other_1, h2_all))
    pieces_1 = (own_1, mate_1, far_1, swap(other_1, 3))
    n_row = n.reshape(1).astype(jnp.int32)
    half_row = half.reshape(1).astype(jnp.int32)

    def send_grads(e, rows, da, down_grad):
        own, mate, far, far_mate = weight_grad_call(e, n_row, rows, da, down_grad)
        own, da = lax.optimization_barrier((own, da))
        return da, (own, swap(mate, 1), swap(far, 2), swap(far_mate, 3))

    rows_0, da_0, y_0, dgate_0, down_grad_0 = expert_call(0, h2_all, dy_all, table_all, pieces_0, ())
    rows_0, wq_block = lax.optimization_barrier((rows_0, wq_block))
    w_full = lax.all_gather(wq_block, "wide", axis=0, tiled=False)
    da_0, grads_0 = send_grads(0, rows_0, da_0, down_grad_0)
    part_0 = rows_grad_call(0, da_0, table_all, pieces_0, ())
    pieces_1, part_0, own_0 = lax.optimization_barrier((pieces_1, part_0, grads_0[0]))
    grads_0 = (own_0,) + grads_0[1:]
    rows_1, da_1, y_1, dgate, down_grad_1 = expert_call(
        1, h2_all, dy_all, table_all, pieces_1, (y_0, dgate_0)
    )
    da_1, grads_1 = send_grads(1, rows_1, da_1, down_grad_1)
    part = rows_grad_call(1, da_1, table_all, pieces_1, (part_0,))
    block_out, in_grad, q_grad, k_grad, v_grad, o_grad, sums, gain_sum = backward_call(
        part, y_1, dgate, h2_all, w_out, w_full, h1, qkv, lse, o_heads, angle, start,
        x_own, mid, gate, gain_rows, dy_own,
    )
    sums_0 = owner_sum_call(0, half_row, grads_0, (), gain_sum)
    gate_up_sum, down_sum = owner_sum_call(1, half_row, grads_1, sums_0, gain_sum)
    lanes = (me % 4) * 32
    router_grad = lax.dynamic_slice(sums, (0, lanes), (32, 32)).T
    moe_gain_grad = lax.dynamic_slice(sums, (32, lanes), (1, 32)).reshape(32)
    attn_gain_grad = lax.dynamic_slice(gain_sum, (0, lanes), (1, 32)).reshape(32)
    expert_load = sums[33, 0:32].astype(jnp.int32)
    return (
        block_out.reshape(hidden_in.shape),
        in_grad.reshape(hidden_in.shape),
        attn_gain_grad,
        q_grad,
        k_grad,
        v_grad,
        o_grad,
        moe_gain_grad,
        router_grad,
        gate_up_sum,
        down_sum,
        expert_load,
    )


def solution(mesh):
    planned = mesh.shape["narrow"] == NARROW and mesh.shape["wide"] == WIDE
    return jax.shard_map(
        fast_device if planned else general_device,
        mesh=mesh,
        in_specs=(
            P("narrow", "wide", None),
            P("narrow", "wide", None),
            P("narrow", "wide"),
            P("narrow", "wide", None),
            P(("narrow", "wide")),
            P(("narrow", "wide"), None),
            P(("narrow", "wide"), None),
            P(("narrow", "wide"), None),
            P(("narrow", "wide"), None),
            P(("narrow", "wide")),
            P(("narrow", "wide"), None),
            P("wide", "narrow", None),
            P("wide", "narrow", None),
        ),
        out_specs=(
            P("narrow", "wide", None),
            P("narrow", "wide", None),
            P(("narrow", "wide")),
            P(("narrow", "wide"), None),
            P(("narrow", "wide"), None),
            P(("narrow", "wide"), None),
            P(("narrow", "wide"), None),
            P(("narrow", "wide")),
            P(("narrow", "wide"), None),
            P("wide", "narrow", None),
            P("wide", "narrow", None),
            P(),
        ),
        check_vma=False,
    )
```

```python
import math

import functools
import jax
import jax.numpy as jnp
import numpy as np
from jax import lax
from jax.experimental import pallas as pl
from jax.experimental.pallas import tpu as pltpu
from jax.sharding import PartitionSpec as P

KV_HEADS = 8
HEAD_DIM = 64
EXPERTS = 32
TOP = 8
FF = 512
CAP = 80


EPSILON = 1e-06
THETA = 10000.0
MASKED = -1e30


def rms_scale(values):
    return lax.rsqrt(jnp.mean(values * values, axis=-1, keepdims=True) + EPSILON)


def norm_back(values, scale, gain, upstream):
    weighted = upstream * gain
    inner_mean = jnp.mean(weighted * values, axis=-1, keepdims=True)
    value_grad = weighted * scale - values * (scale * scale * scale) * inner_mean
    gain_grad = jnp.sum(upstream * values * scale, axis=0)
    return (value_grad, gain_grad)


def lane_turn(head_dim):
    lane_ids = jnp.arange(128)
    lane_local = lane_ids % head_dim
    half_dim = head_dim // 2
    same_head = lane_ids[:, None] // head_dim == lane_ids[None, :] // head_dim
    from_upper = (lane_local[None, :] < half_dim) & (
        lane_local[:, None] == lane_local[None, :] + half_dim
    )
    from_lower = (lane_local[None, :] >= half_dim) & (
        lane_local[:, None] + half_dim == lane_local[None, :]
    )
    return jnp.where(
        same_head & from_upper, -1.0, jnp.where(same_head & from_lower, 1.0, 0.0)
    ).astype(jnp.float32)


def lane_angles(positions, head_dim):
    lane_ids = jnp.arange(128) % head_dim % (head_dim // 2)
    inverse = 1.0 / THETA ** (lane_ids.astype(jnp.float32) * 2.0 / head_dim)
    return positions[..., None] * inverse


def rotate(values, cos_table, sin_table, turner):
    dims_in = values.shape
    blocks = values.reshape(dims_in[0], dims_in[1], -1, 128)
    turned = jnp.einsum("abnl,lm->abnm", blocks, turner, precision=lax.Precision.HIGHEST)
    return (blocks * cos_table[:, :, None, :] + turned * sin_table[:, :, None, :]).reshape(dims_in)


def rotate_back(grad_in, cos_table, sin_table, turner):
    dims_in = grad_in.shape
    blocks = grad_in.reshape(dims_in[0], dims_in[1], -1, 128)
    turned = jnp.einsum(
        "abnm,lm->abnl", blocks * sin_table[:, :, None, :], turner, precision=lax.Precision.HIGHEST
    )
    return (blocks * cos_table[:, :, None, :] + turned).reshape(dims_in)


def masked_scores(query_five, key_block, seg_query, seg_key, place_query, place_key, factor):
    scores = (
        jnp.einsum("abgjd,akgd->agjbk", query_five, key_block, preferred_element_type=jnp.float32)
        * factor
    )
    allowed = (seg_query[:, :, None] == seg_key[:, None, :]) & (
        place_query[:, :, None] >= place_key[:, None, :]
    )
    return jnp.where(allowed[:, None, None], scores, MASKED)


def general_device(
    hidden_in,
    out_grad,
    seg_ids,
    expert_ids,
    attn_gain,
    w_query,
    w_key,
    w_value,
    w_output,
    moe_gain,
    w_router,
    w_gate_up,
    w_down,
):
    row_count, span_len, feat_dim = hidden_in.shape
    tok_count = row_count * span_len
    factor = HEAD_DIM ** (-0.5)
    kv_width = KV_HEADS * HEAD_DIM
    gain_one, query_w, key_w, value_w, output_w, gain_two, router_w = (
        lax.all_gather(attn_gain, ("narrow", "wide"), axis=0, tiled=True),
        lax.all_gather(w_query, ("narrow", "wide"), axis=0, tiled=True),
        lax.all_gather(w_key, ("narrow", "wide"), axis=0, tiled=True),
        lax.all_gather(w_value, ("narrow", "wide"), axis=0, tiled=True),
        lax.all_gather(w_output, ("narrow", "wide"), axis=0, tiled=True),
        lax.all_gather(moe_gain, ("narrow", "wide"), axis=0, tiled=True),
        lax.all_gather(w_router, ("narrow", "wide"), axis=0, tiled=True),
    )
    gate_up_w, down_w = (
        lax.all_gather(w_gate_up, "narrow", axis=1, tiled=True),
        lax.all_gather(w_down, "narrow", axis=1, tiled=True),
    )
    segs_all = lax.all_gather(seg_ids, "wide", axis=1, tiled=True)
    seq_len = segs_all.shape[1]
    key_step = math.gcd(seq_len, 512)
    place_local = lax.axis_index("wide") * span_len + jnp.arange(span_len, dtype=jnp.int32)
    place_query = place_local[None, :]
    starts = jnp.sum((segs_all[:, None, :] < seg_ids[:, :, None]).astype(jnp.int32), axis=-1)
    positions = (place_query - starts).astype(jnp.float32)
    angles = lane_angles(positions, HEAD_DIM)
    cos_table = jnp.cos(angles)
    sin_table = jnp.sin(angles)
    turner = lane_turn(HEAD_DIM)
    inputs = hidden_in.astype(jnp.float32)
    scale_one = rms_scale(inputs)
    gain_one_f = gain_one.astype(jnp.float32)
    normed_one = (inputs * scale_one * gain_one_f).astype(jnp.bfloat16)
    query_pre = jnp.dot(normed_one, query_w, preferred_element_type=jnp.float32)
    key_pre = jnp.dot(normed_one, key_w, preferred_element_type=jnp.float32)
    value_pre = jnp.dot(normed_one, value_w, preferred_element_type=jnp.float32)
    queries = rotate(query_pre, cos_table, sin_table, turner).astype(jnp.bfloat16)
    keys_local = rotate(key_pre, cos_table, sin_table, turner).astype(jnp.bfloat16)
    values_local = value_pre.astype(jnp.bfloat16)
    key_all, value_all = (
        lax.all_gather(keys_local, "wide", axis=1, tiled=True),
        lax.all_gather(values_local, "wide", axis=1, tiled=True),
    )
    query_five = queries.reshape(row_count, span_len, KV_HEADS, 2, HEAD_DIM)

    def key_slices(key_start, length):
        key_block = lax.dynamic_slice_in_dim(key_all, key_start, length, 1).reshape(
            row_count, length, KV_HEADS, HEAD_DIM
        )
        value_block = lax.dynamic_slice_in_dim(value_all, key_start, length, 1).reshape(
            row_count, length, KV_HEADS, HEAD_DIM
        )
        seg_key = lax.dynamic_slice_in_dim(segs_all, key_start, length, 1)
        place_key = (key_start + jnp.arange(length, dtype=jnp.int32))[None, :]
        return (key_block, value_block, seg_key, place_key)

    def scores_at(key_start, length):
        key_block, value_block, seg_key, place_key = key_slices(key_start, length)
        scores = masked_scores(
            query_five, key_block, seg_ids, seg_key, place_query, place_key, factor
        )
        return (scores, key_block, value_block)

    key_starts = jnp.arange(seq_len // key_step, dtype=jnp.int32) * key_step
    stat_shape = (row_count, KV_HEADS, 2, span_len)
    five_shape = (row_count, span_len, KV_HEADS, 2, HEAD_DIM)

    def top_step(state_now, key_start):
        row_top, row_total = state_now
        scores, unused_key, unused_value = scores_at(key_start, key_step)
        new_top = jnp.maximum(row_top, jnp.max(scores, axis=-1))
        row_total = row_total * jnp.exp(row_top - new_top) + jnp.sum(
            jnp.exp(scores - new_top[..., None]), axis=-1
        )
        return ((new_top, row_total), None)

    (row_top, row_total), unused = lax.scan(
        top_step,
        (jnp.full(stat_shape, MASKED, jnp.float32), jnp.zeros(stat_shape, jnp.float32)),
        key_starts,
    )
    log_total = row_top + jnp.log(row_total)

    def out_step(summed, key_start):
        scores, unused_key, value_block = scores_at(key_start, key_step)
        weights = jnp.exp(scores - log_total[..., None]).astype(jnp.bfloat16)
        return (
            summed
            + jnp.einsum(
                "agjbk,akgd->abgjd", weights, value_block, preferred_element_type=jnp.float32
            ),
            None,
        )

    attended, unused = lax.scan(out_step, jnp.zeros(five_shape, jnp.float32), key_starts)
    attended = attended.reshape(row_count, span_len, -1).astype(jnp.bfloat16)
    middle = inputs + jnp.dot(attended, output_w, preferred_element_type=jnp.float32)
    scale_two = rms_scale(middle)
    gain_two_f = gain_two.astype(jnp.float32)
    normed_two = (middle * scale_two * gain_two_f).astype(jnp.bfloat16)
    flat_two = normed_two.reshape(tok_count, feat_dim)
    logits = jnp.dot(flat_two, router_w, preferred_element_type=jnp.float32)
    expert_table = expert_ids.reshape(tok_count, TOP)
    choose = expert_table[:, :, None] == jnp.arange(EXPERTS, dtype=jnp.int32)[None, None, :]
    chosen = jnp.sum(jnp.where(choose, logits[:, None, :], 0.0), axis=-1)
    gate_vals = jax.nn.softmax(chosen, axis=-1)
    token_hot = jnp.sum(choose.astype(jnp.int32), axis=1)
    expert_load = lax.psum(jnp.sum(token_hot, axis=0), ("narrow", "wide"))
    earlier = jnp.cumsum(token_hot, axis=0) - token_hot
    places = jnp.sum(jnp.where(choose, earlier[:, None, :], 0), axis=-1)
    pair_count = tok_count * TOP
    target = jnp.where(places < CAP, expert_table * CAP + places, EXPERTS * CAP).reshape(-1)
    pair_of_slot = (
        jnp.full((EXPERTS * CAP,), pair_count, jnp.int32)
        .at[target]
        .set(jnp.arange(pair_count, dtype=jnp.int32), mode="drop")
    )
    token_of_slot = pair_of_slot // TOP
    outgoing = jnp.take(flat_two, token_of_slot, axis=0, mode="fill", fill_value=0).reshape(
        EXPERTS, CAP, feat_dim
    )
    received = lax.all_to_all(outgoing, "wide", split_axis=0, concat_axis=1, tiled=True)
    gate_up = jnp.einsum("ecd,edf->ecf", received, gate_up_w, preferred_element_type=jnp.float32)
    gate_half = gate_up[..., :FF]
    up_half = gate_up[..., FF:]
    sigmoid_gate = jax.nn.sigmoid(gate_half)
    activated = gate_half * sigmoid_gate
    hidden_b = (activated * up_half).astype(jnp.bfloat16)
    expert_out = jnp.einsum(
        "ecf,efd->ecd", hidden_b, down_w, preferred_element_type=jnp.float32
    ).astype(jnp.bfloat16)
    returned = lax.all_to_all(expert_out, "wide", split_axis=1, concat_axis=0, tiled=True)
    per_pair = (
        jnp.take(
            returned.reshape(EXPERTS * CAP, feat_dim), target, axis=0, mode="fill", fill_value=0
        )
        .reshape(tok_count, TOP, feat_dim)
        .astype(jnp.float32)
    )
    mixture = jnp.sum(gate_vals[:, :, None] * per_pair, axis=1)
    middle_flat = middle.reshape(tok_count, feat_dim)
    block_out = (middle_flat + mixture).reshape(row_count, span_len, feat_dim).astype(jnp.bfloat16)
    grad_out = out_grad.reshape(tok_count, feat_dim).astype(jnp.float32)
    gate_grad = jnp.sum(grad_out[:, None, :] * per_pair, axis=-1)
    gate_of_slot = jnp.take(gate_vals.reshape(-1), pair_of_slot, mode="fill", fill_value=0.0)
    slot_grad = (
        (
            jnp.take(grad_out, token_of_slot, axis=0, mode="fill", fill_value=0.0)
            * gate_of_slot[:, None]
        )
        .astype(jnp.bfloat16)
        .reshape(EXPERTS, CAP, feat_dim)
    )
    grad_received = lax.all_to_all(slot_grad, "wide", split_axis=0, concat_axis=1, tiled=True)
    down_grad = jnp.einsum(
        "ecf,ecd->efd", hidden_b, grad_received, preferred_element_type=jnp.float32
    )
    hidden_grad = jnp.einsum(
        "ecd,efd->ecf", grad_received, down_w, preferred_element_type=jnp.float32
    )
    gate_half_grad = (
        hidden_grad * up_half * (sigmoid_gate * (1.0 + gate_half * (1.0 - sigmoid_gate)))
    )
    up_half_grad = hidden_grad * activated
    gate_up_grad = jnp.concatenate([gate_half_grad, up_half_grad], axis=-1).astype(jnp.bfloat16)
    gate_up_wgrad = jnp.einsum(
        "ecd,ecf->edf", received, gate_up_grad, preferred_element_type=jnp.float32
    )
    slot_input_grad = jnp.einsum(
        "ecf,edf->ecd", gate_up_grad, gate_up_w, preferred_element_type=jnp.float32
    ).astype(jnp.bfloat16)
    input_back = lax.all_to_all(slot_input_grad, "wide", split_axis=1, concat_axis=0, tiled=True)
    pair_input_grad = jnp.take(
        input_back.reshape(EXPERTS * CAP, feat_dim), target, axis=0, mode="fill", fill_value=0
    ).reshape(tok_count, TOP, feat_dim)
    gate_mean = jnp.sum(gate_vals * gate_grad, axis=-1, keepdims=True)
    chosen_grad = gate_vals * (gate_grad - gate_mean)
    logit_grad = jnp.sum(jnp.where(choose, chosen_grad[:, :, None], 0.0), axis=1).astype(
        jnp.bfloat16
    )
    router_wgrad = jnp.einsum("td,te->de", flat_two, logit_grad, preferred_element_type=jnp.float32)
    normed_two_grad = jnp.sum(pair_input_grad.astype(jnp.float32), axis=1) + jnp.einsum(
        "te,de->td", logit_grad, router_w, preferred_element_type=jnp.float32
    )
    middle_part, gain_two_grad = norm_back(
        middle_flat, scale_two.reshape(tok_count, 1), gain_two_f, normed_two_grad
    )
    middle_grad = grad_out + middle_part
    attn_grad = middle_grad.astype(jnp.bfloat16)
    output_wgrad = jnp.einsum(
        "te,td->ed", attended.reshape(tok_count, -1), attn_grad, preferred_element_type=jnp.float32
    )
    attended_grad = jnp.einsum(
        "td,ed->te", attn_grad, output_w, preferred_element_type=jnp.float32
    ).astype(jnp.bfloat16)
    grad_five = attended_grad.reshape(five_shape)

    def sum_step(summed, key_start):
        scores, unused_key, value_block = scores_at(key_start, key_step)
        weights = jnp.exp(scores - log_total[..., None])
        weight_grad = jnp.einsum(
            "abgjd,akgd->agjbk", grad_five, value_block, preferred_element_type=jnp.float32
        )
        return (summed + jnp.sum(weights * weight_grad, axis=-1), None)

    row_dot, unused = lax.scan(sum_step, jnp.zeros(stat_shape, jnp.float32), key_starts)

    def query_step(summed, key_start):
        scores, key_block, value_block = scores_at(key_start, key_step)
        weights = jnp.exp(scores - log_total[..., None])
        weight_grad = jnp.einsum(
            "abgjd,akgd->agjbk", grad_five, value_block, preferred_element_type=jnp.float32
        )
        score_grad = (weights * (weight_grad - row_dot[..., None])).astype(jnp.bfloat16)
        return (
            summed
            + jnp.einsum(
                "agjbk,akgd->abgjd", score_grad, key_block, preferred_element_type=jnp.float32
            ),
            None,
        )

    query_grad, unused = lax.scan(query_step, jnp.zeros(five_shape, jnp.float32), key_starts)
    query_grad = query_grad.reshape(row_count, span_len, -1) * factor
    term_count = span_len * lax.axis_size("wide")
    sub_len = math.gcd(term_count, 512)

    def key_piece(sub_no):
        key_start = sub_no * sub_len
        key_block, value_block, seg_key, place_key = key_slices(key_start, sub_len)
        scores = masked_scores(
            query_five, key_block, seg_ids, seg_key, place_query, place_key, factor
        )
        weights = jnp.exp(scores - log_total[..., None])
        weight_grad = jnp.einsum(
            "abgjd,akgd->agjbk", grad_five, value_block, preferred_element_type=jnp.float32
        )
        score_grad = (weights * (weight_grad - row_dot[..., None])).astype(jnp.bfloat16)
        key_part = (
            jnp.einsum(
                "agjbk,abgjd->kagd", score_grad, query_five, preferred_element_type=jnp.float32
            )
            * factor
        )
        value_part = jnp.einsum(
            "agjbk,abgjd->kagd",
            weights.astype(jnp.bfloat16),
            grad_five,
            preferred_element_type=jnp.float32,
        )
        return jnp.concatenate(
            [
                key_part.reshape(sub_len, row_count, kv_width),
                value_part.reshape(sub_len, row_count, kv_width),
            ],
            axis=-1,
        )

    pieces = lax.map(key_piece, jnp.arange(term_count // sub_len, dtype=jnp.int32))
    summed_terms = lax.psum_scatter(
        pieces.reshape(term_count, row_count, 2 * kv_width).astype(jnp.bfloat16),
        "wide",
        scatter_dimension=0,
        tiled=True,
    ).astype(jnp.float32)
    key_grad = jnp.transpose(summed_terms[:, :, :kv_width], (1, 0, 2))
    value_grad = jnp.transpose(summed_terms[:, :, kv_width:], (1, 0, 2))
    query_back = (
        rotate_back(query_grad, cos_table, sin_table, turner)
        .astype(jnp.bfloat16)
        .reshape(tok_count, -1)
    )
    key_back = (
        rotate_back(key_grad, cos_table, sin_table, turner)
        .astype(jnp.bfloat16)
        .reshape(tok_count, -1)
    )
    value_back = value_grad.astype(jnp.bfloat16).reshape(tok_count, -1)
    flat_one = normed_one.reshape(tok_count, feat_dim)
    query_wgrad = jnp.einsum("td,te->de", flat_one, query_back, preferred_element_type=jnp.float32)
    key_wgrad = jnp.einsum("td,te->de", flat_one, key_back, preferred_element_type=jnp.float32)
    value_wgrad = jnp.einsum("td,te->de", flat_one, value_back, preferred_element_type=jnp.float32)
    normed_one_grad = (
        jnp.einsum("te,de->td", query_back, query_w, preferred_element_type=jnp.float32)
        + jnp.einsum("te,de->td", key_back, key_w, preferred_element_type=jnp.float32)
        + jnp.einsum("te,de->td", value_back, value_w, preferred_element_type=jnp.float32)
    )
    input_part, gain_one_grad = norm_back(
        inputs.reshape(tok_count, feat_dim),
        scale_one.reshape(tok_count, 1),
        gain_one_f,
        normed_one_grad,
    )
    input_grad = (
        (middle_grad + input_part).reshape(row_count, span_len, feat_dim).astype(jnp.bfloat16)
    )
    gain_one_sum, query_sum, key_wsum, value_wsum, output_sum, gain_two_sum, router_sum = (
        lax.psum_scatter(gain_one_grad, ("narrow", "wide"), scatter_dimension=0, tiled=True),
        lax.psum_scatter(query_wgrad, ("narrow", "wide"), scatter_dimension=0, tiled=True),
        lax.psum_scatter(key_wgrad, ("narrow", "wide"), scatter_dimension=0, tiled=True),
        lax.psum_scatter(value_wgrad, ("narrow", "wide"), scatter_dimension=0, tiled=True),
        lax.psum_scatter(output_wgrad, ("narrow", "wide"), scatter_dimension=0, tiled=True),
        lax.psum_scatter(gain_two_grad, ("narrow", "wide"), scatter_dimension=0, tiled=True),
        lax.psum_scatter(router_wgrad, ("narrow", "wide"), scatter_dimension=0, tiled=True),
    )
    gate_up_sum, down_sum = (
        lax.psum_scatter(
            gate_up_wgrad.astype(jnp.bfloat16), "narrow", scatter_dimension=1, tiled=True
        ).astype(jnp.float32),
        lax.psum_scatter(
            down_grad.astype(jnp.bfloat16), "narrow", scatter_dimension=1, tiled=True
        ).astype(jnp.float32),
    )
    return (
        block_out,
        input_grad,
        gain_one_sum,
        query_sum,
        key_wsum,
        value_wsum,
        output_sum,
        gain_two_sum,
        router_sum,
        gate_up_sum,
        down_sum,
        expert_load,
    )


MESH = pl.DeviceIdType.MESH
F32 = jnp.float32
BF16 = jnp.bfloat16
IN_HBM = pl.BlockSpec(memory_space=pl.ANY)
IN_VMEM = pl.BlockSpec(memory_space=pltpu.VMEM)
VMEM_BYTES = 60 * 1024 * 1024
NARROW = 4
WIDE = 8
GROUP = 16
TOKENS = 256
SPAN = 128
WIDTH = 1024
SEQ = 1024
SLOTS = 80
MINE = 2
EARLY = 160
CHUNK = 4
NT = (((1,), (1,)), ((), ()))
TN = (((0,), (0,)), ((), ()))


def duration(us):
    return pl.CostEstimate(flops=us * 1000000000, bytes_accessed=us * 3600000, transcendentals=0)


def mm(left, right, dims=(((1,), (0,)), ((), ()))):
    return lax.dot_general(left, right, dims, preferred_element_type=F32)


class Spot:
    def __init__(self):
        self.n = lax.axis_index("narrow")
        self.w = lax.axis_index("wide")
        self.core = lax.rem(self.w, 2)
        self.x = lax.rem(lax.div(self.w, 2), 2)
        self.y = lax.div(self.w, 4)
        self.half = lax.rem(self.n, 2)
        self.me = self.n * WIDE + self.w
        self.sib = self.w + 1 - 2 * self.core
        self.xn = self.w + 2 - 4 * self.x
        self.yn = self.w + 4 - 8 * self.y
        self.diag = self.xn + 4 - 8 * self.y
        self.mate = self.n + 1 - 2 * self.half
        self.slot = self.half * WIDE + self.w

    def wide(self, to):
        return (self.n, to)

    def greet(self, count):
        barrier = pltpu.get_barrier_semaphore()
        base = self.n - self.half

        def signal(step, carry):
            if count == WIDE:
                to = (self.n, lax.rem(self.w + step, WIDE))
            elif count == GROUP:
                other = lax.rem(self.slot + step, GROUP)
                to = (base + lax.div(other, WIDE), lax.rem(other, WIDE))
            else:
                other = lax.rem(self.me + step, NARROW * WIDE)
                to = (lax.div(other, WIDE), lax.rem(other, WIDE))
            pl.semaphore_signal(barrier, inc=1, device_id=to, device_id_type=MESH)
            return carry

        lax.fori_loop(1, count, signal, 0)
        pl.semaphore_wait(barrier, count - 1)


def remote(src, dst, send_sem, recv_sem, to):
    return pltpu.make_async_remote_copy(
        src_ref=src, dst_ref=dst, send_sem=send_sem, recv_sem=recv_sem, device_id=to, device_id_type=MESH
    )


def halves(ref, which):
    return ref.at[pl.ds(which * SPAN, SPAN)]


class PlaneGather:
    COPIES = 11

    def __init__(self, spot, source, place, send, recv):
        self.spot, self.source, self.place = spot, source, place
        self.send, self.recv = send, recv
        self.started = []

    def put(self, src, dst, number, to):
        copy = remote(src, dst, self.send.at[number], self.recv.at[number], self.spot.wide(to))
        copy.start()
        self.started.append(copy)

    def pass_on(self, who, half, number, to):
        place = self.place(who, half)
        self.put(place, place, number, to)

    def got(self, who, half, number):
        dst = self.place(who, half)
        remote(dst, dst, self.send.at[number], self.recv.at[number], self.spot.wide(self.spot.sib)).wait_recv()

    def begin(self):
        s = self.spot
        self.put(self.source(0), self.place(s.w, 0), 0, s.xn)
        self.put(self.source(1), self.place(s.w, 1), 2, s.yn)
        self.put(self.source(1), self.place(s.w, 1), 1, s.xn)
        self.put(self.source(0), self.place(s.w, 0), 3, s.yn)
        self.put(self.source(None), self.place(s.w, None), 4, s.sib)

    def middle(self):
        s = self.spot
        self.got(s.xn, 0, 0)
        self.pass_on(s.xn, 0, 5, s.yn)
        self.got(s.yn, 1, 2)
        self.pass_on(s.yn, 1, 6, s.xn)

    def late(self):
        s = self.spot
        self.got(s.xn, 1, 1)
        self.pass_on(s.xn, None, 7, s.sib)
        self.got(s.yn, 0, 3)
        self.pass_on(s.yn, None, 8, s.sib)

    def last(self):
        s = self.spot
        self.got(s.diag, 0, 5)
        self.pass_on(s.diag, 0, 9, s.sib)
        self.got(s.diag, 1, 6)
        self.pass_on(s.diag, 1, 10, s.sib)

    def finish(self):
        s = self.spot
        sib_x = s.sib + 2 - 4 * s.x
        sib_y = s.sib + 4 - 8 * s.y
        sib_d = sib_x + 4 - 8 * s.y
        self.got(s.sib, None, 4)
        self.got(sib_x, None, 7)
        self.got(sib_y, None, 8)
        self.got(sib_d, 0, 9)
        self.got(sib_d, 1, 10)
        for copy in self.started:
            copy.wait_send()


def gather_tokens(spot, own, out, base, send, recv):
    def part(ref, half):
        return ref if half is None else ref.at[pl.ds(half * SPAN, SPAN)]

    return PlaneGather(
        spot, lambda half: part(own, half), lambda who, half: part(out.at[base + who], half), send, recv
    )


def gather_kernel(
    x_ref, dy_ref, seg_in, q_ref, k_ref, v_ref, o_ref, router_ref, gain_one_ref, gain_two_ref, gu_ref,
    x_all, w_all, g_all, seg_all, wo_block, dy_pair, far_gu, w_ref,
    g_ref, seg_ref, wo_ref, send, recv, local, ws, wr, gs, gr, ss, sr, zs, zr, ds, dr, es, er,
):
    spot = Spot()
    for head in range(WIDE):
        at = 256 * head
        w_ref[:, at : at + 128] = q_ref[:, 128 * head : 128 * head + 128]
        w_ref[:, at + 128 : at + 256] = jnp.concatenate(
            [k_ref[:, 64 * head : 64 * head + 64], v_ref[:, 64 * head : 64 * head + 64]], axis=1
        )
    wo_ref[:, 0:WIDTH] = o_ref[...]
    wo_ref[:, WIDTH : WIDTH + 128] = jnp.concatenate([router_ref[...], jnp.zeros((32, 96), BF16)], axis=1)
    g_ref[...] = jnp.zeros_like(g_ref)
    g_ref[0:1, 0:32] = gain_one_ref[...].astype(F32)
    g_ref[1:2, 0:32] = gain_two_ref[...].astype(F32)
    seg_ref[...] = jnp.zeros_like(seg_ref)
    seg_ref[0:2, :] = seg_in[...]
    spot.greet(NARROW * WIDE)
    own = [
        pltpu.make_async_copy(x_ref, x_all.at[spot.w], local.at[0]),
        pltpu.make_async_copy(w_ref.at[:, pl.ds(pl.multiple_of(spot.w * 256, 256), 256)], w_all.at[spot.me], local.at[1]),
        pltpu.make_async_copy(g_ref, g_all.at[spot.me], local.at[2]),
        pltpu.make_async_copy(seg_ref, seg_all.at[spot.w], local.at[3]),
        pltpu.make_async_copy(wo_ref, wo_block.at[spot.n], local.at[4]),
        pltpu.make_async_copy(dy_ref, dy_pair.at[spot.half], local.at[5]),
    ]
    gather = gather_tokens(spot, x_ref, x_all, 0, send, recv)

    def others(step):
        other = lax.rem(spot.me + step, NARROW * WIDE)
        return other, lax.div(other, WIDE), lax.rem(other, WIDE)

    def weights(step, arriving):
        other, o_n, o_w = others(step)
        source = w_ref.at[:, pl.ds(pl.multiple_of(o_w * 256, 256), 256)]
        place = other if arriving else spot.me
        return (
            remote(source, w_all.at[place], ws.at[other], wr.at[place], (o_n, o_w)),
            remote(g_ref, g_all.at[place], gs.at[other], gr.at[place], (o_n, o_w)),
        )

    def documents(step, arriving):
        other = lax.rem(spot.w + step, WIDE)
        place = other if arriving else spot.w
        return remote(seg_ref, seg_all.at[place], ss.at[other], sr.at[place], spot.wide(other))

    def column(step, arriving):
        other = lax.rem(spot.n + step, NARROW)
        place = other if arriving else spot.n
        return remote(wo_ref, wo_block.at[place], zs.at[other], zr.at[place], (other, spot.w))

    def start(step, carry):
        for copy in weights(step, False):
            copy.start()
        return carry

    def start_column(step, carry):
        column(step, False).start()
        return carry

    def start_documents(step, carry):
        documents(step, False).start()
        return carry

    lax.fori_loop(1, WIDE, start_documents, 0)
    lax.fori_loop(1, NARROW * WIDE, start, 0)
    gather.begin()
    lax.fori_loop(1, NARROW, start_column, 0)
    for copy in own:
        copy.start()
    across = remote(dy_ref, dy_pair.at[spot.half], ds.at[0], dr.at[0], (spot.mate, spot.w))
    across.start()
    far = remote(
        gu_ref.at[2 * spot.half, pl.ds(0, EARLY)], far_gu, es.at[0], er.at[0],
        (spot.n + 2 - 4 * lax.div(spot.n, 2), spot.w),
    )
    far.start()
    gather.middle()
    gather.late()
    gather.last()

    def wait(step, carry):
        for copy in weights(step, False):
            copy.wait_send()
        for copy in weights(step, True):
            copy.wait_recv()
        return carry

    def wait_column(step, carry):
        column(step, False).wait_send()
        column(step, True).wait_recv()
        return carry

    def wait_documents(step, carry):
        documents(step, False).wait_send()
        documents(step, True).wait_recv()
        return carry

    lax.fori_loop(1, WIDE, wait_documents, 0)
    lax.fori_loop(1, NARROW * WIDE, wait, 0)
    lax.fori_loop(1, NARROW, wait_column, 0)
    gather.finish()
    across.wait_send()
    arrived = dy_pair.at[1 - spot.half]
    remote(arrived, arrived, ds.at[0], dr.at[0], (spot.mate, spot.w)).wait_recv()
    for copy in own:
        copy.wait()
    far.wait_send()
    far.wait_recv()


def gather_call(*operands):
    dma = pltpu.SemaphoreType.DMA
    return pl.pallas_call(
        gather_kernel,
        name="gather_inputs",
        out_shape=(
            jax.ShapeDtypeStruct((WIDE, TOKENS, WIDTH), BF16),
            jax.ShapeDtypeStruct((NARROW * WIDE, 32, 256), BF16),
            jax.ShapeDtypeStruct((NARROW * WIDE, 8, 128), F32),
            jax.ShapeDtypeStruct((WIDE, 8, 128), jnp.int32),
            jax.ShapeDtypeStruct((NARROW, 32, WIDTH + 128), BF16),
            jax.ShapeDtypeStruct((2, TOKENS, WIDTH), BF16),
            jax.ShapeDtypeStruct((EARLY, WIDTH), BF16),
            jax.ShapeDtypeStruct((32, 2 * WIDTH), BF16),
        ),
        in_specs=[IN_VMEM] * 10 + [IN_HBM],
        out_specs=(IN_HBM,) * 7 + (IN_VMEM,),
        scratch_shapes=[
            pltpu.VMEM((8, 128), F32),
            pltpu.VMEM((8, 128), jnp.int32),
            pltpu.VMEM((32, WIDTH + 128), BF16),
            dma((PlaneGather.COPIES,)),
            dma((PlaneGather.COPIES,)),
            dma((6,)),
            dma((NARROW * WIDE,)),
            dma((NARROW * WIDE,)),
            dma((NARROW * WIDE,)),
            dma((NARROW * WIDE,)),
            dma((WIDE,)),
            dma((WIDE,)),
            dma((NARROW,)),
            dma((NARROW,)),
            dma((1,)),
            dma((1,)),
            dma((1,)),
            dma((1,)),
        ],
        compiler_params=pltpu.CompilerParams(collective_id=1, has_side_effects=True),
        cost_estimate=duration(1),
    )(*operands)


def lane_half():
    lanes = lax.broadcasted_iota(jnp.int32, (1, 128), 1)
    return lax.rem(lanes, 64) < 32


def turn(values, first_half):
    return jnp.where(first_half, -pltpu.roll(values, 96, 1), pltpu.roll(values, 32, 1))


def turn_back(values, first_half):
    return jnp.where(first_half, pltpu.roll(values, 96, 1), -pltpu.roll(values, 32, 1))


def gather_gain(gains):
    lane = lax.broadcasted_iota(jnp.int32, (128, WIDTH), 0)
    column = lax.broadcasted_iota(jnp.int32, (128, WIDTH), 1)
    spread = (lax.rem(column, 32) == lane).astype(BF16)
    tiled = mm(gains.astype(BF16), spread)
    owner = lax.broadcasted_iota(jnp.int32, (32, WIDTH), 0)
    place = lax.broadcasted_iota(jnp.int32, (32, WIDTH), 1)
    return jnp.sum(jnp.where(lax.div(place, 32) == owner, tiled, 0.0), axis=0, keepdims=True)


class Attention:
    def __init__(self, x_ref, w_ref, seg_ref, cos_ref, sin_ref, freq_ref, gain_one, h1_ref, qkv_ref, lse_ref, o_ref, angle_ref):
        self.x_ref, self.seg_ref, self.cos_ref, self.sin_ref = x_ref, seg_ref, cos_ref, sin_ref
        self.h1_ref, self.qkv_ref, self.lse_ref, self.o_ref = h1_ref, qkv_ref, lse_ref, o_ref
        self.angle_ref = angle_ref
        self.gain_one = gain_one
        self.w_ref = w_ref
        self.first_half = lane_half()
        self.is_key = lax.broadcasted_iota(jnp.int32, (1, 128), 1) < 64
        self.starts, self.start_cos, self.start_sin = [], [], []
        for row in range(2):
            segs = [seg_ref[c, row : row + 1, :] for c in range(WIDE)]
            starts = [jnp.zeros((1, 1), F32)]
            for doc in range(5):
                total = jnp.zeros((1, 128), F32)
                for seg in segs:
                    total = total + jnp.where(seg == doc, 1.0, 0.0)
                starts.append(starts[-1] + jnp.sum(total, axis=1, keepdims=True))
            angle = jnp.concatenate(starts + starts[:2], axis=0) * freq_ref[0:1, :]
            self.starts.append(starts)
            self.start_cos.append(jnp.cos(angle))
            self.start_sin.append(jnp.sin(angle))

    def chunk(self, row, i):
        tokens = pl.ds(i * 256, 256)
        starts, start_cos, start_sin = self.starts[row], self.start_cos[row], self.start_sin[row]
        seg_cols = []
        for part in range(2):
            seg = self.seg_ref[2 * i + part, row : row + 1, :].astype(F32)
            seg_cols.append(jnp.transpose(jnp.broadcast_to(seg, (128, 128))))
        seg_col = jnp.concatenate(seg_cols, axis=0)
        start_col = jnp.zeros((256, 128), F32)
        cos_s = jnp.broadcast_to(start_cos[0:1], (256, 128))
        sin_s = jnp.broadcast_to(start_sin[0:1], (256, 128))
        for doc in range(1, 6):
            here = seg_col == float(doc)
            start_col = jnp.where(here, starts[doc], start_col)
            cos_s = jnp.where(here, start_cos[doc : doc + 1], cos_s)
            sin_s = jnp.where(here, start_sin[doc : doc + 1], sin_s)
        cos_t = self.cos_ref[tokens, :]
        sin_t = self.sin_ref[tokens, :]
        cosine = cos_t * cos_s + sin_t * sin_s
        sine = sin_t * cos_s - cos_t * sin_s
        self.angle_ref[row, tokens, 0:128] = cosine
        self.angle_ref[row, tokens, 128:256] = sine
        x = self.x_ref[2 * i : 2 * i + 2, row].reshape(256, WIDTH).astype(F32)
        scale = lax.rsqrt(jnp.mean(x * x, axis=1, keepdims=True) + EPSILON)
        h1 = (x * scale * self.gain_one).astype(BF16)
        self.h1_ref[row, tokens, :] = h1
        qkv = mm(h1, self.w_ref[...].reshape(WIDTH, 256))
        q = qkv[:, 0:128]
        kv = qkv[:, 128:256]
        q = (q * cosine + turn(q, self.first_half) * sine).astype(BF16)
        kv = jnp.where(self.is_key, kv * cosine + turn(kv, self.first_half) * sine, kv).astype(BF16)
        self.qkv_ref[row, tokens, 0:128] = q
        self.qkv_ref[row, tokens, 128:256] = kv
        length = 256 * (i + 1)
        keys = self.qkv_ref[row, 0:length, 128:192]
        values = self.qkv_ref[row, 0:length, 192:256]
        place_key = lax.broadcasted_iota(jnp.int32, (256, length), 1).astype(F32)
        place_query = (lax.broadcasted_iota(jnp.int32, (256, length), 0) + 256 * i).astype(F32)
        allowed = (place_key <= place_query) & (place_key >= start_col[:, 0:1])
        outs, logs = [], []
        for head in range(2):
            query = q[:, 64 * head : 64 * head + 64]
            scores = jnp.where(allowed, mm(query, keys, NT) * (HEAD_DIM**-0.5), MASKED)
            top = jnp.max(scores, axis=1, keepdims=True)
            log_total = top + jnp.log(jnp.sum(jnp.exp(scores - top), axis=1, keepdims=True))
            outs.append(mm(jnp.exp(scores - log_total).astype(BF16), values))
            logs.append(log_total)
        self.o_ref[row, tokens, :] = jnp.concatenate(outs, axis=1).astype(BF16)
        self.lse_ref[row, tokens, :] = jnp.where(
            self.is_key, jnp.where(self.first_half, logs[0], start_col), logs[1]
        )


def piece_copies(spot, gu_ref, down_ref, e, kind, target, send, recv, number):
    pair = lax.div(spot.n, 2)
    plane = spot.n if kind == 2 else spot.mate
    if kind >= 2:
        plane = plane + 2 - 4 * pair
    half = spot.half if kind == 2 else 1 - spot.half
    to = (plane, spot.w)
    return [
        remote(gu_ref.at[2 * half + e], target.at[pl.ds(0, 256)], send.at[number], recv.at[number], to),
        remote(down_ref.at[2 * half + e], target.at[pl.ds(256, 128)], send.at[number + 1], recv.at[number + 1], to),
    ]


def start_all(copies):
    for copy in copies:
        copy.start()


def forward_kernel(
    x_ref, w_ref, g_ref, seg_ref, cos_ref, sin_ref, freq_ref, wo_ref, ids_ref, dy_ref, gu_ref, down_ref,
    h1_out, qkv_ref, lse_ref, o_ref, angle_ref, gain_ref, mid_ref, gate_ref, w_all,
    h2_all, dy_all, table_all, mate_0, far_rest_0, far_mate_0, mate_1, far_1,
    h1_ref, o_full, h2_own, table_own,
    os, orv, w_send, w_recv, a_send, a_recv, b_send, b_recv, s0, r0, s1, r1, ts, tr, zs, zr, es, er, local,
):
    spot = Spot()
    spot.greet(NARROW * WIDE)
    mate_base = (1 - spot.half) * WIDE
    own_base = spot.half * WIDE
    mate_slot = mate_base + spot.w

    def w_source(half):
        return wo_ref if half is None else wo_ref.at[pl.ds(2 * half, 2)]

    def w_place(who, half):
        return w_all.at[:, who] if half is None else w_all.at[pl.ds(2 * half, 2), who]

    w_gather = PlaneGather(spot, w_source, w_place, w_send, w_recv)
    dy_gather = gather_tokens(spot, dy_ref.at[spot.half], dy_all, own_base, a_send, a_recv)
    mate_dy_gather = gather_tokens(spot, dy_ref.at[1 - spot.half], dy_all, mate_base, b_send, b_recv)
    w_gather.begin()
    dy_gather.begin()
    far_plane = (spot.n + 2 - 4 * lax.div(spot.n, 2), spot.w)
    first_expert = [
        remote(
            gu_ref.at[2 * spot.half, pl.ds(EARLY, 256 - EARLY)], far_rest_0.at[pl.ds(0, 256 - EARLY)],
            es.at[0], er.at[0], far_plane,
        ),
        remote(
            down_ref.at[2 * spot.half], far_rest_0.at[pl.ds(256 - EARLY, 128)], es.at[1], er.at[1], far_plane
        ),
    ]
    first_expert += piece_copies(spot, gu_ref, down_ref, 0, 3, far_mate_0, es, er, 2)
    first_expert += piece_copies(spot, gu_ref, down_ref, 0, 1, mate_0, es, er, 4)
    start_all(first_expert)

    keep = [
        pltpu.make_async_copy(wo_ref, w_place(spot.w, None), local.at[0]),
        pltpu.make_async_copy(dy_ref.at[spot.half], dy_all.at[spot.slot], local.at[1]),
        pltpu.make_async_copy(dy_ref.at[1 - spot.half], dy_all.at[mate_slot], local.at[2]),
    ]
    for copy in keep:
        copy.start()

    def heads(to, place):
        return (
            o_ref.at[:, pl.ds(to * SPAN, SPAN), :],
            o_full.at[:, :, pl.ds(pl.multiple_of(place * 128, 128), 128)],
        )

    def each_head_copy(to, act_local, act_remote):
        source, target = heads(to, spot.w)

        @pl.when(spot.w == to)
        def _():
            act_local(pltpu.make_async_copy(source, target, local.at[3]))

        @pl.when(spot.w != to)
        def _():
            act_remote(remote(source, target, os.at[to], orv.at[spot.w], spot.wide(to)))

    expert = lax.broadcasted_iota(jnp.int32, (32, TOKENS), 0).astype(F32)
    named = jnp.zeros((32, TOKENS), F32)
    ids = ids_ref[...].astype(F32)
    ids = jnp.transpose(jnp.concatenate([ids, jnp.zeros((TOKENS, 128 - TOP), F32)], axis=1))
    for k in range(TOP):
        named = jnp.where(expert == ids[k : k + 1, :], 1.0, named)
    before = lax.broadcasted_iota(jnp.int32, (TOKENS, TOKENS), 0) < lax.broadcasted_iota(
        jnp.int32, (TOKENS, TOKENS), 1
    )
    places = mm(named.astype(BF16), jnp.where(before, 1.0, 0.0).astype(BF16))
    kept = jnp.where((named > 0.5) & (places < float(CAP)), places, -1.0)

    gains = g_ref[...]
    gain_one = gather_gain(gains[:, 0, :])
    gain_two = gather_gain(gains[:, 1, :])
    gain_ref[...] = jnp.concatenate([gain_one, gain_two, jnp.zeros((6, WIDTH), F32)], axis=0)
    attention = Attention(
        x_ref, w_ref, seg_ref, cos_ref, sin_ref, freq_ref, gain_one,
        h1_ref, qkv_ref, lse_ref, o_ref, angle_ref,
    )
    between = {1: [w_gather.middle], 2: [w_gather.late, dy_gather.middle], 3: [w_gather.last, dy_gather.late]}
    for i in range(4):
        for row in range(2):
            attention.chunk(row, i)
        for to in (2 * i, 2 * i + 1):
            each_head_copy(to, lambda copy: copy.start(), lambda copy: copy.start())
        for step in between.get(i, []):
            step()
    far = piece_copies(spot, gu_ref, down_ref, 1, 2, far_1, es, er, 6)
    near = piece_copies(spot, gu_ref, down_ref, 1, 1, mate_1, es, er, 8)
    h1_copy = pltpu.make_async_copy(h1_ref, h1_out, local.at[4])
    h1_copy.start()
    dy_gather.last()
    mate_dy_gather.begin()
    w_gather.finish()
    keep[0].wait()
    for to in range(WIDE):
        each_head_copy(to, lambda copy: copy.wait(), lambda copy: copy.wait_send())

    def wait_heads(step, carry):
        other = lax.rem(spot.w + step, WIDE)
        target = o_full.at[:, :, pl.ds(pl.multiple_of(other * 128, 128), 128)]
        remote(target, target, os.at[0], orv.at[other], spot.wide(other)).wait_recv()
        return carry

    lax.fori_loop(1, WIDE, wait_heads, 0)
    attended = o_full[...].reshape(TOKENS, WIDTH)
    x_own = x_ref[spot.w].reshape(TOKENS, WIDTH).astype(F32)
    mid = x_own + mm(attended, w_all[:, :, :, 0:WIDTH].reshape(WIDTH, WIDTH))
    mid_ref[...] = mid
    scale = lax.rsqrt(jnp.mean(mid * mid, axis=1, keepdims=True) + EPSILON)
    h2 = (mid * scale * gain_two).astype(BF16)
    h2_own[...] = h2
    across = remote(h2_own, h2_all.at[spot.slot], zs.at[0], zr.at[0], (spot.mate, spot.w))
    across.start()
    first = gather_tokens(spot, h2_own, h2_all, own_base, s0, r0)
    first.begin()
    keep_own = pltpu.make_async_copy(h2_own, h2_all.at[spot.slot], local.at[5])
    keep_own.start()

    logits = jnp.transpose(mm(h2, w_all[:, :, :, WIDTH : WIDTH + 128].reshape(WIDTH, 128)))[0:32]
    chosen = jnp.where(named > 0.5, logits, MASKED)
    rise = jnp.where(named > 0.5, jnp.exp(chosen - jnp.max(chosen, axis=0, keepdims=True)), 0.0)
    gate = rise / jnp.sum(rise, axis=0, keepdims=True)
    gate_ref[0:32, :] = gate
    gate_ref[32:64, :] = named
    for owner in range(GROUP):
        table_own[owner, 0:2, :] = kept[2 * owner : 2 * owner + 2]
        table_own[owner, 2:4, :] = gate[2 * owner : 2 * owner + 2]
        table_own[owner, 4:8, :] = jnp.zeros((4, TOKENS), F32)

    def tables(step, arriving):
        other = lax.rem(spot.slot + step, GROUP)
        o_half, o_w = lax.div(other, WIDE), lax.rem(other, WIDE)
        place = other if arriving else spot.slot
        return remote(
            table_own.at[2 * o_w + o_half], table_all.at[place], ts.at[other], tr.at[place],
            (spot.n - spot.half + o_half, o_w),
        )

    def start_table(step, carry):
        tables(step, False).start()
        return carry

    lax.fori_loop(1, GROUP, start_table, 0)
    table_mine = pltpu.make_async_copy(
        table_own.at[2 * spot.w + spot.half], table_all.at[spot.slot], local.at[6]
    )
    table_mine.start()

    mate_dy_gather.middle()
    mate_dy_gather.late()
    first.middle()
    mate_dy_gather.last()
    first.late()
    first.last()
    arriving = h2_all.at[mate_slot]
    remote(arriving, arriving, zs.at[0], zr.at[0], (spot.mate, spot.w)).wait_recv()
    second = gather_tokens(spot, arriving, h2_all, mate_base, s1, r1)
    second.begin()
    start_all(far + near)
    second.middle()
    second.late()
    second.last()

    def wait_table(step, carry):
        tables(step, False).wait_send()
        tables(step, True).wait_recv()
        return carry

    lax.fori_loop(1, GROUP, wait_table, 0)
    dy_gather.finish()
    mate_dy_gather.finish()
    first.finish()
    second.finish()
    across.wait_send()
    keep[1].wait()
    keep[2].wait()
    keep_own.wait()
    table_mine.wait()
    h1_copy.wait()
    for copy in first_expert + far + near:
        copy.wait_send()
        copy.wait_recv()


def forward_call(x_all, w_all, g_all, seg_all, cos_table, sin_table, freq, wo_block, ids, dy_pair, w_gate_up, w_down):
    dma = pltpu.SemaphoreType.DMA
    copies = PlaneGather.COPIES
    return pl.pallas_call(
        forward_kernel,
        name="forward",
        out_shape=(
            jax.ShapeDtypeStruct((2, SEQ, WIDTH), BF16),
            jax.ShapeDtypeStruct((2, SEQ, 256), BF16),
            jax.ShapeDtypeStruct((2, SEQ, 128), F32),
            jax.ShapeDtypeStruct((2, SEQ, 128), BF16),
            jax.ShapeDtypeStruct((2, SEQ, 256), F32),
            jax.ShapeDtypeStruct((8, WIDTH), F32),
            jax.ShapeDtypeStruct((TOKENS, WIDTH), F32),
            jax.ShapeDtypeStruct((64, TOKENS), F32),
            jax.ShapeDtypeStruct((NARROW, WIDE, 32, WIDTH + 128), BF16),
            jax.ShapeDtypeStruct((GROUP, TOKENS, WIDTH), BF16),
            jax.ShapeDtypeStruct((GROUP, TOKENS, WIDTH), BF16),
            jax.ShapeDtypeStruct((GROUP, 8, TOKENS), F32),
        )
        + tuple(jax.ShapeDtypeStruct((depth, WIDTH), BF16) for depth in (384, 384 - EARLY, 384, 384, 384)),
        in_specs=[IN_VMEM] * 7 + [IN_HBM, IN_VMEM, IN_VMEM, IN_HBM, IN_HBM],
        out_specs=(IN_HBM,) + (IN_VMEM,) * 8 + (IN_HBM,) * 8,
        scratch_shapes=[
            pltpu.VMEM((2, SEQ, WIDTH), BF16),
            pltpu.VMEM((2, SPAN, WIDTH), BF16),
            pltpu.VMEM((TOKENS, WIDTH), BF16),
            pltpu.VMEM((GROUP, 8, TOKENS), F32),
            dma((WIDE,)),
            dma((WIDE,)),
        ]
        + [dma((copies,))] * 10
        + [dma((GROUP,)), dma((GROUP,)), dma((1,)), dma((1,)), dma((10,)), dma((10,)), dma((7,))],
        compiler_params=pltpu.CompilerParams(collective_id=2, has_side_effects=True, vmem_limit_bytes=VMEM_BYTES),
        cost_estimate=duration(1),
    )(x_all.reshape(WIDE, 2, SPAN, WIDTH), w_all, g_all, seg_all, cos_table, sin_table, freq, wo_block, ids, dy_pair, w_gate_up, w_down)


def load_quarters(own, pieces, w_gu, w_down, sems):
    n = lax.axis_index("narrow")
    half, pair = lax.rem(n, 2), lax.div(n, 2)
    mate = n + 1 - 2 * half
    far = n + 2 - 4 * pair
    far_mate = mate + 2 - 4 * pair
    copies = []
    for quarter, parts in zip((n, mate, far, far_mate), (own,) + pieces):
        first = 0
        for part in parts if isinstance(parts, tuple) else (parts,):
            depth = part.shape[0]
            for start, rows, target in ((0, 256, w_gu), (256, 128, w_down)):
                low, high = max(first, start), min(first + depth, start + rows)
                if low < high:
                    place = quarter * rows + (low - start)
                    copies.append(
                        pltpu.make_async_copy(
                            part.at[pl.ds(low - first, high - low)],
                            target.at[pl.ds(pl.multiple_of(place, 32), high - low)],
                            sems.at[len(copies)],
                        )
                    )
            first += depth
    return copies


def pick(table_ref, source, expert):
    slot = lax.broadcasted_iota(jnp.int32, (SLOTS, TOKENS), 0).astype(F32)
    return slot == table_ref[source, expert : expert + 1, :]


STEPS = GROUP // CHUNK
ROWS = CHUNK * SLOTS


def start_weights(e, gu_ref, down_ref, pieces, w_gu, w_down, gu_sum, down_sum, sems):
    mine = 2 * lax.rem(lax.axis_index("narrow"), 2) + e
    copies = load_quarters((gu_ref.at[mine], down_ref.at[mine]), pieces, w_gu, w_down, sems)
    for copy in copies:
        copy.start()
    gu_sum[...] = jnp.zeros_like(gu_sum)
    down_sum[...] = jnp.zeros_like(down_sum)
    for copy in copies:
        copy.wait()


def slot_gates(table_ref, masks, e):
    return jnp.concatenate(
        [
            jnp.sum(jnp.where(masks[s], table_ref[s, 2 + e : 3 + e, :], 0.0), axis=1, keepdims=True)
            for s in range(CHUNK)
        ],
        axis=0,
    )


def expert_math(rows, grad_rows, gates, w_gu, w_down, gu_sum, down_sum):
    g = mm(rows, w_gu[:, 0:FF])
    u = mm(rows, w_gu[:, FF : 2 * FF])
    sigmoid = 1.0 / (1.0 + jnp.exp(-g))
    active = g * sigmoid
    hidden = (active * u).astype(BF16)
    grad_rows = grad_rows.astype(F32)
    dy_pair = (grad_rows * gates).astype(BF16)
    dhid = mm(dy_pair, w_down[...], NT)
    da_g = (dhid * u * (sigmoid * (1.0 + g * (1.0 - sigmoid)))).astype(BF16)
    da_u = (dhid * active).astype(BF16)
    y = mm(hidden, w_down[...]).astype(BF16).astype(F32)
    slot_dgate = jnp.sum(y * grad_rows, axis=1, keepdims=True)
    down_sum[...] += mm(hidden, dy_pair, TN)
    gu_sum[:, 0:FF] += mm(rows, da_g, TN)
    gu_sum[:, FF : 2 * FF] += mm(rows, da_u, TN)
    dx = (mm(da_g, w_gu[:, 0:FF], NT) + mm(da_u, w_gu[:, FF : 2 * FF], NT)).astype(BF16)
    return (y * gates).astype(BF16), dx, slot_dgate


def token_dgate(dgate_ref, masks, slot_dgate, e):
    for s in range(CHUNK):
        part = slot_dgate[s * SLOTS : (s + 1) * SLOTS]
        dgate_ref[s, e : e + 1, :] = jnp.sum(jnp.where(masks[s], part, 0.0), axis=0, keepdims=True)


def store_quarters(outs, gu_sum, down_sum):
    n = lax.axis_index("narrow")
    half, pair = lax.rem(n, 2), lax.div(n, 2)
    mate = n + 1 - 2 * half
    far = n + 2 - 4 * pair
    far_mate = mate + 2 - 4 * pair
    for out, quarter in zip(outs, (n, mate, far, far_mate)):
        out[0:256, :] = gu_sum[pl.ds(pl.multiple_of(quarter * 256, 256), 256), :].astype(BF16)
        out[256:384, :] = down_sum[pl.ds(pl.multiple_of(quarter * 128, 128), 128), :].astype(BF16)


def expert_0_kernel(
    h2_ref, dy_ref, table_ref, gu_ref, down_ref, w1, w2_early, w2_rest, w3,
    gated_ref, dx_ref, rows_ref, grad_rows_ref, dgate_ref, own, mate, far, far_mate, far_mate_1,
    w_gu, w_down, gu_sum, down_sum, sems, es, er,
):
    step = pl.program_id(0)
    spot = Spot()
    second_expert = piece_copies(spot, gu_ref, down_ref, 1, 3, far_mate_1, es, er, 0)

    @pl.when(step == 0)
    def _():
        barrier = pltpu.get_barrier_semaphore()
        plane = spot.mate + 2 - 4 * lax.div(spot.n, 2)
        pl.semaphore_signal(barrier, inc=1, device_id=(plane, spot.w), device_id_type=MESH)
        pl.semaphore_wait(barrier, 1)
        start_all(second_expert)
        start_weights(0, gu_ref, down_ref, (w1, (w2_early, w2_rest), w3), w_gu, w_down, gu_sum, down_sum, sems)

    masks = [[pick(table_ref, s, e) for s in range(CHUNK)] for e in range(MINE)]
    rows, grad_rows = [], []
    for s in range(CHUNK):
        hot = jnp.concatenate([jnp.where(masks[e][s], 1.0, 0.0) for e in range(MINE)], axis=0).astype(BF16)
        rows.append(mm(hot, h2_ref[s]).astype(BF16))
        grad_rows.append(mm(hot, dy_ref[s]).astype(BF16))
    for s in range(CHUNK):
        rows_ref[0, s * SLOTS : (s + 1) * SLOTS, :] = rows[s][SLOTS:]
        grad_rows_ref[0, s * SLOTS : (s + 1) * SLOTS, :] = grad_rows[s][SLOTS:]
    rows = jnp.concatenate([r[:SLOTS] for r in rows], axis=0)
    grad_rows = jnp.concatenate([r[:SLOTS] for r in grad_rows], axis=0)
    gated, dx, slot_dgate = expert_math(
        rows, grad_rows, slot_gates(table_ref, masks[0], 0), w_gu, w_down, gu_sum, down_sum
    )
    gated_ref[0] = gated
    dx_ref[0] = dx
    dgate_ref[...] = jnp.zeros_like(dgate_ref)
    token_dgate(dgate_ref, masks[0], slot_dgate, 0)

    @pl.when(step == STEPS - 1)
    def _():
        store_quarters((own, mate, far, far_mate), gu_sum, down_sum)
        for copy in second_expert:
            copy.wait_send()
            copy.wait_recv()


def expert_1_kernel(
    rows_ref, grad_rows_ref, gated_before, dx_before, dgate_before, table_ref, gu_ref, down_ref, w1, w2, w3,
    y_ref, part_ref, dgate_ref, own, mate, far, far_mate,
    w_gu, w_down, gu_sum, down_sum, sems,
):
    step = pl.program_id(0)

    @pl.when(step == 0)
    def _():
        start_weights(1, gu_ref, down_ref, (w1, w2, w3), w_gu, w_down, gu_sum, down_sum, sems)

    masks = [[pick(table_ref, s, e) for s in range(CHUNK)] for e in range(MINE)]
    gated, dx, slot_dgate = expert_math(
        rows_ref[0], grad_rows_ref[0], slot_gates(table_ref, masks[1], 1), w_gu, w_down, gu_sum, down_sum
    )
    dgate_ref[...] = dgate_before[...]
    token_dgate(dgate_ref, masks[1], slot_dgate, 1)
    for s in range(CHUNK):
        at = slice(s * SLOTS, (s + 1) * SLOTS)
        hot = jnp.concatenate([jnp.where(masks[e][s], 1.0, 0.0) for e in range(MINE)], axis=0).astype(BF16)
        y_ref[s] = mm(hot, jnp.concatenate([gated_before[0, at, :], gated[at]], axis=0), TN).astype(BF16)
        part_ref[s] = mm(hot, jnp.concatenate([dx_before[0, at, :], dx[at]], axis=0), TN).astype(BF16)

    @pl.when(step == STEPS - 1)
    def _():
        store_quarters((own, mate, far, far_mate), gu_sum, down_sum)


def expert_specs():
    block = pl.BlockSpec((CHUNK, TOKENS, WIDTH), lambda c: (c, 0, 0))
    small = pl.BlockSpec((CHUNK, 8, TOKENS), lambda c: (c, 0, 0))
    slots = pl.BlockSpec((1, ROWS, WIDTH), lambda c: (c, 0, 0))
    quarter = pl.BlockSpec((384, WIDTH), lambda c: (0, 0))
    return block, small, slots, quarter


def expert_scratch():
    return [
        pltpu.VMEM((WIDTH, 2 * FF), BF16),
        pltpu.VMEM((FF, WIDTH), BF16),
        pltpu.VMEM((WIDTH, 2 * FF), F32),
        pltpu.VMEM((FF, WIDTH), F32),
        pltpu.SemaphoreType.DMA((10,)),
    ]


SLOT_ROWS = jax.ShapeDtypeStruct((STEPS, ROWS, WIDTH), BF16)
TOKEN_ROWS = jax.ShapeDtypeStruct((GROUP, TOKENS, WIDTH), BF16)
TABLES = jax.ShapeDtypeStruct((GROUP, 8, TOKENS), F32)
QUARTER = jax.ShapeDtypeStruct((384, WIDTH), BF16)


def expert_0_call(h2_all, dy_all, table_all, w_gate_up, w_down, pieces):
    block, small, slots, quarter = expert_specs()
    return pl.pallas_call(
        expert_0_kernel,
        name="expert_0",
        grid=(STEPS,),
        out_shape=(SLOT_ROWS,) * 4 + (TABLES,) + (QUARTER,) * 5,
        in_specs=[block, block, small] + [IN_HBM] * 6,
        out_specs=(slots,) * 4 + (small,) + (quarter,) * 4 + (IN_HBM,),
        scratch_shapes=expert_scratch() + [pltpu.SemaphoreType.DMA((2,)), pltpu.SemaphoreType.DMA((2,))],
        compiler_params=pltpu.CompilerParams(collective_id=4, has_side_effects=True, vmem_limit_bytes=VMEM_BYTES),
        cost_estimate=duration(1),
    )(h2_all, dy_all, table_all, w_gate_up, w_down, *pieces)


def expert_1_call(rows, grad_rows, gated, dx, dgate, table_all, w_gate_up, w_down, pieces):
    block, small, slots, quarter = expert_specs()
    return pl.pallas_call(
        expert_1_kernel,
        name="expert_1",
        grid=(STEPS,),
        out_shape=(TOKEN_ROWS,) * 2 + (TABLES,) + (QUARTER,) * 4,
        in_specs=[slots] * 4 + [small, small] + [IN_HBM] * 5,
        out_specs=(block, block, small) + (quarter,) * 4,
        scratch_shapes=expert_scratch(),
        compiler_params=pltpu.CompilerParams(vmem_limit_bytes=VMEM_BYTES),
        cost_estimate=duration(1),
    )(rows, grad_rows, gated, dx, dgate, table_all, w_gate_up, w_down, *pieces)


RESULTS = 6


def results_kernel(*refs):
    pieces, arrays, small = refs[:8], refs[8 : 8 + RESULTS], refs[8 + RESULTS : 11 + RESULTS]
    refs = refs[11 + RESULTS :]
    gate_up_ref, down_ref, outs, small_outs = refs[0], refs[1], refs[2 : 2 + RESULTS], refs[2 + RESULTS : 6 + RESULTS]
    refs = refs[6 + RESULTS :]
    loaded, totals, held, sems, out_sems, held_sems = refs[0], refs[1], refs[2 : 2 + RESULTS], *refs[2 + RESULTS :]
    half = lax.rem(lax.axis_index("narrow"), 2)
    loads = [pltpu.make_async_copy(piece, loaded.at[i], sems.at[i]) for i, piece in enumerate(pieces)]
    through = [pltpu.make_async_copy(a, h, held_sems.at[i]) for i, (a, h) in enumerate(zip(arrays, held))]
    start_all([loads[i] for i in (0, 2, 1, 3, 4, 6, 5, 7)])
    start_all(through)
    router, gains, load = small
    small_outs[0][...] = router[...]
    small_outs[1][...] = gains[0:1, :]
    small_outs[2][...] = gains[1:2, :]
    small_outs[3][...] = load[...]
    stores = []
    for e in range(2):
        for which in range(2):
            left, right = 4 * e + which, 4 * e + which + 2
            loads[left].wait()
            loads[right].wait()
            number = 2 * e + which
            place = 2 * (half if which == 0 else 1 - half) + e
            totals[number] = loaded[left].astype(F32) + loaded[right].astype(F32)
            for part, (out, first, depth) in enumerate(((gate_up_ref, 0, 256), (down_ref, 256, 128))):
                copy = pltpu.make_async_copy(
                    totals.at[number, pl.ds(first, depth)], out.at[place], out_sems.at[2 * number + part]
                )
                copy.start()
                stores.append(copy)
    for i, copy in enumerate(through):
        copy.wait()
        copy = pltpu.make_async_copy(held[i], outs[i], held_sems.at[i])
        copy.start()
        stores.append(copy)
    for copy in stores:
        copy.wait()


def results_call(first, second, arrays, small):
    shapes = [jax.ShapeDtypeStruct(a.shape, a.dtype) for a in arrays]
    row = jax.ShapeDtypeStruct((1, 32), F32)
    return pl.pallas_call(
        results_kernel,
        name="results",
        out_shape=(
            jax.ShapeDtypeStruct((4, 256, WIDTH), F32),
            jax.ShapeDtypeStruct((4, 128, WIDTH), F32),
            *shapes,
            jax.ShapeDtypeStruct((32, 32), F32),
            row,
            row,
            jax.ShapeDtypeStruct((1, 32), jnp.int32),
        ),
        in_specs=[IN_HBM] * (8 + RESULTS) + [IN_VMEM] * 3,
        out_specs=(IN_HBM,) * (2 + RESULTS) + (IN_VMEM,) * 4,
        scratch_shapes=[pltpu.VMEM((8, 384, WIDTH), BF16), pltpu.VMEM((4, 384, WIDTH), F32)]
        + [pltpu.VMEM(s.shape, s.dtype) for s in shapes]
        + [pltpu.SemaphoreType.DMA((8,)), pltpu.SemaphoreType.DMA((8,)), pltpu.SemaphoreType.DMA((RESULTS,))],
        compiler_params=pltpu.CompilerParams(vmem_limit_bytes=VMEM_BYTES),
        cost_estimate=duration(1),
    )(*first, *second, *arrays, *small)


def widen(ref_value):
    return ref_value.astype(F32)


class PlaneReduce:
    COPIES = 10

    def __init__(self, spot, part, buffers, send, recv, local):
        self.spot, self.part = spot, part
        self.acc, self.from_core, self.from_one, self.from_two = buffers
        self.send, self.recv, self.local = send, recv, local
        self.started = []
        s = spot
        self.q_own = 2 * s.y + s.x
        self.q_x = 2 * s.y + 1 - s.x
        self.q_y = 2 - 2 * s.y + s.x
        self.q_d = 3 - self.q_own

    def put(self, src, dst, number, to):
        copy = remote(src, dst, self.send.at[number], self.recv.at[number], self.spot.wide(to))
        copy.start()
        self.started.append(copy)

    def got(self, dst, number):
        remote(dst, dst, self.send.at[number], self.recv.at[number], self.spot.wide(self.spot.sib)).wait_recv()

    def begin(self):
        s = self.spot
        self.loads = []
        for number, q in enumerate((self.q_d, self.q_x, self.q_y, self.q_own)):
            self.put(self.part(2 * q + 1 - s.core), self.from_core.at[q], number, s.sib)
            copy = pltpu.make_async_copy(self.part(2 * q + s.core), self.acc.at[q], self.local.at[number])
            copy.start()
            self.loads.append(copy)

    def add_core(self, number, q):
        self.loads[number].wait()
        self.got(self.from_core.at[q], number)
        self.acc[q] = (widen(self.acc[q]) + widen(self.from_core[q])).astype(BF16)

    def across_core(self):
        s = self.spot
        self.add_core(0, self.q_d)
        self.put(halves(self.acc.at[self.q_d], 0), self.from_one.at[1], 5, s.xn)
        self.put(halves(self.acc.at[self.q_d], 1), self.from_one.at[3], 7, s.yn)
        self.add_core(1, self.q_x)
        self.put(halves(self.acc.at[self.q_x], 0), self.from_one.at[0], 4, s.xn)
        self.add_core(2, self.q_y)
        self.put(halves(self.acc.at[self.q_y], 1), self.from_one.at[2], 6, s.yn)
        self.add_core(3, self.q_own)

    def across_one(self):
        s = self.spot
        self.got(self.from_one.at[1], 5)
        upper = halves(self.acc.at[self.q_y], 0)
        upper[...] = (widen(upper[...]) + widen(self.from_one[1])).astype(BF16)
        self.put(upper, self.from_two.at[0], 8, s.yn)
        self.got(self.from_one.at[3], 7)
        lower = halves(self.acc.at[self.q_x], 1)
        lower[...] = (widen(lower[...]) + widen(self.from_one[3])).astype(BF16)
        self.put(lower, self.from_two.at[1], 9, s.xn)

    def total(self, out):
        self.got(self.from_one.at[0], 4)
        self.got(self.from_two.at[0], 8)
        own = self.acc.at[self.q_own]
        out[0:SPAN, :] = widen(own[0:SPAN, :]) + widen(self.from_one[0]) + widen(self.from_two[0])
        self.got(self.from_one.at[2], 6)
        self.got(self.from_two.at[1], 9)
        out[SPAN:TOKENS, :] = widen(own[SPAN:TOKENS, :]) + widen(self.from_one[2]) + widen(self.from_two[1])

    def finish(self):
        for copy in self.started:
            copy.wait_send()


def halves(ref, which):
    return ref.at[pl.ds(which * SPAN, SPAN)]


class GroupReduce:
    def __init__(self, spot, theirs, ours, scratch):
        acc, from_core, from_one, from_two, total, mate_send, mate_recv, send, recv, local, zs, zr = scratch
        self.total_ref, self.mate_send, self.mate_recv = total, mate_send, mate_recv
        parts = []
        for which, part in enumerate((theirs, ours)):
            buffers = (acc.at[which], from_core.at[which], from_one.at[which], from_two.at[which])
            parts.append(PlaneReduce(spot, part, buffers, send.at[which], recv.at[which], local.at[which]))
        self.theirs, self.ours = parts
        self.across = remote(mate_send, mate_recv, zs.at[0], zr.at[0], (spot.mate, spot.w))

    def begin(self):
        self.theirs.begin()
        self.ours.begin()

    def across_core(self):
        self.theirs.across_core()
        self.ours.across_core()

    def across_one(self):
        self.theirs.across_one()
        self.ours.across_one()

    def to_mate(self):
        self.theirs.total(self.total_ref)
        self.mate_send[...] = self.total_ref[...].astype(BF16)
        self.across.start()

    def finish(self):
        self.ours.total(self.total_ref)
        self.across.wait_recv()
        self.total_ref[...] += widen(self.mate_recv[...])
        self.theirs.finish()
        self.ours.finish()
        self.across.wait_send()


def reduce_scratch():
    dma = pltpu.SemaphoreType.DMA
    return [
        pltpu.VMEM((2, 4, TOKENS, WIDTH), BF16),
        pltpu.VMEM((2, 4, TOKENS, WIDTH), BF16),
        pltpu.VMEM((2, 4, SPAN, WIDTH), BF16),
        pltpu.VMEM((2, 2, SPAN, WIDTH), BF16),
        pltpu.VMEM((TOKENS, WIDTH), F32),
        pltpu.VMEM((TOKENS, WIDTH), BF16),
        pltpu.VMEM((TOKENS, WIDTH), BF16),
        dma((2, PlaneReduce.COPIES)),
        dma((2, PlaneReduce.COPIES)),
        dma((2, 4)),
        dma((1,)),
        dma((1,)),
    ]


REDUCE_REFS = 12


class AttentionBack:
    def __init__(self, dattn_all, w_rows, qkv_ref, lse_ref, o_ref, angle_ref, dqkv_ref, dkv_ref, dq_ref, osum):
        self.dattn_all, self.w_rows, self.qkv, self.lse, self.o = dattn_all, w_rows, qkv_ref, lse_ref, o_ref
        self.angle = angle_ref
        self.dqkv, self.dkv, self.dq, self.osum = dqkv_ref, dkv_ref, dq_ref, osum
        self.first_half = lane_half()
        self.is_key = lax.broadcasted_iota(jnp.int32, (1, 128), 1) < 64
        dkv_ref[...] = jnp.zeros_like(dkv_ref)
        osum[...] = jnp.zeros_like(osum)

    def stack(self, both):
        return jnp.concatenate([both[:, 0:64], both[:, 64:128]], axis=0)

    def chunk(self, row, q):
        first = pl.multiple_of(q * 256, 256)
        tokens = pl.ds(first, 256)
        dattn = self.dattn_all[pl.ds(2 * q, 2), pl.ds(row * SPAN, SPAN), :].reshape(256, WIDTH)
        outs = self.o[row, tokens, :]
        do = mm(dattn, self.w_rows[...], NT).astype(BF16)
        self.osum[...] += mm(outs, dattn, TN)
        inner = do.astype(F32) * outs.astype(F32)
        delta = jnp.concatenate(
            [
                jnp.sum(jnp.where(self.is_key, inner, 0.0), axis=1, keepdims=True),
                jnp.sum(jnp.where(self.is_key, 0.0, inner), axis=1, keepdims=True),
            ],
            axis=0,
        )
        query = self.stack(self.qkv[row, tokens, 0:128])
        do = self.stack(do)
        log_total = jnp.concatenate([self.lse[row, tokens, 0:1], self.lse[row, tokens, 64:65]], axis=0)
        start = self.lse[row, tokens, 32:33]
        start = jnp.concatenate([start, start], axis=0)
        place = lax.broadcasted_iota(jnp.int32, (256, 1), 0)
        place_query = (jnp.concatenate([place, place], axis=0) + q * 256).astype(F32)
        self.dq[...] = jnp.zeros_like(self.dq)

        def key_block(block, carry):
            keys_at = pl.ds(pl.multiple_of(block * 256, 256), 256)
            keys = self.qkv[row, keys_at, 128:192]
            values = self.qkv[row, keys_at, 192:256]
            place_key = (lax.broadcasted_iota(jnp.int32, (1, 256), 1) + block * 256).astype(F32)
            allowed = (place_key <= place_query) & (place_key >= start)
            scores = jnp.where(allowed, mm(query, keys, NT) * (HEAD_DIM**-0.5), MASKED)
            weights = jnp.exp(scores - log_total)
            dp = mm(do, values, NT)
            ds = (weights * (dp - delta)).astype(BF16)
            self.dq[...] += mm(ds, keys)
            dk = mm(ds, query, TN) * (HEAD_DIM**-0.5)
            dv = mm(weights.astype(BF16), do, TN)
            self.dkv[row, keys_at, :] += jnp.concatenate([dk, dv], axis=1)
            return carry

        lax.fori_loop(0, q + 1, key_block, 0)
        dq = jnp.concatenate([self.dq[0:256], self.dq[256:512]], axis=1) * (HEAD_DIM**-0.5)
        cosine = self.angle[row, tokens, 0:128]
        sine = self.angle[row, tokens, 128:256]
        self.dqkv[row, tokens, 0:128] = (dq * cosine + turn_back(dq * sine, self.first_half)).astype(BF16)

    def keys(self, row):
        cosine = self.angle[row, :, 0:128]
        sine = self.angle[row, :, 128:256]
        dkv = self.dkv[row]
        turned = dkv * cosine + turn_back(dkv * sine, self.first_half)
        self.dqkv[row, :, 128:256] = jnp.where(self.is_key, turned, dkv).astype(BF16)


def backward_kernel(*refs):
    (
        part_ref, y_ref, dgate_ref, h2_ref, w_out_ref, w_full_ref, h1_ref, qkv_ref, lse_ref, o_ref,
        angle_ref, mate_1, far_1, far_mate_1,
        x_ref, mid_ref, gate_ref, gain_ref, dy_ref, w_own, gain_col,
    ) = refs[:21]
    (
        block_out, in_grad, q_grad, k_grad, v_grad, o_grad, router_grad, two_gains, load_out, *quarters_recv,
    ) = refs[21:33]
    (
        dgate_all, h2_own, dattn_all, dmid_ref, small_ref, small_all, small_sum, w_router, w_rows, w_full,
        h1, qkv, lse, outs, angle, dqkv_ref, dkv_ref, dq_ref, osum, og_ref, wg_ref,
        dq_full, w_recv, o_recv, s_recv,
        ts, tr, s0, r0, bs, br, qs, qr, ks, kr, ws, wr, os, orv, ss, sr, gs, gr, local,
    ) = refs[33:77]
    h2_sum_refs = refs[77 : 77 + REDUCE_REFS]
    y_sum_refs = refs[77 + REDUCE_REFS :]

    spot = Spot()
    everyone = NARROW * WIDE
    spot.greet(everyone)
    base, mate_base = spot.half * WIDE, (1 - spot.half) * WIDE
    h2_sum = GroupReduce(
        spot, lambda who: part_ref.at[mate_base + who], lambda who: part_ref.at[base + who], h2_sum_refs
    )
    y_sum = GroupReduce(spot, lambda who: y_ref.at[mate_base + who], lambda who: y_ref.at[base + who], y_sum_refs)
    h2_sum.begin()

    def tables(step, arriving):
        other = lax.rem(spot.slot + step, GROUP)
        o_half, o_w = lax.div(other, WIDE), lax.rem(other, WIDE)
        place = other if arriving else spot.slot
        return remote(
            dgate_ref.at[other], dgate_all.at[place], ts.at[other], tr.at[place],
            (spot.n - spot.half + o_half, o_w),
        )

    def start_table(step, carry):
        tables(step, False).start()
        return carry

    lax.fori_loop(1, GROUP, start_table, 0)
    rows = pl.ds(pl.multiple_of(spot.w * 128, 128), 128)
    loads = [
        (dgate_ref.at[spot.slot], dgate_all.at[spot.slot]),
        (h2_ref.at[spot.slot], h2_own),
        (w_out_ref.at[:, pl.ds(WIDTH, 128)], w_router),
        (w_out_ref.at[rows, pl.ds(0, WIDTH)], w_rows),
        (qkv_ref, qkv),
        (lse_ref, lse),
        (o_ref, outs),
        (angle_ref, angle),
        (h1_ref, h1),
    ]
    loads = [pltpu.make_async_copy(src, dst, local.at[i]) for i, (src, dst) in enumerate(loads)]
    w_loads = [pltpu.make_async_copy(w_full_ref.at[who], w_full.at[who], local.at[10 + who]) for who in range(WIDE)]
    h2_sum.across_core()
    start_all(loads + w_loads)
    y_sum.begin()
    far_plane = 2 - 4 * lax.div(spot.n, 2)
    quarter_copies = [
        remote(piece, quarters_recv[number], gs.at[number], gr.at[number], (plane, spot.w))
        for number, (piece, plane) in enumerate(
            ((mate_1, spot.mate), (far_1, spot.n + far_plane), (far_mate_1, spot.mate + far_plane))
        )
    ]
    h2_sum.across_one()
    h2_sum.to_mate()
    h2_sum.finish()
    start_all(quarter_copies)

    def wait_table(step, carry):
        tables(step, False).wait_send()
        tables(step, True).wait_recv()
        return carry

    lax.fori_loop(1, GROUP, wait_table, 0)
    for copy in loads[:4]:
        copy.wait()

    gate = gate_ref[0:32, :]
    dgate = jnp.concatenate([dgate_all[(o % 2) * WIDE + o // 2, 0:2, :] for o in range(GROUP)], axis=0)
    dsel = gate * (dgate - jnp.sum(gate * dgate, axis=0, keepdims=True))
    dlogits = jnp.concatenate([dsel, jnp.zeros((96, TOKENS), F32)], axis=0)
    dh2 = h2_sum.total_ref[...] + mm(jnp.transpose(dlogits).astype(BF16), w_router[...], NT)
    mid = mid_ref[...]
    scale = lax.rsqrt(jnp.mean(mid * mid, axis=1, keepdims=True) + EPSILON)
    weighted = dh2 * gain_ref[1:2, :]
    inner = jnp.mean(weighted * mid, axis=1, keepdims=True)
    dmid = dy_ref[...].astype(F32) + weighted * scale - mid * (scale * scale * scale) * inner
    dmid_ref[...] = dmid
    dattn_all[spot.w] = dmid.astype(BF16)
    mine = dattn_all.at[spot.w]
    gather = PlaneGather(
        spot,
        lambda half: mine if half is None else halves(mine, half),
        lambda who, half: dattn_all.at[who] if half is None else halves(dattn_all.at[who], half),
        s0, r0,
    )
    gather.begin()
    small_ref[0:32, :] = mm(dsel.astype(BF16), h2_own[...])
    small_ref[32:33, :] = jnp.sum(dh2 * mid * scale, axis=0, keepdims=True)
    lane = lax.broadcasted_iota(jnp.int32, (32, WIDTH), 1)
    column = lax.broadcasted_iota(jnp.int32, (32, WIDTH), 0)
    count = jnp.sum(gate_ref[32:64, :], axis=1, keepdims=True)
    small_ref[33:34, :] = jnp.sum(jnp.where(lax.rem(lane, 128) == column, count, 0.0), axis=0, keepdims=True)
    small_ref[34:40, :] = jnp.zeros((6, WIDTH), F32)

    def lanes_to(step, arriving):
        other = lax.rem(spot.w + step, WIDE)
        place = other if arriving else spot.w
        return remote(
            small_ref.at[:, pl.ds(pl.multiple_of(other * 128, 128), 128)], small_all.at[place],
            bs.at[other], br.at[place], spot.wide(other),
        )

    def start_lanes(step, carry):
        lanes_to(step, False).start()
        return carry

    lax.fori_loop(1, WIDE, start_lanes, 0)
    small_all[spot.w] = small_ref[:, pl.ds(pl.multiple_of(spot.w * 128, 128), 128)]

    for copy in loads[4:8]:
        copy.wait()
    back = AttentionBack(dattn_all, w_rows, qkv, lse, outs, angle, dqkv_ref, dkv_ref, dq_ref, osum)
    order = h2_sum.ours
    sib_x = spot.sib + 2 - 4 * spot.x
    sib_y = spot.sib + 4 - 8 * spot.y
    sib_d = sib_x + 4 - 8 * spot.y

    def to_tokens(other, place, first, send, recv):
        return remote(
            dqkv_ref.at[:, pl.ds(pl.multiple_of(other * SPAN, SPAN), SPAN), pl.ds(first, 128)],
            dq_full.at[:, :, pl.ds(pl.multiple_of(place * 256 + first, 128), 128)],
            send.at[other], recv.at[place], spot.wide(other),
        )

    def send_queries(who):
        for other in who:
            to_tokens(other, spot.w, 0, qs, qr).start()

    gather.got(spot.sib, None, 4)
    back.chunk(0, order.q_own)
    gather.middle()
    back.chunk(1, order.q_own)
    send_queries((spot.sib,))
    gather.late()
    gather.got(sib_x, None, 7)
    back.chunk(0, order.q_x)
    gather.last()
    y_sum.across_core()
    back.chunk(1, order.q_x)
    send_queries((spot.xn, sib_x))
    gather.got(sib_y, None, 8)
    back.chunk(0, order.q_y)
    back.chunk(1, order.q_y)
    send_queries((spot.yn, sib_y))
    gather.got(sib_d, 0, 9)
    gather.got(sib_d, 1, 10)
    back.chunk(0, order.q_d)
    back.chunk(1, order.q_d)
    send_queries((spot.diag, sib_d))
    for copy in gather.started:
        copy.wait_send()
    back.keys(0)
    back.keys(1)

    def others(step):
        other = lax.rem(spot.me + step, everyone)
        return other, (lax.div(other, WIDE), lax.rem(other, WIDE))

    def rows_of(ref, owner):
        return ref.at[pl.ds(pl.multiple_of(owner * 32, 32), 32)]

    def to_owner(step, arriving):
        other, to = others(step)
        place = other if arriving else spot.me
        return remote(rows_of(wg_ref, other), w_recv.at[place], ws.at[other], wr.at[place], to)

    def start_owner(step, carry):
        to_owner(step, False).start()
        return carry

    def start_keys(step, carry):
        to_tokens(lax.rem(spot.w + step, WIDE), spot.w, 128, ks, kr).start()
        return carry

    lax.fori_loop(1, WIDE, start_keys, 0)
    plane_mine = pltpu.make_async_copy(
        dqkv_ref.at[:, pl.ds(pl.multiple_of(spot.w * SPAN, SPAN), SPAN), :],
        dq_full.at[:, :, pl.ds(pl.multiple_of(spot.w * 256, 256), 256)],
        local.at[0],
    )
    plane_mine.start()
    og_ref[...] = osum[...].astype(BF16)

    def wait_lanes(step, carry):
        lanes_to(step, False).wait_send()
        lanes_to(step, True).wait_recv()
        return carry

    lax.fori_loop(1, WIDE, wait_lanes, 0)
    lane_total = small_all[0]
    for device in range(1, WIDE):
        lane_total = lane_total + small_all[device]
    small_sum[...] = lane_total
    def output_copies(act_local, act_send, act_recv):
        for i in range(4):
            owner = 4 * spot.w + i
            to = (lax.div(owner, WIDE), lax.rem(owner, WIDE))
            source = og_ref.at[pl.ds(i * 32, 32)]
            here = owner == spot.me

            @pl.when(here)
            def _():
                act_local(pltpu.make_async_copy(source, o_recv.at[spot.n], local.at[3]))
                act_local(pltpu.make_async_copy(small_sum, s_recv.at[spot.n], local.at[2]))

            @pl.when(jnp.logical_not(here))
            def _():
                act_send(remote(source, o_recv.at[spot.n], os.at[i], orv.at[spot.n], to))
                act_send(remote(small_sum, s_recv.at[spot.n], ss.at[i], sr.at[spot.n], to))

        for plane in range(NARROW):
            giver = lax.div(spot.me, 4)
            here = (plane == spot.n) & (giver == spot.w)

            @pl.when(jnp.logical_not(here))
            def _():
                place = o_recv.at[plane]
                act_recv(remote(place, place, os.at[0], orv.at[plane], (plane, giver)))
                small = s_recv.at[plane]
                act_recv(remote(small, small, ss.at[0], sr.at[plane], (plane, giver)))

    def nothing(copy):
        return None

    output_copies(lambda c: c.start(), lambda c: c.start(), nothing)
    y_sum.across_one()

    loads[8].wait()
    wg_ref[...] = (mm(h1[0], dqkv_ref[0], TN) + mm(h1[1], dqkv_ref[1], TN)).astype(BF16)
    lax.fori_loop(1, everyone, start_owner, 0)
    owner_mine = pltpu.make_async_copy(rows_of(wg_ref, spot.me), w_recv.at[spot.me], local.at[1])
    owner_mine.start()
    y_sum.to_mate()

    def wait_plane(step, carry):
        other = lax.rem(spot.w + step, WIDE)
        for first, send, recv in ((0, qs, qr), (128, ks, kr)):
            to_tokens(other, spot.w, first, send, recv).wait_send()
            to_tokens(other, other, first, send, recv).wait_recv()
        return carry

    lax.fori_loop(1, WIDE, wait_plane, 0)
    plane_mine.wait()
    for copy in w_loads:
        copy.wait()
    dh1 = jnp.zeros((TOKENS, WIDTH), F32)
    for who in range(WIDE):
        grads = dq_full[:, :, 256 * who : 256 * who + 256].reshape(TOKENS, 256)
        dh1 = dh1 + mm(grads, w_full[who], NT)
    x = x_ref[...].astype(F32)
    scale = lax.rsqrt(jnp.mean(x * x, axis=1, keepdims=True) + EPSILON)
    weighted = dh1 * gain_ref[0:1, :]
    inner = jnp.mean(weighted * x, axis=1, keepdims=True)
    in_grad[...] = (dmid_ref[...] + weighted * scale - x * (scale * scale * scale) * inner).astype(BF16)
    y_sum.finish()
    block_out[...] = (mid_ref[...] + y_sum.total_ref[...]).astype(BF16)

    def wait_owner(step, carry):
        to_owner(step, False).wait_send()
        to_owner(step, True).wait_recv()
        return carry

    lax.fori_loop(1, everyone, wait_owner, 0)
    owner_mine.wait()
    output_copies(lambda c: c.wait(), lambda c: c.wait_send(), lambda c: c.wait_recv())
    gain_total = jnp.zeros((32, 1), F32)
    for w in range(WIDE):
        total = widen(w_recv[w])
        for plane in range(1, NARROW):
            total = total + widen(w_recv[plane * WIDE + w])
        q_grad[:, 128 * w : 128 * w + 128] = total[:, 0:128]
        k_grad[:, 64 * w : 64 * w + 64] = total[:, 128:192]
        v_grad[:, 64 * w : 64 * w + 64] = total[:, 192:256]
        gain_total += jnp.sum(total * widen(w_own[:, 256 * w : 256 * w + 256]), axis=1, keepdims=True)
    gain_total = gain_total / gain_col[...].astype(F32)
    total = widen(o_recv[0])
    for plane in range(1, NARROW):
        total = total + widen(o_recv[plane])
    o_grad[...] = total
    total = s_recv[0]
    for plane in range(1, NARROW):
        total = total + s_recv[plane]
    load_out[...] = total[33:34, 0:32].astype(jnp.int32)
    lane = lax.rem(spot.me, 4)
    mine = jnp.zeros((40, 32), F32)
    for part in range(4):
        mine = mine + jnp.where(lane == part, 1.0, 0.0) * total[:, 32 * part : 32 * part + 32]
    square = jnp.concatenate([mine, jnp.zeros((40, 96), F32)], axis=1)
    square = jnp.concatenate([square, jnp.zeros((88, 128), F32)], axis=0)
    router_grad[...] = jnp.transpose(square)[0:32, 0:32]
    column = jnp.concatenate([jnp.broadcast_to(gain_total, (32, 128)), jnp.zeros((96, 128), F32)], axis=0)
    two_gains[...] = jnp.concatenate([jnp.transpose(column)[0:1, 0:32], mine[32:33]], axis=0)

    for copy in quarter_copies:
        copy.wait_send()
        copy.wait_recv()


def backward_call(*operands):
    dma = pltpu.SemaphoreType.DMA
    vmem = pltpu.VMEM
    everyone = NARROW * WIDE
    copies = PlaneGather.COPIES
    return pl.pallas_call(
        backward_kernel,
        name="backward",
        out_shape=(
            jax.ShapeDtypeStruct((TOKENS, WIDTH), BF16),
            jax.ShapeDtypeStruct((TOKENS, WIDTH), BF16),
            jax.ShapeDtypeStruct((32, WIDTH), F32),
            jax.ShapeDtypeStruct((32, WIDTH // 2), F32),
            jax.ShapeDtypeStruct((32, WIDTH // 2), F32),
            jax.ShapeDtypeStruct((32, WIDTH), F32),
            jax.ShapeDtypeStruct((32, 32), F32),
            jax.ShapeDtypeStruct((2, 32), F32),
            jax.ShapeDtypeStruct((1, 32), jnp.int32),
        )
        + (QUARTER,) * 3,
        in_specs=[IN_HBM] * 14 + [IN_VMEM] * 7,
        out_specs=(IN_VMEM,) * 9 + (IN_HBM,) * 3,
        scratch_shapes=[
            vmem((GROUP, 8, TOKENS), F32),
            vmem((TOKENS, WIDTH), BF16),
            vmem((WIDE, TOKENS, WIDTH), BF16),
            vmem((TOKENS, WIDTH), F32),
            vmem((40, WIDTH), F32),
            vmem((WIDE, 40, 128), F32),
            vmem((40, 128), F32),
            vmem((WIDTH, 128), BF16),
            vmem((128, WIDTH), BF16),
            vmem((WIDE, WIDTH, 256), BF16),
            vmem((2, SEQ, WIDTH), BF16),
            vmem((2, SEQ, 256), BF16),
            vmem((2, SEQ, 128), F32),
            vmem((2, SEQ, 128), BF16),
            vmem((2, SEQ, 256), F32),
            vmem((2, SEQ, 256), BF16),
            vmem((2, SEQ, 128), F32),
            vmem((512, HEAD_DIM), F32),
            vmem((128, WIDTH), F32),
            vmem((128, WIDTH), BF16),
            vmem((WIDTH, 256), BF16),
            vmem((2, SPAN, 2 * WIDTH), BF16),
            vmem((everyone, 32, 256), BF16),
            vmem((NARROW, 32, WIDTH), BF16),
            vmem((NARROW, 40, 128), F32),
            dma((GROUP,)),
            dma((GROUP,)),
            dma((copies,)),
            dma((copies,)),
            dma((WIDE,)),
            dma((WIDE,)),
            dma((WIDE,)),
            dma((WIDE,)),
            dma((WIDE,)),
            dma((WIDE,)),
            dma((everyone,)),
            dma((everyone,)),
            dma((4,)),
            dma((NARROW,)),
            dma((4,)),
            dma((NARROW,)),
            dma((3,)),
            dma((3,)),
            dma((18,)),
        ]
        + reduce_scratch()
        + reduce_scratch(),
        compiler_params=pltpu.CompilerParams(collective_id=3, has_side_effects=True, vmem_limit_bytes=VMEM_BYTES),
        cost_estimate=duration(1),
    )(*operands)


def swap(values, distance):
    return lax.ppermute(values, "narrow", [(i, i ^ distance) for i in range(NARROW)])


def position_tables():
    freq = (1.0 / np.float32(THETA) ** (np.arange(32, dtype=np.float32) * np.float32(2.0) / np.float32(HEAD_DIM))).astype(np.float32)
    angle = np.arange(SEQ, dtype=np.float32)[:, None] * freq[None, :]
    cosine = np.tile(np.cos(angle.astype(np.float64)), (1, 4)).astype(np.float32)
    sine = np.tile(np.sin(angle.astype(np.float64)), (1, 4)).astype(np.float32)
    return cosine, sine, np.tile(freq[None, :], (8, 4)).astype(np.float32)


def fast_device(
    hidden_in, out_grad, seg_ids, expert_ids, attn_gain, w_query, w_key, w_value, w_output,
    moe_gain, w_router, w_gate_up, w_down,
):
    n = lax.axis_index("narrow")
    w = lax.axis_index("wide")
    half = n % 2
    me = n * WIDE + w
    cos_table, sin_table, freq = position_tables()

    x_own = hidden_in.reshape(TOKENS, WIDTH)
    dy_own = out_grad.reshape(TOKENS, WIDTH)
    ids = expert_ids.reshape(TOKENS, TOP)
    x_all, w_all, g_all, seg_all, wo_block, dy_pair, far_early_0, w_own = gather_call(
        x_own, dy_own, seg_ids, w_query, w_key, w_value, w_output, w_router,
        attn_gain.reshape(1, 32), moe_gain.reshape(1, 32), w_gate_up,
    )
    (
        h1, qkv, lse, o_heads, angle, gain_rows, mid, gate, w_out, h2_all, dy_all, table_all,
        mate_0, far_rest_0, far_mate_0, mate_1, far_1,
    ) = forward_call(
        x_all, w_all, g_all, seg_all, cos_table, sin_table, freq, wo_block, ids, dy_pair, w_gate_up, w_down
    )
    w_out = w_out.reshape(WIDTH, WIDTH + 128)

    def send_grads(own, mate, far, far_mate):
        return own, swap(mate, 1), swap(far, 2), swap(far_mate, 3)

    gated_0, dx_0, rows_1, grad_rows_1, dgate_0, *grads_0, far_mate_1 = expert_0_call(
        h2_all, dy_all, table_all, w_gate_up, w_down, (mate_0, far_early_0, far_rest_0, far_mate_0)
    )
    dgate_0, w_heads = lax.optimization_barrier((dgate_0, w_all))
    w_full = lax.all_gather(w_heads.reshape(WIDTH, 256), "wide", axis=0, tiled=False)
    grads_0 = send_grads(*grads_0)
    y, part, dgate, *grads_1 = expert_1_call(
        rows_1, grad_rows_1, gated_0, dx_0, dgate_0, table_all, w_gate_up, w_down, (mate_1, far_1, far_mate_1)
    )
    (
        block_out, in_grad, q_grad, k_grad, v_grad, o_grad, router_grad, two_gains, load, *arrived_1,
    ) = backward_call(
        part, y, dgate, h2_all, w_out, w_full, h1, qkv, lse, o_heads, angle, *grads_1[1:],
        x_own, mid, gate, gain_rows, dy_own, w_own, attn_gain.reshape(32, 1),
    )
    (
        gate_up_sum, down_sum, block_out, in_grad, q_grad, k_grad, v_grad, o_grad,
        router_grad, attn_gain_grad, moe_gain_grad, load,
    ) = results_call(
        grads_0, (grads_1[0], *arrived_1),
        (block_out, in_grad, q_grad, k_grad, v_grad, o_grad), (router_grad, two_gains, load),
    )
    return (
        block_out.reshape(hidden_in.shape),
        in_grad.reshape(hidden_in.shape),
        attn_gain_grad.reshape(32),
        q_grad,
        k_grad,
        v_grad,
        o_grad,
        moe_gain_grad.reshape(32),
        router_grad,
        gate_up_sum,
        down_sum,
        load.reshape(32),
    )


def solution(mesh):
    planned = mesh.shape["narrow"] == NARROW and mesh.shape["wide"] == WIDE
    return jax.shard_map(
        fast_device if planned else general_device,
        mesh=mesh,
        in_specs=(
            P("narrow", "wide", None),
            P("narrow", "wide", None),
            P("narrow", "wide"),
            P("narrow", "wide", None),
            P(("narrow", "wide")),
            P(("narrow", "wide"), None),
            P(("narrow", "wide"), None),
            P(("narrow", "wide"), None),
            P(("narrow", "wide"), None),
            P(("narrow", "wide")),
            P(("narrow", "wide"), None),
            P("wide", "narrow", None),
            P("wide", "narrow", None),
        ),
        out_specs=(
            P("narrow", "wide", None),
            P("narrow", "wide", None),
            P(("narrow", "wide")),
            P(("narrow", "wide"), None),
            P(("narrow", "wide"), None),
            P(("narrow", "wide"), None),
            P(("narrow", "wide"), None),
            P(("narrow", "wide")),
            P(("narrow", "wide"), None),
            P("wide", "narrow", None),
            P("wide", "narrow", None),
            P(),
        ),
        check_vma=False,
    )
```

```python
import math

import functools
import jax
import jax.numpy as jnp
import numpy as np
from jax import lax
from jax.experimental import pallas as pl
from jax.experimental.pallas import tpu as pltpu
from jax.sharding import PartitionSpec as P

KV_HEADS = 8
HEAD_DIM = 64
EXPERTS = 32
TOP = 8
FF = 512
CAP = 80


EPSILON = 1e-06
THETA = 10000.0
MASKED = -1e30


def rms_scale(values):
    return lax.rsqrt(jnp.mean(values * values, axis=-1, keepdims=True) + EPSILON)


def norm_back(values, scale, gain, upstream):
    weighted = upstream * gain
    inner_mean = jnp.mean(weighted * values, axis=-1, keepdims=True)
    value_grad = weighted * scale - values * (scale * scale * scale) * inner_mean
    gain_grad = jnp.sum(upstream * values * scale, axis=0)
    return (value_grad, gain_grad)


def lane_turn(head_dim):
    lane_ids = jnp.arange(128)
    lane_local = lane_ids % head_dim
    half_dim = head_dim // 2
    same_head = lane_ids[:, None] // head_dim == lane_ids[None, :] // head_dim
    from_upper = (lane_local[None, :] < half_dim) & (
        lane_local[:, None] == lane_local[None, :] + half_dim
    )
    from_lower = (lane_local[None, :] >= half_dim) & (
        lane_local[:, None] + half_dim == lane_local[None, :]
    )
    return jnp.where(
        same_head & from_upper, -1.0, jnp.where(same_head & from_lower, 1.0, 0.0)
    ).astype(jnp.float32)


def lane_angles(positions, head_dim):
    lane_ids = jnp.arange(128) % head_dim % (head_dim // 2)
    inverse = 1.0 / THETA ** (lane_ids.astype(jnp.float32) * 2.0 / head_dim)
    return positions[..., None] * inverse


def rotate(values, cos_table, sin_table, turner):
    dims_in = values.shape
    blocks = values.reshape(dims_in[0], dims_in[1], -1, 128)
    turned = jnp.einsum("abnl,lm->abnm", blocks, turner, precision=lax.Precision.HIGHEST)
    return (blocks * cos_table[:, :, None, :] + turned * sin_table[:, :, None, :]).reshape(dims_in)


def rotate_back(grad_in, cos_table, sin_table, turner):
    dims_in = grad_in.shape
    blocks = grad_in.reshape(dims_in[0], dims_in[1], -1, 128)
    turned = jnp.einsum(
        "abnm,lm->abnl", blocks * sin_table[:, :, None, :], turner, precision=lax.Precision.HIGHEST
    )
    return (blocks * cos_table[:, :, None, :] + turned).reshape(dims_in)


def masked_scores(query_five, key_block, seg_query, seg_key, place_query, place_key, factor):
    scores = (
        jnp.einsum("abgjd,akgd->agjbk", query_five, key_block, preferred_element_type=jnp.float32)
        * factor
    )
    allowed = (seg_query[:, :, None] == seg_key[:, None, :]) & (
        place_query[:, :, None] >= place_key[:, None, :]
    )
    return jnp.where(allowed[:, None, None], scores, MASKED)


def general_device(
    hidden_in,
    out_grad,
    seg_ids,
    expert_ids,
    attn_gain,
    w_query,
    w_key,
    w_value,
    w_output,
    moe_gain,
    w_router,
    w_gate_up,
    w_down,
):
    row_count, span_len, feat_dim = hidden_in.shape
    tok_count = row_count * span_len
    factor = HEAD_DIM ** (-0.5)
    kv_width = KV_HEADS * HEAD_DIM
    gain_one, query_w, key_w, value_w, output_w, gain_two, router_w = (
        lax.all_gather(attn_gain, ("narrow", "wide"), axis=0, tiled=True),
        lax.all_gather(w_query, ("narrow", "wide"), axis=0, tiled=True),
        lax.all_gather(w_key, ("narrow", "wide"), axis=0, tiled=True),
        lax.all_gather(w_value, ("narrow", "wide"), axis=0, tiled=True),
        lax.all_gather(w_output, ("narrow", "wide"), axis=0, tiled=True),
        lax.all_gather(moe_gain, ("narrow", "wide"), axis=0, tiled=True),
        lax.all_gather(w_router, ("narrow", "wide"), axis=0, tiled=True),
    )
    gate_up_w, down_w = (
        lax.all_gather(w_gate_up, "narrow", axis=1, tiled=True),
        lax.all_gather(w_down, "narrow", axis=1, tiled=True),
    )
    segs_all = lax.all_gather(seg_ids, "wide", axis=1, tiled=True)
    seq_len = segs_all.shape[1]
    key_step = math.gcd(seq_len, 512)
    place_local = lax.axis_index("wide") * span_len + jnp.arange(span_len, dtype=jnp.int32)
    place_query = place_local[None, :]
    starts = jnp.sum((segs_all[:, None, :] < seg_ids[:, :, None]).astype(jnp.int32), axis=-1)
    positions = (place_query - starts).astype(jnp.float32)
    angles = lane_angles(positions, HEAD_DIM)
    cos_table = jnp.cos(angles)
    sin_table = jnp.sin(angles)
    turner = lane_turn(HEAD_DIM)
    inputs = hidden_in.astype(jnp.float32)
    scale_one = rms_scale(inputs)
    gain_one_f = gain_one.astype(jnp.float32)
    normed_one = (inputs * scale_one * gain_one_f).astype(jnp.bfloat16)
    query_pre = jnp.dot(normed_one, query_w, preferred_element_type=jnp.float32)
    key_pre = jnp.dot(normed_one, key_w, preferred_element_type=jnp.float32)
    value_pre = jnp.dot(normed_one, value_w, preferred_element_type=jnp.float32)
    queries = rotate(query_pre, cos_table, sin_table, turner).astype(jnp.bfloat16)
    keys_local = rotate(key_pre, cos_table, sin_table, turner).astype(jnp.bfloat16)
    values_local = value_pre.astype(jnp.bfloat16)
    key_all, value_all = (
        lax.all_gather(keys_local, "wide", axis=1, tiled=True),
        lax.all_gather(values_local, "wide", axis=1, tiled=True),
    )
    query_five = queries.reshape(row_count, span_len, KV_HEADS, 2, HEAD_DIM)

    def key_slices(key_start, length):
        key_block = lax.dynamic_slice_in_dim(key_all, key_start, length, 1).reshape(
            row_count, length, KV_HEADS, HEAD_DIM
        )
        value_block = lax.dynamic_slice_in_dim(value_all, key_start, length, 1).reshape(
            row_count, length, KV_HEADS, HEAD_DIM
        )
        seg_key = lax.dynamic_slice_in_dim(segs_all, key_start, length, 1)
        place_key = (key_start + jnp.arange(length, dtype=jnp.int32))[None, :]
        return (key_block, value_block, seg_key, place_key)

    def scores_at(key_start, length):
        key_block, value_block, seg_key, place_key = key_slices(key_start, length)
        scores = masked_scores(
            query_five, key_block, seg_ids, seg_key, place_query, place_key, factor
        )
        return (scores, key_block, value_block)

    key_starts = jnp.arange(seq_len // key_step, dtype=jnp.int32) * key_step
    stat_shape = (row_count, KV_HEADS, 2, span_len)
    five_shape = (row_count, span_len, KV_HEADS, 2, HEAD_DIM)

    def top_step(state_now, key_start):
        row_top, row_total = state_now
        scores, unused_key, unused_value = scores_at(key_start, key_step)
        new_top = jnp.maximum(row_top, jnp.max(scores, axis=-1))
        row_total = row_total * jnp.exp(row_top - new_top) + jnp.sum(
            jnp.exp(scores - new_top[..., None]), axis=-1
        )
        return ((new_top, row_total), None)

    (row_top, row_total), unused = lax.scan(
        top_step,
        (jnp.full(stat_shape, MASKED, jnp.float32), jnp.zeros(stat_shape, jnp.float32)),
        key_starts,
    )
    log_total = row_top + jnp.log(row_total)

    def out_step(summed, key_start):
        scores, unused_key, value_block = scores_at(key_start, key_step)
        weights = jnp.exp(scores - log_total[..., None]).astype(jnp.bfloat16)
        return (
            summed
            + jnp.einsum(
                "agjbk,akgd->abgjd", weights, value_block, preferred_element_type=jnp.float32
            ),
            None,
        )

    attended, unused = lax.scan(out_step, jnp.zeros(five_shape, jnp.float32), key_starts)
    attended = attended.reshape(row_count, span_len, -1).astype(jnp.bfloat16)
    middle = inputs + jnp.dot(attended, output_w, preferred_element_type=jnp.float32)
    scale_two = rms_scale(middle)
    gain_two_f = gain_two.astype(jnp.float32)
    normed_two = (middle * scale_two * gain_two_f).astype(jnp.bfloat16)
    flat_two = normed_two.reshape(tok_count, feat_dim)
    logits = jnp.dot(flat_two, router_w, preferred_element_type=jnp.float32)
    expert_table = expert_ids.reshape(tok_count, TOP)
    choose = expert_table[:, :, None] == jnp.arange(EXPERTS, dtype=jnp.int32)[None, None, :]
    chosen = jnp.sum(jnp.where(choose, logits[:, None, :], 0.0), axis=-1)
    gate_vals = jax.nn.softmax(chosen, axis=-1)
    token_hot = jnp.sum(choose.astype(jnp.int32), axis=1)
    expert_load = lax.psum(jnp.sum(token_hot, axis=0), ("narrow", "wide"))
    earlier = jnp.cumsum(token_hot, axis=0) - token_hot
    places = jnp.sum(jnp.where(choose, earlier[:, None, :], 0), axis=-1)
    pair_count = tok_count * TOP
    target = jnp.where(places < CAP, expert_table * CAP + places, EXPERTS * CAP).reshape(-1)
    pair_of_slot = (
        jnp.full((EXPERTS * CAP,), pair_count, jnp.int32)
        .at[target]
        .set(jnp.arange(pair_count, dtype=jnp.int32), mode="drop")
    )
    token_of_slot = pair_of_slot // TOP
    outgoing = jnp.take(flat_two, token_of_slot, axis=0, mode="fill", fill_value=0).reshape(
        EXPERTS, CAP, feat_dim
    )
    received = lax.all_to_all(outgoing, "wide", split_axis=0, concat_axis=1, tiled=True)
    gate_up = jnp.einsum("ecd,edf->ecf", received, gate_up_w, preferred_element_type=jnp.float32)
    gate_half = gate_up[..., :FF]
    up_half = gate_up[..., FF:]
    sigmoid_gate = jax.nn.sigmoid(gate_half)
    activated = gate_half * sigmoid_gate
    hidden_b = (activated * up_half).astype(jnp.bfloat16)
    expert_out = jnp.einsum(
        "ecf,efd->ecd", hidden_b, down_w, preferred_element_type=jnp.float32
    ).astype(jnp.bfloat16)
    returned = lax.all_to_all(expert_out, "wide", split_axis=1, concat_axis=0, tiled=True)
    per_pair = (
        jnp.take(
            returned.reshape(EXPERTS * CAP, feat_dim), target, axis=0, mode="fill", fill_value=0
        )
        .reshape(tok_count, TOP, feat_dim)
        .astype(jnp.float32)
    )
    mixture = jnp.sum(gate_vals[:, :, None] * per_pair, axis=1)
    middle_flat = middle.reshape(tok_count, feat_dim)
    block_out = (middle_flat + mixture).reshape(row_count, span_len, feat_dim).astype(jnp.bfloat16)
    grad_out = out_grad.reshape(tok_count, feat_dim).astype(jnp.float32)
    gate_grad = jnp.sum(grad_out[:, None, :] * per_pair, axis=-1)
    gate_of_slot = jnp.take(gate_vals.reshape(-1), pair_of_slot, mode="fill", fill_value=0.0)
    slot_grad = (
        (
            jnp.take(grad_out, token_of_slot, axis=0, mode="fill", fill_value=0.0)
            * gate_of_slot[:, None]
        )
        .astype(jnp.bfloat16)
        .reshape(EXPERTS, CAP, feat_dim)
    )
    grad_received = lax.all_to_all(slot_grad, "wide", split_axis=0, concat_axis=1, tiled=True)
    down_grad = jnp.einsum(
        "ecf,ecd->efd", hidden_b, grad_received, preferred_element_type=jnp.float32
    )
    hidden_grad = jnp.einsum(
        "ecd,efd->ecf", grad_received, down_w, preferred_element_type=jnp.float32
    )
    gate_half_grad = (
        hidden_grad * up_half * (sigmoid_gate * (1.0 + gate_half * (1.0 - sigmoid_gate)))
    )
    up_half_grad = hidden_grad * activated
    gate_up_grad = jnp.concatenate([gate_half_grad, up_half_grad], axis=-1).astype(jnp.bfloat16)
    gate_up_wgrad = jnp.einsum(
        "ecd,ecf->edf", received, gate_up_grad, preferred_element_type=jnp.float32
    )
    slot_input_grad = jnp.einsum(
        "ecf,edf->ecd", gate_up_grad, gate_up_w, preferred_element_type=jnp.float32
    ).astype(jnp.bfloat16)
    input_back = lax.all_to_all(slot_input_grad, "wide", split_axis=1, concat_axis=0, tiled=True)
    pair_input_grad = jnp.take(
        input_back.reshape(EXPERTS * CAP, feat_dim), target, axis=0, mode="fill", fill_value=0
    ).reshape(tok_count, TOP, feat_dim)
    gate_mean = jnp.sum(gate_vals * gate_grad, axis=-1, keepdims=True)
    chosen_grad = gate_vals * (gate_grad - gate_mean)
    logit_grad = jnp.sum(jnp.where(choose, chosen_grad[:, :, None], 0.0), axis=1).astype(
        jnp.bfloat16
    )
    router_wgrad = jnp.einsum("td,te->de", flat_two, logit_grad, preferred_element_type=jnp.float32)
    normed_two_grad = jnp.sum(pair_input_grad.astype(jnp.float32), axis=1) + jnp.einsum(
        "te,de->td", logit_grad, router_w, preferred_element_type=jnp.float32
    )
    middle_part, gain_two_grad = norm_back(
        middle_flat, scale_two.reshape(tok_count, 1), gain_two_f, normed_two_grad
    )
    middle_grad = grad_out + middle_part
    attn_grad = middle_grad.astype(jnp.bfloat16)
    output_wgrad = jnp.einsum(
        "te,td->ed", attended.reshape(tok_count, -1), attn_grad, preferred_element_type=jnp.float32
    )
    attended_grad = jnp.einsum(
        "td,ed->te", attn_grad, output_w, preferred_element_type=jnp.float32
    ).astype(jnp.bfloat16)
    grad_five = attended_grad.reshape(five_shape)

    def sum_step(summed, key_start):
        scores, unused_key, value_block = scores_at(key_start, key_step)
        weights = jnp.exp(scores - log_total[..., None])
        weight_grad = jnp.einsum(
            "abgjd,akgd->agjbk", grad_five, value_block, preferred_element_type=jnp.float32
        )
        return (summed + jnp.sum(weights * weight_grad, axis=-1), None)

    row_dot, unused = lax.scan(sum_step, jnp.zeros(stat_shape, jnp.float32), key_starts)

    def query_step(summed, key_start):
        scores, key_block, value_block = scores_at(key_start, key_step)
        weights = jnp.exp(scores - log_total[..., None])
        weight_grad = jnp.einsum(
            "abgjd,akgd->agjbk", grad_five, value_block, preferred_element_type=jnp.float32
        )
        score_grad = (weights * (weight_grad - row_dot[..., None])).astype(jnp.bfloat16)
        return (
            summed
            + jnp.einsum(
                "agjbk,akgd->abgjd", score_grad, key_block, preferred_element_type=jnp.float32
            ),
            None,
        )

    query_grad, unused = lax.scan(query_step, jnp.zeros(five_shape, jnp.float32), key_starts)
    query_grad = query_grad.reshape(row_count, span_len, -1) * factor
    term_count = span_len * lax.axis_size("wide")
    sub_len = math.gcd(term_count, 512)

    def key_piece(sub_no):
        key_start = sub_no * sub_len
        key_block, value_block, seg_key, place_key = key_slices(key_start, sub_len)
        scores = masked_scores(
            query_five, key_block, seg_ids, seg_key, place_query, place_key, factor
        )
        weights = jnp.exp(scores - log_total[..., None])
        weight_grad = jnp.einsum(
            "abgjd,akgd->agjbk", grad_five, value_block, preferred_element_type=jnp.float32
        )
        score_grad = (weights * (weight_grad - row_dot[..., None])).astype(jnp.bfloat16)
        key_part = (
            jnp.einsum(
                "agjbk,abgjd->kagd", score_grad, query_five, preferred_element_type=jnp.float32
            )
            * factor
        )
        value_part = jnp.einsum(
            "agjbk,abgjd->kagd",
            weights.astype(jnp.bfloat16),
            grad_five,
            preferred_element_type=jnp.float32,
        )
        return jnp.concatenate(
            [
                key_part.reshape(sub_len, row_count, kv_width),
                value_part.reshape(sub_len, row_count, kv_width),
            ],
            axis=-1,
        )

    pieces = lax.map(key_piece, jnp.arange(term_count // sub_len, dtype=jnp.int32))
    summed_terms = lax.psum_scatter(
        pieces.reshape(term_count, row_count, 2 * kv_width).astype(jnp.bfloat16),
        "wide",
        scatter_dimension=0,
        tiled=True,
    ).astype(jnp.float32)
    key_grad = jnp.transpose(summed_terms[:, :, :kv_width], (1, 0, 2))
    value_grad = jnp.transpose(summed_terms[:, :, kv_width:], (1, 0, 2))
    query_back = (
        rotate_back(query_grad, cos_table, sin_table, turner)
        .astype(jnp.bfloat16)
        .reshape(tok_count, -1)
    )
    key_back = (
        rotate_back(key_grad, cos_table, sin_table, turner)
        .astype(jnp.bfloat16)
        .reshape(tok_count, -1)
    )
    value_back = value_grad.astype(jnp.bfloat16).reshape(tok_count, -1)
    flat_one = normed_one.reshape(tok_count, feat_dim)
    query_wgrad = jnp.einsum("td,te->de", flat_one, query_back, preferred_element_type=jnp.float32)
    key_wgrad = jnp.einsum("td,te->de", flat_one, key_back, preferred_element_type=jnp.float32)
    value_wgrad = jnp.einsum("td,te->de", flat_one, value_back, preferred_element_type=jnp.float32)
    normed_one_grad = (
        jnp.einsum("te,de->td", query_back, query_w, preferred_element_type=jnp.float32)
        + jnp.einsum("te,de->td", key_back, key_w, preferred_element_type=jnp.float32)
        + jnp.einsum("te,de->td", value_back, value_w, preferred_element_type=jnp.float32)
    )
    input_part, gain_one_grad = norm_back(
        inputs.reshape(tok_count, feat_dim),
        scale_one.reshape(tok_count, 1),
        gain_one_f,
        normed_one_grad,
    )
    input_grad = (
        (middle_grad + input_part).reshape(row_count, span_len, feat_dim).astype(jnp.bfloat16)
    )
    gain_one_sum, query_sum, key_wsum, value_wsum, output_sum, gain_two_sum, router_sum = (
        lax.psum_scatter(gain_one_grad, ("narrow", "wide"), scatter_dimension=0, tiled=True),
        lax.psum_scatter(query_wgrad, ("narrow", "wide"), scatter_dimension=0, tiled=True),
        lax.psum_scatter(key_wgrad, ("narrow", "wide"), scatter_dimension=0, tiled=True),
        lax.psum_scatter(value_wgrad, ("narrow", "wide"), scatter_dimension=0, tiled=True),
        lax.psum_scatter(output_wgrad, ("narrow", "wide"), scatter_dimension=0, tiled=True),
        lax.psum_scatter(gain_two_grad, ("narrow", "wide"), scatter_dimension=0, tiled=True),
        lax.psum_scatter(router_wgrad, ("narrow", "wide"), scatter_dimension=0, tiled=True),
    )
    gate_up_sum, down_sum = (
        lax.psum_scatter(
            gate_up_wgrad.astype(jnp.bfloat16), "narrow", scatter_dimension=1, tiled=True
        ).astype(jnp.float32),
        lax.psum_scatter(
            down_grad.astype(jnp.bfloat16), "narrow", scatter_dimension=1, tiled=True
        ).astype(jnp.float32),
    )
    return (
        block_out,
        input_grad,
        gain_one_sum,
        query_sum,
        key_wsum,
        value_wsum,
        output_sum,
        gain_two_sum,
        router_sum,
        gate_up_sum,
        down_sum,
        expert_load,
    )


MESH = pl.DeviceIdType.MESH
F32 = jnp.float32
BF16 = jnp.bfloat16
IN_HBM = pl.BlockSpec(memory_space=pl.ANY)
IN_VMEM = pl.BlockSpec(memory_space=pltpu.VMEM)
VMEM_BYTES = 60 * 1024 * 1024
NARROW = 4
WIDE = 8
GROUP = 16
TOKENS = 256
SPAN = 128
WIDTH = 1024
SEQ = 1024
SLOTS = 80
MINE = 2
EARLY = 160
MIDDLE = 96
CHUNK = 4
NT = (((1,), (1,)), ((), ()))
TN = (((0,), (0,)), ((), ()))


def duration(us):
    return pl.CostEstimate(flops=us * 1000000000, bytes_accessed=us * 3600000, transcendentals=0)


def mm(left, right, dims=(((1,), (0,)), ((), ()))):
    return lax.dot_general(left, right, dims, preferred_element_type=F32)


class Spot:
    def __init__(self):
        self.n = lax.axis_index("narrow")
        self.w = lax.axis_index("wide")
        self.core = lax.rem(self.w, 2)
        self.x = lax.rem(lax.div(self.w, 2), 2)
        self.y = lax.div(self.w, 4)
        self.half = lax.rem(self.n, 2)
        self.me = self.n * WIDE + self.w
        self.sib = self.w + 1 - 2 * self.core
        self.xn = self.w + 2 - 4 * self.x
        self.yn = self.w + 4 - 8 * self.y
        self.diag = self.xn + 4 - 8 * self.y
        self.mate = self.n + 1 - 2 * self.half
        self.slot = self.half * WIDE + self.w

    def wide(self, to):
        return (self.n, to)

    def greet(self, count):
        barrier = pltpu.get_barrier_semaphore()
        base = self.n - self.half

        def signal(step, carry):
            if count == WIDE:
                to = (self.n, lax.rem(self.w + step, WIDE))
            elif count == GROUP:
                other = lax.rem(self.slot + step, GROUP)
                to = (base + lax.div(other, WIDE), lax.rem(other, WIDE))
            else:
                other = lax.rem(self.me + step, NARROW * WIDE)
                to = (lax.div(other, WIDE), lax.rem(other, WIDE))
            pl.semaphore_signal(barrier, inc=1, device_id=to, device_id_type=MESH)
            return carry

        lax.fori_loop(1, count, signal, 0)
        pl.semaphore_wait(barrier, count - 1)


def remote(src, dst, send_sem, recv_sem, to):
    return pltpu.make_async_remote_copy(
        src_ref=src, dst_ref=dst, send_sem=send_sem, recv_sem=recv_sem, device_id=to, device_id_type=MESH
    )


def halves(ref, which):
    return ref.at[pl.ds(which * SPAN, SPAN)]


class PlaneGather:
    COPIES = 11

    def __init__(self, spot, source, place, send, recv):
        self.spot, self.source, self.place = spot, source, place
        self.send, self.recv = send, recv
        self.started = []

    def put(self, src, dst, number, to):
        copy = remote(src, dst, self.send.at[number], self.recv.at[number], self.spot.wide(to))
        copy.start()
        self.started.append(copy)

    def pass_on(self, who, half, number, to):
        place = self.place(who, half)
        self.put(place, place, number, to)

    def got(self, who, half, number):
        dst = self.place(who, half)
        remote(dst, dst, self.send.at[number], self.recv.at[number], self.spot.wide(self.spot.sib)).wait_recv()

    def begin(self):
        s = self.spot
        self.put(self.source(0), self.place(s.w, 0), 0, s.xn)
        self.put(self.source(1), self.place(s.w, 1), 2, s.yn)
        self.put(self.source(1), self.place(s.w, 1), 1, s.xn)
        self.put(self.source(0), self.place(s.w, 0), 3, s.yn)
        self.put(self.source(None), self.place(s.w, None), 4, s.sib)

    def middle(self):
        s = self.spot
        self.got(s.xn, 0, 0)
        self.pass_on(s.xn, 0, 5, s.yn)
        self.got(s.yn, 1, 2)
        self.pass_on(s.yn, 1, 6, s.xn)

    def late(self):
        s = self.spot
        self.got(s.xn, 1, 1)
        self.pass_on(s.xn, None, 7, s.sib)
        self.got(s.yn, 0, 3)
        self.pass_on(s.yn, None, 8, s.sib)

    def last(self):
        s = self.spot
        self.got(s.diag, 0, 5)
        self.pass_on(s.diag, 0, 9, s.sib)
        self.got(s.diag, 1, 6)
        self.pass_on(s.diag, 1, 10, s.sib)

    def finish(self):
        s = self.spot
        sib_x = s.sib + 2 - 4 * s.x
        sib_y = s.sib + 4 - 8 * s.y
        sib_d = sib_x + 4 - 8 * s.y
        self.got(s.sib, None, 4)
        self.got(sib_x, None, 7)
        self.got(sib_y, None, 8)
        self.got(sib_d, 0, 9)
        self.got(sib_d, 1, 10)
        for copy in self.started:
            copy.wait_send()


def gather_tokens(spot, own, out, base, send, recv):
    def part(ref, half):
        return ref if half is None else ref.at[pl.ds(half * SPAN, SPAN)]

    return PlaneGather(
        spot, lambda half: part(own, half), lambda who, half: part(out.at[base + who], half), send, recv
    )


def gather_kernel(
    x_ref, dy_ref, seg_in, q_ref, k_ref, v_ref, o_ref, router_ref, gain_one_ref, gain_two_ref, gu_ref,
    x_all, w_all, g_all, seg_all, wo_block, dy_pair, far_gu, w_ref,
    g_ref, seg_ref, wo_ref, send, recv, local, ws, wr, gs, gr, ss, sr, zs, zr, ds, dr, es, er,
):
    spot = Spot()
    for head in range(WIDE):
        at = 256 * head
        w_ref[:, at : at + 128] = q_ref[:, 128 * head : 128 * head + 128]
        w_ref[:, at + 128 : at + 256] = jnp.concatenate(
            [k_ref[:, 64 * head : 64 * head + 64], v_ref[:, 64 * head : 64 * head + 64]], axis=1
        )
    wo_ref[:, 0:WIDTH] = o_ref[...]
    wo_ref[:, WIDTH : WIDTH + 128] = jnp.concatenate([router_ref[...], jnp.zeros((32, 96), BF16)], axis=1)
    g_ref[...] = jnp.zeros_like(g_ref)
    g_ref[0:1, 0:32] = gain_one_ref[...].astype(F32)
    g_ref[1:2, 0:32] = gain_two_ref[...].astype(F32)
    seg_ref[...] = jnp.zeros_like(seg_ref)
    seg_ref[0:2, :] = seg_in[...]
    spot.greet(NARROW * WIDE)
    own = [
        pltpu.make_async_copy(x_ref, x_all.at[spot.w], local.at[0]),
        pltpu.make_async_copy(w_ref.at[:, pl.ds(pl.multiple_of(spot.w * 256, 256), 256)], w_all.at[spot.me], local.at[1]),
        pltpu.make_async_copy(g_ref, g_all.at[spot.me], local.at[2]),
        pltpu.make_async_copy(seg_ref, seg_all.at[spot.w], local.at[3]),
        pltpu.make_async_copy(wo_ref, wo_block.at[spot.n], local.at[4]),
        pltpu.make_async_copy(dy_ref, dy_pair.at[spot.half], local.at[5]),
    ]
    gather = gather_tokens(spot, x_ref, x_all, 0, send, recv)

    def others(step):
        other = lax.rem(spot.me + step, NARROW * WIDE)
        return other, lax.div(other, WIDE), lax.rem(other, WIDE)

    def weights(step, arriving):
        other, o_n, o_w = others(step)
        source = w_ref.at[:, pl.ds(pl.multiple_of(o_w * 256, 256), 256)]
        place = other if arriving else spot.me
        return (
            remote(source, w_all.at[place], ws.at[other], wr.at[place], (o_n, o_w)),
            remote(g_ref, g_all.at[place], gs.at[other], gr.at[place], (o_n, o_w)),
        )

    def documents(step, arriving):
        other = lax.rem(spot.w + step, WIDE)
        place = other if arriving else spot.w
        return remote(seg_ref, seg_all.at[place], ss.at[other], sr.at[place], spot.wide(other))

    def column(step, arriving):
        other = lax.rem(spot.n + step, NARROW)
        place = other if arriving else spot.n
        return remote(wo_ref, wo_block.at[place], zs.at[other], zr.at[place], (other, spot.w))

    def start(step, carry):
        for copy in weights(step, False):
            copy.start()
        return carry

    def start_column(step, carry):
        column(step, False).start()
        return carry

    def start_documents(step, carry):
        documents(step, False).start()
        return carry

    lax.fori_loop(1, WIDE, start_documents, 0)
    lax.fori_loop(1, NARROW * WIDE, start, 0)
    gather.begin()
    lax.fori_loop(1, NARROW, start_column, 0)
    for copy in own:
        copy.start()
    across = remote(dy_ref, dy_pair.at[spot.half], ds.at[0], dr.at[0], (spot.mate, spot.w))
    across.start()
    far = remote(
        gu_ref.at[2 * spot.half, pl.ds(0, EARLY)], far_gu, es.at[0], er.at[0],
        (spot.n + 2 - 4 * lax.div(spot.n, 2), spot.w),
    )
    far.start()
    gather.middle()
    gather.late()
    gather.last()

    def wait(step, carry):
        for copy in weights(step, False):
            copy.wait_send()
        for copy in weights(step, True):
            copy.wait_recv()
        return carry

    def wait_column(step, carry):
        column(step, False).wait_send()
        column(step, True).wait_recv()
        return carry

    def wait_documents(step, carry):
        documents(step, False).wait_send()
        documents(step, True).wait_recv()
        return carry

    lax.fori_loop(1, WIDE, wait_documents, 0)
    lax.fori_loop(1, NARROW * WIDE, wait, 0)
    lax.fori_loop(1, NARROW, wait_column, 0)
    gather.finish()
    across.wait_send()
    arrived = dy_pair.at[1 - spot.half]
    remote(arrived, arrived, ds.at[0], dr.at[0], (spot.mate, spot.w)).wait_recv()
    for copy in own:
        copy.wait()
    far.wait_send()
    far.wait_recv()


def gather_call(*operands):
    dma = pltpu.SemaphoreType.DMA
    return pl.pallas_call(
        gather_kernel,
        name="gather_inputs",
        out_shape=(
            jax.ShapeDtypeStruct((WIDE, TOKENS, WIDTH), BF16),
            jax.ShapeDtypeStruct((NARROW * WIDE, 32, 256), BF16),
            jax.ShapeDtypeStruct((NARROW * WIDE, 8, 128), F32),
            jax.ShapeDtypeStruct((WIDE, 8, 128), jnp.int32),
            jax.ShapeDtypeStruct((NARROW, 32, WIDTH + 128), BF16),
            jax.ShapeDtypeStruct((2, TOKENS, WIDTH), BF16),
            jax.ShapeDtypeStruct((EARLY, WIDTH), BF16),
            jax.ShapeDtypeStruct((32, 2 * WIDTH), BF16),
        ),
        in_specs=[IN_VMEM] * 10 + [IN_HBM],
        out_specs=(IN_HBM,) * 7 + (IN_VMEM,),
        scratch_shapes=[
            pltpu.VMEM((8, 128), F32),
            pltpu.VMEM((8, 128), jnp.int32),
            pltpu.VMEM((32, WIDTH + 128), BF16),
            dma((PlaneGather.COPIES,)),
            dma((PlaneGather.COPIES,)),
            dma((6,)),
            dma((NARROW * WIDE,)),
            dma((NARROW * WIDE,)),
            dma((NARROW * WIDE,)),
            dma((NARROW * WIDE,)),
            dma((WIDE,)),
            dma((WIDE,)),
            dma((NARROW,)),
            dma((NARROW,)),
            dma((1,)),
            dma((1,)),
            dma((1,)),
            dma((1,)),
        ],
        compiler_params=pltpu.CompilerParams(collective_id=1, has_side_effects=True),
        cost_estimate=duration(1),
    )(*operands)


def lane_half():
    lanes = lax.broadcasted_iota(jnp.int32, (1, 128), 1)
    return lax.rem(lanes, 64) < 32


def turn(values, first_half):
    return jnp.where(first_half, -pltpu.roll(values, 96, 1), pltpu.roll(values, 32, 1))


def turn_back(values, first_half):
    return jnp.where(first_half, pltpu.roll(values, 96, 1), -pltpu.roll(values, 32, 1))


def gather_gain(gains):
    lane = lax.broadcasted_iota(jnp.int32, (128, WIDTH), 0)
    column = lax.broadcasted_iota(jnp.int32, (128, WIDTH), 1)
    spread = (lax.rem(column, 32) == lane).astype(BF16)
    tiled = mm(gains.astype(BF16), spread)
    owner = lax.broadcasted_iota(jnp.int32, (32, WIDTH), 0)
    place = lax.broadcasted_iota(jnp.int32, (32, WIDTH), 1)
    return jnp.sum(jnp.where(lax.div(place, 32) == owner, tiled, 0.0), axis=0, keepdims=True)


class Attention:
    def __init__(self, x_ref, w_ref, seg_ref, cos_ref, sin_ref, freq_ref, gain_one, h1_ref, qkv_ref, lse_ref, o_ref, angle_ref):
        self.x_ref, self.seg_ref, self.cos_ref, self.sin_ref = x_ref, seg_ref, cos_ref, sin_ref
        self.h1_ref, self.qkv_ref, self.lse_ref, self.o_ref = h1_ref, qkv_ref, lse_ref, o_ref
        self.angle_ref = angle_ref
        self.gain_one = gain_one
        self.w_ref = w_ref
        self.first_half = lane_half()
        self.is_key = lax.broadcasted_iota(jnp.int32, (1, 128), 1) < 64
        self.starts, self.start_cos, self.start_sin = [], [], []
        for row in range(2):
            segs = [seg_ref[c, row : row + 1, :] for c in range(WIDE)]
            starts = [jnp.zeros((1, 1), F32)]
            for doc in range(5):
                total = jnp.zeros((1, 128), F32)
                for seg in segs:
                    total = total + jnp.where(seg == doc, 1.0, 0.0)
                starts.append(starts[-1] + jnp.sum(total, axis=1, keepdims=True))
            angle = jnp.concatenate(starts + starts[:2], axis=0) * freq_ref[0:1, :]
            self.starts.append(starts)
            self.start_cos.append(jnp.cos(angle))
            self.start_sin.append(jnp.sin(angle))

    def chunk(self, row, i):
        tokens = pl.ds(i * 256, 256)
        starts, start_cos, start_sin = self.starts[row], self.start_cos[row], self.start_sin[row]
        seg_cols = []
        for part in range(2):
            seg = self.seg_ref[2 * i + part, row : row + 1, :].astype(F32)
            seg_cols.append(jnp.transpose(jnp.broadcast_to(seg, (128, 128))))
        seg_col = jnp.concatenate(seg_cols, axis=0)
        start_col = jnp.zeros((256, 128), F32)
        cos_s = jnp.broadcast_to(start_cos[0:1], (256, 128))
        sin_s = jnp.broadcast_to(start_sin[0:1], (256, 128))
        for doc in range(1, 6):
            here = seg_col == float(doc)
            start_col = jnp.where(here, starts[doc], start_col)
            cos_s = jnp.where(here, start_cos[doc : doc + 1], cos_s)
            sin_s = jnp.where(here, start_sin[doc : doc + 1], sin_s)
        cos_t = self.cos_ref[tokens, :]
        sin_t = self.sin_ref[tokens, :]
        cosine = cos_t * cos_s + sin_t * sin_s
        sine = sin_t * cos_s - cos_t * sin_s
        self.angle_ref[row, tokens, 0:128] = cosine
        self.angle_ref[row, tokens, 128:256] = sine
        x = self.x_ref[2 * i : 2 * i + 2, row].reshape(256, WIDTH).astype(F32)
        scale = lax.rsqrt(jnp.mean(x * x, axis=1, keepdims=True) + EPSILON)
        h1 = (x * scale * self.gain_one).astype(BF16)
        self.h1_ref[row, tokens, :] = h1
        qkv = mm(h1, self.w_ref[...].reshape(WIDTH, 256))
        q = qkv[:, 0:128]
        kv = qkv[:, 128:256]
        q = (q * cosine + turn(q, self.first_half) * sine).astype(BF16)
        kv = jnp.where(self.is_key, kv * cosine + turn(kv, self.first_half) * sine, kv).astype(BF16)
        self.qkv_ref[row, tokens, 0:128] = q
        self.qkv_ref[row, tokens, 128:256] = kv
        length = 256 * (i + 1)
        keys = self.qkv_ref[row, 0:length, 128:192]
        values = self.qkv_ref[row, 0:length, 192:256]
        place_key = lax.broadcasted_iota(jnp.int32, (256, length), 1).astype(F32)
        place_query = (lax.broadcasted_iota(jnp.int32, (256, length), 0) + 256 * i).astype(F32)
        allowed = (place_key <= place_query) & (place_key >= start_col[:, 0:1])
        outs, logs = [], []
        for head in range(2):
            query = q[:, 64 * head : 64 * head + 64]
            scores = jnp.where(allowed, mm(query, keys, NT) * (HEAD_DIM**-0.5), MASKED)
            top = jnp.max(scores, axis=1, keepdims=True)
            log_total = top + jnp.log(jnp.sum(jnp.exp(scores - top), axis=1, keepdims=True))
            outs.append(mm(jnp.exp(scores - log_total).astype(BF16), values))
            logs.append(log_total)
        self.o_ref[row, tokens, :] = jnp.concatenate(outs, axis=1).astype(BF16)
        self.lse_ref[row, tokens, :] = jnp.where(
            self.is_key, jnp.where(self.first_half, logs[0], start_col), logs[1]
        )


def piece_copies(spot, gu_ref, down_ref, e, kind, target, send, recv, number, first=0, last=384):
    pair = lax.div(spot.n, 2)
    plane = spot.n if kind == 2 else spot.mate
    if kind >= 2:
        plane = plane + 2 - 4 * pair
    half = spot.half if kind == 2 else 1 - spot.half
    to = (plane, spot.w)
    copies = []
    for part, (ref, start, rows) in enumerate(((gu_ref, 0, 256), (down_ref, 256, 128))):
        low, high = max(first, start), min(last, start + rows)
        if low < high:
            copies.append(
                remote(
                    ref.at[2 * half + e, pl.ds(low - start, high - low)], target.at[pl.ds(low - first, high - low)],
                    send.at[number + part], recv.at[number + part], to,
                )
            )
    return copies


def start_all(copies):
    for copy in copies:
        copy.start()


def forward_kernel(
    x_ref, w_ref, g_ref, seg_ref, cos_ref, sin_ref, freq_ref, wo_ref, ids_ref, dy_ref, gu_ref, down_ref,
    h1_out, qkv_ref, lse_ref, o_ref, angle_ref, gain_ref, mid_ref, gate_ref, w_all,
    h2_all, dy_all, table_all, mate_0, far_rest_0, far_mate_0, mate_1, far_1, far_mate_early_1,
    h1_ref, o_full, h2_own, table_own,
    os, orv, w_send, w_recv, a_send, a_recv, b_send, b_recv, s0, r0, s1, r1, ts, tr, zs, zr, es, er, local,
):
    spot = Spot()
    spot.greet(NARROW * WIDE)
    mate_base = (1 - spot.half) * WIDE
    own_base = spot.half * WIDE
    mate_slot = mate_base + spot.w

    def w_source(half):
        return wo_ref if half is None else wo_ref.at[pl.ds(2 * half, 2)]

    def w_place(who, half):
        return w_all.at[:, who] if half is None else w_all.at[pl.ds(2 * half, 2), who]

    w_gather = PlaneGather(spot, w_source, w_place, w_send, w_recv)
    dy_gather = gather_tokens(spot, dy_ref.at[spot.half], dy_all, own_base, a_send, a_recv)
    mate_dy_gather = gather_tokens(spot, dy_ref.at[1 - spot.half], dy_all, mate_base, b_send, b_recv)
    w_gather.begin()
    dy_gather.begin()
    first_expert = piece_copies(spot, gu_ref, down_ref, 0, 2, far_rest_0, es, er, 0, first=EARLY)
    first_expert += piece_copies(spot, gu_ref, down_ref, 0, 3, far_mate_0, es, er, 2)
    first_expert += piece_copies(spot, gu_ref, down_ref, 0, 1, mate_0, es, er, 4)
    start_all(first_expert)

    keep = [
        pltpu.make_async_copy(wo_ref, w_place(spot.w, None), local.at[0]),
        pltpu.make_async_copy(dy_ref.at[spot.half], dy_all.at[spot.slot], local.at[1]),
        pltpu.make_async_copy(dy_ref.at[1 - spot.half], dy_all.at[mate_slot], local.at[2]),
    ]
    for copy in keep:
        copy.start()

    def heads(to, place):
        return (
            o_ref.at[:, pl.ds(to * SPAN, SPAN), :],
            o_full.at[:, :, pl.ds(pl.multiple_of(place * 128, 128), 128)],
        )

    def each_head_copy(to, act_local, act_remote):
        source, target = heads(to, spot.w)

        @pl.when(spot.w == to)
        def _():
            act_local(pltpu.make_async_copy(source, target, local.at[3]))

        @pl.when(spot.w != to)
        def _():
            act_remote(remote(source, target, os.at[to], orv.at[spot.w], spot.wide(to)))

    expert = lax.broadcasted_iota(jnp.int32, (32, TOKENS), 0).astype(F32)
    named = jnp.zeros((32, TOKENS), F32)
    ids = ids_ref[...].astype(F32)
    ids = jnp.transpose(jnp.concatenate([ids, jnp.zeros((TOKENS, 128 - TOP), F32)], axis=1))
    for k in range(TOP):
        named = jnp.where(expert == ids[k : k + 1, :], 1.0, named)
    before = lax.broadcasted_iota(jnp.int32, (TOKENS, TOKENS), 0) < lax.broadcasted_iota(
        jnp.int32, (TOKENS, TOKENS), 1
    )
    places = mm(named.astype(BF16), jnp.where(before, 1.0, 0.0).astype(BF16))
    kept = jnp.where((named > 0.5) & (places < float(CAP)), places, -1.0)

    gains = g_ref[...]
    gain_one = gather_gain(gains[:, 0, :])
    gain_two = gather_gain(gains[:, 1, :])
    gain_ref[...] = jnp.concatenate([gain_one, gain_two, jnp.zeros((6, WIDTH), F32)], axis=0)
    attention = Attention(
        x_ref, w_ref, seg_ref, cos_ref, sin_ref, freq_ref, gain_one,
        h1_ref, qkv_ref, lse_ref, o_ref, angle_ref,
    )
    between = {1: [w_gather.middle], 2: [w_gather.late, dy_gather.middle], 3: [w_gather.last, dy_gather.late]}
    for i in range(4):
        for row in range(2):
            attention.chunk(row, i)
        for to in (2 * i, 2 * i + 1):
            each_head_copy(to, lambda copy: copy.start(), lambda copy: copy.start())
        for step in between.get(i, []):
            step()
    far = piece_copies(spot, gu_ref, down_ref, 1, 2, far_1, es, er, 6)
    near = piece_copies(spot, gu_ref, down_ref, 1, 1, mate_1, es, er, 8)
    far_mate = piece_copies(spot, gu_ref, down_ref, 1, 3, far_mate_early_1, es, er, 10, last=MIDDLE)
    h1_copy = pltpu.make_async_copy(h1_ref, h1_out, local.at[4])
    h1_copy.start()
    dy_gather.last()
    mate_dy_gather.begin()
    w_gather.finish()
    keep[0].wait()
    for to in range(WIDE):
        each_head_copy(to, lambda copy: copy.wait(), lambda copy: copy.wait_send())

    def wait_heads(step, carry):
        other = lax.rem(spot.w + step, WIDE)
        target = o_full.at[:, :, pl.ds(pl.multiple_of(other * 128, 128), 128)]
        remote(target, target, os.at[0], orv.at[other], spot.wide(other)).wait_recv()
        return carry

    lax.fori_loop(1, WIDE, wait_heads, 0)
    attended = o_full[...].reshape(TOKENS, WIDTH)
    x_own = x_ref[spot.w].reshape(TOKENS, WIDTH).astype(F32)
    mid = x_own + mm(attended, w_all[:, :, :, 0:WIDTH].reshape(WIDTH, WIDTH))
    mid_ref[...] = mid
    scale = lax.rsqrt(jnp.mean(mid * mid, axis=1, keepdims=True) + EPSILON)
    h2 = (mid * scale * gain_two).astype(BF16)
    h2_own[...] = h2
    across = remote(h2_own, h2_all.at[spot.slot], zs.at[0], zr.at[0], (spot.mate, spot.w))
    across.start()
    first = gather_tokens(spot, h2_own, h2_all, own_base, s0, r0)
    first.begin()
    keep_own = pltpu.make_async_copy(h2_own, h2_all.at[spot.slot], local.at[5])
    keep_own.start()

    logits = jnp.transpose(mm(h2, w_all[:, :, :, WIDTH : WIDTH + 128].reshape(WIDTH, 128)))[0:32]
    chosen = jnp.where(named > 0.5, logits, MASKED)
    rise = jnp.where(named > 0.5, jnp.exp(chosen - jnp.max(chosen, axis=0, keepdims=True)), 0.0)
    gate = rise / jnp.sum(rise, axis=0, keepdims=True)
    gate_ref[0:32, :] = gate
    gate_ref[32:64, :] = named
    for owner in range(GROUP):
        table_own[owner, 0:2, :] = kept[2 * owner : 2 * owner + 2]
        table_own[owner, 2:4, :] = gate[2 * owner : 2 * owner + 2]
        table_own[owner, 4:8, :] = jnp.zeros((4, TOKENS), F32)

    def tables(step, arriving):
        other = lax.rem(spot.slot + step, GROUP)
        o_half, o_w = lax.div(other, WIDE), lax.rem(other, WIDE)
        place = other if arriving else spot.slot
        return remote(
            table_own.at[2 * o_w + o_half], table_all.at[place], ts.at[other], tr.at[place],
            (spot.n - spot.half + o_half, o_w),
        )

    def start_table(step, carry):
        tables(step, False).start()
        return carry

    lax.fori_loop(1, GROUP, start_table, 0)
    table_mine = pltpu.make_async_copy(
        table_own.at[2 * spot.w + spot.half], table_all.at[spot.slot], local.at[6]
    )
    table_mine.start()

    mate_dy_gather.middle()
    mate_dy_gather.late()
    start_all(far)
    first.middle()
    mate_dy_gather.last()
    first.late()
    first.last()
    arriving = h2_all.at[mate_slot]
    remote(arriving, arriving, zs.at[0], zr.at[0], (spot.mate, spot.w)).wait_recv()
    second = gather_tokens(spot, arriving, h2_all, mate_base, s1, r1)
    second.begin()
    start_all(far_mate + near)
    second.middle()
    second.late()
    second.last()

    def wait_table(step, carry):
        tables(step, False).wait_send()
        tables(step, True).wait_recv()
        return carry

    lax.fori_loop(1, GROUP, wait_table, 0)
    dy_gather.finish()
    mate_dy_gather.finish()
    first.finish()
    second.finish()
    across.wait_send()
    keep[1].wait()
    keep[2].wait()
    keep_own.wait()
    table_mine.wait()
    h1_copy.wait()
    for copy in first_expert + far + far_mate + near:
        copy.wait_send()
        copy.wait_recv()


def forward_call(x_all, w_all, g_all, seg_all, cos_table, sin_table, freq, wo_block, ids, dy_pair, w_gate_up, w_down):
    dma = pltpu.SemaphoreType.DMA
    copies = PlaneGather.COPIES
    return pl.pallas_call(
        forward_kernel,
        name="forward",
        out_shape=(
            jax.ShapeDtypeStruct((2, SEQ, WIDTH), BF16),
            jax.ShapeDtypeStruct((2, SEQ, 256), BF16),
            jax.ShapeDtypeStruct((2, SEQ, 128), F32),
            jax.ShapeDtypeStruct((2, SEQ, 128), BF16),
            jax.ShapeDtypeStruct((2, SEQ, 256), F32),
            jax.ShapeDtypeStruct((8, WIDTH), F32),
            jax.ShapeDtypeStruct((TOKENS, WIDTH), F32),
            jax.ShapeDtypeStruct((64, TOKENS), F32),
            jax.ShapeDtypeStruct((NARROW, WIDE, 32, WIDTH + 128), BF16),
            jax.ShapeDtypeStruct((GROUP, TOKENS, WIDTH), BF16),
            jax.ShapeDtypeStruct((GROUP, TOKENS, WIDTH), BF16),
            jax.ShapeDtypeStruct((GROUP, 8, TOKENS), F32),
        )
        + tuple(jax.ShapeDtypeStruct((depth, WIDTH), BF16) for depth in (384, 384 - EARLY, 384, 384, 384, MIDDLE)),
        in_specs=[IN_VMEM] * 7 + [IN_HBM, IN_VMEM, IN_VMEM, IN_HBM, IN_HBM],
        out_specs=(IN_HBM,) + (IN_VMEM,) * 8 + (IN_HBM,) * 9,
        scratch_shapes=[
            pltpu.VMEM((2, SEQ, WIDTH), BF16),
            pltpu.VMEM((2, SPAN, WIDTH), BF16),
            pltpu.VMEM((TOKENS, WIDTH), BF16),
            pltpu.VMEM((GROUP, 8, TOKENS), F32),
            dma((WIDE,)),
            dma((WIDE,)),
        ]
        + [dma((copies,))] * 10
        + [dma((GROUP,)), dma((GROUP,)), dma((1,)), dma((1,)), dma((12,)), dma((12,)), dma((7,))],
        compiler_params=pltpu.CompilerParams(collective_id=2, has_side_effects=True, vmem_limit_bytes=VMEM_BYTES),
        cost_estimate=duration(1),
    )(x_all.reshape(WIDE, 2, SPAN, WIDTH), w_all, g_all, seg_all, cos_table, sin_table, freq, wo_block, ids, dy_pair, w_gate_up, w_down)


def load_quarters(own, pieces, w_gu, w_down, sems):
    n = lax.axis_index("narrow")
    half, pair = lax.rem(n, 2), lax.div(n, 2)
    mate = n + 1 - 2 * half
    far = n + 2 - 4 * pair
    far_mate = mate + 2 - 4 * pair
    copies = []
    for quarter, parts in zip((n, mate, far, far_mate), (own,) + pieces):
        first = 0
        for part in parts if isinstance(parts, tuple) else (parts,):
            depth = part.shape[0]
            for start, rows, target in ((0, 256, w_gu), (256, 128, w_down)):
                low, high = max(first, start), min(first + depth, start + rows)
                if low < high:
                    place = quarter * rows + (low - start)
                    copies.append(
                        pltpu.make_async_copy(
                            part.at[pl.ds(low - first, high - low)],
                            target.at[pl.ds(pl.multiple_of(place, 32), high - low)],
                            sems.at[len(copies)],
                        )
                    )
            first += depth
    return copies


def pick(table_ref, source, expert):
    slot = lax.broadcasted_iota(jnp.int32, (SLOTS, TOKENS), 0).astype(F32)
    return slot == table_ref[source, expert : expert + 1, :]


STEPS = GROUP // CHUNK
ROWS = CHUNK * SLOTS


def start_weights(e, gu_ref, down_ref, pieces, w_gu, w_down, gu_sum, down_sum, sems):
    mine = 2 * lax.rem(lax.axis_index("narrow"), 2) + e
    copies = load_quarters((gu_ref.at[mine], down_ref.at[mine]), pieces, w_gu, w_down, sems)
    for copy in copies:
        copy.start()
    gu_sum[...] = jnp.zeros_like(gu_sum)
    down_sum[...] = jnp.zeros_like(down_sum)
    for copy in copies:
        copy.wait()


def slot_gates(table_ref, masks, e):
    return jnp.concatenate(
        [
            jnp.sum(jnp.where(masks[s], table_ref[s, 2 + e : 3 + e, :], 0.0), axis=1, keepdims=True)
            for s in range(CHUNK)
        ],
        axis=0,
    )


def expert_math(rows, grad_rows, gates, w_gu, w_down, gu_sum, down_sum):
    g = mm(rows, w_gu[:, 0:FF])
    u = mm(rows, w_gu[:, FF : 2 * FF])
    sigmoid = 1.0 / (1.0 + jnp.exp(-g))
    active = g * sigmoid
    hidden = (active * u).astype(BF16)
    grad_rows = grad_rows.astype(F32)
    dy_pair = (grad_rows * gates).astype(BF16)
    dhid = mm(dy_pair, w_down[...], NT)
    da_g = (dhid * u * (sigmoid * (1.0 + g * (1.0 - sigmoid)))).astype(BF16)
    da_u = (dhid * active).astype(BF16)
    y = mm(hidden, w_down[...]).astype(BF16).astype(F32)
    slot_dgate = jnp.sum(y * grad_rows, axis=1, keepdims=True)
    down_sum[...] += mm(hidden, dy_pair, TN)
    gu_sum[:, 0:FF] += mm(rows, da_g, TN)
    gu_sum[:, FF : 2 * FF] += mm(rows, da_u, TN)
    dx = (mm(da_g, w_gu[:, 0:FF], NT) + mm(da_u, w_gu[:, FF : 2 * FF], NT)).astype(BF16)
    return (y * gates).astype(BF16), dx, slot_dgate


def token_dgate(dgate_ref, masks, slot_dgate, e):
    for s in range(CHUNK):
        part = slot_dgate[s * SLOTS : (s + 1) * SLOTS]
        dgate_ref[s, e : e + 1, :] = jnp.sum(jnp.where(masks[s], part, 0.0), axis=0, keepdims=True)


def store_quarters(outs, gu_sum, down_sum):
    n = lax.axis_index("narrow")
    half, pair = lax.rem(n, 2), lax.div(n, 2)
    mate = n + 1 - 2 * half
    far = n + 2 - 4 * pair
    far_mate = mate + 2 - 4 * pair
    for out, quarter in zip(outs, (n, mate, far, far_mate)):
        out[0:256, :] = gu_sum[pl.ds(pl.multiple_of(quarter * 256, 256), 256), :].astype(BF16)
        out[256:384, :] = down_sum[pl.ds(pl.multiple_of(quarter * 128, 128), 128), :].astype(BF16)


def expert_0_kernel(
    h2_ref, dy_ref, table_ref, gu_ref, down_ref, w1, w2_early, w2_rest, w3,
    gated_ref, dx_ref, rows_ref, grad_rows_ref, dgate_ref, own, mate, far, far_mate, far_mate_1,
    w_gu, w_down, gu_sum, down_sum, sems, es, er,
):
    step = pl.program_id(0)
    spot = Spot()
    second_expert = piece_copies(spot, gu_ref, down_ref, 1, 3, far_mate_1, es, er, 0, first=MIDDLE)

    @pl.when(step == 0)
    def _():
        barrier = pltpu.get_barrier_semaphore()
        plane = spot.mate + 2 - 4 * lax.div(spot.n, 2)
        pl.semaphore_signal(barrier, inc=1, device_id=(plane, spot.w), device_id_type=MESH)
        pl.semaphore_wait(barrier, 1)
        start_all(second_expert)
        start_weights(0, gu_ref, down_ref, (w1, (w2_early, w2_rest), w3), w_gu, w_down, gu_sum, down_sum, sems)

    masks = [[pick(table_ref, s, e) for s in range(CHUNK)] for e in range(MINE)]
    rows, grad_rows = [], []
    for s in range(CHUNK):
        hot = jnp.concatenate([jnp.where(masks[e][s], 1.0, 0.0) for e in range(MINE)], axis=0).astype(BF16)
        rows.append(mm(hot, h2_ref[s]).astype(BF16))
        grad_rows.append(mm(hot, dy_ref[s]).astype(BF16))
    for s in range(CHUNK):
        rows_ref[0, s * SLOTS : (s + 1) * SLOTS, :] = rows[s][SLOTS:]
        grad_rows_ref[0, s * SLOTS : (s + 1) * SLOTS, :] = grad_rows[s][SLOTS:]
    rows = jnp.concatenate([r[:SLOTS] for r in rows], axis=0)
    grad_rows = jnp.concatenate([r[:SLOTS] for r in grad_rows], axis=0)
    gated, dx, slot_dgate = expert_math(
        rows, grad_rows, slot_gates(table_ref, masks[0], 0), w_gu, w_down, gu_sum, down_sum
    )
    gated_ref[0] = gated
    dx_ref[0] = dx
    dgate_ref[...] = jnp.zeros_like(dgate_ref)
    token_dgate(dgate_ref, masks[0], slot_dgate, 0)

    @pl.when(step == STEPS - 1)
    def _():
        store_quarters((own, mate, far, far_mate), gu_sum, down_sum)
        for copy in second_expert:
            copy.wait_send()
            copy.wait_recv()


def expert_1_kernel(
    rows_ref, grad_rows_ref, gated_before, dx_before, dgate_before, table_ref, gu_ref, down_ref, w1, w2, w3_early, w3_rest,
    y_here, y_there, part_here, part_there, dgate_ref, own, mate, far, far_mate,
    w_gu, w_down, gu_sum, down_sum, sems, held, local, send, recv,
):
    step = pl.program_id(0)
    spot = Spot()
    slot = lax.rem(step, 2)
    outs = ((y_here, y_there), (part_here, part_there))

    def copies(at_step, at_slot):
        result = []
        for kind, (here, there) in enumerate(outs):
            for pair in range(CHUNK // 2):
                block = at_step * (CHUNK // 2) + pair
                source = held.at[kind, at_slot]
                result.append(
                    pltpu.make_async_copy(
                        source.at[2 * pair + spot.core], here.at[block], local.at[kind, at_slot, pair]
                    )
                )
                other = source.at[2 * pair + 1 - spot.core]
                if kind == 0:
                    result.append(pltpu.make_async_copy(other, there.at[block], send.at[kind, at_slot, pair]))
                else:
                    result.append(
                        remote(
                            other, there.at[block], send.at[kind, at_slot, pair], recv.at[block],
                            spot.wide(spot.sib),
                        )
                    )
        return result

    def finish(at_step, at_slot):
        done = copies(at_step, at_slot)
        for number, copy in enumerate(done):
            if number % 2 == 1 and number >= CHUNK:
                copy.wait_send()
            else:
                copy.wait()

    @pl.when(step == 0)
    def _():
        barrier = pltpu.get_barrier_semaphore()
        pl.semaphore_signal(barrier, inc=1, device_id=spot.wide(spot.sib), device_id_type=MESH)
        pl.semaphore_wait(barrier, 1)
        start_weights(1, gu_ref, down_ref, (w1, w2, (w3_early, w3_rest)), w_gu, w_down, gu_sum, down_sum, sems)

    masks = [[pick(table_ref, s, e) for s in range(CHUNK)] for e in range(MINE)]
    gated, dx, slot_dgate = expert_math(
        rows_ref[0], grad_rows_ref[0], slot_gates(table_ref, masks[1], 1), w_gu, w_down, gu_sum, down_sum
    )
    dgate_ref[...] = dgate_before[...]
    token_dgate(dgate_ref, masks[1], slot_dgate, 1)

    @pl.when(step >= 2)
    def _():
        finish(step - 2, slot)

    for s in range(CHUNK):
        at = slice(s * SLOTS, (s + 1) * SLOTS)
        hot = jnp.concatenate([jnp.where(masks[e][s], 1.0, 0.0) for e in range(MINE)], axis=0).astype(BF16)
        held[0, slot, s] = mm(hot, jnp.concatenate([gated_before[0, at, :], gated[at]], axis=0), TN).astype(BF16)
        held[1, slot, s] = mm(hot, jnp.concatenate([dx_before[0, at, :], dx[at]], axis=0), TN).astype(BF16)
    start_all(copies(step, slot))

    @pl.when(step == STEPS - 1)
    def _():
        store_quarters((own, mate, far, far_mate), gu_sum, down_sum)
        for last in (STEPS - 2, STEPS - 1):
            finish(last, last % 2)
        for block in range(WIDE):
            place = part_there.at[block]
            remote(place, place, send.at[0, 0, 0], recv.at[block], spot.wide(spot.sib)).wait_recv()


def expert_specs():
    block = pl.BlockSpec((CHUNK, TOKENS, WIDTH), lambda c: (c, 0, 0))
    small = pl.BlockSpec((CHUNK, 8, TOKENS), lambda c: (c, 0, 0))
    slots = pl.BlockSpec((1, ROWS, WIDTH), lambda c: (c, 0, 0))
    quarter = pl.BlockSpec((384, WIDTH), lambda c: (0, 0))
    return block, small, slots, quarter


def expert_scratch():
    return [
        pltpu.VMEM((WIDTH, 2 * FF), BF16),
        pltpu.VMEM((FF, WIDTH), BF16),
        pltpu.VMEM((WIDTH, 2 * FF), F32),
        pltpu.VMEM((FF, WIDTH), F32),
        pltpu.SemaphoreType.DMA((10,)),
    ]


SLOT_ROWS = jax.ShapeDtypeStruct((STEPS, ROWS, WIDTH), BF16)
CORE_BLOCKS = jax.ShapeDtypeStruct((WIDE, TOKENS, WIDTH), BF16)
TABLES = jax.ShapeDtypeStruct((GROUP, 8, TOKENS), F32)
QUARTER = jax.ShapeDtypeStruct((384, WIDTH), BF16)


def expert_0_call(h2_all, dy_all, table_all, w_gate_up, w_down, pieces):
    block, small, slots, quarter = expert_specs()
    return pl.pallas_call(
        expert_0_kernel,
        name="expert_0",
        grid=(STEPS,),
        out_shape=(SLOT_ROWS,) * 4
        + (TABLES,)
        + (QUARTER,) * 4
        + (jax.ShapeDtypeStruct((384 - MIDDLE, WIDTH), BF16),),
        in_specs=[block, block, small] + [IN_HBM] * 6,
        out_specs=(slots,) * 4 + (small,) + (quarter,) * 4 + (IN_HBM,),
        scratch_shapes=expert_scratch() + [pltpu.SemaphoreType.DMA((2,)), pltpu.SemaphoreType.DMA((2,))],
        compiler_params=pltpu.CompilerParams(collective_id=4, has_side_effects=True, vmem_limit_bytes=VMEM_BYTES),
        cost_estimate=duration(1),
    )(h2_all, dy_all, table_all, w_gate_up, w_down, *pieces)


def expert_1_call(rows, grad_rows, gated, dx, dgate, table_all, w_gate_up, w_down, pieces):
    block, small, slots, quarter = expert_specs()
    return pl.pallas_call(
        expert_1_kernel,
        name="expert_1",
        grid=(STEPS,),
        out_shape=(CORE_BLOCKS,) * 4 + (TABLES,) + (QUARTER,) * 4,
        in_specs=[slots] * 4 + [small, small] + [IN_HBM] * 6,
        out_specs=(IN_HBM,) * 4 + (small,) + (quarter,) * 4,
        scratch_shapes=expert_scratch()
        + [
            pltpu.VMEM((2, 2, CHUNK, TOKENS, WIDTH), BF16),
            pltpu.SemaphoreType.DMA((2, 2, CHUNK // 2)),
            pltpu.SemaphoreType.DMA((2, 2, CHUNK // 2)),
            pltpu.SemaphoreType.DMA((WIDE,)),
        ],
        compiler_params=pltpu.CompilerParams(collective_id=5, has_side_effects=True, vmem_limit_bytes=VMEM_BYTES),
        cost_estimate=duration(1),
    )(rows, grad_rows, gated, dx, dgate, table_all, w_gate_up, w_down, *pieces)


RESULTS = 6


def results_kernel(*refs):
    pieces, arrays, small = refs[:8], refs[8 : 8 + RESULTS], refs[8 + RESULTS : 11 + RESULTS]
    refs = refs[11 + RESULTS :]
    gate_up_ref, down_ref, outs, small_outs = refs[0], refs[1], refs[2 : 2 + RESULTS], refs[2 + RESULTS : 6 + RESULTS]
    refs = refs[6 + RESULTS :]
    loaded, totals, held, sems, out_sems, held_sems = refs[0], refs[1], refs[2 : 2 + RESULTS], *refs[2 + RESULTS :]
    half = lax.rem(lax.axis_index("narrow"), 2)
    loads = [pltpu.make_async_copy(piece, loaded.at[i], sems.at[i]) for i, piece in enumerate(pieces)]
    through = [pltpu.make_async_copy(a, h, held_sems.at[i]) for i, (a, h) in enumerate(zip(arrays, held))]
    start_all([loads[i] for i in (0, 2, 1, 3, 4, 6, 5, 7)])
    start_all(through)
    router, gains, load = small
    small_outs[0][...] = router[...]
    small_outs[1][...] = gains[0:1, :]
    small_outs[2][...] = gains[1:2, :]
    small_outs[3][...] = load[...]
    stores = []
    for e in range(2):
        for which in range(2):
            left, right = 4 * e + which, 4 * e + which + 2
            loads[left].wait()
            loads[right].wait()
            number = 2 * e + which
            place = 2 * (half if which == 0 else 1 - half) + e
            totals[number] = loaded[left].astype(F32) + loaded[right].astype(F32)
            for part, (out, first, depth) in enumerate(((gate_up_ref, 0, 256), (down_ref, 256, 128))):
                copy = pltpu.make_async_copy(
                    totals.at[number, pl.ds(first, depth)], out.at[place], out_sems.at[2 * number + part]
                )
                copy.start()
                stores.append(copy)
    for i, copy in enumerate(through):
        copy.wait()
        copy = pltpu.make_async_copy(held[i], outs[i], held_sems.at[i])
        copy.start()
        stores.append(copy)
    for copy in stores:
        copy.wait()


def results_call(first, second, arrays, small):
    shapes = [jax.ShapeDtypeStruct(a.shape, a.dtype) for a in arrays]
    row = jax.ShapeDtypeStruct((1, 32), F32)
    return pl.pallas_call(
        results_kernel,
        name="results",
        out_shape=(
            jax.ShapeDtypeStruct((4, 256, WIDTH), F32),
            jax.ShapeDtypeStruct((4, 128, WIDTH), F32),
            *shapes,
            jax.ShapeDtypeStruct((32, 32), F32),
            row,
            row,
            jax.ShapeDtypeStruct((1, 32), jnp.int32),
        ),
        in_specs=[IN_HBM] * (8 + RESULTS) + [IN_VMEM] * 3,
        out_specs=(IN_HBM,) * (2 + RESULTS) + (IN_VMEM,) * 4,
        scratch_shapes=[pltpu.VMEM((8, 384, WIDTH), BF16), pltpu.VMEM((4, 384, WIDTH), F32)]
        + [pltpu.VMEM(s.shape, s.dtype) for s in shapes]
        + [pltpu.SemaphoreType.DMA((8,)), pltpu.SemaphoreType.DMA((8,)), pltpu.SemaphoreType.DMA((RESULTS,))],
        compiler_params=pltpu.CompilerParams(vmem_limit_bytes=VMEM_BYTES),
        cost_estimate=duration(1),
    )(*first, *second, *arrays, *small)


def widen(ref_value):
    return ref_value.astype(F32)


class PlaneReduce:
    COPIES = 10

    def __init__(self, spot, here, there, arrived, first, buffers, send, recv, local):
        self.spot, self.arrived = spot, arrived
        self.acc, self.from_core, self.from_one, self.from_two = buffers
        self.send, self.recv = send, recv
        self.started = []
        s = spot
        self.q_own = 2 * s.y + s.x
        self.q_x = 2 * s.y + 1 - s.x
        self.q_y = 2 - 2 * s.y + s.x
        self.q_d = 3 - self.q_own
        self.order = (self.q_d, self.q_x, self.q_y, self.q_own)
        self.loads = []
        for number, q in enumerate(self.order):
            mine = pltpu.make_async_copy(here.at[first + q], self.acc.at[q], local.at[number])
            if arrived:
                other = pltpu.make_async_copy(there.at[first + q], self.from_core.at[q], local.at[4 + number])
            else:
                other = remote(
                    there.at[first + q], self.from_core.at[q], send.at[6 + number], recv.at[6 + number], s.wide(s.sib)
                )
                self.started.append(other)
            self.loads.append((mine, other))

    def put(self, src, dst, number, to):
        copy = remote(src, dst, self.send.at[number], self.recv.at[number], self.spot.wide(to))
        copy.start()
        self.started.append(copy)

    def got(self, dst, number):
        remote(dst, dst, self.send.at[number], self.recv.at[number], self.spot.wide(self.spot.sib)).wait_recv()

    def begin(self):
        for pair in self.loads:
            start_all(pair)

    def add_core(self, number):
        mine, other = self.loads[number]
        mine.wait()
        other.wait() if self.arrived else other.wait_recv()
        q = self.order[number]
        self.acc[q] = self.acc[q] + self.from_core[q]

    def across_core(self):
        s = self.spot
        self.add_core(0)
        self.put(halves(self.acc.at[self.q_d], 0), self.from_one.at[1], 1, s.xn)
        self.put(halves(self.acc.at[self.q_d], 1), self.from_one.at[3], 3, s.yn)
        self.add_core(1)
        self.put(halves(self.acc.at[self.q_x], 0), self.from_one.at[0], 0, s.xn)
        self.add_core(2)
        self.put(halves(self.acc.at[self.q_y], 1), self.from_one.at[2], 2, s.yn)
        self.add_core(3)

    def across_one(self):
        s = self.spot
        self.got(self.from_one.at[1], 1)
        upper = halves(self.acc.at[self.q_y], 0)
        upper[...] = upper[...] + self.from_one[1]
        self.put(upper, self.from_two.at[0], 4, s.yn)
        self.got(self.from_one.at[3], 3)
        lower = halves(self.acc.at[self.q_x], 1)
        lower[...] = lower[...] + self.from_one[3]
        self.put(lower, self.from_two.at[1], 5, s.xn)

    def total(self, out):
        self.got(self.from_one.at[0], 0)
        self.got(self.from_two.at[0], 4)
        own = self.acc.at[self.q_own]
        out[0:SPAN, :] = widen(own[0:SPAN, :]) + widen(self.from_one[0]) + widen(self.from_two[0])
        self.got(self.from_one.at[2], 2)
        self.got(self.from_two.at[1], 5)
        out[SPAN:TOKENS, :] = widen(own[SPAN:TOKENS, :]) + widen(self.from_one[2]) + widen(self.from_two[1])

    def finish(self):
        for copy in self.started:
            copy.wait_send()


def halves(ref, which):
    return ref.at[pl.ds(which * SPAN, SPAN)]


class GroupReduce:
    def __init__(self, spot, here, there, arrived, scratch):
        acc, from_core, from_one, from_two, total, mate_send, mate_recv, send, recv, local, zs, zr = scratch
        self.total_ref, self.mate_send, self.mate_recv = total, mate_send, mate_recv
        parts = []
        for which, first in enumerate((4 * (1 - spot.half), 4 * spot.half)):
            buffers = (acc.at[which], from_core.at[which], from_one.at[which], from_two.at[which])
            parts.append(
                PlaneReduce(
                    spot, here, there, arrived, first, buffers, send.at[which], recv.at[which], local.at[which]
                )
            )
        self.theirs, self.ours = parts
        self.across = remote(mate_send, mate_recv, zs.at[0], zr.at[0], (spot.mate, spot.w))

    def begin(self):
        self.theirs.begin()
        self.ours.begin()

    def across_core(self):
        self.theirs.across_core()
        self.ours.across_core()

    def across_one(self):
        self.theirs.across_one()
        self.ours.across_one()

    def to_mate(self):
        self.theirs.total(self.total_ref)
        self.mate_send[...] = self.total_ref[...].astype(BF16)
        self.across.start()

    def finish(self):
        self.ours.total(self.total_ref)
        self.across.wait_recv()
        self.total_ref[...] += widen(self.mate_recv[...])
        self.theirs.finish()
        self.ours.finish()
        self.across.wait_send()


def reduce_scratch():
    dma = pltpu.SemaphoreType.DMA
    return [
        pltpu.VMEM((2, 4, TOKENS, WIDTH), BF16),
        pltpu.VMEM((2, 4, TOKENS, WIDTH), BF16),
        pltpu.VMEM((2, 4, SPAN, WIDTH), BF16),
        pltpu.VMEM((2, 2, SPAN, WIDTH), BF16),
        pltpu.VMEM((TOKENS, WIDTH), F32),
        pltpu.VMEM((TOKENS, WIDTH), BF16),
        pltpu.VMEM((TOKENS, WIDTH), BF16),
        dma((2, PlaneReduce.COPIES)),
        dma((2, PlaneReduce.COPIES)),
        dma((2, 8)),
        dma((1,)),
        dma((1,)),
    ]


REDUCE_REFS = 12


class AttentionBack:
    def __init__(self, dattn_all, w_rows, qkv_ref, lse_ref, o_ref, angle_ref, dqkv_ref, dkv_ref, dq_ref, osum):
        self.dattn_all, self.w_rows, self.qkv, self.lse, self.o = dattn_all, w_rows, qkv_ref, lse_ref, o_ref
        self.angle = angle_ref
        self.dqkv, self.dkv, self.dq, self.osum = dqkv_ref, dkv_ref, dq_ref, osum
        self.first_half = lane_half()
        self.is_key = lax.broadcasted_iota(jnp.int32, (1, 128), 1) < 64
        dkv_ref[...] = jnp.zeros_like(dkv_ref)
        osum[...] = jnp.zeros_like(osum)

    def stack(self, both):
        return jnp.concatenate([both[:, 0:64], both[:, 64:128]], axis=0)

    def chunk(self, row, q):
        first = pl.multiple_of(q * 256, 256)
        tokens = pl.ds(first, 256)
        dattn = self.dattn_all[pl.ds(2 * q, 2), pl.ds(row * SPAN, SPAN), :].reshape(256, WIDTH)
        outs = self.o[row, tokens, :]
        do = mm(dattn, self.w_rows[...], NT).astype(BF16)
        self.osum[...] += mm(outs, dattn, TN)
        inner = do.astype(F32) * outs.astype(F32)
        delta = jnp.concatenate(
            [
                jnp.sum(jnp.where(self.is_key, inner, 0.0), axis=1, keepdims=True),
                jnp.sum(jnp.where(self.is_key, 0.0, inner), axis=1, keepdims=True),
            ],
            axis=0,
        )
        query = self.stack(self.qkv[row, tokens, 0:128])
        do = self.stack(do)
        log_total = jnp.concatenate([self.lse[row, tokens, 0:1], self.lse[row, tokens, 64:65]], axis=0)
        start = self.lse[row, tokens, 32:33]
        start = jnp.concatenate([start, start], axis=0)
        place = lax.broadcasted_iota(jnp.int32, (256, 1), 0)
        place_query = (jnp.concatenate([place, place], axis=0) + q * 256).astype(F32)
        self.dq[...] = jnp.zeros_like(self.dq)

        def key_block(block, carry):
            keys_at = pl.ds(pl.multiple_of(block * 256, 256), 256)
            keys = self.qkv[row, keys_at, 128:192]
            values = self.qkv[row, keys_at, 192:256]
            place_key = (lax.broadcasted_iota(jnp.int32, (1, 256), 1) + block * 256).astype(F32)
            allowed = (place_key <= place_query) & (place_key >= start)
            scores = jnp.where(allowed, mm(query, keys, NT) * (HEAD_DIM**-0.5), MASKED)
            weights = jnp.exp(scores - log_total)
            dp = mm(do, values, NT)
            ds = (weights * (dp - delta)).astype(BF16)
            self.dq[...] += mm(ds, keys)
            dk = mm(ds, query, TN) * (HEAD_DIM**-0.5)
            dv = mm(weights.astype(BF16), do, TN)
            self.dkv[row, keys_at, :] += jnp.concatenate([dk, dv], axis=1)
            return carry

        lax.fori_loop(0, q + 1, key_block, 0)
        dq = jnp.concatenate([self.dq[0:256], self.dq[256:512]], axis=1) * (HEAD_DIM**-0.5)
        cosine = self.angle[row, tokens, 0:128]
        sine = self.angle[row, tokens, 128:256]
        self.dqkv[row, tokens, 0:128] = (dq * cosine + turn_back(dq * sine, self.first_half)).astype(BF16)

    def keys(self, row):
        cosine = self.angle[row, :, 0:128]
        sine = self.angle[row, :, 128:256]
        dkv = self.dkv[row]
        turned = dkv * cosine + turn_back(dkv * sine, self.first_half)
        self.dqkv[row, :, 128:256] = jnp.where(self.is_key, turned, dkv).astype(BF16)


def backward_kernel(*refs):
    (
        part_here, part_there, y_here, y_there, dgate_ref, h2_ref, w_out_ref, w_full_ref, h1_ref, qkv_ref, lse_ref, o_ref,
        angle_ref, mate_1, far_1, far_mate_1,
        x_ref, mid_ref, gate_ref, gain_ref, dy_ref, w_own, gain_col,
    ) = refs[:23]
    (
        block_out, in_grad, q_grad, k_grad, v_grad, o_grad, router_grad, two_gains, load_out, *quarters_recv,
    ) = refs[23:35]
    (
        dgate_all, h2_own, dattn_all, dmid_ref, small_ref, small_all, small_sum, w_router, w_rows, w_full,
        h1, qkv, lse, outs, angle, dqkv_ref, dkv_ref, dq_ref, osum, og_ref, wg_ref,
        dq_full, w_recv, o_held, s_held, o_recv, s_recv,
        ts, tr, s0, r0, bs, br, qs, qr, ks, kr, ws, wr, os, orv, ss, sr, gs, gr, local,
    ) = refs[35:81]
    h2_sum_refs = refs[81 : 81 + REDUCE_REFS]
    y_sum_refs = refs[81 + REDUCE_REFS :]

    spot = Spot()
    everyone = NARROW * WIDE
    h2_sum = GroupReduce(spot, part_here, part_there, True, h2_sum_refs)
    y_sum = GroupReduce(spot, y_here, y_there, False, y_sum_refs)
    h2_sum.begin()
    spot.greet(everyone)

    def tables(step, arriving):
        other = lax.rem(spot.slot + step, GROUP)
        o_half, o_w = lax.div(other, WIDE), lax.rem(other, WIDE)
        place = other if arriving else spot.slot
        return remote(
            dgate_ref.at[other], dgate_all.at[place], ts.at[other], tr.at[place],
            (spot.n - spot.half + o_half, o_w),
        )

    def start_table(step, carry):
        tables(step, False).start()
        return carry

    lax.fori_loop(1, GROUP, start_table, 0)
    rows = pl.ds(pl.multiple_of(spot.w * 128, 128), 128)
    loads = [
        (dgate_ref.at[spot.slot], dgate_all.at[spot.slot]),
        (h2_ref.at[spot.slot], h2_own),
        (w_out_ref.at[:, pl.ds(WIDTH, 128)], w_router),
        (w_out_ref.at[rows, pl.ds(0, WIDTH)], w_rows),
        (qkv_ref, qkv),
        (lse_ref, lse),
        (o_ref, outs),
        (angle_ref, angle),
        (h1_ref, h1),
    ]
    loads = [pltpu.make_async_copy(src, dst, local.at[i]) for i, (src, dst) in enumerate(loads)]
    w_loads = [pltpu.make_async_copy(w_full_ref.at[who], w_full.at[who], local.at[10 + who]) for who in range(WIDE)]
    h2_sum.theirs.across_core()
    start_all(loads + w_loads)
    y_sum.begin()
    h2_sum.theirs.across_one()
    h2_sum.ours.across_core()
    far_plane = 2 - 4 * lax.div(spot.n, 2)
    quarter_copies = [
        remote(piece, quarters_recv[number], gs.at[number], gr.at[number], (plane, spot.w))
        for number, (piece, plane) in enumerate(
            ((mate_1, spot.mate), (far_1, spot.n + far_plane), (far_mate_1, spot.mate + far_plane))
        )
    ]
    h2_sum.to_mate()
    h2_sum.ours.across_one()
    y_sum.across_core()
    h2_sum.finish()
    start_all(quarter_copies)

    def wait_table(step, carry):
        tables(step, False).wait_send()
        tables(step, True).wait_recv()
        return carry

    lax.fori_loop(1, GROUP, wait_table, 0)
    for copy in loads[:4]:
        copy.wait()

    gate = gate_ref[0:32, :]
    dgate = jnp.concatenate([dgate_all[(o % 2) * WIDE + o // 2, 0:2, :] for o in range(GROUP)], axis=0)
    dsel = gate * (dgate - jnp.sum(gate * dgate, axis=0, keepdims=True))
    dlogits = jnp.concatenate([dsel, jnp.zeros((96, TOKENS), F32)], axis=0)
    dh2 = h2_sum.total_ref[...] + mm(jnp.transpose(dlogits).astype(BF16), w_router[...], NT)
    mid = mid_ref[...]
    scale = lax.rsqrt(jnp.mean(mid * mid, axis=1, keepdims=True) + EPSILON)
    weighted = dh2 * gain_ref[1:2, :]
    inner = jnp.mean(weighted * mid, axis=1, keepdims=True)
    dmid = dy_ref[...].astype(F32) + weighted * scale - mid * (scale * scale * scale) * inner
    dmid_ref[...] = dmid
    dattn_all[spot.w] = dmid.astype(BF16)
    mine = dattn_all.at[spot.w]
    gather = PlaneGather(
        spot,
        lambda half: mine if half is None else halves(mine, half),
        lambda who, half: dattn_all.at[who] if half is None else halves(dattn_all.at[who], half),
        s0, r0,
    )
    gather.begin()
    small_ref[0:32, :] = mm(dsel.astype(BF16), h2_own[...])
    small_ref[32:33, :] = jnp.sum(dh2 * mid * scale, axis=0, keepdims=True)
    lane = lax.broadcasted_iota(jnp.int32, (32, WIDTH), 1)
    column = lax.broadcasted_iota(jnp.int32, (32, WIDTH), 0)
    count = jnp.sum(gate_ref[32:64, :], axis=1, keepdims=True)
    small_ref[33:34, :] = jnp.sum(jnp.where(lax.rem(lane, 128) == column, count, 0.0), axis=0, keepdims=True)
    small_ref[34:40, :] = jnp.zeros((6, WIDTH), F32)

    def lanes_to(step, arriving):
        other = lax.rem(spot.w + step, WIDE)
        place = other if arriving else spot.w
        return remote(
            small_ref.at[:, pl.ds(pl.multiple_of(other * 128, 128), 128)], small_all.at[place],
            bs.at[other], br.at[place], spot.wide(other),
        )

    def start_lanes(step, carry):
        lanes_to(step, False).start()
        return carry

    lax.fori_loop(1, WIDE, start_lanes, 0)
    small_all[spot.w] = small_ref[:, pl.ds(pl.multiple_of(spot.w * 128, 128), 128)]

    for copy in loads[4:8]:
        copy.wait()
    back = AttentionBack(dattn_all, w_rows, qkv, lse, outs, angle, dqkv_ref, dkv_ref, dq_ref, osum)
    order = h2_sum.ours
    sib_x = spot.sib + 2 - 4 * spot.x
    sib_y = spot.sib + 4 - 8 * spot.y
    sib_d = sib_x + 4 - 8 * spot.y

    def to_tokens(other, place, first, send, recv):
        return remote(
            dqkv_ref.at[:, pl.ds(pl.multiple_of(other * SPAN, SPAN), SPAN), pl.ds(first, 128)],
            dq_full.at[:, :, pl.ds(pl.multiple_of(place * 256 + first, 128), 128)],
            send.at[other], recv.at[place], spot.wide(other),
        )

    def send_queries(who):
        for other in who:
            to_tokens(other, spot.w, 0, qs, qr).start()

    gather.got(spot.sib, None, 4)
    back.chunk(0, order.q_own)
    gather.middle()
    back.chunk(1, order.q_own)
    send_queries((spot.sib,))
    gather.late()
    gather.got(sib_x, None, 7)
    back.chunk(0, order.q_x)
    back.chunk(1, order.q_x)
    send_queries((spot.xn, sib_x))
    gather.last()
    y_sum.across_one()
    gather.got(sib_y, None, 8)
    back.chunk(0, order.q_y)
    back.chunk(1, order.q_y)
    send_queries((spot.yn, sib_y))
    gather.got(sib_d, 0, 9)
    gather.got(sib_d, 1, 10)
    back.chunk(0, order.q_d)
    back.chunk(1, order.q_d)
    send_queries((spot.diag, sib_d))
    y_sum.to_mate()
    for copy in gather.started:
        copy.wait_send()
    back.keys(0)
    back.keys(1)

    def others(step):
        other = lax.rem(spot.me + step, everyone)
        return other, (lax.div(other, WIDE), lax.rem(other, WIDE))

    def rows_of(ref, owner):
        return ref.at[pl.ds(pl.multiple_of(owner * 32, 32), 32)]

    def to_owner(step, arriving):
        other, to = others(step)
        place = other if arriving else spot.me
        return remote(rows_of(wg_ref, other), w_recv.at[place], ws.at[other], wr.at[place], to)

    def start_owner(step, carry):
        to_owner(step, False).start()
        return carry

    def start_keys(step, carry):
        to_tokens(lax.rem(spot.w + step, WIDE), spot.w, 128, ks, kr).start()
        return carry

    lax.fori_loop(1, WIDE, start_keys, 0)
    plane_mine = pltpu.make_async_copy(
        dqkv_ref.at[:, pl.ds(pl.multiple_of(spot.w * SPAN, SPAN), SPAN), :],
        dq_full.at[:, :, pl.ds(pl.multiple_of(spot.w * 256, 256), 256)],
        local.at[0],
    )
    plane_mine.start()
    og_ref[...] = osum[...].astype(BF16)

    def wait_lanes(step, carry):
        lanes_to(step, False).wait_send()
        lanes_to(step, True).wait_recv()
        return carry

    lax.fori_loop(1, WIDE, wait_lanes, 0)
    lane_total = small_all[0]
    for device in range(1, WIDE):
        lane_total = lane_total + small_all[device]
    small_sum[...] = lane_total
    odd = 4 * lax.rem(spot.w, 2)

    def first_hop(i, act_local, act_remote):
        to = odd + i
        source = og_ref.at[pl.ds(i * 32, 32)]
        place = lax.div(spot.w, 2)

        @pl.when(to == spot.w)
        def _():
            act_local(pltpu.make_async_copy(source, o_held.at[place], local.at[2]))
            act_local(pltpu.make_async_copy(small_sum, s_held.at[place], local.at[3]))

        @pl.when(to != spot.w)
        def _():
            act_remote(remote(source, o_held.at[place], os.at[i], orv.at[place], spot.wide(to)))
            act_remote(remote(small_sum, s_held.at[place], ss.at[i], sr.at[place], spot.wide(to)))

    def first_arrival(place, act):
        giver = 2 * place + lax.div(spot.w, 4)

        @pl.when(giver != spot.w)
        def _():
            held, small = o_held.at[place], s_held.at[place]
            act(remote(held, held, os.at[0], orv.at[place], spot.wide(giver)))
            act(remote(small, small, ss.at[0], sr.at[place], spot.wide(giver)))

    def second_hop(step, arriving):
        plane = lax.rem(spot.n + step, NARROW)
        place = plane if arriving else spot.n
        to = (plane, spot.w)
        return (
            remote(o_held.at[plane], o_recv.at[place], os.at[4 + step], orv.at[4 + place], to),
            remote(s_held.at[plane], s_recv.at[place], ss.at[4 + step], sr.at[4 + place], to),
        )

    for i in range(4):
        first_hop(i, lambda c: c.start(), lambda c: c.start())

    loads[8].wait()
    wg_ref[...] = (mm(h1[0], dqkv_ref[0], TN) + mm(h1[1], dqkv_ref[1], TN)).astype(BF16)
    lax.fori_loop(1, everyone, start_owner, 0)
    owner_mine = pltpu.make_async_copy(rows_of(wg_ref, spot.me), w_recv.at[spot.me], local.at[1])
    owner_mine.start()
    for i in range(4):
        first_hop(i, lambda c: c.wait(), lambda c: c.wait_send())
    for place in range(NARROW):
        first_arrival(place, lambda c: c.wait_recv())
    for step in range(1, NARROW):
        start_all(second_hop(step, False))

    def wait_plane(step, carry):
        other = lax.rem(spot.w + step, WIDE)
        for first, send, recv in ((0, qs, qr), (128, ks, kr)):
            to_tokens(other, spot.w, first, send, recv).wait_send()
            to_tokens(other, other, first, send, recv).wait_recv()
        return carry

    lax.fori_loop(1, WIDE, wait_plane, 0)
    plane_mine.wait()
    for copy in w_loads:
        copy.wait()
    dh1 = jnp.zeros((TOKENS, WIDTH), F32)
    for who in range(WIDE):
        grads = dq_full[:, :, 256 * who : 256 * who + 256].reshape(TOKENS, 256)
        dh1 = dh1 + mm(grads, w_full[who], NT)
    x = x_ref[...].astype(F32)
    scale = lax.rsqrt(jnp.mean(x * x, axis=1, keepdims=True) + EPSILON)
    weighted = dh1 * gain_ref[0:1, :]
    inner = jnp.mean(weighted * x, axis=1, keepdims=True)
    in_grad[...] = (dmid_ref[...] + weighted * scale - x * (scale * scale * scale) * inner).astype(BF16)
    y_sum.finish()
    block_out[...] = (mid_ref[...] + y_sum.total_ref[...]).astype(BF16)

    def wait_owner(step, carry):
        to_owner(step, False).wait_send()
        to_owner(step, True).wait_recv()
        return carry

    lax.fori_loop(1, everyone, wait_owner, 0)
    owner_mine.wait()
    for step in range(1, NARROW):
        for copy in second_hop(step, False):
            copy.wait_send()
        for copy in second_hop(step, True):
            copy.wait_recv()
    gain_total = jnp.zeros((32, 1), F32)
    for w in range(WIDE):
        total = widen(w_recv[w])
        for plane in range(1, NARROW):
            total = total + widen(w_recv[plane * WIDE + w])
        q_grad[:, 128 * w : 128 * w + 128] = total[:, 0:128]
        k_grad[:, 64 * w : 64 * w + 64] = total[:, 128:192]
        v_grad[:, 64 * w : 64 * w + 64] = total[:, 192:256]
        gain_total += jnp.sum(total * widen(w_own[:, 256 * w : 256 * w + 256]), axis=1, keepdims=True)
    gain_total = gain_total / gain_col[...].astype(F32)
    o_recv[spot.n] = o_held[spot.n]
    s_recv[spot.n] = s_held[spot.n]
    total = widen(o_recv[0])
    for plane in range(1, NARROW):
        total = total + widen(o_recv[plane])
    o_grad[...] = total
    total = s_recv[0]
    for plane in range(1, NARROW):
        total = total + s_recv[plane]
    load_out[...] = total[33:34, 0:32].astype(jnp.int32)
    lane = lax.rem(spot.me, 4)
    mine = jnp.zeros((40, 32), F32)
    for part in range(4):
        mine = mine + jnp.where(lane == part, 1.0, 0.0) * total[:, 32 * part : 32 * part + 32]
    square = jnp.concatenate([mine, jnp.zeros((40, 96), F32)], axis=1)
    square = jnp.concatenate([square, jnp.zeros((88, 128), F32)], axis=0)
    router_grad[...] = jnp.transpose(square)[0:32, 0:32]
    column = jnp.concatenate([jnp.broadcast_to(gain_total, (32, 128)), jnp.zeros((96, 128), F32)], axis=0)
    two_gains[...] = jnp.concatenate([jnp.transpose(column)[0:1, 0:32], mine[32:33]], axis=0)

    for copy in quarter_copies:
        copy.wait_send()
        copy.wait_recv()


def backward_call(*operands):
    dma = pltpu.SemaphoreType.DMA
    vmem = pltpu.VMEM
    everyone = NARROW * WIDE
    copies = PlaneGather.COPIES
    return pl.pallas_call(
        backward_kernel,
        name="backward",
        out_shape=(
            jax.ShapeDtypeStruct((TOKENS, WIDTH), BF16),
            jax.ShapeDtypeStruct((TOKENS, WIDTH), BF16),
            jax.ShapeDtypeStruct((32, WIDTH), F32),
            jax.ShapeDtypeStruct((32, WIDTH // 2), F32),
            jax.ShapeDtypeStruct((32, WIDTH // 2), F32),
            jax.ShapeDtypeStruct((32, WIDTH), F32),
            jax.ShapeDtypeStruct((32, 32), F32),
            jax.ShapeDtypeStruct((2, 32), F32),
            jax.ShapeDtypeStruct((1, 32), jnp.int32),
        )
        + (QUARTER,) * 3,
        in_specs=[IN_HBM] * 16 + [IN_VMEM] * 7,
        out_specs=(IN_VMEM,) * 9 + (IN_HBM,) * 3,
        scratch_shapes=[
            vmem((GROUP, 8, TOKENS), F32),
            vmem((TOKENS, WIDTH), BF16),
            vmem((WIDE, TOKENS, WIDTH), BF16),
            vmem((TOKENS, WIDTH), F32),
            vmem((40, WIDTH), F32),
            vmem((WIDE, 40, 128), F32),
            vmem((40, 128), F32),
            vmem((WIDTH, 128), BF16),
            vmem((128, WIDTH), BF16),
            vmem((WIDE, WIDTH, 256), BF16),
            vmem((2, SEQ, WIDTH), BF16),
            vmem((2, SEQ, 256), BF16),
            vmem((2, SEQ, 128), F32),
            vmem((2, SEQ, 128), BF16),
            vmem((2, SEQ, 256), F32),
            vmem((2, SEQ, 256), BF16),
            vmem((2, SEQ, 128), F32),
            vmem((512, HEAD_DIM), F32),
            vmem((128, WIDTH), F32),
            vmem((128, WIDTH), BF16),
            vmem((WIDTH, 256), BF16),
            vmem((2, SPAN, 2 * WIDTH), BF16),
            vmem((everyone, 32, 256), BF16),
            vmem((NARROW, 32, WIDTH), BF16),
            vmem((NARROW, 40, 128), F32),
            vmem((NARROW, 32, WIDTH), BF16),
            vmem((NARROW, 40, 128), F32),
            dma((GROUP,)),
            dma((GROUP,)),
            dma((copies,)),
            dma((copies,)),
            dma((WIDE,)),
            dma((WIDE,)),
            dma((WIDE,)),
            dma((WIDE,)),
            dma((WIDE,)),
            dma((WIDE,)),
            dma((everyone,)),
            dma((everyone,)),
            dma((8,)),
            dma((8,)),
            dma((8,)),
            dma((8,)),
            dma((3,)),
            dma((3,)),
            dma((18,)),
        ]
        + reduce_scratch()
        + reduce_scratch(),
        compiler_params=pltpu.CompilerParams(collective_id=3, has_side_effects=True, vmem_limit_bytes=VMEM_BYTES),
        cost_estimate=duration(1),
    )(*operands)


def swap(values, distance):
    return lax.ppermute(values, "narrow", [(i, i ^ distance) for i in range(NARROW)])


def position_tables():
    freq = (1.0 / np.float32(THETA) ** (np.arange(32, dtype=np.float32) * np.float32(2.0) / np.float32(HEAD_DIM))).astype(np.float32)
    angle = np.arange(SEQ, dtype=np.float32)[:, None] * freq[None, :]
    cosine = np.tile(np.cos(angle.astype(np.float64)), (1, 4)).astype(np.float32)
    sine = np.tile(np.sin(angle.astype(np.float64)), (1, 4)).astype(np.float32)
    return cosine, sine, np.tile(freq[None, :], (8, 4)).astype(np.float32)


def fast_device(
    hidden_in, out_grad, seg_ids, expert_ids, attn_gain, w_query, w_key, w_value, w_output,
    moe_gain, w_router, w_gate_up, w_down,
):
    n = lax.axis_index("narrow")
    w = lax.axis_index("wide")
    half = n % 2
    me = n * WIDE + w
    cos_table, sin_table, freq = position_tables()

    x_own = hidden_in.reshape(TOKENS, WIDTH)
    dy_own = out_grad.reshape(TOKENS, WIDTH)
    ids = expert_ids.reshape(TOKENS, TOP)
    x_all, w_all, g_all, seg_all, wo_block, dy_pair, far_early_0, w_own = gather_call(
        x_own, dy_own, seg_ids, w_query, w_key, w_value, w_output, w_router,
        attn_gain.reshape(1, 32), moe_gain.reshape(1, 32), w_gate_up,
    )
    (
        h1, qkv, lse, o_heads, angle, gain_rows, mid, gate, w_out, h2_all, dy_all, table_all,
        mate_0, far_rest_0, far_mate_0, mate_1, far_1, far_mate_early_1,
    ) = forward_call(
        x_all, w_all, g_all, seg_all, cos_table, sin_table, freq, wo_block, ids, dy_pair, w_gate_up, w_down
    )
    w_out = w_out.reshape(WIDTH, WIDTH + 128)

    def send_grads(own, mate, far, far_mate):
        return own, swap(mate, 1), swap(far, 2), swap(far_mate, 3)

    gated_0, dx_0, rows_1, grad_rows_1, dgate_0, *grads_0, far_mate_rest_1 = expert_0_call(
        h2_all, dy_all, table_all, w_gate_up, w_down, (mate_0, far_early_0, far_rest_0, far_mate_0)
    )
    dgate_0, w_heads = lax.optimization_barrier((dgate_0, w_all))
    w_full = lax.all_gather(w_heads.reshape(WIDTH, 256), "wide", axis=0, tiled=False)
    grads_0 = send_grads(*grads_0)
    y_here, y_there, part_here, part_there, dgate, *grads_1 = expert_1_call(
        rows_1, grad_rows_1, gated_0, dx_0, dgate_0, table_all, w_gate_up, w_down, (mate_1, far_1, far_mate_early_1, far_mate_rest_1)
    )
    (
        block_out, in_grad, q_grad, k_grad, v_grad, o_grad, router_grad, two_gains, load, *arrived_1,
    ) = backward_call(
        part_here, part_there, y_here, y_there, dgate, h2_all, w_out, w_full, h1, qkv, lse, o_heads, angle, *grads_1[1:],
        x_own, mid, gate, gain_rows, dy_own, w_own, attn_gain.reshape(32, 1),
    )
    (
        gate_up_sum, down_sum, block_out, in_grad, q_grad, k_grad, v_grad, o_grad,
        router_grad, attn_gain_grad, moe_gain_grad, load,
    ) = results_call(
        grads_0, (grads_1[0], *arrived_1),
        (block_out, in_grad, q_grad, k_grad, v_grad, o_grad), (router_grad, two_gains, load),
    )
    return (
        block_out.reshape(hidden_in.shape),
        in_grad.reshape(hidden_in.shape),
        attn_gain_grad.reshape(32),
        q_grad,
        k_grad,
        v_grad,
        o_grad,
        moe_gain_grad.reshape(32),
        router_grad,
        gate_up_sum,
        down_sum,
        load.reshape(32),
    )


def solution(mesh):
    planned = mesh.shape["narrow"] == NARROW and mesh.shape["wide"] == WIDE
    return jax.shard_map(
        fast_device if planned else general_device,
        mesh=mesh,
        in_specs=(
            P("narrow", "wide", None),
            P("narrow", "wide", None),
            P("narrow", "wide"),
            P("narrow", "wide", None),
            P(("narrow", "wide")),
            P(("narrow", "wide"), None),
            P(("narrow", "wide"), None),
            P(("narrow", "wide"), None),
            P(("narrow", "wide"), None),
            P(("narrow", "wide")),
            P(("narrow", "wide"), None),
            P("wide", "narrow", None),
            P("wide", "narrow", None),
        ),
        out_specs=(
            P("narrow", "wide", None),
            P("narrow", "wide", None),
            P(("narrow", "wide")),
            P(("narrow", "wide"), None),
            P(("narrow", "wide"), None),
            P(("narrow", "wide"), None),
            P(("narrow", "wide"), None),
            P(("narrow", "wide")),
            P(("narrow", "wide"), None),
            P("wide", "narrow", None),
            P("wide", "narrow", None),
            P(),
        ),
        check_vma=False,
    )
```

```python
import math

import functools
import jax
import jax.numpy as jnp
import numpy as np
from jax import lax
from jax.experimental import pallas as pl
from jax.experimental.pallas import tpu as pltpu
from jax.sharding import PartitionSpec as P

KV_HEADS = 8
HEAD_DIM = 64
EXPERTS = 32
TOP = 8
FF = 512
CAP = 80


EPSILON = 1e-06
THETA = 10000.0
MASKED = -1e30


def rms_scale(values):
    return lax.rsqrt(jnp.mean(values * values, axis=-1, keepdims=True) + EPSILON)


def norm_back(values, scale, gain, upstream):
    weighted = upstream * gain
    inner_mean = jnp.mean(weighted * values, axis=-1, keepdims=True)
    value_grad = weighted * scale - values * (scale * scale * scale) * inner_mean
    gain_grad = jnp.sum(upstream * values * scale, axis=0)
    return (value_grad, gain_grad)


def lane_turn(head_dim):
    lane_ids = jnp.arange(128)
    lane_local = lane_ids % head_dim
    half_dim = head_dim // 2
    same_head = lane_ids[:, None] // head_dim == lane_ids[None, :] // head_dim
    from_upper = (lane_local[None, :] < half_dim) & (
        lane_local[:, None] == lane_local[None, :] + half_dim
    )
    from_lower = (lane_local[None, :] >= half_dim) & (
        lane_local[:, None] + half_dim == lane_local[None, :]
    )
    return jnp.where(
        same_head & from_upper, -1.0, jnp.where(same_head & from_lower, 1.0, 0.0)
    ).astype(jnp.float32)


def lane_angles(positions, head_dim):
    lane_ids = jnp.arange(128) % head_dim % (head_dim // 2)
    inverse = 1.0 / THETA ** (lane_ids.astype(jnp.float32) * 2.0 / head_dim)
    return positions[..., None] * inverse


def rotate(values, cos_table, sin_table, turner):
    dims_in = values.shape
    blocks = values.reshape(dims_in[0], dims_in[1], -1, 128)
    turned = jnp.einsum("abnl,lm->abnm", blocks, turner, precision=lax.Precision.HIGHEST)
    return (blocks * cos_table[:, :, None, :] + turned * sin_table[:, :, None, :]).reshape(dims_in)


def rotate_back(grad_in, cos_table, sin_table, turner):
    dims_in = grad_in.shape
    blocks = grad_in.reshape(dims_in[0], dims_in[1], -1, 128)
    turned = jnp.einsum(
        "abnm,lm->abnl", blocks * sin_table[:, :, None, :], turner, precision=lax.Precision.HIGHEST
    )
    return (blocks * cos_table[:, :, None, :] + turned).reshape(dims_in)


def masked_scores(query_five, key_block, seg_query, seg_key, place_query, place_key, factor):
    scores = (
        jnp.einsum("abgjd,akgd->agjbk", query_five, key_block, preferred_element_type=jnp.float32)
        * factor
    )
    allowed = (seg_query[:, :, None] == seg_key[:, None, :]) & (
        place_query[:, :, None] >= place_key[:, None, :]
    )
    return jnp.where(allowed[:, None, None], scores, MASKED)


def general_device(
    hidden_in,
    out_grad,
    seg_ids,
    expert_ids,
    attn_gain,
    w_query,
    w_key,
    w_value,
    w_output,
    moe_gain,
    w_router,
    w_gate_up,
    w_down,
):
    row_count, span_len, feat_dim = hidden_in.shape
    tok_count = row_count * span_len
    factor = HEAD_DIM ** (-0.5)
    kv_width = KV_HEADS * HEAD_DIM
    gain_one, query_w, key_w, value_w, output_w, gain_two, router_w = (
        lax.all_gather(attn_gain, ("narrow", "wide"), axis=0, tiled=True),
        lax.all_gather(w_query, ("narrow", "wide"), axis=0, tiled=True),
        lax.all_gather(w_key, ("narrow", "wide"), axis=0, tiled=True),
        lax.all_gather(w_value, ("narrow", "wide"), axis=0, tiled=True),
        lax.all_gather(w_output, ("narrow", "wide"), axis=0, tiled=True),
        lax.all_gather(moe_gain, ("narrow", "wide"), axis=0, tiled=True),
        lax.all_gather(w_router, ("narrow", "wide"), axis=0, tiled=True),
    )
    gate_up_w, down_w = (
        lax.all_gather(w_gate_up, "narrow", axis=1, tiled=True),
        lax.all_gather(w_down, "narrow", axis=1, tiled=True),
    )
    segs_all = lax.all_gather(seg_ids, "wide", axis=1, tiled=True)
    seq_len = segs_all.shape[1]
    key_step = math.gcd(seq_len, 512)
    place_local = lax.axis_index("wide") * span_len + jnp.arange(span_len, dtype=jnp.int32)
    place_query = place_local[None, :]
    starts = jnp.sum((segs_all[:, None, :] < seg_ids[:, :, None]).astype(jnp.int32), axis=-1)
    positions = (place_query - starts).astype(jnp.float32)
    angles = lane_angles(positions, HEAD_DIM)
    cos_table = jnp.cos(angles)
    sin_table = jnp.sin(angles)
    turner = lane_turn(HEAD_DIM)
    inputs = hidden_in.astype(jnp.float32)
    scale_one = rms_scale(inputs)
    gain_one_f = gain_one.astype(jnp.float32)
    normed_one = (inputs * scale_one * gain_one_f).astype(jnp.bfloat16)
    query_pre = jnp.dot(normed_one, query_w, preferred_element_type=jnp.float32)
    key_pre = jnp.dot(normed_one, key_w, preferred_element_type=jnp.float32)
    value_pre = jnp.dot(normed_one, value_w, preferred_element_type=jnp.float32)
    queries = rotate(query_pre, cos_table, sin_table, turner).astype(jnp.bfloat16)
    keys_local = rotate(key_pre, cos_table, sin_table, turner).astype(jnp.bfloat16)
    values_local = value_pre.astype(jnp.bfloat16)
    key_all, value_all = (
        lax.all_gather(keys_local, "wide", axis=1, tiled=True),
        lax.all_gather(values_local, "wide", axis=1, tiled=True),
    )
    query_five = queries.reshape(row_count, span_len, KV_HEADS, 2, HEAD_DIM)

    def key_slices(key_start, length):
        key_block = lax.dynamic_slice_in_dim(key_all, key_start, length, 1).reshape(
            row_count, length, KV_HEADS, HEAD_DIM
        )
        value_block = lax.dynamic_slice_in_dim(value_all, key_start, length, 1).reshape(
            row_count, length, KV_HEADS, HEAD_DIM
        )
        seg_key = lax.dynamic_slice_in_dim(segs_all, key_start, length, 1)
        place_key = (key_start + jnp.arange(length, dtype=jnp.int32))[None, :]
        return (key_block, value_block, seg_key, place_key)

    def scores_at(key_start, length):
        key_block, value_block, seg_key, place_key = key_slices(key_start, length)
        scores = masked_scores(
            query_five, key_block, seg_ids, seg_key, place_query, place_key, factor
        )
        return (scores, key_block, value_block)

    key_starts = jnp.arange(seq_len // key_step, dtype=jnp.int32) * key_step
    stat_shape = (row_count, KV_HEADS, 2, span_len)
    five_shape = (row_count, span_len, KV_HEADS, 2, HEAD_DIM)

    def top_step(state_now, key_start):
        row_top, row_total = state_now
        scores, unused_key, unused_value = scores_at(key_start, key_step)
        new_top = jnp.maximum(row_top, jnp.max(scores, axis=-1))
        row_total = row_total * jnp.exp(row_top - new_top) + jnp.sum(
            jnp.exp(scores - new_top[..., None]), axis=-1
        )
        return ((new_top, row_total), None)

    (row_top, row_total), unused = lax.scan(
        top_step,
        (jnp.full(stat_shape, MASKED, jnp.float32), jnp.zeros(stat_shape, jnp.float32)),
        key_starts,
    )
    log_total = row_top + jnp.log(row_total)

    def out_step(summed, key_start):
        scores, unused_key, value_block = scores_at(key_start, key_step)
        weights = jnp.exp(scores - log_total[..., None]).astype(jnp.bfloat16)
        return (
            summed
            + jnp.einsum(
                "agjbk,akgd->abgjd", weights, value_block, preferred_element_type=jnp.float32
            ),
            None,
        )

    attended, unused = lax.scan(out_step, jnp.zeros(five_shape, jnp.float32), key_starts)
    attended = attended.reshape(row_count, span_len, -1).astype(jnp.bfloat16)
    middle = inputs + jnp.dot(attended, output_w, preferred_element_type=jnp.float32)
    scale_two = rms_scale(middle)
    gain_two_f = gain_two.astype(jnp.float32)
    normed_two = (middle * scale_two * gain_two_f).astype(jnp.bfloat16)
    flat_two = normed_two.reshape(tok_count, feat_dim)
    logits = jnp.dot(flat_two, router_w, preferred_element_type=jnp.float32)
    expert_table = expert_ids.reshape(tok_count, TOP)
    choose = expert_table[:, :, None] == jnp.arange(EXPERTS, dtype=jnp.int32)[None, None, :]
    chosen = jnp.sum(jnp.where(choose, logits[:, None, :], 0.0), axis=-1)
    gate_vals = jax.nn.softmax(chosen, axis=-1)
    token_hot = jnp.sum(choose.astype(jnp.int32), axis=1)
    expert_load = lax.psum(jnp.sum(token_hot, axis=0), ("narrow", "wide"))
    earlier = jnp.cumsum(token_hot, axis=0) - token_hot
    places = jnp.sum(jnp.where(choose, earlier[:, None, :], 0), axis=-1)
    pair_count = tok_count * TOP
    target = jnp.where(places < CAP, expert_table * CAP + places, EXPERTS * CAP).reshape(-1)
    pair_of_slot = (
        jnp.full((EXPERTS * CAP,), pair_count, jnp.int32)
        .at[target]
        .set(jnp.arange(pair_count, dtype=jnp.int32), mode="drop")
    )
    token_of_slot = pair_of_slot // TOP
    outgoing = jnp.take(flat_two, token_of_slot, axis=0, mode="fill", fill_value=0).reshape(
        EXPERTS, CAP, feat_dim
    )
    received = lax.all_to_all(outgoing, "wide", split_axis=0, concat_axis=1, tiled=True)
    gate_up = jnp.einsum("ecd,edf->ecf", received, gate_up_w, preferred_element_type=jnp.float32)
    gate_half = gate_up[..., :FF]
    up_half = gate_up[..., FF:]
    sigmoid_gate = jax.nn.sigmoid(gate_half)
    activated = gate_half * sigmoid_gate
    hidden_b = (activated * up_half).astype(jnp.bfloat16)
    expert_out = jnp.einsum(
        "ecf,efd->ecd", hidden_b, down_w, preferred_element_type=jnp.float32
    ).astype(jnp.bfloat16)
    returned = lax.all_to_all(expert_out, "wide", split_axis=1, concat_axis=0, tiled=True)
    per_pair = (
        jnp.take(
            returned.reshape(EXPERTS * CAP, feat_dim), target, axis=0, mode="fill", fill_value=0
        )
        .reshape(tok_count, TOP, feat_dim)
        .astype(jnp.float32)
    )
    mixture = jnp.sum(gate_vals[:, :, None] * per_pair, axis=1)
    middle_flat = middle.reshape(tok_count, feat_dim)
    block_out = (middle_flat + mixture).reshape(row_count, span_len, feat_dim).astype(jnp.bfloat16)
    grad_out = out_grad.reshape(tok_count, feat_dim).astype(jnp.float32)
    gate_grad = jnp.sum(grad_out[:, None, :] * per_pair, axis=-1)
    gate_of_slot = jnp.take(gate_vals.reshape(-1), pair_of_slot, mode="fill", fill_value=0.0)
    slot_grad = (
        (
            jnp.take(grad_out, token_of_slot, axis=0, mode="fill", fill_value=0.0)
            * gate_of_slot[:, None]
        )
        .astype(jnp.bfloat16)
        .reshape(EXPERTS, CAP, feat_dim)
    )
    grad_received = lax.all_to_all(slot_grad, "wide", split_axis=0, concat_axis=1, tiled=True)
    down_grad = jnp.einsum(
        "ecf,ecd->efd", hidden_b, grad_received, preferred_element_type=jnp.float32
    )
    hidden_grad = jnp.einsum(
        "ecd,efd->ecf", grad_received, down_w, preferred_element_type=jnp.float32
    )
    gate_half_grad = (
        hidden_grad * up_half * (sigmoid_gate * (1.0 + gate_half * (1.0 - sigmoid_gate)))
    )
    up_half_grad = hidden_grad * activated
    gate_up_grad = jnp.concatenate([gate_half_grad, up_half_grad], axis=-1).astype(jnp.bfloat16)
    gate_up_wgrad = jnp.einsum(
        "ecd,ecf->edf", received, gate_up_grad, preferred_element_type=jnp.float32
    )
    slot_input_grad = jnp.einsum(
        "ecf,edf->ecd", gate_up_grad, gate_up_w, preferred_element_type=jnp.float32
    ).astype(jnp.bfloat16)
    input_back = lax.all_to_all(slot_input_grad, "wide", split_axis=1, concat_axis=0, tiled=True)
    pair_input_grad = jnp.take(
        input_back.reshape(EXPERTS * CAP, feat_dim), target, axis=0, mode="fill", fill_value=0
    ).reshape(tok_count, TOP, feat_dim)
    gate_mean = jnp.sum(gate_vals * gate_grad, axis=-1, keepdims=True)
    chosen_grad = gate_vals * (gate_grad - gate_mean)
    logit_grad = jnp.sum(jnp.where(choose, chosen_grad[:, :, None], 0.0), axis=1).astype(
        jnp.bfloat16
    )
    router_wgrad = jnp.einsum("td,te->de", flat_two, logit_grad, preferred_element_type=jnp.float32)
    normed_two_grad = jnp.sum(pair_input_grad.astype(jnp.float32), axis=1) + jnp.einsum(
        "te,de->td", logit_grad, router_w, preferred_element_type=jnp.float32
    )
    middle_part, gain_two_grad = norm_back(
        middle_flat, scale_two.reshape(tok_count, 1), gain_two_f, normed_two_grad
    )
    middle_grad = grad_out + middle_part
    attn_grad = middle_grad.astype(jnp.bfloat16)
    output_wgrad = jnp.einsum(
        "te,td->ed", attended.reshape(tok_count, -1), attn_grad, preferred_element_type=jnp.float32
    )
    attended_grad = jnp.einsum(
        "td,ed->te", attn_grad, output_w, preferred_element_type=jnp.float32
    ).astype(jnp.bfloat16)
    grad_five = attended_grad.reshape(five_shape)

    def sum_step(summed, key_start):
        scores, unused_key, value_block = scores_at(key_start, key_step)
        weights = jnp.exp(scores - log_total[..., None])
        weight_grad = jnp.einsum(
            "abgjd,akgd->agjbk", grad_five, value_block, preferred_element_type=jnp.float32
        )
        return (summed + jnp.sum(weights * weight_grad, axis=-1), None)

    row_dot, unused = lax.scan(sum_step, jnp.zeros(stat_shape, jnp.float32), key_starts)

    def query_step(summed, key_start):
        scores, key_block, value_block = scores_at(key_start, key_step)
        weights = jnp.exp(scores - log_total[..., None])
        weight_grad = jnp.einsum(
            "abgjd,akgd->agjbk", grad_five, value_block, preferred_element_type=jnp.float32
        )
        score_grad = (weights * (weight_grad - row_dot[..., None])).astype(jnp.bfloat16)
        return (
            summed
            + jnp.einsum(
                "agjbk,akgd->abgjd", score_grad, key_block, preferred_element_type=jnp.float32
            ),
            None,
        )

    query_grad, unused = lax.scan(query_step, jnp.zeros(five_shape, jnp.float32), key_starts)
    query_grad = query_grad.reshape(row_count, span_len, -1) * factor
    term_count = span_len * lax.axis_size("wide")
    sub_len = math.gcd(term_count, 512)

    def key_piece(sub_no):
        key_start = sub_no * sub_len
        key_block, value_block, seg_key, place_key = key_slices(key_start, sub_len)
        scores = masked_scores(
            query_five, key_block, seg_ids, seg_key, place_query, place_key, factor
        )
        weights = jnp.exp(scores - log_total[..., None])
        weight_grad = jnp.einsum(
            "abgjd,akgd->agjbk", grad_five, value_block, preferred_element_type=jnp.float32
        )
        score_grad = (weights * (weight_grad - row_dot[..., None])).astype(jnp.bfloat16)
        key_part = (
            jnp.einsum(
                "agjbk,abgjd->kagd", score_grad, query_five, preferred_element_type=jnp.float32
            )
            * factor
        )
        value_part = jnp.einsum(
            "agjbk,abgjd->kagd",
            weights.astype(jnp.bfloat16),
            grad_five,
            preferred_element_type=jnp.float32,
        )
        return jnp.concatenate(
            [
                key_part.reshape(sub_len, row_count, kv_width),
                value_part.reshape(sub_len, row_count, kv_width),
            ],
            axis=-1,
        )

    pieces = lax.map(key_piece, jnp.arange(term_count // sub_len, dtype=jnp.int32))
    summed_terms = lax.psum_scatter(
        pieces.reshape(term_count, row_count, 2 * kv_width).astype(jnp.bfloat16),
        "wide",
        scatter_dimension=0,
        tiled=True,
    ).astype(jnp.float32)
    key_grad = jnp.transpose(summed_terms[:, :, :kv_width], (1, 0, 2))
    value_grad = jnp.transpose(summed_terms[:, :, kv_width:], (1, 0, 2))
    query_back = (
        rotate_back(query_grad, cos_table, sin_table, turner)
        .astype(jnp.bfloat16)
        .reshape(tok_count, -1)
    )
    key_back = (
        rotate_back(key_grad, cos_table, sin_table, turner)
        .astype(jnp.bfloat16)
        .reshape(tok_count, -1)
    )
    value_back = value_grad.astype(jnp.bfloat16).reshape(tok_count, -1)
    flat_one = normed_one.reshape(tok_count, feat_dim)
    query_wgrad = jnp.einsum("td,te->de", flat_one, query_back, preferred_element_type=jnp.float32)
    key_wgrad = jnp.einsum("td,te->de", flat_one, key_back, preferred_element_type=jnp.float32)
    value_wgrad = jnp.einsum("td,te->de", flat_one, value_back, preferred_element_type=jnp.float32)
    normed_one_grad = (
        jnp.einsum("te,de->td", query_back, query_w, preferred_element_type=jnp.float32)
        + jnp.einsum("te,de->td", key_back, key_w, preferred_element_type=jnp.float32)
        + jnp.einsum("te,de->td", value_back, value_w, preferred_element_type=jnp.float32)
    )
    input_part, gain_one_grad = norm_back(
        inputs.reshape(tok_count, feat_dim),
        scale_one.reshape(tok_count, 1),
        gain_one_f,
        normed_one_grad,
    )
    input_grad = (
        (middle_grad + input_part).reshape(row_count, span_len, feat_dim).astype(jnp.bfloat16)
    )
    gain_one_sum, query_sum, key_wsum, value_wsum, output_sum, gain_two_sum, router_sum = (
        lax.psum_scatter(gain_one_grad, ("narrow", "wide"), scatter_dimension=0, tiled=True),
        lax.psum_scatter(query_wgrad, ("narrow", "wide"), scatter_dimension=0, tiled=True),
        lax.psum_scatter(key_wgrad, ("narrow", "wide"), scatter_dimension=0, tiled=True),
        lax.psum_scatter(value_wgrad, ("narrow", "wide"), scatter_dimension=0, tiled=True),
        lax.psum_scatter(output_wgrad, ("narrow", "wide"), scatter_dimension=0, tiled=True),
        lax.psum_scatter(gain_two_grad, ("narrow", "wide"), scatter_dimension=0, tiled=True),
        lax.psum_scatter(router_wgrad, ("narrow", "wide"), scatter_dimension=0, tiled=True),
    )
    gate_up_sum, down_sum = (
        lax.psum_scatter(
            gate_up_wgrad.astype(jnp.bfloat16), "narrow", scatter_dimension=1, tiled=True
        ).astype(jnp.float32),
        lax.psum_scatter(
            down_grad.astype(jnp.bfloat16), "narrow", scatter_dimension=1, tiled=True
        ).astype(jnp.float32),
    )
    return (
        block_out,
        input_grad,
        gain_one_sum,
        query_sum,
        key_wsum,
        value_wsum,
        output_sum,
        gain_two_sum,
        router_sum,
        gate_up_sum,
        down_sum,
        expert_load,
    )


MESH = pl.DeviceIdType.MESH
F32 = jnp.float32
BF16 = jnp.bfloat16
IN_HBM = pl.BlockSpec(memory_space=pl.ANY)
IN_VMEM = pl.BlockSpec(memory_space=pltpu.VMEM)
VMEM_BYTES = 60 * 1024 * 1024
NARROW = 4
WIDE = 8
GROUP = 16
TOKENS = 256
SPAN = 128
WIDTH = 1024
SEQ = 1024
SLOTS = 80
MINE = 2
MIDDLE = 96
CHUNK = 4
NT = (((1,), (1,)), ((), ()))
TN = (((0,), (0,)), ((), ()))


def duration(us):
    return pl.CostEstimate(flops=us * 1000000000, bytes_accessed=us * 3600000, transcendentals=0)


def mm(left, right, dims=(((1,), (0,)), ((), ()))):
    return lax.dot_general(left, right, dims, preferred_element_type=F32)


class Spot:
    def __init__(self):
        self.n = lax.axis_index("narrow")
        self.w = lax.axis_index("wide")
        self.core = lax.rem(self.w, 2)
        self.x = lax.rem(lax.div(self.w, 2), 2)
        self.y = lax.div(self.w, 4)
        self.half = lax.rem(self.n, 2)
        self.me = self.n * WIDE + self.w
        self.sib = self.w + 1 - 2 * self.core
        self.xn = self.w + 2 - 4 * self.x
        self.yn = self.w + 4 - 8 * self.y
        self.diag = self.xn + 4 - 8 * self.y
        self.mate = self.n + 1 - 2 * self.half
        self.slot = self.half * WIDE + self.w

    def wide(self, to):
        return (self.n, to)

    def greet(self, count):
        barrier = pltpu.get_barrier_semaphore()
        base = self.n - self.half

        def signal(step, carry):
            if count == WIDE:
                to = (self.n, lax.rem(self.w + step, WIDE))
            elif count == GROUP:
                other = lax.rem(self.slot + step, GROUP)
                to = (base + lax.div(other, WIDE), lax.rem(other, WIDE))
            else:
                other = lax.rem(self.me + step, NARROW * WIDE)
                to = (lax.div(other, WIDE), lax.rem(other, WIDE))
            pl.semaphore_signal(barrier, inc=1, device_id=to, device_id_type=MESH)
            return carry

        lax.fori_loop(1, count, signal, 0)
        pl.semaphore_wait(barrier, count - 1)


def remote(src, dst, send_sem, recv_sem, to):
    return pltpu.make_async_remote_copy(
        src_ref=src, dst_ref=dst, send_sem=send_sem, recv_sem=recv_sem, device_id=to, device_id_type=MESH
    )


def halves(ref, which):
    return ref.at[pl.ds(which * SPAN, SPAN)]


class PlaneGather:
    COPIES = 11

    def __init__(self, spot, source, place, send, recv):
        self.spot, self.source, self.place = spot, source, place
        self.send, self.recv = send, recv
        self.started = []

    def put(self, src, dst, number, to):
        copy = remote(src, dst, self.send.at[number], self.recv.at[number], self.spot.wide(to))
        copy.start()
        self.started.append(copy)

    def pass_on(self, who, half, number, to):
        place = self.place(who, half)
        self.put(place, place, number, to)

    def got(self, who, half, number):
        dst = self.place(who, half)
        remote(dst, dst, self.send.at[number], self.recv.at[number], self.spot.wide(self.spot.sib)).wait_recv()

    def begin(self):
        s = self.spot
        self.put(self.source(0), self.place(s.w, 0), 0, s.xn)
        self.put(self.source(1), self.place(s.w, 1), 2, s.yn)
        self.put(self.source(1), self.place(s.w, 1), 1, s.xn)
        self.put(self.source(0), self.place(s.w, 0), 3, s.yn)
        self.put(self.source(None), self.place(s.w, None), 4, s.sib)

    def middle(self):
        s = self.spot
        self.got(s.xn, 0, 0)
        self.pass_on(s.xn, 0, 5, s.yn)
        self.got(s.yn, 1, 2)
        self.pass_on(s.yn, 1, 6, s.xn)

    def late(self):
        s = self.spot
        self.got(s.xn, 1, 1)
        self.pass_on(s.xn, None, 7, s.sib)
        self.got(s.yn, 0, 3)
        self.pass_on(s.yn, None, 8, s.sib)

    def last(self):
        s = self.spot
        self.got(s.diag, 0, 5)
        self.pass_on(s.diag, 0, 9, s.sib)
        self.got(s.diag, 1, 6)
        self.pass_on(s.diag, 1, 10, s.sib)

    def finish(self):
        s = self.spot
        sib_x = s.sib + 2 - 4 * s.x
        sib_y = s.sib + 4 - 8 * s.y
        sib_d = sib_x + 4 - 8 * s.y
        self.got(s.sib, None, 4)
        self.got(sib_x, None, 7)
        self.got(sib_y, None, 8)
        self.got(sib_d, 0, 9)
        self.got(sib_d, 1, 10)
        for copy in self.started:
            copy.wait_send()


def gather_tokens(spot, own, out, base, send, recv):
    def part(ref, half):
        return ref if half is None else ref.at[pl.ds(half * SPAN, SPAN)]

    return PlaneGather(
        spot, lambda half: part(own, half), lambda who, half: part(out.at[base + who], half), send, recv
    )


def lane_half():
    lanes = lax.broadcasted_iota(jnp.int32, (1, 128), 1)
    return lax.rem(lanes, 64) < 32


def turn(values, first_half):
    return jnp.where(first_half, -pltpu.roll(values, 96, 1), pltpu.roll(values, 32, 1))


def turn_back(values, first_half):
    return jnp.where(first_half, pltpu.roll(values, 96, 1), -pltpu.roll(values, 32, 1))


def gather_gain(gains):
    lane = lax.broadcasted_iota(jnp.int32, (128, WIDTH), 0)
    column = lax.broadcasted_iota(jnp.int32, (128, WIDTH), 1)
    spread = (lax.rem(column, 32) == lane).astype(BF16)
    tiled = mm(gains.astype(BF16), spread)
    owner = lax.broadcasted_iota(jnp.int32, (32, WIDTH), 0)
    place = lax.broadcasted_iota(jnp.int32, (32, WIDTH), 1)
    return jnp.sum(jnp.where(lax.div(place, 32) == owner, tiled, 0.0), axis=0, keepdims=True)


class Attention:
    def __init__(self, x_ref, w_ref, seg_ref, cos_ref, sin_ref, freq_ref, gain_one, h1_ref, qkv_ref, lse_ref, o_ref, angle_ref):
        self.x_ref, self.seg_ref, self.cos_ref, self.sin_ref = x_ref, seg_ref, cos_ref, sin_ref
        self.h1_ref, self.qkv_ref, self.lse_ref, self.o_ref = h1_ref, qkv_ref, lse_ref, o_ref
        self.angle_ref = angle_ref
        self.gain_one = gain_one
        self.w_ref = w_ref
        self.first_half = lane_half()
        self.is_key = lax.broadcasted_iota(jnp.int32, (1, 128), 1) < 64
        self.starts, self.start_cos, self.start_sin = [], [], []
        for row in range(2):
            segs = [seg_ref[c, row : row + 1, :] for c in range(WIDE)]
            starts = [jnp.zeros((1, 1), F32)]
            for doc in range(5):
                total = jnp.zeros((1, 128), F32)
                for seg in segs:
                    total = total + jnp.where(seg == doc, 1.0, 0.0)
                starts.append(starts[-1] + jnp.sum(total, axis=1, keepdims=True))
            angle = jnp.concatenate(starts + starts[:2], axis=0) * freq_ref[0:1, :]
            self.starts.append(starts)
            self.start_cos.append(jnp.cos(angle))
            self.start_sin.append(jnp.sin(angle))

    def chunk(self, row, i):
        tokens = pl.ds(i * 256, 256)
        starts, start_cos, start_sin = self.starts[row], self.start_cos[row], self.start_sin[row]
        seg_cols = []
        for part in range(2):
            seg = self.seg_ref[2 * i + part, row : row + 1, :].astype(F32)
            seg_cols.append(jnp.transpose(jnp.broadcast_to(seg, (128, 128))))
        seg_col = jnp.concatenate(seg_cols, axis=0)
        start_col = jnp.zeros((256, 128), F32)
        cos_s = jnp.broadcast_to(start_cos[0:1], (256, 128))
        sin_s = jnp.broadcast_to(start_sin[0:1], (256, 128))
        for doc in range(1, 6):
            here = seg_col == float(doc)
            start_col = jnp.where(here, starts[doc], start_col)
            cos_s = jnp.where(here, start_cos[doc : doc + 1], cos_s)
            sin_s = jnp.where(here, start_sin[doc : doc + 1], sin_s)
        cos_t = self.cos_ref[tokens, :]
        sin_t = self.sin_ref[tokens, :]
        cosine = cos_t * cos_s + sin_t * sin_s
        sine = sin_t * cos_s - cos_t * sin_s
        self.angle_ref[row, tokens, 0:128] = cosine
        self.angle_ref[row, tokens, 128:256] = sine
        x = self.x_ref[2 * i : 2 * i + 2, row].reshape(256, WIDTH).astype(F32)
        scale = lax.rsqrt(jnp.mean(x * x, axis=1, keepdims=True) + EPSILON)
        h1 = (x * scale * self.gain_one).astype(BF16)
        self.h1_ref[row, tokens, :] = h1
        qkv = mm(h1, self.w_ref[...].reshape(WIDTH, 256))
        q = qkv[:, 0:128]
        kv = qkv[:, 128:256]
        q = (q * cosine + turn(q, self.first_half) * sine).astype(BF16)
        kv = jnp.where(self.is_key, kv * cosine + turn(kv, self.first_half) * sine, kv).astype(BF16)
        self.qkv_ref[row, tokens, 0:128] = q
        self.qkv_ref[row, tokens, 128:256] = kv
        length = 256 * (i + 1)
        keys = self.qkv_ref[row, 0:length, 128:192]
        values = self.qkv_ref[row, 0:length, 192:256]
        place_key = lax.broadcasted_iota(jnp.int32, (256, length), 1).astype(F32)
        place_query = (lax.broadcasted_iota(jnp.int32, (256, length), 0) + 256 * i).astype(F32)
        allowed = (place_key <= place_query) & (place_key >= start_col[:, 0:1])
        outs, logs = [], []
        for head in range(2):
            query = q[:, 64 * head : 64 * head + 64]
            scores = jnp.where(allowed, mm(query, keys, NT) * (HEAD_DIM**-0.5), MASKED)
            top = jnp.max(scores, axis=1, keepdims=True)
            log_total = top + jnp.log(jnp.sum(jnp.exp(scores - top), axis=1, keepdims=True))
            outs.append(mm(jnp.exp(scores - log_total).astype(BF16), values))
            logs.append(log_total)
        self.o_ref[row, tokens, :] = jnp.concatenate(outs, axis=1).astype(BF16)
        self.lse_ref[row, tokens, :] = jnp.where(
            self.is_key, jnp.where(self.first_half, logs[0], start_col), logs[1]
        )


def piece_copies(spot, gu_ref, down_ref, e, kind, target, send, recv, number, first=0, last=384):
    pair = lax.div(spot.n, 2)
    plane = spot.n if kind == 2 else spot.mate
    if kind >= 2:
        plane = plane + 2 - 4 * pair
    half = spot.half if kind == 2 else 1 - spot.half
    to = (plane, spot.w)
    copies = []
    for part, (ref, start, rows) in enumerate(((gu_ref, 0, 256), (down_ref, 256, 128))):
        low, high = max(first, start), min(last, start + rows)
        if low < high:
            copies.append(
                remote(
                    ref.at[2 * half + e, pl.ds(low - start, high - low)], target.at[pl.ds(low - first, high - low)],
                    send.at[number + part], recv.at[number + part], to,
                )
            )
    return copies


def start_all(copies):
    for copy in copies:
        copy.start()


def forward_kernel(
    x_in, dy_ref, seg_in, wq_in, wk_in, wv_in, wo_in, router_in, gain_one_in, gain_two_in,
    cos_ref, sin_ref, freq_ref, ids_ref, gu_ref, down_ref,
    h1_out, qkv_ref, lse_ref, o_ref, angle_ref, gain_ref, mid_ref, gate_ref, w_all, w_ref, w_own,
    h2_all, dy_all, table_all, mate_0, far_0, far_mate_0, mate_1, far_1, far_mate_early_1,
    x_ref, g_ref, seg_ref, wo_ref, dy_mate, g_own, seg_own, wo_own, h1_ref, o_full, h2_own, table_own,
    xs, xr, ws, wr, gs, gr, ss, sr, cs, cr, ds, dr, early,
    os, orv, w_send, w_recv, a_send, a_recv, b_send, b_recv, s0, r0, s1, r1, ts, tr, zs, zr, es, er, local,
):
    spot = Spot()
    everyone = NARROW * WIDE
    for head in range(WIDE):
        at = 256 * head
        w_own[:, at : at + 128] = wq_in[:, 128 * head : 128 * head + 128]
        w_own[:, at + 128 : at + 256] = jnp.concatenate(
            [wk_in[:, 64 * head : 64 * head + 64], wv_in[:, 64 * head : 64 * head + 64]], axis=1
        )
    wo_own[:, 0:WIDTH] = wo_in[...]
    wo_own[:, WIDTH : WIDTH + 128] = jnp.concatenate([router_in[...], jnp.zeros((32, 96), BF16)], axis=1)
    g_own[...] = jnp.zeros_like(g_own)
    g_own[0:1, 0:32] = gain_one_in[...].astype(F32)
    g_own[1:2, 0:32] = gain_two_in[...].astype(F32)
    seg_own[...] = jnp.zeros_like(seg_own)
    seg_own[0:2, :] = seg_in[...]
    spot.greet(everyone)

    def others(step):
        other = lax.rem(spot.me + step, everyone)
        return other, lax.div(other, WIDE), lax.rem(other, WIDE)

    def columns_of(o_w):
        return w_own.at[:, pl.ds(pl.multiple_of(o_w * 256, 256), 256)]

    def weights(step, arriving):
        other, o_n, o_w = others(step)
        place = other if arriving else spot.me
        return (
            remote(columns_of(o_w), w_ref.at[place], ws.at[other], wr.at[place], (o_n, o_w)),
            remote(g_own, g_ref.at[place], gs.at[other], gr.at[place], (o_n, o_w)),
        )

    def documents(step, arriving):
        other = lax.rem(spot.w + step, WIDE)
        place = other if arriving else spot.w
        return remote(seg_own, seg_ref.at[place], ss.at[other], sr.at[place], spot.wide(other))

    def column(step, arriving):
        other = lax.rem(spot.n + step, NARROW)
        place = other if arriving else spot.n
        return remote(wo_own, wo_ref.at[place], cs.at[other], cr.at[place], (other, spot.w))

    def start_weights_out(step, carry):
        start_all(weights(step, False))
        return carry

    def start_column(step, carry):
        column(step, False).start()
        return carry

    def start_documents(step, carry):
        documents(step, False).start()
        return carry

    def wait_weights(step, carry):
        for copy in weights(step, False):
            copy.wait_send()
        for copy in weights(step, True):
            copy.wait_recv()
        return carry

    def wait_column(step, carry):
        column(step, False).wait_send()
        column(step, True).wait_recv()
        return carry

    def wait_documents(step, carry):
        documents(step, False).wait_send()
        documents(step, True).wait_recv()
        return carry

    x_gather = PlaneGather(
        spot,
        lambda half: x_in if half is None else x_in.at[half],
        lambda who, half: x_ref.at[who] if half is None else x_ref.at[who, half],
        xs, xr,
    )
    lax.fori_loop(1, WIDE, start_documents, 0)
    lax.fori_loop(1, everyone, start_weights_out, 0)
    x_gather.begin()
    lax.fori_loop(1, NARROW, start_column, 0)
    dy_across = remote(dy_ref, dy_mate, ds.at[0], dr.at[0], (spot.mate, spot.w))
    dy_across.start()
    mine = [
        pltpu.make_async_copy(x_in, x_ref.at[spot.w], early.at[0]),
        pltpu.make_async_copy(columns_of(spot.w), w_ref.at[spot.me], early.at[1]),
        pltpu.make_async_copy(g_own, g_ref.at[spot.me], early.at[2]),
        pltpu.make_async_copy(seg_own, seg_ref.at[spot.w], early.at[3]),
        pltpu.make_async_copy(wo_own, wo_ref.at[spot.n], early.at[4]),
    ]
    start_all(mine)
    mate_base = (1 - spot.half) * WIDE
    own_base = spot.half * WIDE
    mate_slot = mate_base + spot.w

    def w_source(half):
        return wo_ref if half is None else wo_ref.at[pl.ds(2 * half, 2)]

    def w_place(who, half):
        return w_all.at[:, who] if half is None else w_all.at[pl.ds(2 * half, 2), who]

    w_gather = PlaneGather(spot, w_source, w_place, w_send, w_recv)
    dy_gather = gather_tokens(spot, dy_ref, dy_all, own_base, a_send, a_recv)
    mate_dy_gather = gather_tokens(spot, dy_mate, dy_all, mate_base, b_send, b_recv)
    x_gather.middle()
    first_expert = piece_copies(spot, gu_ref, down_ref, 0, 2, far_0, es, er, 0)
    first_expert += piece_copies(spot, gu_ref, down_ref, 0, 3, far_mate_0, es, er, 2)
    first_expert += piece_copies(spot, gu_ref, down_ref, 0, 1, mate_0, es, er, 4)
    start_all(first_expert)
    x_gather.late()
    x_gather.last()
    lax.fori_loop(1, WIDE, wait_documents, 0)
    lax.fori_loop(1, everyone, wait_weights, 0)
    lax.fori_loop(1, NARROW, wait_column, 0)
    for copy in mine:
        copy.wait()
    w_gather.begin()
    dy_gather.begin()

    x_gather.finish()
    keep = [
        pltpu.make_async_copy(wo_ref, w_place(spot.w, None), local.at[0]),
        pltpu.make_async_copy(dy_ref, dy_all.at[spot.slot], local.at[1]),
    ]
    for copy in keep:
        copy.start()

    def heads(to, place):
        return (
            o_ref.at[:, pl.ds(to * SPAN, SPAN), :],
            o_full.at[:, :, pl.ds(pl.multiple_of(place * 128, 128), 128)],
        )

    def each_head_copy(to, act_local, act_remote):
        source, target = heads(to, spot.w)

        @pl.when(spot.w == to)
        def _():
            act_local(pltpu.make_async_copy(source, target, local.at[3]))

        @pl.when(spot.w != to)
        def _():
            act_remote(remote(source, target, os.at[to], orv.at[spot.w], spot.wide(to)))

    expert = lax.broadcasted_iota(jnp.int32, (32, TOKENS), 0).astype(F32)
    named = jnp.zeros((32, TOKENS), F32)
    ids = jnp.concatenate([ids_ref[0], ids_ref[1]], axis=1).astype(F32)
    for k in range(TOP):
        named = jnp.where(expert == ids[k : k + 1, :], 1.0, named)
    before = lax.broadcasted_iota(jnp.int32, (TOKENS, TOKENS), 0) < lax.broadcasted_iota(
        jnp.int32, (TOKENS, TOKENS), 1
    )
    places = mm(named.astype(BF16), jnp.where(before, 1.0, 0.0).astype(BF16))
    kept = jnp.where((named > 0.5) & (places < float(CAP)), places, -1.0)

    gains = g_ref[...]
    gain_one = gather_gain(gains[:, 0, :])
    gain_two = gather_gain(gains[:, 1, :])
    gain_ref[...] = jnp.concatenate([gain_one, gain_two, jnp.zeros((6, WIDTH), F32)], axis=0)
    attention = Attention(
        x_ref, w_ref, seg_ref, cos_ref, sin_ref, freq_ref, gain_one,
        h1_ref, qkv_ref, lse_ref, o_ref, angle_ref,
    )
    between = {1: [w_gather.middle], 2: [w_gather.late, dy_gather.middle], 3: [w_gather.last, dy_gather.late]}
    for i in range(4):
        for row in range(2):
            attention.chunk(row, i)
        for to in (2 * i, 2 * i + 1):
            each_head_copy(to, lambda copy: copy.start(), lambda copy: copy.start())
        for step in between.get(i, []):
            step()
    far = piece_copies(spot, gu_ref, down_ref, 1, 2, far_1, es, er, 6)
    near = piece_copies(spot, gu_ref, down_ref, 1, 1, mate_1, es, er, 8)
    far_mate = piece_copies(spot, gu_ref, down_ref, 1, 3, far_mate_early_1, es, er, 10, last=MIDDLE)
    h1_copy = pltpu.make_async_copy(h1_ref, h1_out, local.at[4])
    h1_copy.start()
    dy_gather.last()
    dy_across.wait_send()
    dy_across.wait_recv()
    keep_mate = pltpu.make_async_copy(dy_mate, dy_all.at[mate_slot], local.at[2])
    keep_mate.start()
    mate_dy_gather.begin()
    w_gather.finish()
    keep[0].wait()
    for to in range(WIDE):
        each_head_copy(to, lambda copy: copy.wait(), lambda copy: copy.wait_send())

    def wait_heads(step, carry):
        other = lax.rem(spot.w + step, WIDE)
        target = o_full.at[:, :, pl.ds(pl.multiple_of(other * 128, 128), 128)]
        remote(target, target, os.at[0], orv.at[other], spot.wide(other)).wait_recv()
        return carry

    lax.fori_loop(1, WIDE, wait_heads, 0)
    attended = o_full[...].reshape(TOKENS, WIDTH)
    x_own = x_ref[spot.w].reshape(TOKENS, WIDTH).astype(F32)
    mid = x_own + mm(attended, w_all[:, :, :, 0:WIDTH].reshape(WIDTH, WIDTH))
    mid_ref[...] = mid
    scale = lax.rsqrt(jnp.mean(mid * mid, axis=1, keepdims=True) + EPSILON)
    h2 = (mid * scale * gain_two).astype(BF16)
    h2_own[...] = h2
    across = remote(h2_own, h2_all.at[spot.slot], zs.at[0], zr.at[0], (spot.mate, spot.w))
    across.start()
    first = gather_tokens(spot, h2_own, h2_all, own_base, s0, r0)
    first.begin()
    keep_own = pltpu.make_async_copy(h2_own, h2_all.at[spot.slot], local.at[5])
    keep_own.start()

    logits = jnp.transpose(mm(h2, w_all[:, :, :, WIDTH : WIDTH + 128].reshape(WIDTH, 128)))[0:32]
    chosen = jnp.where(named > 0.5, logits, MASKED)
    rise = jnp.where(named > 0.5, jnp.exp(chosen - jnp.max(chosen, axis=0, keepdims=True)), 0.0)
    gate = rise / jnp.sum(rise, axis=0, keepdims=True)
    gate_ref[0:32, :] = gate
    gate_ref[32:64, :] = named
    for owner in range(GROUP):
        table_own[owner, 0:2, :] = kept[2 * owner : 2 * owner + 2]
        table_own[owner, 2:4, :] = gate[2 * owner : 2 * owner + 2]
        table_own[owner, 4:8, :] = jnp.zeros((4, TOKENS), F32)

    def tables(step, arriving):
        other = lax.rem(spot.slot + step, GROUP)
        o_half, o_w = lax.div(other, WIDE), lax.rem(other, WIDE)
        place = other if arriving else spot.slot
        return remote(
            table_own.at[2 * o_w + o_half], table_all.at[place], ts.at[other], tr.at[place],
            (spot.n - spot.half + o_half, o_w),
        )

    def start_table(step, carry):
        tables(step, False).start()
        return carry

    lax.fori_loop(1, GROUP, start_table, 0)
    table_mine = pltpu.make_async_copy(
        table_own.at[2 * spot.w + spot.half], table_all.at[spot.slot], local.at[6]
    )
    table_mine.start()

    mate_dy_gather.middle()
    mate_dy_gather.late()
    start_all(far)
    first.middle()
    mate_dy_gather.last()
    first.late()
    first.last()
    arriving = h2_all.at[mate_slot]
    remote(arriving, arriving, zs.at[0], zr.at[0], (spot.mate, spot.w)).wait_recv()
    second = gather_tokens(spot, arriving, h2_all, mate_base, s1, r1)
    second.begin()
    start_all(far_mate + near)
    second.middle()
    second.late()
    second.last()

    def wait_table(step, carry):
        tables(step, False).wait_send()
        tables(step, True).wait_recv()
        return carry

    lax.fori_loop(1, GROUP, wait_table, 0)
    dy_gather.finish()
    mate_dy_gather.finish()
    first.finish()
    second.finish()
    across.wait_send()
    keep[1].wait()
    keep_mate.wait()
    keep_own.wait()
    table_mine.wait()
    h1_copy.wait()
    for copy in first_expert + far + far_mate + near:
        copy.wait_send()
        copy.wait_recv()


def forward_call(*operands):
    dma = pltpu.SemaphoreType.DMA
    copies = PlaneGather.COPIES
    everyone = NARROW * WIDE
    return pl.pallas_call(
        forward_kernel,
        name="forward",
        out_shape=(
            jax.ShapeDtypeStruct((2, SEQ, WIDTH), BF16),
            jax.ShapeDtypeStruct((2, SEQ, 256), BF16),
            jax.ShapeDtypeStruct((2, SEQ, 128), F32),
            jax.ShapeDtypeStruct((2, SEQ, 128), BF16),
            jax.ShapeDtypeStruct((2, SEQ, 256), F32),
            jax.ShapeDtypeStruct((8, WIDTH), F32),
            jax.ShapeDtypeStruct((TOKENS, WIDTH), F32),
            jax.ShapeDtypeStruct((64, TOKENS), F32),
            jax.ShapeDtypeStruct((NARROW, WIDE, 32, WIDTH + 128), BF16),
            jax.ShapeDtypeStruct((everyone, 32, 256), BF16),
            jax.ShapeDtypeStruct((32, 2 * WIDTH), BF16),
            jax.ShapeDtypeStruct((GROUP, TOKENS, WIDTH), BF16),
            jax.ShapeDtypeStruct((GROUP, TOKENS, WIDTH), BF16),
            jax.ShapeDtypeStruct((GROUP, 8, TOKENS), F32),
        )
        + tuple(jax.ShapeDtypeStruct((depth, WIDTH), BF16) for depth in (384, 384, 384, 384, 384, MIDDLE)),
        in_specs=[IN_VMEM] * 14 + [IN_HBM, IN_HBM],
        out_specs=(IN_HBM,) + (IN_VMEM,) * 10 + (IN_HBM,) * 9,
        scratch_shapes=[
            pltpu.VMEM((WIDE, 2, SPAN, WIDTH), BF16),
            pltpu.VMEM((everyone, 8, 128), F32),
            pltpu.VMEM((WIDE, 8, 128), jnp.int32),
            pltpu.VMEM((NARROW, 32, WIDTH + 128), BF16),
            pltpu.VMEM((TOKENS, WIDTH), BF16),
            pltpu.VMEM((8, 128), F32),
            pltpu.VMEM((8, 128), jnp.int32),
            pltpu.VMEM((32, WIDTH + 128), BF16),
            pltpu.VMEM((2, SEQ, WIDTH), BF16),
            pltpu.VMEM((2, SPAN, WIDTH), BF16),
            pltpu.VMEM((TOKENS, WIDTH), BF16),
            pltpu.VMEM((GROUP, 8, TOKENS), F32),
            dma((copies,)),
            dma((copies,)),
        ]
        + [dma((everyone,))] * 4
        + [dma((WIDE,))] * 2
        + [dma((NARROW,))] * 2
        + [dma((1,)), dma((1,)), dma((5,)), dma((WIDE,)), dma((WIDE,))]
        + [dma((copies,))] * 10
        + [dma((GROUP,)), dma((GROUP,)), dma((1,)), dma((1,)), dma((12,)), dma((12,)), dma((7,))],
        compiler_params=pltpu.CompilerParams(collective_id=1, has_side_effects=True, vmem_limit_bytes=VMEM_BYTES),
        cost_estimate=duration(1),
    )(*operands)


def load_quarters(own, pieces, w_gu, w_down, sems):
    n = lax.axis_index("narrow")
    half, pair = lax.rem(n, 2), lax.div(n, 2)
    mate = n + 1 - 2 * half
    far = n + 2 - 4 * pair
    far_mate = mate + 2 - 4 * pair
    copies = []
    for quarter, parts in zip((n, mate, far, far_mate), (own,) + pieces):
        first = 0
        for part in parts if isinstance(parts, tuple) else (parts,):
            depth = part.shape[0]
            for start, rows, target in ((0, 256, w_gu), (256, 128, w_down)):
                low, high = max(first, start), min(first + depth, start + rows)
                if low < high:
                    place = quarter * rows + (low - start)
                    copies.append(
                        pltpu.make_async_copy(
                            part.at[pl.ds(low - first, high - low)],
                            target.at[pl.ds(pl.multiple_of(place, 32), high - low)],
                            sems.at[len(copies)],
                        )
                    )
            first += depth
    return copies


def pick(table_ref, source, expert):
    slot = lax.broadcasted_iota(jnp.int32, (SLOTS, TOKENS), 0).astype(F32)
    return slot == table_ref[source, expert : expert + 1, :]


STEPS = GROUP // CHUNK
ROWS = CHUNK * SLOTS


def start_weights(e, gu_ref, down_ref, pieces, w_gu, w_down, gu_sum, down_sum, sems):
    mine = 2 * lax.rem(lax.axis_index("narrow"), 2) + e
    copies = load_quarters((gu_ref.at[mine], down_ref.at[mine]), pieces, w_gu, w_down, sems)
    for copy in copies:
        copy.start()
    gu_sum[...] = jnp.zeros_like(gu_sum)
    down_sum[...] = jnp.zeros_like(down_sum)
    for copy in copies:
        copy.wait()


def slot_gates(table_ref, masks, e):
    return jnp.concatenate(
        [
            jnp.sum(jnp.where(masks[s], table_ref[s, 2 + e : 3 + e, :], 0.0), axis=1, keepdims=True)
            for s in range(CHUNK)
        ],
        axis=0,
    )


def expert_math(rows, grad_rows, gates, w_gu, w_down, gu_sum, down_sum):
    g = mm(rows, w_gu[:, 0:FF])
    u = mm(rows, w_gu[:, FF : 2 * FF])
    sigmoid = 1.0 / (1.0 + jnp.exp(-g))
    active = g * sigmoid
    hidden = (active * u).astype(BF16)
    grad_rows = grad_rows.astype(F32)
    dy_pair = (grad_rows * gates).astype(BF16)
    dhid = mm(dy_pair, w_down[...], NT)
    da_g = (dhid * u * (sigmoid * (1.0 + g * (1.0 - sigmoid)))).astype(BF16)
    da_u = (dhid * active).astype(BF16)
    y = mm(hidden, w_down[...]).astype(BF16).astype(F32)
    slot_dgate = jnp.sum(y * grad_rows, axis=1, keepdims=True)
    down_sum[...] += mm(hidden, dy_pair, TN)
    gu_sum[:, 0:FF] += mm(rows, da_g, TN)
    gu_sum[:, FF : 2 * FF] += mm(rows, da_u, TN)
    dx = (mm(da_g, w_gu[:, 0:FF], NT) + mm(da_u, w_gu[:, FF : 2 * FF], NT)).astype(BF16)
    return (y * gates).astype(BF16), dx, slot_dgate


def token_dgate(dgate_ref, masks, slot_dgate, e):
    for s in range(CHUNK):
        part = slot_dgate[s * SLOTS : (s + 1) * SLOTS]
        dgate_ref[s, e : e + 1, :] = jnp.sum(jnp.where(masks[s], part, 0.0), axis=0, keepdims=True)


def store_quarters(outs, gu_sum, down_sum):
    n = lax.axis_index("narrow")
    half, pair = lax.rem(n, 2), lax.div(n, 2)
    mate = n + 1 - 2 * half
    far = n + 2 - 4 * pair
    far_mate = mate + 2 - 4 * pair
    for out, quarter in zip(outs, (n, mate, far, far_mate)):
        out[0:256, :] = gu_sum[pl.ds(pl.multiple_of(quarter * 256, 256), 256), :].astype(BF16)
        out[256:384, :] = down_sum[pl.ds(pl.multiple_of(quarter * 128, 128), 128), :].astype(BF16)


def expert_0_kernel(
    h2_ref, dy_ref, table_ref, gu_ref, down_ref, w1, w2, w3,
    gated_ref, dx_ref, rows_ref, grad_rows_ref, dgate_ref, own, mate, far, far_mate, far_mate_1,
    w_gu, w_down, gu_sum, down_sum, sems, es, er,
):
    step = pl.program_id(0)
    spot = Spot()
    second_expert = piece_copies(spot, gu_ref, down_ref, 1, 3, far_mate_1, es, er, 0, first=MIDDLE)

    @pl.when(step == 0)
    def _():
        barrier = pltpu.get_barrier_semaphore()
        plane = spot.mate + 2 - 4 * lax.div(spot.n, 2)
        pl.semaphore_signal(barrier, inc=1, device_id=(plane, spot.w), device_id_type=MESH)
        pl.semaphore_wait(barrier, 1)
        start_all(second_expert)
        start_weights(0, gu_ref, down_ref, (w1, w2, w3), w_gu, w_down, gu_sum, down_sum, sems)

    masks = [[pick(table_ref, s, e) for s in range(CHUNK)] for e in range(MINE)]
    rows, grad_rows = [], []
    for s in range(CHUNK):
        hot = jnp.concatenate([jnp.where(masks[e][s], 1.0, 0.0) for e in range(MINE)], axis=0).astype(BF16)
        rows.append(mm(hot, h2_ref[s]).astype(BF16))
        grad_rows.append(mm(hot, dy_ref[s]).astype(BF16))
    for s in range(CHUNK):
        rows_ref[0, s * SLOTS : (s + 1) * SLOTS, :] = rows[s][SLOTS:]
        grad_rows_ref[0, s * SLOTS : (s + 1) * SLOTS, :] = grad_rows[s][SLOTS:]
    rows = jnp.concatenate([r[:SLOTS] for r in rows], axis=0)
    grad_rows = jnp.concatenate([r[:SLOTS] for r in grad_rows], axis=0)
    gated, dx, slot_dgate = expert_math(
        rows, grad_rows, slot_gates(table_ref, masks[0], 0), w_gu, w_down, gu_sum, down_sum
    )
    gated_ref[0] = gated
    dx_ref[0] = dx
    dgate_ref[...] = jnp.zeros_like(dgate_ref)
    token_dgate(dgate_ref, masks[0], slot_dgate, 0)

    @pl.when(step == STEPS - 1)
    def _():
        store_quarters((own, mate, far, far_mate), gu_sum, down_sum)
        for copy in second_expert:
            copy.wait_send()
            copy.wait_recv()


def expert_1_kernel(
    rows_ref, grad_rows_ref, gated_before, dx_before, dgate_before, table_ref, gu_ref, down_ref, w1, w2, w3_early, w3_rest,
    y_here, y_there, part_here, part_there, dgate_ref, own, mate, far, far_mate,
    w_gu, w_down, gu_sum, down_sum, sems, held, local, send, recv,
):
    step = pl.program_id(0)
    spot = Spot()
    slot = lax.rem(step, 2)
    outs = ((y_here, y_there), (part_here, part_there))

    def copies(at_step, at_slot):
        result = []
        for kind, (here, there) in enumerate(outs):
            for pair in range(CHUNK // 2):
                block = at_step * (CHUNK // 2) + pair
                source = held.at[kind, at_slot]
                result.append(
                    pltpu.make_async_copy(
                        source.at[2 * pair + spot.core], here.at[block], local.at[kind, at_slot, pair]
                    )
                )
                other = source.at[2 * pair + 1 - spot.core]
                if kind == 0:
                    result.append(pltpu.make_async_copy(other, there.at[block], send.at[kind, at_slot, pair]))
                else:
                    result.append(
                        remote(
                            other, there.at[block], send.at[kind, at_slot, pair], recv.at[block],
                            spot.wide(spot.sib),
                        )
                    )
        return result

    def finish(at_step, at_slot):
        done = copies(at_step, at_slot)
        for number, copy in enumerate(done):
            if number % 2 == 1 and number >= CHUNK:
                copy.wait_send()
            else:
                copy.wait()

    @pl.when(step == 0)
    def _():
        barrier = pltpu.get_barrier_semaphore()
        pl.semaphore_signal(barrier, inc=1, device_id=spot.wide(spot.sib), device_id_type=MESH)
        pl.semaphore_wait(barrier, 1)
        start_weights(1, gu_ref, down_ref, (w1, w2, (w3_early, w3_rest)), w_gu, w_down, gu_sum, down_sum, sems)

    masks = [[pick(table_ref, s, e) for s in range(CHUNK)] for e in range(MINE)]
    gated, dx, slot_dgate = expert_math(
        rows_ref[0], grad_rows_ref[0], slot_gates(table_ref, masks[1], 1), w_gu, w_down, gu_sum, down_sum
    )
    dgate_ref[...] = dgate_before[...]
    token_dgate(dgate_ref, masks[1], slot_dgate, 1)

    @pl.when(step >= 2)
    def _():
        finish(step - 2, slot)

    for s in range(CHUNK):
        at = slice(s * SLOTS, (s + 1) * SLOTS)
        hot = jnp.concatenate([jnp.where(masks[e][s], 1.0, 0.0) for e in range(MINE)], axis=0).astype(BF16)
        held[0, slot, s] = mm(hot, jnp.concatenate([gated_before[0, at, :], gated[at]], axis=0), TN).astype(BF16)
        held[1, slot, s] = mm(hot, jnp.concatenate([dx_before[0, at, :], dx[at]], axis=0), TN).astype(BF16)
    start_all(copies(step, slot))

    @pl.when(step == STEPS - 1)
    def _():
        store_quarters((own, mate, far, far_mate), gu_sum, down_sum)
        for last in (STEPS - 2, STEPS - 1):
            finish(last, last % 2)
        for block in range(WIDE):
            place = part_there.at[block]
            remote(place, place, send.at[0, 0, 0], recv.at[block], spot.wide(spot.sib)).wait_recv()


def expert_specs():
    block = pl.BlockSpec((CHUNK, TOKENS, WIDTH), lambda c: (c, 0, 0))
    small = pl.BlockSpec((CHUNK, 8, TOKENS), lambda c: (c, 0, 0))
    slots = pl.BlockSpec((1, ROWS, WIDTH), lambda c: (c, 0, 0))
    quarter = pl.BlockSpec((384, WIDTH), lambda c: (0, 0))
    return block, small, slots, quarter


def expert_scratch():
    return [
        pltpu.VMEM((WIDTH, 2 * FF), BF16),
        pltpu.VMEM((FF, WIDTH), BF16),
        pltpu.VMEM((WIDTH, 2 * FF), F32),
        pltpu.VMEM((FF, WIDTH), F32),
        pltpu.SemaphoreType.DMA((10,)),
    ]


SLOT_ROWS = jax.ShapeDtypeStruct((STEPS, ROWS, WIDTH), BF16)
CORE_BLOCKS = jax.ShapeDtypeStruct((WIDE, TOKENS, WIDTH), BF16)
TABLES = jax.ShapeDtypeStruct((GROUP, 8, TOKENS), F32)
QUARTER = jax.ShapeDtypeStruct((384, WIDTH), BF16)


def expert_0_call(h2_all, dy_all, table_all, w_gate_up, w_down, pieces):
    block, small, slots, quarter = expert_specs()
    return pl.pallas_call(
        expert_0_kernel,
        name="expert_0",
        grid=(STEPS,),
        out_shape=(SLOT_ROWS,) * 4
        + (TABLES,)
        + (QUARTER,) * 4
        + (jax.ShapeDtypeStruct((384 - MIDDLE, WIDTH), BF16),),
        in_specs=[block, block, small] + [IN_HBM] * 5,
        out_specs=(slots,) * 4 + (small,) + (quarter,) * 4 + (IN_HBM,),
        scratch_shapes=expert_scratch() + [pltpu.SemaphoreType.DMA((2,)), pltpu.SemaphoreType.DMA((2,))],
        compiler_params=pltpu.CompilerParams(collective_id=4, has_side_effects=True, vmem_limit_bytes=VMEM_BYTES),
        cost_estimate=duration(1),
    )(h2_all, dy_all, table_all, w_gate_up, w_down, *pieces)


def expert_1_call(rows, grad_rows, gated, dx, dgate, table_all, w_gate_up, w_down, pieces):
    block, small, slots, quarter = expert_specs()
    return pl.pallas_call(
        expert_1_kernel,
        name="expert_1",
        grid=(STEPS,),
        out_shape=(CORE_BLOCKS,) * 4 + (TABLES,) + (QUARTER,) * 4,
        in_specs=[slots] * 4 + [small, small] + [IN_HBM] * 6,
        out_specs=(IN_HBM,) * 4 + (small,) + (quarter,) * 4,
        scratch_shapes=expert_scratch()
        + [
            pltpu.VMEM((2, 2, CHUNK, TOKENS, WIDTH), BF16),
            pltpu.SemaphoreType.DMA((2, 2, CHUNK // 2)),
            pltpu.SemaphoreType.DMA((2, 2, CHUNK // 2)),
            pltpu.SemaphoreType.DMA((WIDE,)),
        ],
        compiler_params=pltpu.CompilerParams(collective_id=5, has_side_effects=True, vmem_limit_bytes=VMEM_BYTES),
        cost_estimate=duration(1),
    )(rows, grad_rows, gated, dx, dgate, table_all, w_gate_up, w_down, *pieces)


RESULTS = 6


def results_kernel(*refs):
    pieces, arrays, small = refs[:8], refs[8 : 8 + RESULTS], refs[8 + RESULTS : 11 + RESULTS]
    refs = refs[11 + RESULTS :]
    gate_up_ref, down_ref, outs, small_outs = refs[0], refs[1], refs[2 : 2 + RESULTS], refs[2 + RESULTS : 6 + RESULTS]
    refs = refs[6 + RESULTS :]
    loaded, totals, held, sems, out_sems, held_sems = refs[0], refs[1], refs[2 : 2 + RESULTS], *refs[2 + RESULTS :]
    half = lax.rem(lax.axis_index("narrow"), 2)
    loads = [pltpu.make_async_copy(piece, loaded.at[i], sems.at[i]) for i, piece in enumerate(pieces)]
    through = [pltpu.make_async_copy(a, h, held_sems.at[i]) for i, (a, h) in enumerate(zip(arrays, held))]
    start_all([loads[i] for i in (0, 2, 1, 3, 4, 6, 5, 7)])
    start_all(through)
    router, gains, load = small
    small_outs[0][...] = router[...]
    small_outs[1][...] = gains[0:1, :]
    small_outs[2][...] = gains[1:2, :]
    small_outs[3][...] = load[...]
    stores = []
    for e in range(2):
        for which in range(2):
            left, right = 4 * e + which, 4 * e + which + 2
            loads[left].wait()
            loads[right].wait()
            number = 2 * e + which
            place = 2 * (half if which == 0 else 1 - half) + e
            totals[number] = loaded[left].astype(F32) + loaded[right].astype(F32)
            for part, (out, first, depth) in enumerate(((gate_up_ref, 0, 256), (down_ref, 256, 128))):
                copy = pltpu.make_async_copy(
                    totals.at[number, pl.ds(first, depth)], out.at[place], out_sems.at[2 * number + part]
                )
                copy.start()
                stores.append(copy)
    for i, copy in enumerate(through):
        copy.wait()
        copy = pltpu.make_async_copy(held[i], outs[i], held_sems.at[i])
        copy.start()
        stores.append(copy)
    for copy in stores:
        copy.wait()


def results_call(first, second, arrays, small):
    shapes = [jax.ShapeDtypeStruct(a.shape, a.dtype) for a in arrays]
    row = jax.ShapeDtypeStruct((1, 32), F32)
    return pl.pallas_call(
        results_kernel,
        name="results",
        out_shape=(
            jax.ShapeDtypeStruct((4, 256, WIDTH), F32),
            jax.ShapeDtypeStruct((4, 128, WIDTH), F32),
            *shapes,
            jax.ShapeDtypeStruct((32, 32), F32),
            row,
            row,
            jax.ShapeDtypeStruct((1, 32), jnp.int32),
        ),
        in_specs=[IN_HBM] * (8 + RESULTS) + [IN_VMEM] * 3,
        out_specs=(IN_HBM,) * (2 + RESULTS) + (IN_VMEM,) * 4,
        scratch_shapes=[pltpu.VMEM((8, 384, WIDTH), BF16), pltpu.VMEM((4, 384, WIDTH), F32)]
        + [pltpu.VMEM(s.shape, s.dtype) for s in shapes]
        + [pltpu.SemaphoreType.DMA((8,)), pltpu.SemaphoreType.DMA((8,)), pltpu.SemaphoreType.DMA((RESULTS,))],
        compiler_params=pltpu.CompilerParams(vmem_limit_bytes=VMEM_BYTES),
        cost_estimate=duration(1),
    )(*first, *second, *arrays, *small)


def widen(ref_value):
    return ref_value.astype(F32)


class PlaneReduce:
    COPIES = 10

    def __init__(self, spot, here, there, arrived, first, buffers, send, recv, local):
        self.spot, self.arrived = spot, arrived
        self.acc, self.from_core, self.from_one, self.from_two = buffers
        self.send, self.recv = send, recv
        self.started = []
        s = spot
        self.q_own = 2 * s.y + s.x
        self.q_x = 2 * s.y + 1 - s.x
        self.q_y = 2 - 2 * s.y + s.x
        self.q_d = 3 - self.q_own
        self.order = (self.q_d, self.q_x, self.q_y, self.q_own)
        self.loads = []
        for number, q in enumerate(self.order):
            mine = pltpu.make_async_copy(here.at[first + q], self.acc.at[q], local.at[number])
            if arrived:
                other = pltpu.make_async_copy(there.at[first + q], self.from_core.at[q], local.at[4 + number])
            else:
                other = remote(
                    there.at[first + q], self.from_core.at[q], send.at[6 + number], recv.at[6 + number], s.wide(s.sib)
                )
                self.started.append(other)
            self.loads.append((mine, other))

    def put(self, src, dst, number, to):
        copy = remote(src, dst, self.send.at[number], self.recv.at[number], self.spot.wide(to))
        copy.start()
        self.started.append(copy)

    def got(self, dst, number):
        remote(dst, dst, self.send.at[number], self.recv.at[number], self.spot.wide(self.spot.sib)).wait_recv()

    def begin(self):
        for pair in self.loads:
            start_all(pair)

    def add_core(self, number):
        mine, other = self.loads[number]
        mine.wait()
        other.wait() if self.arrived else other.wait_recv()
        q = self.order[number]
        self.acc[q] = self.acc[q] + self.from_core[q]

    def across_core(self):
        s = self.spot
        self.add_core(0)
        self.put(halves(self.acc.at[self.q_d], 0), self.from_one.at[1], 1, s.xn)
        self.put(halves(self.acc.at[self.q_d], 1), self.from_one.at[3], 3, s.yn)
        self.add_core(1)
        self.put(halves(self.acc.at[self.q_x], 0), self.from_one.at[0], 0, s.xn)
        self.add_core(2)
        self.put(halves(self.acc.at[self.q_y], 1), self.from_one.at[2], 2, s.yn)
        self.add_core(3)

    def across_one(self):
        s = self.spot
        self.got(self.from_one.at[1], 1)
        upper = halves(self.acc.at[self.q_y], 0)
        upper[...] = upper[...] + self.from_one[1]
        self.put(upper, self.from_two.at[0], 4, s.yn)
        self.got(self.from_one.at[3], 3)
        lower = halves(self.acc.at[self.q_x], 1)
        lower[...] = lower[...] + self.from_one[3]
        self.put(lower, self.from_two.at[1], 5, s.xn)

    def total(self, out):
        self.got(self.from_one.at[0], 0)
        self.got(self.from_two.at[0], 4)
        own = self.acc.at[self.q_own]
        out[0:SPAN, :] = widen(own[0:SPAN, :]) + widen(self.from_one[0]) + widen(self.from_two[0])
        self.got(self.from_one.at[2], 2)
        self.got(self.from_two.at[1], 5)
        out[SPAN:TOKENS, :] = widen(own[SPAN:TOKENS, :]) + widen(self.from_one[2]) + widen(self.from_two[1])

    def finish(self):
        for copy in self.started:
            copy.wait_send()


def halves(ref, which):
    return ref.at[pl.ds(which * SPAN, SPAN)]


class GroupReduce:
    def __init__(self, spot, here, there, arrived, scratch):
        acc, from_core, from_one, from_two, total, mate_send, mate_recv, send, recv, local, zs, zr = scratch
        self.total_ref, self.mate_send, self.mate_recv = total, mate_send, mate_recv
        parts = []
        for which, first in enumerate((4 * (1 - spot.half), 4 * spot.half)):
            buffers = (acc.at[which], from_core.at[which], from_one.at[which], from_two.at[which])
            parts.append(
                PlaneReduce(
                    spot, here, there, arrived, first, buffers, send.at[which], recv.at[which], local.at[which]
                )
            )
        self.theirs, self.ours = parts
        self.across = remote(mate_send, mate_recv, zs.at[0], zr.at[0], (spot.mate, spot.w))

    def begin(self):
        self.theirs.begin()
        self.ours.begin()

    def across_core(self):
        self.theirs.across_core()
        self.ours.across_core()

    def across_one(self):
        self.theirs.across_one()
        self.ours.across_one()

    def to_mate(self):
        self.theirs.total(self.total_ref)
        self.mate_send[...] = self.total_ref[...].astype(BF16)
        self.across.start()

    def finish(self):
        self.ours.total(self.total_ref)
        self.across.wait_recv()
        self.total_ref[...] += widen(self.mate_recv[...])
        self.theirs.finish()
        self.ours.finish()
        self.across.wait_send()


def reduce_scratch():
    dma = pltpu.SemaphoreType.DMA
    return [
        pltpu.VMEM((2, 4, TOKENS, WIDTH), BF16),
        pltpu.VMEM((2, 4, TOKENS, WIDTH), BF16),
        pltpu.VMEM((2, 4, SPAN, WIDTH), BF16),
        pltpu.VMEM((2, 2, SPAN, WIDTH), BF16),
        pltpu.VMEM((TOKENS, WIDTH), F32),
        pltpu.VMEM((TOKENS, WIDTH), BF16),
        pltpu.VMEM((TOKENS, WIDTH), BF16),
        dma((2, PlaneReduce.COPIES)),
        dma((2, PlaneReduce.COPIES)),
        dma((2, 8)),
        dma((1,)),
        dma((1,)),
    ]


REDUCE_REFS = 12


class AttentionBack:
    def __init__(self, dattn_all, w_rows, qkv_ref, lse_ref, o_ref, angle_ref, dqkv_ref, dkv_ref, dq_ref, osum):
        self.dattn_all, self.w_rows, self.qkv, self.lse, self.o = dattn_all, w_rows, qkv_ref, lse_ref, o_ref
        self.angle = angle_ref
        self.dqkv, self.dkv, self.dq, self.osum = dqkv_ref, dkv_ref, dq_ref, osum
        self.first_half = lane_half()
        self.is_key = lax.broadcasted_iota(jnp.int32, (1, 128), 1) < 64
        dkv_ref[...] = jnp.zeros_like(dkv_ref)
        osum[...] = jnp.zeros_like(osum)

    def stack(self, both):
        return jnp.concatenate([both[:, 0:64], both[:, 64:128]], axis=0)

    def chunk(self, row, q):
        first = pl.multiple_of(q * 256, 256)
        tokens = pl.ds(first, 256)
        dattn = self.dattn_all[pl.ds(2 * q, 2), pl.ds(row * SPAN, SPAN), :].reshape(256, WIDTH)
        outs = self.o[row, tokens, :]
        do = mm(dattn, self.w_rows[...], NT).astype(BF16)
        self.osum[...] += mm(outs, dattn, TN)
        inner = do.astype(F32) * outs.astype(F32)
        delta = jnp.concatenate(
            [
                jnp.sum(jnp.where(self.is_key, inner, 0.0), axis=1, keepdims=True),
                jnp.sum(jnp.where(self.is_key, 0.0, inner), axis=1, keepdims=True),
            ],
            axis=0,
        )
        query = self.stack(self.qkv[row, tokens, 0:128])
        do = self.stack(do)
        log_total = jnp.concatenate([self.lse[row, tokens, 0:1], self.lse[row, tokens, 64:65]], axis=0)
        start = self.lse[row, tokens, 32:33]
        start = jnp.concatenate([start, start], axis=0)
        place = lax.broadcasted_iota(jnp.int32, (256, 1), 0)
        place_query = (jnp.concatenate([place, place], axis=0) + q * 256).astype(F32)
        self.dq[...] = jnp.zeros_like(self.dq)

        def key_block(block, carry):
            keys_at = pl.ds(pl.multiple_of(block * 256, 256), 256)
            keys = self.qkv[row, keys_at, 128:192]
            values = self.qkv[row, keys_at, 192:256]
            place_key = (lax.broadcasted_iota(jnp.int32, (1, 256), 1) + block * 256).astype(F32)
            allowed = (place_key <= place_query) & (place_key >= start)
            scores = jnp.where(allowed, mm(query, keys, NT) * (HEAD_DIM**-0.5), MASKED)
            weights = jnp.exp(scores - log_total)
            dp = mm(do, values, NT)
            ds = (weights * (dp - delta)).astype(BF16)
            self.dq[...] += mm(ds, keys)
            dk = mm(ds, query, TN) * (HEAD_DIM**-0.5)
            dv = mm(weights.astype(BF16), do, TN)
            self.dkv[row, keys_at, :] += jnp.concatenate([dk, dv], axis=1)
            return carry

        lax.fori_loop(0, q + 1, key_block, 0)
        dq = jnp.concatenate([self.dq[0:256], self.dq[256:512]], axis=1) * (HEAD_DIM**-0.5)
        cosine = self.angle[row, tokens, 0:128]
        sine = self.angle[row, tokens, 128:256]
        self.dqkv[row, tokens, 0:128] = (dq * cosine + turn_back(dq * sine, self.first_half)).astype(BF16)

    def keys(self, row):
        cosine = self.angle[row, :, 0:128]
        sine = self.angle[row, :, 128:256]
        dkv = self.dkv[row]
        turned = dkv * cosine + turn_back(dkv * sine, self.first_half)
        self.dqkv[row, :, 128:256] = jnp.where(self.is_key, turned, dkv).astype(BF16)


def backward_kernel(*refs):
    (
        part_here, part_there, y_here, y_there, dgate_ref, h2_ref, w_out_ref, w_full_ref, h1_ref, qkv_ref, lse_ref, o_ref,
        angle_ref, mate_1, far_1, far_mate_1,
        x_ref, mid_ref, gate_ref, gain_ref, dy_ref, w_own, gain_col,
    ) = refs[:23]
    (
        block_out, in_grad, q_grad, k_grad, v_grad, o_grad, router_grad, two_gains, load_out, *quarters_recv,
    ) = refs[23:35]
    (
        dgate_all, h2_own, dattn_all, dmid_ref, small_ref, small_all, small_sum, w_router, w_rows, w_full,
        h1, qkv, lse, outs, angle, dqkv_ref, dkv_ref, dq_ref, osum, og_ref, wg_ref,
        dq_full, w_recv, o_held, s_held, o_recv, s_recv,
        ts, tr, s0, r0, bs, br, qs, qr, ks, kr, ws, wr, os, orv, ss, sr, gs, gr, local,
    ) = refs[35:81]
    h2_sum_refs = refs[81 : 81 + REDUCE_REFS]
    y_sum_refs = refs[81 + REDUCE_REFS :]

    spot = Spot()
    everyone = NARROW * WIDE
    h2_sum = GroupReduce(spot, part_here, part_there, True, h2_sum_refs)
    y_sum = GroupReduce(spot, y_here, y_there, False, y_sum_refs)
    h2_sum.begin()
    spot.greet(everyone)

    def tables(step, arriving):
        other = lax.rem(spot.slot + step, GROUP)
        o_half, o_w = lax.div(other, WIDE), lax.rem(other, WIDE)
        place = other if arriving else spot.slot
        return remote(
            dgate_ref.at[other], dgate_all.at[place], ts.at[other], tr.at[place],
            (spot.n - spot.half + o_half, o_w),
        )

    def start_table(step, carry):
        tables(step, False).start()
        return carry

    lax.fori_loop(1, GROUP, start_table, 0)
    rows = pl.ds(pl.multiple_of(spot.w * 128, 128), 128)
    loads = [
        (dgate_ref.at[spot.slot], dgate_all.at[spot.slot]),
        (h2_ref.at[spot.slot], h2_own),
        (w_out_ref.at[:, pl.ds(WIDTH, 128)], w_router),
        (w_out_ref.at[rows, pl.ds(0, WIDTH)], w_rows),
        (qkv_ref, qkv),
        (lse_ref, lse),
        (o_ref, outs),
        (angle_ref, angle),
        (h1_ref, h1),
    ]
    loads = [pltpu.make_async_copy(src, dst, local.at[i]) for i, (src, dst) in enumerate(loads)]
    w_loads = [pltpu.make_async_copy(w_full_ref.at[who], w_full.at[who], local.at[10 + who]) for who in range(WIDE)]
    h2_sum.theirs.across_core()
    start_all(loads + w_loads)
    y_sum.begin()
    h2_sum.theirs.across_one()
    h2_sum.ours.across_core()
    far_plane = 2 - 4 * lax.div(spot.n, 2)
    quarter_copies = [
        remote(piece, quarters_recv[number], gs.at[number], gr.at[number], (plane, spot.w))
        for number, (piece, plane) in enumerate(
            ((mate_1, spot.mate), (far_1, spot.n + far_plane), (far_mate_1, spot.mate + far_plane))
        )
    ]
    h2_sum.to_mate()
    h2_sum.ours.across_one()
    y_sum.across_core()
    h2_sum.finish()
    start_all(quarter_copies)

    def wait_table(step, carry):
        tables(step, False).wait_send()
        tables(step, True).wait_recv()
        return carry

    lax.fori_loop(1, GROUP, wait_table, 0)
    for copy in loads[:4]:
        copy.wait()

    gate = gate_ref[0:32, :]
    dgate = jnp.concatenate([dgate_all[(o % 2) * WIDE + o // 2, 0:2, :] for o in range(GROUP)], axis=0)
    dsel = gate * (dgate - jnp.sum(gate * dgate, axis=0, keepdims=True))
    dlogits = jnp.concatenate([dsel, jnp.zeros((96, TOKENS), F32)], axis=0)
    dh2 = h2_sum.total_ref[...] + mm(jnp.transpose(dlogits).astype(BF16), w_router[...], NT)
    mid = mid_ref[...]
    scale = lax.rsqrt(jnp.mean(mid * mid, axis=1, keepdims=True) + EPSILON)
    weighted = dh2 * gain_ref[1:2, :]
    inner = jnp.mean(weighted * mid, axis=1, keepdims=True)
    dmid = dy_ref[...].astype(F32) + weighted * scale - mid * (scale * scale * scale) * inner
    dmid_ref[...] = dmid
    dattn_all[spot.w] = dmid.astype(BF16)
    mine = dattn_all.at[spot.w]
    gather = PlaneGather(
        spot,
        lambda half: mine if half is None else halves(mine, half),
        lambda who, half: dattn_all.at[who] if half is None else halves(dattn_all.at[who], half),
        s0, r0,
    )
    gather.begin()
    small_ref[0:32, :] = mm(dsel.astype(BF16), h2_own[...])
    small_ref[32:33, :] = jnp.sum(dh2 * mid * scale, axis=0, keepdims=True)
    lane = lax.broadcasted_iota(jnp.int32, (32, WIDTH), 1)
    column = lax.broadcasted_iota(jnp.int32, (32, WIDTH), 0)
    count = jnp.sum(gate_ref[32:64, :], axis=1, keepdims=True)
    small_ref[33:34, :] = jnp.sum(jnp.where(lax.rem(lane, 128) == column, count, 0.0), axis=0, keepdims=True)
    small_ref[34:40, :] = jnp.zeros((6, WIDTH), F32)

    def lanes_to(step, arriving):
        other = lax.rem(spot.w + step, WIDE)
        place = other if arriving else spot.w
        return remote(
            small_ref.at[:, pl.ds(pl.multiple_of(other * 128, 128), 128)], small_all.at[place],
            bs.at[other], br.at[place], spot.wide(other),
        )

    def start_lanes(step, carry):
        lanes_to(step, False).start()
        return carry

    lax.fori_loop(1, WIDE, start_lanes, 0)
    small_all[spot.w] = small_ref[:, pl.ds(pl.multiple_of(spot.w * 128, 128), 128)]

    for copy in loads[4:8]:
        copy.wait()
    back = AttentionBack(dattn_all, w_rows, qkv, lse, outs, angle, dqkv_ref, dkv_ref, dq_ref, osum)
    order = h2_sum.ours
    sib_x = spot.sib + 2 - 4 * spot.x
    sib_y = spot.sib + 4 - 8 * spot.y
    sib_d = sib_x + 4 - 8 * spot.y

    def to_tokens(other, place, first, send, recv):
        return remote(
            dqkv_ref.at[:, pl.ds(pl.multiple_of(other * SPAN, SPAN), SPAN), pl.ds(first, 128)],
            dq_full.at[:, :, pl.ds(pl.multiple_of(place * 256 + first, 128), 128)],
            send.at[other], recv.at[place], spot.wide(other),
        )

    def send_queries(who):
        for other in who:
            to_tokens(other, spot.w, 0, qs, qr).start()

    gather.got(spot.sib, None, 4)
    back.chunk(0, order.q_own)
    gather.middle()
    back.chunk(1, order.q_own)
    send_queries((spot.sib,))
    gather.late()
    gather.got(sib_x, None, 7)
    back.chunk(0, order.q_x)
    back.chunk(1, order.q_x)
    send_queries((spot.xn, sib_x))
    gather.last()
    y_sum.across_one()
    gather.got(sib_y, None, 8)
    back.chunk(0, order.q_y)
    back.chunk(1, order.q_y)
    send_queries((spot.yn, sib_y))
    gather.got(sib_d, 0, 9)
    gather.got(sib_d, 1, 10)
    back.chunk(0, order.q_d)
    back.chunk(1, order.q_d)
    send_queries((spot.diag, sib_d))
    y_sum.to_mate()
    for copy in gather.started:
        copy.wait_send()
    back.keys(0)
    back.keys(1)

    def others(step):
        other = lax.rem(spot.me + step, everyone)
        return other, (lax.div(other, WIDE), lax.rem(other, WIDE))

    def rows_of(ref, owner):
        return ref.at[pl.ds(pl.multiple_of(owner * 32, 32), 32)]

    def to_owner(step, arriving):
        other, to = others(step)
        place = other if arriving else spot.me
        return remote(rows_of(wg_ref, other), w_recv.at[place], ws.at[other], wr.at[place], to)

    def start_owner(step, carry):
        to_owner(step, False).start()
        return carry

    def start_keys(step, carry):
        to_tokens(lax.rem(spot.w + step, WIDE), spot.w, 128, ks, kr).start()
        return carry

    lax.fori_loop(1, WIDE, start_keys, 0)
    plane_mine = pltpu.make_async_copy(
        dqkv_ref.at[:, pl.ds(pl.multiple_of(spot.w * SPAN, SPAN), SPAN), :],
        dq_full.at[:, :, pl.ds(pl.multiple_of(spot.w * 256, 256), 256)],
        local.at[0],
    )
    plane_mine.start()
    og_ref[...] = osum[...].astype(BF16)

    def wait_lanes(step, carry):
        lanes_to(step, False).wait_send()
        lanes_to(step, True).wait_recv()
        return carry

    lax.fori_loop(1, WIDE, wait_lanes, 0)
    lane_total = small_all[0]
    for device in range(1, WIDE):
        lane_total = lane_total + small_all[device]
    small_sum[...] = lane_total
    odd = 4 * lax.rem(spot.w, 2)

    def first_hop(i, act_local, act_remote):
        to = odd + i
        source = og_ref.at[pl.ds(i * 32, 32)]
        place = lax.div(spot.w, 2)

        @pl.when(to == spot.w)
        def _():
            act_local(pltpu.make_async_copy(source, o_held.at[place], local.at[2]))
            act_local(pltpu.make_async_copy(small_sum, s_held.at[place], local.at[3]))

        @pl.when(to != spot.w)
        def _():
            act_remote(remote(source, o_held.at[place], os.at[i], orv.at[place], spot.wide(to)))
            act_remote(remote(small_sum, s_held.at[place], ss.at[i], sr.at[place], spot.wide(to)))

    def first_arrival(place, act):
        giver = 2 * place + lax.div(spot.w, 4)

        @pl.when(giver != spot.w)
        def _():
            held, small = o_held.at[place], s_held.at[place]
            act(remote(held, held, os.at[0], orv.at[place], spot.wide(giver)))
            act(remote(small, small, ss.at[0], sr.at[place], spot.wide(giver)))

    def second_hop(step, arriving):
        plane = lax.rem(spot.n + step, NARROW)
        place = plane if arriving else spot.n
        to = (plane, spot.w)
        return (
            remote(o_held.at[plane], o_recv.at[place], os.at[4 + step], orv.at[4 + place], to),
            remote(s_held.at[plane], s_recv.at[place], ss.at[4 + step], sr.at[4 + place], to),
        )

    for i in range(4):
        first_hop(i, lambda c: c.start(), lambda c: c.start())

    loads[8].wait()
    wg_ref[...] = (mm(h1[0], dqkv_ref[0], TN) + mm(h1[1], dqkv_ref[1], TN)).astype(BF16)
    lax.fori_loop(1, everyone, start_owner, 0)
    owner_mine = pltpu.make_async_copy(rows_of(wg_ref, spot.me), w_recv.at[spot.me], local.at[1])
    owner_mine.start()
    for i in range(4):
        first_hop(i, lambda c: c.wait(), lambda c: c.wait_send())
    for place in range(NARROW):
        first_arrival(place, lambda c: c.wait_recv())
    for step in range(1, NARROW):
        start_all(second_hop(step, False))

    def wait_plane(step, carry):
        other = lax.rem(spot.w + step, WIDE)
        for first, send, recv in ((0, qs, qr), (128, ks, kr)):
            to_tokens(other, spot.w, first, send, recv).wait_send()
            to_tokens(other, other, first, send, recv).wait_recv()
        return carry

    lax.fori_loop(1, WIDE, wait_plane, 0)
    plane_mine.wait()
    for copy in w_loads:
        copy.wait()
    dh1 = jnp.zeros((TOKENS, WIDTH), F32)
    for who in range(WIDE):
        grads = dq_full[:, :, 256 * who : 256 * who + 256].reshape(TOKENS, 256)
        dh1 = dh1 + mm(grads, w_full[who], NT)
    x = x_ref[...].astype(F32)
    scale = lax.rsqrt(jnp.mean(x * x, axis=1, keepdims=True) + EPSILON)
    weighted = dh1 * gain_ref[0:1, :]
    inner = jnp.mean(weighted * x, axis=1, keepdims=True)
    in_grad[...] = (dmid_ref[...] + weighted * scale - x * (scale * scale * scale) * inner).astype(BF16)
    y_sum.finish()
    block_out[...] = (mid_ref[...] + y_sum.total_ref[...]).astype(BF16)

    def wait_owner(step, carry):
        to_owner(step, False).wait_send()
        to_owner(step, True).wait_recv()
        return carry

    lax.fori_loop(1, everyone, wait_owner, 0)
    owner_mine.wait()
    for step in range(1, NARROW):
        for copy in second_hop(step, False):
            copy.wait_send()
        for copy in second_hop(step, True):
            copy.wait_recv()
    gain_total = jnp.zeros((32, 1), F32)
    for w in range(WIDE):
        total = widen(w_recv[w])
        for plane in range(1, NARROW):
            total = total + widen(w_recv[plane * WIDE + w])
        q_grad[:, 128 * w : 128 * w + 128] = total[:, 0:128]
        k_grad[:, 64 * w : 64 * w + 64] = total[:, 128:192]
        v_grad[:, 64 * w : 64 * w + 64] = total[:, 192:256]
        gain_total += jnp.sum(total * widen(w_own[:, 256 * w : 256 * w + 256]), axis=1, keepdims=True)
    gain_total = gain_total / gain_col[...].astype(F32)
    o_recv[spot.n] = o_held[spot.n]
    s_recv[spot.n] = s_held[spot.n]
    total = widen(o_recv[0])
    for plane in range(1, NARROW):
        total = total + widen(o_recv[plane])
    o_grad[...] = total
    total = s_recv[0]
    for plane in range(1, NARROW):
        total = total + s_recv[plane]
    load_out[...] = total[33:34, 0:32].astype(jnp.int32)
    lane = lax.rem(spot.me, 4)
    mine = jnp.zeros((40, 32), F32)
    for part in range(4):
        mine = mine + jnp.where(lane == part, 1.0, 0.0) * total[:, 32 * part : 32 * part + 32]
    square = jnp.concatenate([mine, jnp.zeros((40, 96), F32)], axis=1)
    square = jnp.concatenate([square, jnp.zeros((88, 128), F32)], axis=0)
    router_grad[...] = jnp.transpose(square)[0:32, 0:32]
    column = jnp.concatenate([jnp.broadcast_to(gain_total, (32, 128)), jnp.zeros((96, 128), F32)], axis=0)
    two_gains[...] = jnp.concatenate([jnp.transpose(column)[0:1, 0:32], mine[32:33]], axis=0)

    for copy in quarter_copies:
        copy.wait_send()
        copy.wait_recv()


def backward_call(*operands):
    dma = pltpu.SemaphoreType.DMA
    vmem = pltpu.VMEM
    everyone = NARROW * WIDE
    copies = PlaneGather.COPIES
    return pl.pallas_call(
        backward_kernel,
        name="backward",
        out_shape=(
            jax.ShapeDtypeStruct((TOKENS, WIDTH), BF16),
            jax.ShapeDtypeStruct((TOKENS, WIDTH), BF16),
            jax.ShapeDtypeStruct((32, WIDTH), F32),
            jax.ShapeDtypeStruct((32, WIDTH // 2), F32),
            jax.ShapeDtypeStruct((32, WIDTH // 2), F32),
            jax.ShapeDtypeStruct((32, WIDTH), F32),
            jax.ShapeDtypeStruct((32, 32), F32),
            jax.ShapeDtypeStruct((2, 32), F32),
            jax.ShapeDtypeStruct((1, 32), jnp.int32),
        )
        + (QUARTER,) * 3,
        in_specs=[IN_HBM] * 16 + [IN_VMEM] * 7,
        out_specs=(IN_VMEM,) * 9 + (IN_HBM,) * 3,
        scratch_shapes=[
            vmem((GROUP, 8, TOKENS), F32),
            vmem((TOKENS, WIDTH), BF16),
            vmem((WIDE, TOKENS, WIDTH), BF16),
            vmem((TOKENS, WIDTH), F32),
            vmem((40, WIDTH), F32),
            vmem((WIDE, 40, 128), F32),
            vmem((40, 128), F32),
            vmem((WIDTH, 128), BF16),
            vmem((128, WIDTH), BF16),
            vmem((WIDE, WIDTH, 256), BF16),
            vmem((2, SEQ, WIDTH), BF16),
            vmem((2, SEQ, 256), BF16),
            vmem((2, SEQ, 128), F32),
            vmem((2, SEQ, 128), BF16),
            vmem((2, SEQ, 256), F32),
            vmem((2, SEQ, 256), BF16),
            vmem((2, SEQ, 128), F32),
            vmem((512, HEAD_DIM), F32),
            vmem((128, WIDTH), F32),
            vmem((128, WIDTH), BF16),
            vmem((WIDTH, 256), BF16),
            vmem((2, SPAN, 2 * WIDTH), BF16),
            vmem((everyone, 32, 256), BF16),
            vmem((NARROW, 32, WIDTH), BF16),
            vmem((NARROW, 40, 128), F32),
            vmem((NARROW, 32, WIDTH), BF16),
            vmem((NARROW, 40, 128), F32),
            dma((GROUP,)),
            dma((GROUP,)),
            dma((copies,)),
            dma((copies,)),
            dma((WIDE,)),
            dma((WIDE,)),
            dma((WIDE,)),
            dma((WIDE,)),
            dma((WIDE,)),
            dma((WIDE,)),
            dma((everyone,)),
            dma((everyone,)),
            dma((8,)),
            dma((8,)),
            dma((8,)),
            dma((8,)),
            dma((3,)),
            dma((3,)),
            dma((18,)),
        ]
        + reduce_scratch()
        + reduce_scratch(),
        compiler_params=pltpu.CompilerParams(collective_id=3, has_side_effects=True, vmem_limit_bytes=VMEM_BYTES),
        cost_estimate=duration(1),
    )(*operands)


def swap(values, distance):
    return lax.ppermute(values, "narrow", [(i, i ^ distance) for i in range(NARROW)])


def position_tables():
    freq = (1.0 / np.float32(THETA) ** (np.arange(32, dtype=np.float32) * np.float32(2.0) / np.float32(HEAD_DIM))).astype(np.float32)
    angle = np.arange(SEQ, dtype=np.float32)[:, None] * freq[None, :]
    cosine = np.tile(np.cos(angle.astype(np.float64)), (1, 4)).astype(np.float32)
    sine = np.tile(np.sin(angle.astype(np.float64)), (1, 4)).astype(np.float32)
    return cosine, sine, np.tile(freq[None, :], (8, 4)).astype(np.float32)


def fast_device(
    hidden_in, out_grad, seg_ids, expert_ids, attn_gain, w_query, w_key, w_value, w_output,
    moe_gain, w_router, w_gate_up, w_down,
):
    n = lax.axis_index("narrow")
    w = lax.axis_index("wide")
    half = n % 2
    me = n * WIDE + w
    cos_table, sin_table, freq = position_tables()

    x_own = hidden_in.reshape(TOKENS, WIDTH)
    dy_own = out_grad.reshape(TOKENS, WIDTH)
    (
        h1, qkv, lse, o_heads, angle, gain_rows, mid, gate, w_out, w_heads, w_own, h2_all, dy_all, table_all,
        mate_0, far_0, far_mate_0, mate_1, far_1, far_mate_early_1,
    ) = forward_call(
        hidden_in, dy_own, seg_ids, w_query, w_key, w_value, w_output, w_router,
        attn_gain.reshape(1, 32), moe_gain.reshape(1, 32), cos_table, sin_table, freq,
        jnp.transpose(expert_ids, (0, 2, 1)), w_gate_up, w_down,
    )
    w_out = w_out.reshape(WIDTH, WIDTH + 128)

    def send_grads(own, mate, far, far_mate):
        return own, swap(mate, 1), swap(far, 2), swap(far_mate, 3)

    gated_0, dx_0, rows_1, grad_rows_1, dgate_0, *grads_0, far_mate_rest_1 = expert_0_call(
        h2_all, dy_all, table_all, w_gate_up, w_down, (mate_0, far_0, far_mate_0)
    )
    dgate_0, w_heads = lax.optimization_barrier((dgate_0, w_heads))
    w_full = lax.all_gather(w_heads.reshape(WIDTH, 256), "wide", axis=0, tiled=False)
    grads_0 = send_grads(*grads_0)
    y_here, y_there, part_here, part_there, dgate, *grads_1 = expert_1_call(
        rows_1, grad_rows_1, gated_0, dx_0, dgate_0, table_all, w_gate_up, w_down, (mate_1, far_1, far_mate_early_1, far_mate_rest_1)
    )
    (
        block_out, in_grad, q_grad, k_grad, v_grad, o_grad, router_grad, two_gains, load, *arrived_1,
    ) = backward_call(
        part_here, part_there, y_here, y_there, dgate, h2_all, w_out, w_full, h1, qkv, lse, o_heads, angle, *grads_1[1:],
        x_own, mid, gate, gain_rows, dy_own, w_own, attn_gain.reshape(32, 1),
    )
    (
        gate_up_sum, down_sum, block_out, in_grad, q_grad, k_grad, v_grad, o_grad,
        router_grad, attn_gain_grad, moe_gain_grad, load,
    ) = results_call(
        grads_0, (grads_1[0], *arrived_1),
        (block_out, in_grad, q_grad, k_grad, v_grad, o_grad), (router_grad, two_gains, load),
    )
    return (
        block_out.reshape(hidden_in.shape),
        in_grad.reshape(hidden_in.shape),
        attn_gain_grad.reshape(32),
        q_grad,
        k_grad,
        v_grad,
        o_grad,
        moe_gain_grad.reshape(32),
        router_grad,
        gate_up_sum,
        down_sum,
        load.reshape(32),
    )


def solution(mesh):
    planned = mesh.shape["narrow"] == NARROW and mesh.shape["wide"] == WIDE
    return jax.shard_map(
        fast_device if planned else general_device,
        mesh=mesh,
        in_specs=(
            P("narrow", "wide", None),
            P("narrow", "wide", None),
            P("narrow", "wide"),
            P("narrow", "wide", None),
            P(("narrow", "wide")),
            P(("narrow", "wide"), None),
            P(("narrow", "wide"), None),
            P(("narrow", "wide"), None),
            P(("narrow", "wide"), None),
            P(("narrow", "wide")),
            P(("narrow", "wide"), None),
            P("wide", "narrow", None),
            P("wide", "narrow", None),
        ),
        out_specs=(
            P("narrow", "wide", None),
            P("narrow", "wide", None),
            P(("narrow", "wide")),
            P(("narrow", "wide"), None),
            P(("narrow", "wide"), None),
            P(("narrow", "wide"), None),
            P(("narrow", "wide"), None),
            P(("narrow", "wide")),
            P(("narrow", "wide"), None),
            P("wide", "narrow", None),
            P("wide", "narrow", None),
            P(),
        ),
        check_vma=False,
    )
```

```python
import math

import functools
import jax
import jax.numpy as jnp
import numpy as np
from jax import lax
from jax.experimental import pallas as pl
from jax.experimental.pallas import tpu as pltpu
from jax.sharding import PartitionSpec as P

KV_HEADS = 8
HEAD_DIM = 64
EXPERTS = 32
TOP = 8
FF = 512
CAP = 80


EPSILON = 1e-06
THETA = 10000.0
MASKED = -1e30


def rms_scale(values):
    return lax.rsqrt(jnp.mean(values * values, axis=-1, keepdims=True) + EPSILON)


def norm_back(values, scale, gain, upstream):
    weighted = upstream * gain
    inner_mean = jnp.mean(weighted * values, axis=-1, keepdims=True)
    value_grad = weighted * scale - values * (scale * scale * scale) * inner_mean
    gain_grad = jnp.sum(upstream * values * scale, axis=0)
    return (value_grad, gain_grad)


def lane_turn(head_dim):
    lane_ids = jnp.arange(128)
    lane_local = lane_ids % head_dim
    half_dim = head_dim // 2
    same_head = lane_ids[:, None] // head_dim == lane_ids[None, :] // head_dim
    from_upper = (lane_local[None, :] < half_dim) & (
        lane_local[:, None] == lane_local[None, :] + half_dim
    )
    from_lower = (lane_local[None, :] >= half_dim) & (
        lane_local[:, None] + half_dim == lane_local[None, :]
    )
    return jnp.where(
        same_head & from_upper, -1.0, jnp.where(same_head & from_lower, 1.0, 0.0)
    ).astype(jnp.float32)


def lane_angles(positions, head_dim):
    lane_ids = jnp.arange(128) % head_dim % (head_dim // 2)
    inverse = 1.0 / THETA ** (lane_ids.astype(jnp.float32) * 2.0 / head_dim)
    return positions[..., None] * inverse


def rotate(values, cos_table, sin_table, turner):
    dims_in = values.shape
    blocks = values.reshape(dims_in[0], dims_in[1], -1, 128)
    turned = jnp.einsum("abnl,lm->abnm", blocks, turner, precision=lax.Precision.HIGHEST)
    return (blocks * cos_table[:, :, None, :] + turned * sin_table[:, :, None, :]).reshape(dims_in)


def rotate_back(grad_in, cos_table, sin_table, turner):
    dims_in = grad_in.shape
    blocks = grad_in.reshape(dims_in[0], dims_in[1], -1, 128)
    turned = jnp.einsum(
        "abnm,lm->abnl", blocks * sin_table[:, :, None, :], turner, precision=lax.Precision.HIGHEST
    )
    return (blocks * cos_table[:, :, None, :] + turned).reshape(dims_in)


def masked_scores(query_five, key_block, seg_query, seg_key, place_query, place_key, factor):
    scores = (
        jnp.einsum("abgjd,akgd->agjbk", query_five, key_block, preferred_element_type=jnp.float32)
        * factor
    )
    allowed = (seg_query[:, :, None] == seg_key[:, None, :]) & (
        place_query[:, :, None] >= place_key[:, None, :]
    )
    return jnp.where(allowed[:, None, None], scores, MASKED)


def general_device(
    hidden_in,
    out_grad,
    seg_ids,
    expert_ids,
    attn_gain,
    w_query,
    w_key,
    w_value,
    w_output,
    moe_gain,
    w_router,
    w_gate_up,
    w_down,
):
    row_count, span_len, feat_dim = hidden_in.shape
    tok_count = row_count * span_len
    factor = HEAD_DIM ** (-0.5)
    kv_width = KV_HEADS * HEAD_DIM
    gain_one, query_w, key_w, value_w, output_w, gain_two, router_w = (
        lax.all_gather(attn_gain, ("narrow", "wide"), axis=0, tiled=True),
        lax.all_gather(w_query, ("narrow", "wide"), axis=0, tiled=True),
        lax.all_gather(w_key, ("narrow", "wide"), axis=0, tiled=True),
        lax.all_gather(w_value, ("narrow", "wide"), axis=0, tiled=True),
        lax.all_gather(w_output, ("narrow", "wide"), axis=0, tiled=True),
        lax.all_gather(moe_gain, ("narrow", "wide"), axis=0, tiled=True),
        lax.all_gather(w_router, ("narrow", "wide"), axis=0, tiled=True),
    )
    gate_up_w, down_w = (
        lax.all_gather(w_gate_up, "narrow", axis=1, tiled=True),
        lax.all_gather(w_down, "narrow", axis=1, tiled=True),
    )
    segs_all = lax.all_gather(seg_ids, "wide", axis=1, tiled=True)
    seq_len = segs_all.shape[1]
    key_step = math.gcd(seq_len, 512)
    place_local = lax.axis_index("wide") * span_len + jnp.arange(span_len, dtype=jnp.int32)
    place_query = place_local[None, :]
    starts = jnp.sum((segs_all[:, None, :] < seg_ids[:, :, None]).astype(jnp.int32), axis=-1)
    positions = (place_query - starts).astype(jnp.float32)
    angles = lane_angles(positions, HEAD_DIM)
    cos_table = jnp.cos(angles)
    sin_table = jnp.sin(angles)
    turner = lane_turn(HEAD_DIM)
    inputs = hidden_in.astype(jnp.float32)
    scale_one = rms_scale(inputs)
    gain_one_f = gain_one.astype(jnp.float32)
    normed_one = (inputs * scale_one * gain_one_f).astype(jnp.bfloat16)
    query_pre = jnp.dot(normed_one, query_w, preferred_element_type=jnp.float32)
    key_pre = jnp.dot(normed_one, key_w, preferred_element_type=jnp.float32)
    value_pre = jnp.dot(normed_one, value_w, preferred_element_type=jnp.float32)
    queries = rotate(query_pre, cos_table, sin_table, turner).astype(jnp.bfloat16)
    keys_local = rotate(key_pre, cos_table, sin_table, turner).astype(jnp.bfloat16)
    values_local = value_pre.astype(jnp.bfloat16)
    key_all, value_all = (
        lax.all_gather(keys_local, "wide", axis=1, tiled=True),
        lax.all_gather(values_local, "wide", axis=1, tiled=True),
    )
    query_five = queries.reshape(row_count, span_len, KV_HEADS, 2, HEAD_DIM)

    def key_slices(key_start, length):
        key_block = lax.dynamic_slice_in_dim(key_all, key_start, length, 1).reshape(
            row_count, length, KV_HEADS, HEAD_DIM
        )
        value_block = lax.dynamic_slice_in_dim(value_all, key_start, length, 1).reshape(
            row_count, length, KV_HEADS, HEAD_DIM
        )
        seg_key = lax.dynamic_slice_in_dim(segs_all, key_start, length, 1)
        place_key = (key_start + jnp.arange(length, dtype=jnp.int32))[None, :]
        return (key_block, value_block, seg_key, place_key)

    def scores_at(key_start, length):
        key_block, value_block, seg_key, place_key = key_slices(key_start, length)
        scores = masked_scores(
            query_five, key_block, seg_ids, seg_key, place_query, place_key, factor
        )
        return (scores, key_block, value_block)

    key_starts = jnp.arange(seq_len // key_step, dtype=jnp.int32) * key_step
    stat_shape = (row_count, KV_HEADS, 2, span_len)
    five_shape = (row_count, span_len, KV_HEADS, 2, HEAD_DIM)

    def top_step(state_now, key_start):
        row_top, row_total = state_now
        scores, unused_key, unused_value = scores_at(key_start, key_step)
        new_top = jnp.maximum(row_top, jnp.max(scores, axis=-1))
        row_total = row_total * jnp.exp(row_top - new_top) + jnp.sum(
            jnp.exp(scores - new_top[..., None]), axis=-1
        )
        return ((new_top, row_total), None)

    (row_top, row_total), unused = lax.scan(
        top_step,
        (jnp.full(stat_shape, MASKED, jnp.float32), jnp.zeros(stat_shape, jnp.float32)),
        key_starts,
    )
    log_total = row_top + jnp.log(row_total)

    def out_step(summed, key_start):
        scores, unused_key, value_block = scores_at(key_start, key_step)
        weights = jnp.exp(scores - log_total[..., None]).astype(jnp.bfloat16)
        return (
            summed
            + jnp.einsum(
                "agjbk,akgd->abgjd", weights, value_block, preferred_element_type=jnp.float32
            ),
            None,
        )

    attended, unused = lax.scan(out_step, jnp.zeros(five_shape, jnp.float32), key_starts)
    attended = attended.reshape(row_count, span_len, -1).astype(jnp.bfloat16)
    middle = inputs + jnp.dot(attended, output_w, preferred_element_type=jnp.float32)
    scale_two = rms_scale(middle)
    gain_two_f = gain_two.astype(jnp.float32)
    normed_two = (middle * scale_two * gain_two_f).astype(jnp.bfloat16)
    flat_two = normed_two.reshape(tok_count, feat_dim)
    logits = jnp.dot(flat_two, router_w, preferred_element_type=jnp.float32)
    expert_table = expert_ids.reshape(tok_count, TOP)
    choose = expert_table[:, :, None] == jnp.arange(EXPERTS, dtype=jnp.int32)[None, None, :]
    chosen = jnp.sum(jnp.where(choose, logits[:, None, :], 0.0), axis=-1)
    gate_vals = jax.nn.softmax(chosen, axis=-1)
    token_hot = jnp.sum(choose.astype(jnp.int32), axis=1)
    expert_load = lax.psum(jnp.sum(token_hot, axis=0), ("narrow", "wide"))
    earlier = jnp.cumsum(token_hot, axis=0) - token_hot
    places = jnp.sum(jnp.where(choose, earlier[:, None, :], 0), axis=-1)
    pair_count = tok_count * TOP
    target = jnp.where(places < CAP, expert_table * CAP + places, EXPERTS * CAP).reshape(-1)
    pair_of_slot = (
        jnp.full((EXPERTS * CAP,), pair_count, jnp.int32)
        .at[target]
        .set(jnp.arange(pair_count, dtype=jnp.int32), mode="drop")
    )
    token_of_slot = pair_of_slot // TOP
    outgoing = jnp.take(flat_two, token_of_slot, axis=0, mode="fill", fill_value=0).reshape(
        EXPERTS, CAP, feat_dim
    )
    received = lax.all_to_all(outgoing, "wide", split_axis=0, concat_axis=1, tiled=True)
    gate_up = jnp.einsum("ecd,edf->ecf", received, gate_up_w, preferred_element_type=jnp.float32)
    gate_half = gate_up[..., :FF]
    up_half = gate_up[..., FF:]
    sigmoid_gate = jax.nn.sigmoid(gate_half)
    activated = gate_half * sigmoid_gate
    hidden_b = (activated * up_half).astype(jnp.bfloat16)
    expert_out = jnp.einsum(
        "ecf,efd->ecd", hidden_b, down_w, preferred_element_type=jnp.float32
    ).astype(jnp.bfloat16)
    returned = lax.all_to_all(expert_out, "wide", split_axis=1, concat_axis=0, tiled=True)
    per_pair = (
        jnp.take(
            returned.reshape(EXPERTS * CAP, feat_dim), target, axis=0, mode="fill", fill_value=0
        )
        .reshape(tok_count, TOP, feat_dim)
        .astype(jnp.float32)
    )
    mixture = jnp.sum(gate_vals[:, :, None] * per_pair, axis=1)
    middle_flat = middle.reshape(tok_count, feat_dim)
    block_out = (middle_flat + mixture).reshape(row_count, span_len, feat_dim).astype(jnp.bfloat16)
    grad_out = out_grad.reshape(tok_count, feat_dim).astype(jnp.float32)
    gate_grad = jnp.sum(grad_out[:, None, :] * per_pair, axis=-1)
    gate_of_slot = jnp.take(gate_vals.reshape(-1), pair_of_slot, mode="fill", fill_value=0.0)
    slot_grad = (
        (
            jnp.take(grad_out, token_of_slot, axis=0, mode="fill", fill_value=0.0)
            * gate_of_slot[:, None]
        )
        .astype(jnp.bfloat16)
        .reshape(EXPERTS, CAP, feat_dim)
    )
    grad_received = lax.all_to_all(slot_grad, "wide", split_axis=0, concat_axis=1, tiled=True)
    down_grad = jnp.einsum(
        "ecf,ecd->efd", hidden_b, grad_received, preferred_element_type=jnp.float32
    )
    hidden_grad = jnp.einsum(
        "ecd,efd->ecf", grad_received, down_w, preferred_element_type=jnp.float32
    )
    gate_half_grad = (
        hidden_grad * up_half * (sigmoid_gate * (1.0 + gate_half * (1.0 - sigmoid_gate)))
    )
    up_half_grad = hidden_grad * activated
    gate_up_grad = jnp.concatenate([gate_half_grad, up_half_grad], axis=-1).astype(jnp.bfloat16)
    gate_up_wgrad = jnp.einsum(
        "ecd,ecf->edf", received, gate_up_grad, preferred_element_type=jnp.float32
    )
    slot_input_grad = jnp.einsum(
        "ecf,edf->ecd", gate_up_grad, gate_up_w, preferred_element_type=jnp.float32
    ).astype(jnp.bfloat16)
    input_back = lax.all_to_all(slot_input_grad, "wide", split_axis=1, concat_axis=0, tiled=True)
    pair_input_grad = jnp.take(
        input_back.reshape(EXPERTS * CAP, feat_dim), target, axis=0, mode="fill", fill_value=0
    ).reshape(tok_count, TOP, feat_dim)
    gate_mean = jnp.sum(gate_vals * gate_grad, axis=-1, keepdims=True)
    chosen_grad = gate_vals * (gate_grad - gate_mean)
    logit_grad = jnp.sum(jnp.where(choose, chosen_grad[:, :, None], 0.0), axis=1).astype(
        jnp.bfloat16
    )
    router_wgrad = jnp.einsum("td,te->de", flat_two, logit_grad, preferred_element_type=jnp.float32)
    normed_two_grad = jnp.sum(pair_input_grad.astype(jnp.float32), axis=1) + jnp.einsum(
        "te,de->td", logit_grad, router_w, preferred_element_type=jnp.float32
    )
    middle_part, gain_two_grad = norm_back(
        middle_flat, scale_two.reshape(tok_count, 1), gain_two_f, normed_two_grad
    )
    middle_grad = grad_out + middle_part
    attn_grad = middle_grad.astype(jnp.bfloat16)
    output_wgrad = jnp.einsum(
        "te,td->ed", attended.reshape(tok_count, -1), attn_grad, preferred_element_type=jnp.float32
    )
    attended_grad = jnp.einsum(
        "td,ed->te", attn_grad, output_w, preferred_element_type=jnp.float32
    ).astype(jnp.bfloat16)
    grad_five = attended_grad.reshape(five_shape)

    def sum_step(summed, key_start):
        scores, unused_key, value_block = scores_at(key_start, key_step)
        weights = jnp.exp(scores - log_total[..., None])
        weight_grad = jnp.einsum(
            "abgjd,akgd->agjbk", grad_five, value_block, preferred_element_type=jnp.float32
        )
        return (summed + jnp.sum(weights * weight_grad, axis=-1), None)

    row_dot, unused = lax.scan(sum_step, jnp.zeros(stat_shape, jnp.float32), key_starts)

    def query_step(summed, key_start):
        scores, key_block, value_block = scores_at(key_start, key_step)
        weights = jnp.exp(scores - log_total[..., None])
        weight_grad = jnp.einsum(
            "abgjd,akgd->agjbk", grad_five, value_block, preferred_element_type=jnp.float32
        )
        score_grad = (weights * (weight_grad - row_dot[..., None])).astype(jnp.bfloat16)
        return (
            summed
            + jnp.einsum(
                "agjbk,akgd->abgjd", score_grad, key_block, preferred_element_type=jnp.float32
            ),
            None,
        )

    query_grad, unused = lax.scan(query_step, jnp.zeros(five_shape, jnp.float32), key_starts)
    query_grad = query_grad.reshape(row_count, span_len, -1) * factor
    term_count = span_len * lax.axis_size("wide")
    sub_len = math.gcd(term_count, 512)

    def key_piece(sub_no):
        key_start = sub_no * sub_len
        key_block, value_block, seg_key, place_key = key_slices(key_start, sub_len)
        scores = masked_scores(
            query_five, key_block, seg_ids, seg_key, place_query, place_key, factor
        )
        weights = jnp.exp(scores - log_total[..., None])
        weight_grad = jnp.einsum(
            "abgjd,akgd->agjbk", grad_five, value_block, preferred_element_type=jnp.float32
        )
        score_grad = (weights * (weight_grad - row_dot[..., None])).astype(jnp.bfloat16)
        key_part = (
            jnp.einsum(
                "agjbk,abgjd->kagd", score_grad, query_five, preferred_element_type=jnp.float32
            )
            * factor
        )
        value_part = jnp.einsum(
            "agjbk,abgjd->kagd",
            weights.astype(jnp.bfloat16),
            grad_five,
            preferred_element_type=jnp.float32,
        )
        return jnp.concatenate(
            [
                key_part.reshape(sub_len, row_count, kv_width),
                value_part.reshape(sub_len, row_count, kv_width),
            ],
            axis=-1,
        )

    pieces = lax.map(key_piece, jnp.arange(term_count // sub_len, dtype=jnp.int32))
    summed_terms = lax.psum_scatter(
        pieces.reshape(term_count, row_count, 2 * kv_width).astype(jnp.bfloat16),
        "wide",
        scatter_dimension=0,
        tiled=True,
    ).astype(jnp.float32)
    key_grad = jnp.transpose(summed_terms[:, :, :kv_width], (1, 0, 2))
    value_grad = jnp.transpose(summed_terms[:, :, kv_width:], (1, 0, 2))
    query_back = (
        rotate_back(query_grad, cos_table, sin_table, turner)
        .astype(jnp.bfloat16)
        .reshape(tok_count, -1)
    )
    key_back = (
        rotate_back(key_grad, cos_table, sin_table, turner)
        .astype(jnp.bfloat16)
        .reshape(tok_count, -1)
    )
    value_back = value_grad.astype(jnp.bfloat16).reshape(tok_count, -1)
    flat_one = normed_one.reshape(tok_count, feat_dim)
    query_wgrad = jnp.einsum("td,te->de", flat_one, query_back, preferred_element_type=jnp.float32)
    key_wgrad = jnp.einsum("td,te->de", flat_one, key_back, preferred_element_type=jnp.float32)
    value_wgrad = jnp.einsum("td,te->de", flat_one, value_back, preferred_element_type=jnp.float32)
    normed_one_grad = (
        jnp.einsum("te,de->td", query_back, query_w, preferred_element_type=jnp.float32)
        + jnp.einsum("te,de->td", key_back, key_w, preferred_element_type=jnp.float32)
        + jnp.einsum("te,de->td", value_back, value_w, preferred_element_type=jnp.float32)
    )
    input_part, gain_one_grad = norm_back(
        inputs.reshape(tok_count, feat_dim),
        scale_one.reshape(tok_count, 1),
        gain_one_f,
        normed_one_grad,
    )
    input_grad = (
        (middle_grad + input_part).reshape(row_count, span_len, feat_dim).astype(jnp.bfloat16)
    )
    gain_one_sum, query_sum, key_wsum, value_wsum, output_sum, gain_two_sum, router_sum = (
        lax.psum_scatter(gain_one_grad, ("narrow", "wide"), scatter_dimension=0, tiled=True),
        lax.psum_scatter(query_wgrad, ("narrow", "wide"), scatter_dimension=0, tiled=True),
        lax.psum_scatter(key_wgrad, ("narrow", "wide"), scatter_dimension=0, tiled=True),
        lax.psum_scatter(value_wgrad, ("narrow", "wide"), scatter_dimension=0, tiled=True),
        lax.psum_scatter(output_wgrad, ("narrow", "wide"), scatter_dimension=0, tiled=True),
        lax.psum_scatter(gain_two_grad, ("narrow", "wide"), scatter_dimension=0, tiled=True),
        lax.psum_scatter(router_wgrad, ("narrow", "wide"), scatter_dimension=0, tiled=True),
    )
    gate_up_sum, down_sum = (
        lax.psum_scatter(
            gate_up_wgrad.astype(jnp.bfloat16), "narrow", scatter_dimension=1, tiled=True
        ).astype(jnp.float32),
        lax.psum_scatter(
            down_grad.astype(jnp.bfloat16), "narrow", scatter_dimension=1, tiled=True
        ).astype(jnp.float32),
    )
    return (
        block_out,
        input_grad,
        gain_one_sum,
        query_sum,
        key_wsum,
        value_wsum,
        output_sum,
        gain_two_sum,
        router_sum,
        gate_up_sum,
        down_sum,
        expert_load,
    )


MESH = pl.DeviceIdType.MESH
F32 = jnp.float32
BF16 = jnp.bfloat16
IN_HBM = pl.BlockSpec(memory_space=pl.ANY)
IN_VMEM = pl.BlockSpec(memory_space=pltpu.VMEM)
VMEM_BYTES = 60 * 1024 * 1024
NARROW = 4
WIDE = 8
GROUP = 16
TOKENS = 256
SPAN = 128
WIDTH = 1024
SEQ = 1024
SLOTS = 80
MINE = 2
MIDDLE = 96
CHUNK = 4
NT = (((1,), (1,)), ((), ()))
TN = (((0,), (0,)), ((), ()))


def duration(us):
    return pl.CostEstimate(flops=us * 1000000000, bytes_accessed=us * 3600000, transcendentals=0)


def mm(left, right, dims=(((1,), (0,)), ((), ()))):
    return lax.dot_general(left, right, dims, preferred_element_type=F32)


class Spot:
    def __init__(self):
        self.n = lax.axis_index("narrow")
        self.w = lax.axis_index("wide")
        self.core = lax.rem(self.w, 2)
        self.x = lax.rem(lax.div(self.w, 2), 2)
        self.y = lax.div(self.w, 4)
        self.half = lax.rem(self.n, 2)
        self.me = self.n * WIDE + self.w
        self.sib = self.w + 1 - 2 * self.core
        self.xn = self.w + 2 - 4 * self.x
        self.yn = self.w + 4 - 8 * self.y
        self.diag = self.xn + 4 - 8 * self.y
        self.mate = self.n + 1 - 2 * self.half
        self.slot = self.half * WIDE + self.w

    def wide(self, to):
        return (self.n, to)

    def greet(self, count):
        barrier = pltpu.get_barrier_semaphore()
        base = self.n - self.half

        def signal(step, carry):
            if count == WIDE:
                to = (self.n, lax.rem(self.w + step, WIDE))
            elif count == GROUP:
                other = lax.rem(self.slot + step, GROUP)
                to = (base + lax.div(other, WIDE), lax.rem(other, WIDE))
            else:
                other = lax.rem(self.me + step, NARROW * WIDE)
                to = (lax.div(other, WIDE), lax.rem(other, WIDE))
            pl.semaphore_signal(barrier, inc=1, device_id=to, device_id_type=MESH)
            return carry

        lax.fori_loop(1, count, signal, 0)
        pl.semaphore_wait(barrier, count - 1)


def remote(src, dst, send_sem, recv_sem, to):
    return pltpu.make_async_remote_copy(
        src_ref=src, dst_ref=dst, send_sem=send_sem, recv_sem=recv_sem, device_id=to, device_id_type=MESH
    )


def halves(ref, which):
    return ref.at[pl.ds(which * SPAN, SPAN)]


class PlaneGather:
    COPIES = 11

    def __init__(self, spot, source, place, send, recv):
        self.spot, self.source, self.place = spot, source, place
        self.send, self.recv = send, recv
        self.started = []

    def put(self, src, dst, number, to):
        copy = remote(src, dst, self.send.at[number], self.recv.at[number], self.spot.wide(to))
        copy.start()
        self.started.append(copy)

    def pass_on(self, who, half, number, to):
        place = self.place(who, half)
        self.put(place, place, number, to)

    def got(self, who, half, number):
        dst = self.place(who, half)
        remote(dst, dst, self.send.at[number], self.recv.at[number], self.spot.wide(self.spot.sib)).wait_recv()

    def begin(self):
        s = self.spot
        self.put(self.source(0), self.place(s.w, 0), 0, s.xn)
        self.put(self.source(1), self.place(s.w, 1), 2, s.yn)
        self.put(self.source(1), self.place(s.w, 1), 1, s.xn)
        self.put(self.source(0), self.place(s.w, 0), 3, s.yn)
        self.put(self.source(None), self.place(s.w, None), 4, s.sib)

    def middle(self):
        s = self.spot
        self.got(s.xn, 0, 0)
        self.pass_on(s.xn, 0, 5, s.yn)
        self.got(s.yn, 1, 2)
        self.pass_on(s.yn, 1, 6, s.xn)

    def late(self):
        s = self.spot
        self.got(s.xn, 1, 1)
        self.pass_on(s.xn, None, 7, s.sib)
        self.got(s.yn, 0, 3)
        self.pass_on(s.yn, None, 8, s.sib)

    def last(self):
        s = self.spot
        self.got(s.diag, 0, 5)
        self.pass_on(s.diag, 0, 9, s.sib)
        self.got(s.diag, 1, 6)
        self.pass_on(s.diag, 1, 10, s.sib)

    def finish(self):
        s = self.spot
        sib_x = s.sib + 2 - 4 * s.x
        sib_y = s.sib + 4 - 8 * s.y
        sib_d = sib_x + 4 - 8 * s.y
        self.got(s.sib, None, 4)
        self.got(sib_x, None, 7)
        self.got(sib_y, None, 8)
        self.got(sib_d, 0, 9)
        self.got(sib_d, 1, 10)
        for copy in self.started:
            copy.wait_send()


def gather_tokens(spot, own, out, base, send, recv):
    def part(ref, half):
        return ref if half is None else ref.at[pl.ds(half * SPAN, SPAN)]

    return PlaneGather(
        spot, lambda half: part(own, half), lambda who, half: part(out.at[base + who], half), send, recv
    )


def lane_half():
    lanes = lax.broadcasted_iota(jnp.int32, (1, 128), 1)
    return lax.rem(lanes, 64) < 32


def turn(values, first_half):
    return jnp.where(first_half, -pltpu.roll(values, 96, 1), pltpu.roll(values, 32, 1))


def turn_back(values, first_half):
    return jnp.where(first_half, pltpu.roll(values, 96, 1), -pltpu.roll(values, 32, 1))


def gather_gain(gains):
    lane = lax.broadcasted_iota(jnp.int32, (128, WIDTH), 0)
    column = lax.broadcasted_iota(jnp.int32, (128, WIDTH), 1)
    spread = (lax.rem(column, 32) == lane).astype(BF16)
    tiled = mm(gains.astype(BF16), spread)
    owner = lax.broadcasted_iota(jnp.int32, (32, WIDTH), 0)
    place = lax.broadcasted_iota(jnp.int32, (32, WIDTH), 1)
    return jnp.sum(jnp.where(lax.div(place, 32) == owner, tiled, 0.0), axis=0, keepdims=True)


class Attention:
    def __init__(self, x_ref, w_ref, seg_ref, cos_ref, sin_ref, freq_ref, gain_one, h1_ref, qkv_ref, lse_ref, o_ref, angle_ref):
        self.x_ref, self.seg_ref, self.cos_ref, self.sin_ref = x_ref, seg_ref, cos_ref, sin_ref
        self.h1_ref, self.qkv_ref, self.lse_ref, self.o_ref = h1_ref, qkv_ref, lse_ref, o_ref
        self.angle_ref = angle_ref
        self.gain_one = gain_one
        self.w_ref = w_ref
        self.first_half = lane_half()
        self.is_key = lax.broadcasted_iota(jnp.int32, (1, 128), 1) < 64
        self.starts, self.start_cos, self.start_sin = [], [], []
        for row in range(2):
            segs = [seg_ref[c, row : row + 1, :] for c in range(WIDE)]
            starts = [jnp.zeros((1, 1), F32)]
            for doc in range(5):
                total = jnp.zeros((1, 128), F32)
                for seg in segs:
                    total = total + jnp.where(seg == doc, 1.0, 0.0)
                starts.append(starts[-1] + jnp.sum(total, axis=1, keepdims=True))
            angle = jnp.concatenate(starts + starts[:2], axis=0) * freq_ref[0:1, :]
            self.starts.append(starts)
            self.start_cos.append(jnp.cos(angle))
            self.start_sin.append(jnp.sin(angle))

    def chunk(self, row, i):
        tokens = pl.ds(i * 256, 256)
        starts, start_cos, start_sin = self.starts[row], self.start_cos[row], self.start_sin[row]
        seg_cols = []
        for part in range(2):
            seg = self.seg_ref[2 * i + part, row : row + 1, :].astype(F32)
            seg_cols.append(jnp.transpose(jnp.broadcast_to(seg, (128, 128))))
        seg_col = jnp.concatenate(seg_cols, axis=0)
        start_col = jnp.zeros((256, 128), F32)
        cos_s = jnp.broadcast_to(start_cos[0:1], (256, 128))
        sin_s = jnp.broadcast_to(start_sin[0:1], (256, 128))
        for doc in range(1, 6):
            here = seg_col == float(doc)
            start_col = jnp.where(here, starts[doc], start_col)
            cos_s = jnp.where(here, start_cos[doc : doc + 1], cos_s)
            sin_s = jnp.where(here, start_sin[doc : doc + 1], sin_s)
        cos_t = self.cos_ref[tokens, :]
        sin_t = self.sin_ref[tokens, :]
        cosine = cos_t * cos_s + sin_t * sin_s
        sine = sin_t * cos_s - cos_t * sin_s
        self.angle_ref[row, tokens, 0:128] = cosine
        self.angle_ref[row, tokens, 128:256] = sine
        x = self.x_ref[2 * i : 2 * i + 2, row].reshape(256, WIDTH).astype(F32)
        scale = lax.rsqrt(jnp.mean(x * x, axis=1, keepdims=True) + EPSILON)
        h1 = (x * scale * self.gain_one).astype(BF16)
        self.h1_ref[row, tokens, :] = h1
        qkv = mm(h1, self.w_ref[...].reshape(WIDTH, 256))
        q = qkv[:, 0:128]
        kv = qkv[:, 128:256]
        q = (q * cosine + turn(q, self.first_half) * sine).astype(BF16)
        kv = jnp.where(self.is_key, kv * cosine + turn(kv, self.first_half) * sine, kv).astype(BF16)
        self.qkv_ref[row, tokens, 0:128] = q
        self.qkv_ref[row, tokens, 128:256] = kv
        length = 256 * (i + 1)
        keys = self.qkv_ref[row, 0:length, 128:192]
        values = self.qkv_ref[row, 0:length, 192:256]
        place_key = lax.broadcasted_iota(jnp.int32, (256, length), 1).astype(F32)
        place_query = (lax.broadcasted_iota(jnp.int32, (256, length), 0) + 256 * i).astype(F32)
        allowed = (place_key <= place_query) & (place_key >= start_col[:, 0:1])
        outs, logs = [], []
        for head in range(2):
            query = q[:, 64 * head : 64 * head + 64]
            scores = jnp.where(allowed, mm(query, keys, NT) * (HEAD_DIM**-0.5), MASKED)
            top = jnp.max(scores, axis=1, keepdims=True)
            log_total = top + jnp.log(jnp.sum(jnp.exp(scores - top), axis=1, keepdims=True))
            outs.append(mm(jnp.exp(scores - log_total).astype(BF16), values))
            logs.append(log_total)
        self.o_ref[row, tokens, :] = jnp.concatenate(outs, axis=1).astype(BF16)
        self.lse_ref[row, tokens, :] = jnp.where(
            self.is_key, jnp.where(self.first_half, logs[0], start_col), logs[1]
        )


def piece_copies(spot, gu_ref, down_ref, e, kind, target, send, recv, number, first=0, last=384):
    pair = lax.div(spot.n, 2)
    plane = spot.n if kind == 2 else spot.mate
    if kind >= 2:
        plane = plane + 2 - 4 * pair
    half = spot.half if kind == 2 else 1 - spot.half
    to = (plane, spot.w)
    copies = []
    for part, (ref, start, rows) in enumerate(((gu_ref, 0, 256), (down_ref, 256, 128))):
        low, high = max(first, start), min(last, start + rows)
        if low < high:
            copies.append(
                remote(
                    ref.at[2 * half + e, pl.ds(low - start, high - low)], target.at[pl.ds(low - first, high - low)],
                    send.at[number + part], recv.at[number + part], to,
                )
            )
    return copies


def start_all(copies):
    for copy in copies:
        copy.start()


def forward_kernel(
    x_in, dy_ref, seg_in, wq_in, wk_in, wv_in, wo_in, router_in, gain_one_in, gain_two_in,
    cos_ref, sin_ref, freq_ref, ids_ref, gu_ref, down_ref,
    h1_out, qkv_ref, lse_ref, o_ref, angle_ref, gain_ref, mid_ref, gate_ref, w_all, w_ref, w_own,
    h2_all, dy_all, table_all, mate_0, far_0, far_mate_0, mate_1, far_1, far_mate_early_1,
    x_ref, g_ref, seg_ref, wo_ref, dy_mate, g_own, seg_own, wo_own, h1_ref, o_full, h2_own, table_own,
    xs, xr, ws, wr, gs, gr, ss, sr, cs, cr, ds, dr, early,
    os, orv, w_send, w_recv, a_send, a_recv, b_send, b_recv, s0, r0, s1, r1, ts, tr, zs, zr, es, er, local,
):
    spot = Spot()
    everyone = NARROW * WIDE
    for head in range(WIDE):
        at = 256 * head
        w_own[:, at : at + 128] = wq_in[:, 128 * head : 128 * head + 128]
        w_own[:, at + 128 : at + 256] = jnp.concatenate(
            [wk_in[:, 64 * head : 64 * head + 64], wv_in[:, 64 * head : 64 * head + 64]], axis=1
        )
    wo_own[:, 0:WIDTH] = wo_in[...]
    wo_own[:, WIDTH : WIDTH + 128] = jnp.concatenate([router_in[...], jnp.zeros((32, 96), BF16)], axis=1)
    g_own[...] = jnp.zeros_like(g_own)
    g_own[0:1, 0:32] = gain_one_in[...].astype(F32)
    g_own[1:2, 0:32] = gain_two_in[...].astype(F32)
    seg_own[...] = jnp.zeros_like(seg_own)
    seg_own[0:2, :] = seg_in[...]
    spot.greet(everyone)

    def others(step):
        other = lax.rem(spot.me + step, everyone)
        return other, lax.div(other, WIDE), lax.rem(other, WIDE)

    def columns_of(o_w):
        return w_own.at[:, pl.ds(pl.multiple_of(o_w * 256, 256), 256)]

    def weights(step, arriving):
        other, o_n, o_w = others(step)
        place = other if arriving else spot.me
        return (
            remote(columns_of(o_w), w_ref.at[place], ws.at[other], wr.at[place], (o_n, o_w)),
            remote(g_own, g_ref.at[place], gs.at[other], gr.at[place], (o_n, o_w)),
        )

    def documents(step, arriving):
        other = lax.rem(spot.w + step, WIDE)
        place = other if arriving else spot.w
        return remote(seg_own, seg_ref.at[place], ss.at[other], sr.at[place], spot.wide(other))

    def column(step, arriving):
        other = lax.rem(spot.n + step, NARROW)
        place = other if arriving else spot.n
        return remote(wo_own, wo_ref.at[place], cs.at[other], cr.at[place], (other, spot.w))

    def start_weights_out(step, carry):
        start_all(weights(step, False))
        return carry

    def start_column(step, carry):
        column(step, False).start()
        return carry

    def start_documents(step, carry):
        documents(step, False).start()
        return carry

    def wait_weights(step, carry):
        for copy in weights(step, False):
            copy.wait_send()
        for copy in weights(step, True):
            copy.wait_recv()
        return carry

    def wait_column(step, carry):
        column(step, False).wait_send()
        column(step, True).wait_recv()
        return carry

    def wait_documents(step, carry):
        documents(step, False).wait_send()
        documents(step, True).wait_recv()
        return carry

    x_gather = PlaneGather(
        spot,
        lambda half: x_in if half is None else x_in.at[half],
        lambda who, half: x_ref.at[who] if half is None else x_ref.at[who, half],
        xs, xr,
    )
    lax.fori_loop(1, WIDE, start_documents, 0)
    lax.fori_loop(1, everyone, start_weights_out, 0)
    x_gather.begin()
    lax.fori_loop(1, NARROW, start_column, 0)
    dy_across = remote(dy_ref, dy_mate, ds.at[0], dr.at[0], (spot.mate, spot.w))
    dy_across.start()
    mine = [
        pltpu.make_async_copy(x_in, x_ref.at[spot.w], early.at[0]),
        pltpu.make_async_copy(columns_of(spot.w), w_ref.at[spot.me], early.at[1]),
        pltpu.make_async_copy(g_own, g_ref.at[spot.me], early.at[2]),
        pltpu.make_async_copy(seg_own, seg_ref.at[spot.w], early.at[3]),
        pltpu.make_async_copy(wo_own, wo_ref.at[spot.n], early.at[4]),
    ]
    start_all(mine)
    mate_base = (1 - spot.half) * WIDE
    own_base = spot.half * WIDE
    mate_slot = mate_base + spot.w

    def w_source(half):
        return wo_ref if half is None else wo_ref.at[pl.ds(2 * half, 2)]

    def w_place(who, half):
        return w_all.at[:, who] if half is None else w_all.at[pl.ds(2 * half, 2), who]

    w_gather = PlaneGather(spot, w_source, w_place, w_send, w_recv)
    dy_gather = gather_tokens(spot, dy_ref, dy_all, own_base, a_send, a_recv)
    mate_dy_gather = gather_tokens(spot, dy_mate, dy_all, mate_base, b_send, b_recv)
    x_gather.middle()
    first_expert = piece_copies(spot, gu_ref, down_ref, 0, 2, far_0, es, er, 0)
    first_expert += piece_copies(spot, gu_ref, down_ref, 0, 3, far_mate_0, es, er, 2)
    first_expert += piece_copies(spot, gu_ref, down_ref, 0, 1, mate_0, es, er, 4)
    start_all(first_expert)
    x_gather.late()
    x_gather.last()
    lax.fori_loop(1, WIDE, wait_documents, 0)
    lax.fori_loop(1, everyone, wait_weights, 0)
    lax.fori_loop(1, NARROW, wait_column, 0)
    for copy in mine:
        copy.wait()
    w_gather.begin()
    dy_gather.begin()

    x_gather.finish()
    keep = [
        pltpu.make_async_copy(wo_ref, w_place(spot.w, None), local.at[0]),
        pltpu.make_async_copy(dy_ref, dy_all.at[spot.slot], local.at[1]),
    ]
    for copy in keep:
        copy.start()

    def heads(to, place):
        return (
            o_ref.at[:, pl.ds(to * SPAN, SPAN), :],
            o_full.at[:, :, pl.ds(pl.multiple_of(place * 128, 128), 128)],
        )

    def each_head_copy(to, act_local, act_remote):
        source, target = heads(to, spot.w)

        @pl.when(spot.w == to)
        def _():
            act_local(pltpu.make_async_copy(source, target, local.at[3]))

        @pl.when(spot.w != to)
        def _():
            act_remote(remote(source, target, os.at[to], orv.at[spot.w], spot.wide(to)))

    expert = lax.broadcasted_iota(jnp.int32, (32, TOKENS), 0).astype(F32)
    named = jnp.zeros((32, TOKENS), F32)
    ids = jnp.concatenate([ids_ref[0], ids_ref[1]], axis=1).astype(F32)
    for k in range(TOP):
        named = jnp.where(expert == ids[k : k + 1, :], 1.0, named)
    before = lax.broadcasted_iota(jnp.int32, (TOKENS, TOKENS), 0) < lax.broadcasted_iota(
        jnp.int32, (TOKENS, TOKENS), 1
    )
    places = mm(named.astype(BF16), jnp.where(before, 1.0, 0.0).astype(BF16))
    kept = jnp.where((named > 0.5) & (places < float(CAP)), places, -1.0)

    gains = g_ref[...]
    gain_one = gather_gain(gains[:, 0, :])
    gain_two = gather_gain(gains[:, 1, :])
    gain_ref[...] = jnp.concatenate([gain_one, gain_two, jnp.zeros((6, WIDTH), F32)], axis=0)
    attention = Attention(
        x_ref, w_ref, seg_ref, cos_ref, sin_ref, freq_ref, gain_one,
        h1_ref, qkv_ref, lse_ref, o_ref, angle_ref,
    )
    between = {1: [w_gather.middle], 2: [w_gather.late, dy_gather.middle], 3: [w_gather.last, dy_gather.late]}
    for i in range(4):
        for row in range(2):
            attention.chunk(row, i)
        for to in (2 * i, 2 * i + 1):
            each_head_copy(to, lambda copy: copy.start(), lambda copy: copy.start())
        for step in between.get(i, []):
            step()
    far = piece_copies(spot, gu_ref, down_ref, 1, 2, far_1, es, er, 6)
    near = piece_copies(spot, gu_ref, down_ref, 1, 1, mate_1, es, er, 8)
    far_mate = piece_copies(spot, gu_ref, down_ref, 1, 3, far_mate_early_1, es, er, 10, last=MIDDLE)
    h1_copy = pltpu.make_async_copy(h1_ref, h1_out, local.at[4])
    h1_copy.start()
    dy_gather.last()
    dy_across.wait_send()
    dy_across.wait_recv()
    keep_mate = pltpu.make_async_copy(dy_mate, dy_all.at[mate_slot], local.at[2])
    keep_mate.start()
    mate_dy_gather.begin()
    w_gather.finish()
    keep[0].wait()
    for to in range(WIDE):
        each_head_copy(to, lambda copy: copy.wait(), lambda copy: copy.wait_send())

    def wait_heads(step, carry):
        other = lax.rem(spot.w + step, WIDE)
        target = o_full.at[:, :, pl.ds(pl.multiple_of(other * 128, 128), 128)]
        remote(target, target, os.at[0], orv.at[other], spot.wide(other)).wait_recv()
        return carry

    lax.fori_loop(1, WIDE, wait_heads, 0)
    attended = o_full[...].reshape(TOKENS, WIDTH)
    x_own = x_ref[spot.w].reshape(TOKENS, WIDTH).astype(F32)
    mid = x_own + mm(attended, w_all[:, :, :, 0:WIDTH].reshape(WIDTH, WIDTH))
    mid_ref[...] = mid
    scale = lax.rsqrt(jnp.mean(mid * mid, axis=1, keepdims=True) + EPSILON)
    h2 = (mid * scale * gain_two).astype(BF16)
    h2_own[...] = h2
    across = remote(h2_own, h2_all.at[spot.slot], zs.at[0], zr.at[0], (spot.mate, spot.w))
    across.start()
    first = gather_tokens(spot, h2_own, h2_all, own_base, s0, r0)
    first.begin()
    keep_own = pltpu.make_async_copy(h2_own, h2_all.at[spot.slot], local.at[5])
    keep_own.start()

    logits = jnp.transpose(mm(h2, w_all[:, :, :, WIDTH : WIDTH + 128].reshape(WIDTH, 128)))[0:32]
    chosen = jnp.where(named > 0.5, logits, MASKED)
    rise = jnp.where(named > 0.5, jnp.exp(chosen - jnp.max(chosen, axis=0, keepdims=True)), 0.0)
    gate = rise / jnp.sum(rise, axis=0, keepdims=True)
    gate_ref[0:32, :] = gate
    gate_ref[32:64, :] = named
    for owner in range(GROUP):
        table_own[owner, 0:2, :] = kept[2 * owner : 2 * owner + 2]
        table_own[owner, 2:4, :] = gate[2 * owner : 2 * owner + 2]
        table_own[owner, 4:8, :] = jnp.zeros((4, TOKENS), F32)

    def tables(step, arriving):
        other = lax.rem(spot.slot + step, GROUP)
        o_half, o_w = lax.div(other, WIDE), lax.rem(other, WIDE)
        place = other if arriving else spot.slot
        return remote(
            table_own.at[2 * o_w + o_half], table_all.at[place], ts.at[other], tr.at[place],
            (spot.n - spot.half + o_half, o_w),
        )

    def start_table(step, carry):
        tables(step, False).start()
        return carry

    lax.fori_loop(1, GROUP, start_table, 0)
    table_mine = pltpu.make_async_copy(
        table_own.at[2 * spot.w + spot.half], table_all.at[spot.slot], local.at[6]
    )
    table_mine.start()

    mate_dy_gather.middle()
    mate_dy_gather.late()
    start_all(far)
    first.middle()
    mate_dy_gather.last()
    first.late()
    first.last()
    arriving = h2_all.at[mate_slot]
    remote(arriving, arriving, zs.at[0], zr.at[0], (spot.mate, spot.w)).wait_recv()
    second = gather_tokens(spot, arriving, h2_all, mate_base, s1, r1)
    second.begin()
    start_all(far_mate + near)
    second.middle()
    second.late()
    second.last()

    def wait_table(step, carry):
        tables(step, False).wait_send()
        tables(step, True).wait_recv()
        return carry

    lax.fori_loop(1, GROUP, wait_table, 0)
    dy_gather.finish()
    mate_dy_gather.finish()
    first.finish()
    second.finish()
    across.wait_send()
    keep[1].wait()
    keep_mate.wait()
    keep_own.wait()
    table_mine.wait()
    h1_copy.wait()
    for copy in first_expert + far + far_mate + near:
        copy.wait_send()
        copy.wait_recv()


def forward_call(*operands):
    dma = pltpu.SemaphoreType.DMA
    copies = PlaneGather.COPIES
    everyone = NARROW * WIDE
    return pl.pallas_call(
        forward_kernel,
        name="forward",
        out_shape=(
            jax.ShapeDtypeStruct((2, SEQ, WIDTH), BF16),
            jax.ShapeDtypeStruct((2, SEQ, 256), BF16),
            jax.ShapeDtypeStruct((2, SEQ, 128), F32),
            jax.ShapeDtypeStruct((2, SEQ, 128), BF16),
            jax.ShapeDtypeStruct((2, SEQ, 256), F32),
            jax.ShapeDtypeStruct((8, WIDTH), F32),
            jax.ShapeDtypeStruct((TOKENS, WIDTH), F32),
            jax.ShapeDtypeStruct((64, TOKENS), F32),
            jax.ShapeDtypeStruct((NARROW, WIDE, 32, WIDTH + 128), BF16),
            jax.ShapeDtypeStruct((everyone, 32, 256), BF16),
            jax.ShapeDtypeStruct((32, 2 * WIDTH), BF16),
            jax.ShapeDtypeStruct((GROUP, TOKENS, WIDTH), BF16),
            jax.ShapeDtypeStruct((GROUP, TOKENS, WIDTH), BF16),
            jax.ShapeDtypeStruct((GROUP, 8, TOKENS), F32),
        )
        + tuple(jax.ShapeDtypeStruct((depth, WIDTH), BF16) for depth in (384, 384, 384, 384, 384, MIDDLE)),
        in_specs=[IN_VMEM] * 14 + [IN_HBM, IN_HBM],
        out_specs=(IN_HBM,) + (IN_VMEM,) * 10 + (IN_HBM,) * 9,
        scratch_shapes=[
            pltpu.VMEM((WIDE, 2, SPAN, WIDTH), BF16),
            pltpu.VMEM((everyone, 8, 128), F32),
            pltpu.VMEM((WIDE, 8, 128), jnp.int32),
            pltpu.VMEM((NARROW, 32, WIDTH + 128), BF16),
            pltpu.VMEM((TOKENS, WIDTH), BF16),
            pltpu.VMEM((8, 128), F32),
            pltpu.VMEM((8, 128), jnp.int32),
            pltpu.VMEM((32, WIDTH + 128), BF16),
            pltpu.VMEM((2, SEQ, WIDTH), BF16),
            pltpu.VMEM((2, SPAN, WIDTH), BF16),
            pltpu.VMEM((TOKENS, WIDTH), BF16),
            pltpu.VMEM((GROUP, 8, TOKENS), F32),
            dma((copies,)),
            dma((copies,)),
        ]
        + [dma((everyone,))] * 4
        + [dma((WIDE,))] * 2
        + [dma((NARROW,))] * 2
        + [dma((1,)), dma((1,)), dma((5,)), dma((WIDE,)), dma((WIDE,))]
        + [dma((copies,))] * 10
        + [dma((GROUP,)), dma((GROUP,)), dma((1,)), dma((1,)), dma((12,)), dma((12,)), dma((7,))],
        compiler_params=pltpu.CompilerParams(collective_id=1, has_side_effects=True, vmem_limit_bytes=VMEM_BYTES),
        cost_estimate=duration(1),
    )(*operands)


def load_quarters(own, pieces, w_gu, w_down, sems):
    n = lax.axis_index("narrow")
    half, pair = lax.rem(n, 2), lax.div(n, 2)
    mate = n + 1 - 2 * half
    far = n + 2 - 4 * pair
    far_mate = mate + 2 - 4 * pair
    copies = []
    for quarter, parts in zip((n, mate, far, far_mate), (own,) + pieces):
        first = 0
        for part in parts if isinstance(parts, tuple) else (parts,):
            depth = part.shape[0]
            for start, rows, target in ((0, 256, w_gu), (256, 128, w_down)):
                low, high = max(first, start), min(first + depth, start + rows)
                if low < high:
                    place = quarter * rows + (low - start)
                    copies.append(
                        pltpu.make_async_copy(
                            part.at[pl.ds(low - first, high - low)],
                            target.at[pl.ds(pl.multiple_of(place, 32), high - low)],
                            sems.at[len(copies)],
                        )
                    )
            first += depth
    return copies


def pick(table_ref, source, expert):
    slot = lax.broadcasted_iota(jnp.int32, (SLOTS, TOKENS), 0).astype(F32)
    return slot == table_ref[source, expert : expert + 1, :]


STEPS = GROUP // CHUNK
ROWS = CHUNK * SLOTS


def start_weights(e, gu_ref, down_ref, pieces, w_gu, w_down, gu_sum, down_sum, sems):
    mine = 2 * lax.rem(lax.axis_index("narrow"), 2) + e
    copies = load_quarters((gu_ref.at[mine], down_ref.at[mine]), pieces, w_gu, w_down, sems)
    for copy in copies:
        copy.start()
    gu_sum[...] = jnp.zeros_like(gu_sum)
    down_sum[...] = jnp.zeros_like(down_sum)
    for copy in copies:
        copy.wait()


def slot_gates(table_ref, masks, e):
    return jnp.concatenate(
        [
            jnp.sum(jnp.where(masks[s], table_ref[s, 2 + e : 3 + e, :], 0.0), axis=1, keepdims=True)
            for s in range(CHUNK)
        ],
        axis=0,
    )


def expert_math(rows, grad_rows, gates, w_gu, w_down, gu_sum, down_sum):
    g = mm(rows, w_gu[:, 0:FF])
    u = mm(rows, w_gu[:, FF : 2 * FF])
    sigmoid = 1.0 / (1.0 + jnp.exp(-g))
    active = g * sigmoid
    hidden = (active * u).astype(BF16)
    grad_rows = grad_rows.astype(F32)
    dy_pair = (grad_rows * gates).astype(BF16)
    dhid = mm(dy_pair, w_down[...], NT)
    da_g = (dhid * u * (sigmoid * (1.0 + g * (1.0 - sigmoid)))).astype(BF16)
    da_u = (dhid * active).astype(BF16)
    y = mm(hidden, w_down[...]).astype(BF16).astype(F32)
    slot_dgate = jnp.sum(y * grad_rows, axis=1, keepdims=True)
    down_sum[...] += mm(hidden, dy_pair, TN)
    gu_sum[:, 0:FF] += mm(rows, da_g, TN)
    gu_sum[:, FF : 2 * FF] += mm(rows, da_u, TN)
    dx = (mm(da_g, w_gu[:, 0:FF], NT) + mm(da_u, w_gu[:, FF : 2 * FF], NT)).astype(BF16)
    return (y * gates).astype(BF16), dx, slot_dgate


def token_dgate(dgate_ref, masks, slot_dgate, e):
    for s in range(CHUNK):
        part = slot_dgate[s * SLOTS : (s + 1) * SLOTS]
        dgate_ref[s, e : e + 1, :] = jnp.sum(jnp.where(masks[s], part, 0.0), axis=0, keepdims=True)


def store_quarters(outs, gu_sum, down_sum):
    n = lax.axis_index("narrow")
    half, pair = lax.rem(n, 2), lax.div(n, 2)
    mate = n + 1 - 2 * half
    far = n + 2 - 4 * pair
    far_mate = mate + 2 - 4 * pair
    for out, quarter in zip(outs, (n, mate, far, far_mate)):
        out[0:256, :] = gu_sum[pl.ds(pl.multiple_of(quarter * 256, 256), 256), :].astype(BF16)
        out[256:384, :] = down_sum[pl.ds(pl.multiple_of(quarter * 128, 128), 128), :].astype(BF16)


def expert_0_kernel(
    h2_ref, dy_ref, table_ref, gu_ref, down_ref, w1, w2, w3,
    gated_ref, dx_ref, rows_ref, grad_rows_ref, dgate_ref, own, mate, far, far_mate, far_mate_1,
    w_gu, w_down, gu_sum, down_sum, sems, es, er,
):
    step = pl.program_id(0)
    spot = Spot()
    second_expert = piece_copies(spot, gu_ref, down_ref, 1, 3, far_mate_1, es, er, 0, first=MIDDLE)

    @pl.when(step == 0)
    def _():
        barrier = pltpu.get_barrier_semaphore()
        plane = spot.mate + 2 - 4 * lax.div(spot.n, 2)
        pl.semaphore_signal(barrier, inc=1, device_id=(plane, spot.w), device_id_type=MESH)
        pl.semaphore_wait(barrier, 1)
        start_all(second_expert)
        start_weights(0, gu_ref, down_ref, (w1, w2, w3), w_gu, w_down, gu_sum, down_sum, sems)

    masks = [[pick(table_ref, s, e) for s in range(CHUNK)] for e in range(MINE)]
    rows, grad_rows = [], []
    for s in range(CHUNK):
        hot = jnp.concatenate([jnp.where(masks[e][s], 1.0, 0.0) for e in range(MINE)], axis=0).astype(BF16)
        rows.append(mm(hot, h2_ref[s]).astype(BF16))
        grad_rows.append(mm(hot, dy_ref[s]).astype(BF16))
    for s in range(CHUNK):
        rows_ref[0, s * SLOTS : (s + 1) * SLOTS, :] = rows[s][SLOTS:]
        grad_rows_ref[0, s * SLOTS : (s + 1) * SLOTS, :] = grad_rows[s][SLOTS:]
    rows = jnp.concatenate([r[:SLOTS] for r in rows], axis=0)
    grad_rows = jnp.concatenate([r[:SLOTS] for r in grad_rows], axis=0)
    gated, dx, slot_dgate = expert_math(
        rows, grad_rows, slot_gates(table_ref, masks[0], 0), w_gu, w_down, gu_sum, down_sum
    )
    gated_ref[0] = gated
    dx_ref[0] = dx
    dgate_ref[...] = jnp.zeros_like(dgate_ref)
    token_dgate(dgate_ref, masks[0], slot_dgate, 0)

    @pl.when(step == STEPS - 1)
    def _():
        store_quarters((own, mate, far, far_mate), gu_sum, down_sum)
        for copy in second_expert:
            copy.wait_send()
            copy.wait_recv()


def expert_1_kernel(
    rows_ref, grad_rows_ref, gated_before, dx_before, dgate_before, table_ref, gu_ref, down_ref, w1, w2, w3_early, w3_rest,
    y_here, y_there, part_here, part_there, dgate_ref, own, mate, far, far_mate,
    w_gu, w_down, gu_sum, down_sum, sems, held, local, send, recv,
):
    step = pl.program_id(0)
    spot = Spot()
    slot = lax.rem(step, 2)
    outs = ((y_here, y_there), (part_here, part_there))

    def copies(at_step, at_slot):
        result = []
        for kind, (here, there) in enumerate(outs):
            for pair in range(CHUNK // 2):
                block = at_step * (CHUNK // 2) + pair
                source = held.at[kind, at_slot]
                result.append(
                    pltpu.make_async_copy(
                        source.at[2 * pair + spot.core], here.at[block], local.at[kind, at_slot, pair]
                    )
                )
                other = source.at[2 * pair + 1 - spot.core]
                if kind == 0:
                    result.append(pltpu.make_async_copy(other, there.at[block], send.at[kind, at_slot, pair]))
                else:
                    result.append(
                        remote(
                            other, there.at[block], send.at[kind, at_slot, pair], recv.at[block],
                            spot.wide(spot.sib),
                        )
                    )
        return result

    def finish(at_step, at_slot):
        done = copies(at_step, at_slot)
        for number, copy in enumerate(done):
            if number % 2 == 1 and number >= CHUNK:
                copy.wait_send()
            else:
                copy.wait()

    @pl.when(step == 0)
    def _():
        barrier = pltpu.get_barrier_semaphore()
        pl.semaphore_signal(barrier, inc=1, device_id=spot.wide(spot.sib), device_id_type=MESH)
        pl.semaphore_wait(barrier, 1)
        start_weights(1, gu_ref, down_ref, (w1, w2, (w3_early, w3_rest)), w_gu, w_down, gu_sum, down_sum, sems)

    masks = [[pick(table_ref, s, e) for s in range(CHUNK)] for e in range(MINE)]
    gated, dx, slot_dgate = expert_math(
        rows_ref[0], grad_rows_ref[0], slot_gates(table_ref, masks[1], 1), w_gu, w_down, gu_sum, down_sum
    )
    dgate_ref[...] = dgate_before[...]
    token_dgate(dgate_ref, masks[1], slot_dgate, 1)

    @pl.when(step >= 2)
    def _():
        finish(step - 2, slot)

    hots = [
        jnp.concatenate([jnp.where(masks[e][s], 1.0, 0.0) for e in range(MINE)], axis=0).astype(BF16)
        for s in range(CHUNK)
    ]
    leaving = copies(step, slot)
    for kind, before, now in ((1, dx_before, dx), (0, gated_before, gated)):
        for s in range(CHUNK):
            at = slice(s * SLOTS, (s + 1) * SLOTS)
            held[kind, slot, s] = mm(hots[s], jnp.concatenate([before[0, at, :], now[at]], axis=0), TN).astype(BF16)
        start_all(leaving[kind * CHUNK : (kind + 1) * CHUNK])

    @pl.when(step == STEPS - 1)
    def _():
        store_quarters((own, mate, far, far_mate), gu_sum, down_sum)
        for last in (STEPS - 2, STEPS - 1):
            finish(last, last % 2)
        for block in range(WIDE):
            place = part_there.at[block]
            remote(place, place, send.at[0, 0, 0], recv.at[block], spot.wide(spot.sib)).wait_recv()


def expert_specs():
    block = pl.BlockSpec((CHUNK, TOKENS, WIDTH), lambda c: (c, 0, 0))
    small = pl.BlockSpec((CHUNK, 8, TOKENS), lambda c: (c, 0, 0))
    slots = pl.BlockSpec((1, ROWS, WIDTH), lambda c: (c, 0, 0))
    quarter = pl.BlockSpec((384, WIDTH), lambda c: (0, 0))
    return block, small, slots, quarter


def expert_scratch():
    return [
        pltpu.VMEM((WIDTH, 2 * FF), BF16),
        pltpu.VMEM((FF, WIDTH), BF16),
        pltpu.VMEM((WIDTH, 2 * FF), F32),
        pltpu.VMEM((FF, WIDTH), F32),
        pltpu.SemaphoreType.DMA((10,)),
    ]


SLOT_ROWS = jax.ShapeDtypeStruct((STEPS, ROWS, WIDTH), BF16)
CORE_BLOCKS = jax.ShapeDtypeStruct((WIDE, TOKENS, WIDTH), BF16)
TABLES = jax.ShapeDtypeStruct((GROUP, 8, TOKENS), F32)
QUARTER = jax.ShapeDtypeStruct((384, WIDTH), BF16)


def expert_0_call(h2_all, dy_all, table_all, w_gate_up, w_down, pieces):
    block, small, slots, quarter = expert_specs()
    return pl.pallas_call(
        expert_0_kernel,
        name="expert_0",
        grid=(STEPS,),
        out_shape=(SLOT_ROWS,) * 4
        + (TABLES,)
        + (QUARTER,) * 4
        + (jax.ShapeDtypeStruct((384 - MIDDLE, WIDTH), BF16),),
        in_specs=[block, block, small] + [IN_HBM] * 5,
        out_specs=(slots,) * 4 + (small,) + (quarter,) * 4 + (IN_HBM,),
        scratch_shapes=expert_scratch() + [pltpu.SemaphoreType.DMA((2,)), pltpu.SemaphoreType.DMA((2,))],
        compiler_params=pltpu.CompilerParams(collective_id=4, has_side_effects=True, vmem_limit_bytes=VMEM_BYTES),
        cost_estimate=duration(1),
    )(h2_all, dy_all, table_all, w_gate_up, w_down, *pieces)


def expert_1_call(rows, grad_rows, gated, dx, dgate, table_all, w_gate_up, w_down, pieces):
    block, small, slots, quarter = expert_specs()
    return pl.pallas_call(
        expert_1_kernel,
        name="expert_1",
        grid=(STEPS,),
        out_shape=(CORE_BLOCKS,) * 4 + (TABLES,) + (QUARTER,) * 4,
        in_specs=[slots] * 4 + [small, small] + [IN_HBM] * 6,
        out_specs=(IN_HBM,) * 4 + (small,) + (quarter,) * 4,
        scratch_shapes=expert_scratch()
        + [
            pltpu.VMEM((2, 2, CHUNK, TOKENS, WIDTH), BF16),
            pltpu.SemaphoreType.DMA((2, 2, CHUNK // 2)),
            pltpu.SemaphoreType.DMA((2, 2, CHUNK // 2)),
            pltpu.SemaphoreType.DMA((WIDE,)),
        ],
        compiler_params=pltpu.CompilerParams(collective_id=5, has_side_effects=True, vmem_limit_bytes=VMEM_BYTES),
        cost_estimate=duration(1),
    )(rows, grad_rows, gated, dx, dgate, table_all, w_gate_up, w_down, *pieces)


RESULTS = 6


def results_kernel(*refs):
    pieces, arrays, small = refs[:8], refs[8 : 8 + RESULTS], refs[8 + RESULTS : 11 + RESULTS]
    refs = refs[11 + RESULTS :]
    gate_up_ref, down_ref, outs, small_outs = refs[0], refs[1], refs[2 : 2 + RESULTS], refs[2 + RESULTS : 6 + RESULTS]
    refs = refs[6 + RESULTS :]
    loaded, totals, held, sems, out_sems, held_sems = refs[0], refs[1], refs[2 : 2 + RESULTS], *refs[2 + RESULTS :]
    half = lax.rem(lax.axis_index("narrow"), 2)
    loads = [pltpu.make_async_copy(piece, loaded.at[i], sems.at[i]) for i, piece in enumerate(pieces)]
    through = [pltpu.make_async_copy(a, h, held_sems.at[i]) for i, (a, h) in enumerate(zip(arrays, held))]
    start_all([loads[i] for i in (0, 2, 1, 3, 4, 6, 5, 7)])
    start_all(through)
    router, gains, load = small
    small_outs[0][...] = router[...]
    small_outs[1][...] = gains[0:1, :]
    small_outs[2][...] = gains[1:2, :]
    small_outs[3][...] = load[...]
    stores = []
    for e in range(2):
        for which in range(2):
            left, right = 4 * e + which, 4 * e + which + 2
            loads[left].wait()
            loads[right].wait()
            number = 2 * e + which
            place = 2 * (half if which == 0 else 1 - half) + e
            totals[number] = loaded[left].astype(F32) + loaded[right].astype(F32)
            for part, (out, first, depth) in enumerate(((gate_up_ref, 0, 256), (down_ref, 256, 128))):
                copy = pltpu.make_async_copy(
                    totals.at[number, pl.ds(first, depth)], out.at[place], out_sems.at[2 * number + part]
                )
                copy.start()
                stores.append(copy)
    for i, copy in enumerate(through):
        copy.wait()
        copy = pltpu.make_async_copy(held[i], outs[i], held_sems.at[i])
        copy.start()
        stores.append(copy)
    for copy in stores:
        copy.wait()


def results_call(first, second, arrays, small):
    shapes = [jax.ShapeDtypeStruct(a.shape, a.dtype) for a in arrays]
    row = jax.ShapeDtypeStruct((1, 32), F32)
    return pl.pallas_call(
        results_kernel,
        name="results",
        out_shape=(
            jax.ShapeDtypeStruct((4, 256, WIDTH), F32),
            jax.ShapeDtypeStruct((4, 128, WIDTH), F32),
            *shapes,
            jax.ShapeDtypeStruct((32, 32), F32),
            row,
            row,
            jax.ShapeDtypeStruct((1, 32), jnp.int32),
        ),
        in_specs=[IN_HBM] * (8 + RESULTS) + [IN_VMEM] * 3,
        out_specs=(IN_HBM,) * (2 + RESULTS) + (IN_VMEM,) * 4,
        scratch_shapes=[pltpu.VMEM((8, 384, WIDTH), BF16), pltpu.VMEM((4, 384, WIDTH), F32)]
        + [pltpu.VMEM(s.shape, s.dtype) for s in shapes]
        + [pltpu.SemaphoreType.DMA((8,)), pltpu.SemaphoreType.DMA((8,)), pltpu.SemaphoreType.DMA((RESULTS,))],
        compiler_params=pltpu.CompilerParams(vmem_limit_bytes=VMEM_BYTES),
        cost_estimate=duration(1),
    )(*first, *second, *arrays, *small)


def widen(ref_value):
    return ref_value.astype(F32)


class PlaneReduce:
    COPIES = 10

    def __init__(self, spot, here, there, arrived, first, buffers, send, recv, local):
        self.spot, self.arrived = spot, arrived
        self.acc, self.from_core, self.from_one, self.from_two = buffers
        self.send, self.recv = send, recv
        self.started = []
        s = spot
        self.q_own = 2 * s.y + s.x
        self.q_x = 2 * s.y + 1 - s.x
        self.q_y = 2 - 2 * s.y + s.x
        self.q_d = 3 - self.q_own
        self.order = (self.q_d, self.q_x, self.q_y, self.q_own)
        self.loads = []
        for number, q in enumerate(self.order):
            mine = pltpu.make_async_copy(here.at[first + q], self.acc.at[q], local.at[number])
            if arrived:
                other = pltpu.make_async_copy(there.at[first + q], self.from_core.at[q], local.at[4 + number])
            else:
                other = remote(
                    there.at[first + q], self.from_core.at[q], send.at[6 + number], recv.at[6 + number], s.wide(s.sib)
                )
                self.started.append(other)
            self.loads.append((mine, other))

    def put(self, src, dst, number, to):
        copy = remote(src, dst, self.send.at[number], self.recv.at[number], self.spot.wide(to))
        copy.start()
        self.started.append(copy)

    def got(self, dst, number):
        remote(dst, dst, self.send.at[number], self.recv.at[number], self.spot.wide(self.spot.sib)).wait_recv()

    def begin(self):
        for pair in self.loads:
            start_all(pair)

    def add_core(self, number):
        mine, other = self.loads[number]
        mine.wait()
        other.wait() if self.arrived else other.wait_recv()
        q = self.order[number]
        self.acc[q] = self.acc[q] + self.from_core[q]

    def across_core(self):
        s = self.spot
        self.add_core(0)
        self.put(halves(self.acc.at[self.q_d], 0), self.from_one.at[1], 1, s.xn)
        self.put(halves(self.acc.at[self.q_d], 1), self.from_one.at[3], 3, s.yn)
        self.add_core(1)
        self.put(halves(self.acc.at[self.q_x], 0), self.from_one.at[0], 0, s.xn)
        self.add_core(2)
        self.put(halves(self.acc.at[self.q_y], 1), self.from_one.at[2], 2, s.yn)
        self.add_core(3)

    def across_one(self):
        s = self.spot
        self.got(self.from_one.at[1], 1)
        upper = halves(self.acc.at[self.q_y], 0)
        upper[...] = upper[...] + self.from_one[1]
        self.put(upper, self.from_two.at[0], 4, s.yn)
        self.got(self.from_one.at[3], 3)
        lower = halves(self.acc.at[self.q_x], 1)
        lower[...] = lower[...] + self.from_one[3]
        self.put(lower, self.from_two.at[1], 5, s.xn)

    def total(self, out):
        self.got(self.from_one.at[0], 0)
        self.got(self.from_two.at[0], 4)
        own = self.acc.at[self.q_own]
        out[0:SPAN, :] = widen(own[0:SPAN, :]) + widen(self.from_one[0]) + widen(self.from_two[0])
        self.got(self.from_one.at[2], 2)
        self.got(self.from_two.at[1], 5)
        out[SPAN:TOKENS, :] = widen(own[SPAN:TOKENS, :]) + widen(self.from_one[2]) + widen(self.from_two[1])

    def finish(self):
        for copy in self.started:
            copy.wait_send()


def halves(ref, which):
    return ref.at[pl.ds(which * SPAN, SPAN)]


class GroupReduce:
    def __init__(self, spot, here, there, arrived, scratch):
        acc, from_core, from_one, from_two, total, mate_send, mate_recv, send, recv, local, zs, zr = scratch
        self.total_ref, self.mate_send, self.mate_recv = total, mate_send, mate_recv
        parts = []
        for which, first in enumerate((4 * (1 - spot.half), 4 * spot.half)):
            buffers = (acc.at[which], from_core.at[which], from_one.at[which], from_two.at[which])
            parts.append(
                PlaneReduce(
                    spot, here, there, arrived, first, buffers, send.at[which], recv.at[which], local.at[which]
                )
            )
        self.theirs, self.ours = parts
        self.across = remote(mate_send, mate_recv, zs.at[0], zr.at[0], (spot.mate, spot.w))

    def begin(self):
        self.theirs.begin()
        self.ours.begin()

    def across_core(self):
        self.theirs.across_core()
        self.ours.across_core()

    def across_one(self):
        self.theirs.across_one()
        self.ours.across_one()

    def to_mate(self):
        self.theirs.total(self.total_ref)
        self.mate_send[...] = self.total_ref[...].astype(BF16)
        self.across.start()

    def finish(self):
        self.ours.total(self.total_ref)
        self.across.wait_recv()
        self.total_ref[...] += widen(self.mate_recv[...])
        self.theirs.finish()
        self.ours.finish()
        self.across.wait_send()


def reduce_scratch():
    dma = pltpu.SemaphoreType.DMA
    return [
        pltpu.VMEM((2, 4, TOKENS, WIDTH), BF16),
        pltpu.VMEM((2, 4, TOKENS, WIDTH), BF16),
        pltpu.VMEM((2, 4, SPAN, WIDTH), BF16),
        pltpu.VMEM((2, 2, SPAN, WIDTH), BF16),
        pltpu.VMEM((TOKENS, WIDTH), F32),
        pltpu.VMEM((TOKENS, WIDTH), BF16),
        pltpu.VMEM((TOKENS, WIDTH), BF16),
        dma((2, PlaneReduce.COPIES)),
        dma((2, PlaneReduce.COPIES)),
        dma((2, 8)),
        dma((1,)),
        dma((1,)),
    ]


REDUCE_REFS = 12


class AttentionBack:
    def __init__(self, dattn_all, w_rows, qkv_ref, lse_ref, o_ref, angle_ref, dqkv_ref, dkv_ref, dq_ref, osum):
        self.dattn_all, self.w_rows, self.qkv, self.lse, self.o = dattn_all, w_rows, qkv_ref, lse_ref, o_ref
        self.angle = angle_ref
        self.dqkv, self.dkv, self.dq, self.osum = dqkv_ref, dkv_ref, dq_ref, osum
        self.first_half = lane_half()
        self.is_key = lax.broadcasted_iota(jnp.int32, (1, 128), 1) < 64
        dkv_ref[...] = jnp.zeros_like(dkv_ref)
        osum[...] = jnp.zeros_like(osum)

    def stack(self, both):
        return jnp.concatenate([both[:, 0:64], both[:, 64:128]], axis=0)

    def chunk(self, row, q):
        first = pl.multiple_of(q * 256, 256)
        tokens = pl.ds(first, 256)
        dattn = self.dattn_all[pl.ds(2 * q, 2), pl.ds(row * SPAN, SPAN), :].reshape(256, WIDTH)
        outs = self.o[row, tokens, :]
        do = mm(dattn, self.w_rows[...], NT).astype(BF16)
        self.osum[...] += mm(outs, dattn, TN)
        inner = do.astype(F32) * outs.astype(F32)
        delta = jnp.concatenate(
            [
                jnp.sum(jnp.where(self.is_key, inner, 0.0), axis=1, keepdims=True),
                jnp.sum(jnp.where(self.is_key, 0.0, inner), axis=1, keepdims=True),
            ],
            axis=0,
        )
        query = self.stack(self.qkv[row, tokens, 0:128]) * BF16(HEAD_DIM**-0.5)
        do = self.stack(do)
        log_total = jnp.concatenate([self.lse[row, tokens, 0:1], self.lse[row, tokens, 64:65]], axis=0)
        start = self.lse[row, tokens, 32:33]
        start = jnp.concatenate([start, start], axis=0)
        place = lax.broadcasted_iota(jnp.int32, (256, 1), 0)
        place_query = (jnp.concatenate([place, place], axis=0) + q * 256).astype(F32)
        self.dq[...] = jnp.zeros_like(self.dq)

        def key_block(block, diagonal):
            keys_at = pl.ds(pl.multiple_of(block * 256, 256), 256)
            keys = self.qkv[row, keys_at, 128:192]
            values = self.qkv[row, keys_at, 192:256]
            place_key = (lax.broadcasted_iota(jnp.int32, (1, 256), 1) + block * 256).astype(F32)
            allowed = place_key >= start
            if diagonal:
                allowed = allowed & (place_key <= place_query)
            weights = jnp.exp(jnp.where(allowed, mm(query, keys, NT), MASKED) - log_total)
            dp = mm(do, values, NT)
            ds = (weights * (dp - delta)).astype(BF16)
            self.dq[...] += mm(ds, keys)
            dk = mm(ds, query, TN)
            dv = mm(weights.astype(BF16), do, TN)
            self.dkv[row, keys_at, :] += jnp.concatenate([dk, dv], axis=1)

        def below(block, carry):
            key_block(block, False)
            return carry

        lax.fori_loop(0, q, below, 0)
        key_block(q, True)
        dq = jnp.concatenate([self.dq[0:256], self.dq[256:512]], axis=1) * (HEAD_DIM**-0.5)
        cosine = self.angle[row, tokens, 0:128]
        sine = self.angle[row, tokens, 128:256]
        self.dqkv[row, tokens, 0:128] = (dq * cosine + turn_back(dq * sine, self.first_half)).astype(BF16)

    def keys(self, row):
        cosine = self.angle[row, :, 0:128]
        sine = self.angle[row, :, 128:256]
        dkv = self.dkv[row]
        turned = dkv * cosine + turn_back(dkv * sine, self.first_half)
        self.dqkv[row, :, 128:256] = jnp.where(self.is_key, turned, dkv).astype(BF16)


def backward_kernel(*refs):
    (
        part_here, part_there, y_here, y_there, dgate_ref, h2_ref, w_out_ref, w_full_ref, h1_ref, qkv_ref, lse_ref, o_ref,
        angle_ref, mate_1, far_1, far_mate_1,
        x_ref, mid_ref, gate_ref, gain_ref, dy_ref, w_own, gain_own,
    ) = refs[:23]
    (
        block_out, in_grad, q_grad, k_grad, v_grad, o_grad, router_grad, two_gains, load_out, *quarters_recv,
    ) = refs[23:35]
    (
        dgate_all, h2_own, dattn_all, dmid_ref, small_ref, small_all, small_sum, w_router, w_rows, w_full,
        h1, qkv, lse, outs, angle, dqkv_ref, dkv_ref, dq_ref, osum, og_ref, wg_ref,
        dq_full, w_recv, o_held, s_held, o_recv, s_recv,
        ts, tr, s0, r0, bs, br, qs, qr, ks, kr, ws, wr, os, orv, ss, sr, gs, gr, local,
    ) = refs[35:81]
    h2_sum_refs = refs[81 : 81 + REDUCE_REFS]
    y_sum_refs = refs[81 + REDUCE_REFS :]

    spot = Spot()
    everyone = NARROW * WIDE
    h2_sum = GroupReduce(spot, part_here, part_there, True, h2_sum_refs)
    y_sum = GroupReduce(spot, y_here, y_there, False, y_sum_refs)
    h2_sum.begin()
    spot.greet(everyone)

    def tables(step, arriving):
        other = lax.rem(spot.slot + step, GROUP)
        o_half, o_w = lax.div(other, WIDE), lax.rem(other, WIDE)
        place = other if arriving else spot.slot
        return remote(
            dgate_ref.at[other], dgate_all.at[place], ts.at[other], tr.at[place],
            (spot.n - spot.half + o_half, o_w),
        )

    def start_table(step, carry):
        tables(step, False).start()
        return carry

    lax.fori_loop(1, GROUP, start_table, 0)
    rows = pl.ds(pl.multiple_of(spot.w * 128, 128), 128)
    loads = [
        (dgate_ref.at[spot.slot], dgate_all.at[spot.slot]),
        (h2_ref.at[spot.slot], h2_own),
        (w_out_ref.at[:, pl.ds(WIDTH, 128)], w_router),
        (w_out_ref.at[rows, pl.ds(0, WIDTH)], w_rows),
        (qkv_ref, qkv),
        (lse_ref, lse),
        (o_ref, outs),
        (angle_ref, angle),
        (h1_ref, h1),
    ]
    loads = [pltpu.make_async_copy(src, dst, local.at[i]) for i, (src, dst) in enumerate(loads)]
    w_loads = [pltpu.make_async_copy(w_full_ref.at[who], w_full.at[who], local.at[10 + who]) for who in range(WIDE)]
    h2_sum.theirs.across_core()
    start_all(loads + w_loads)
    y_sum.begin()
    h2_sum.theirs.across_one()
    h2_sum.ours.across_core()
    far_plane = 2 - 4 * lax.div(spot.n, 2)
    quarter_copies = [
        remote(piece, quarters_recv[number], gs.at[number], gr.at[number], (plane, spot.w))
        for number, (piece, plane) in enumerate(
            ((mate_1, spot.mate), (far_1, spot.n + far_plane), (far_mate_1, spot.mate + far_plane))
        )
    ]
    h2_sum.to_mate()
    start_all(quarter_copies)
    h2_sum.ours.across_one()
    y_sum.across_core()
    h2_sum.finish()

    def wait_table(step, carry):
        tables(step, False).wait_send()
        tables(step, True).wait_recv()
        return carry

    lax.fori_loop(1, GROUP, wait_table, 0)
    for copy in loads[:4]:
        copy.wait()

    gate = gate_ref[0:32, :]
    dgate = jnp.concatenate([dgate_all[(o % 2) * WIDE + o // 2, 0:2, :] for o in range(GROUP)], axis=0)
    dsel = gate * (dgate - jnp.sum(gate * dgate, axis=0, keepdims=True))
    dlogits = jnp.concatenate([dsel, jnp.zeros((96, TOKENS), F32)], axis=0)
    dh2 = h2_sum.total_ref[...] + mm(jnp.transpose(dlogits).astype(BF16), w_router[...], NT)
    mid = mid_ref[...]
    scale = lax.rsqrt(jnp.mean(mid * mid, axis=1, keepdims=True) + EPSILON)
    weighted = dh2 * gain_ref[1:2, :]
    inner = jnp.mean(weighted * mid, axis=1, keepdims=True)
    dmid = dy_ref[...].astype(F32) + weighted * scale - mid * (scale * scale * scale) * inner
    dmid_ref[...] = dmid
    dattn_all[spot.w] = dmid.astype(BF16)
    mine = dattn_all.at[spot.w]
    gather = PlaneGather(
        spot,
        lambda half: mine if half is None else halves(mine, half),
        lambda who, half: dattn_all.at[who] if half is None else halves(dattn_all.at[who], half),
        s0, r0,
    )
    gather.begin()
    small_ref[0:32, :] = mm(dsel.astype(BF16), h2_own[...])
    small_ref[32:33, :] = jnp.sum(dh2 * mid * scale, axis=0, keepdims=True)
    lane = lax.broadcasted_iota(jnp.int32, (32, WIDTH), 1)
    column = lax.broadcasted_iota(jnp.int32, (32, WIDTH), 0)
    count = jnp.sum(gate_ref[32:64, :], axis=1, keepdims=True)
    small_ref[33:34, :] = jnp.sum(jnp.where(lax.rem(lane, 128) == column, count, 0.0), axis=0, keepdims=True)
    small_ref[34:40, :] = jnp.zeros((6, WIDTH), F32)

    def lanes_to(step, arriving):
        other = lax.rem(spot.w + step, WIDE)
        place = other if arriving else spot.w
        return remote(
            small_ref.at[:, pl.ds(pl.multiple_of(other * 128, 128), 128)], small_all.at[place],
            bs.at[other], br.at[place], spot.wide(other),
        )

    def start_lanes(step, carry):
        lanes_to(step, False).start()
        return carry

    lax.fori_loop(1, WIDE, start_lanes, 0)
    small_all[spot.w] = small_ref[:, pl.ds(pl.multiple_of(spot.w * 128, 128), 128)]

    for copy in loads[4:8]:
        copy.wait()
    back = AttentionBack(dattn_all, w_rows, qkv, lse, outs, angle, dqkv_ref, dkv_ref, dq_ref, osum)
    order = h2_sum.ours
    sib_x = spot.sib + 2 - 4 * spot.x
    sib_y = spot.sib + 4 - 8 * spot.y
    sib_d = sib_x + 4 - 8 * spot.y

    def to_tokens(other, place, first, send, recv):
        return remote(
            dqkv_ref.at[:, pl.ds(pl.multiple_of(other * SPAN, SPAN), SPAN), pl.ds(first, 128)],
            dq_full.at[:, :, pl.ds(pl.multiple_of(place * 256 + first, 128), 128)],
            send.at[other], recv.at[place], spot.wide(other),
        )

    def send_queries(who):
        for other in who:
            to_tokens(other, spot.w, 0, qs, qr).start()

    gather.got(spot.sib, None, 4)
    back.chunk(0, order.q_own)
    gather.middle()
    back.chunk(1, order.q_own)
    send_queries((spot.sib,))
    gather.late()
    gather.got(sib_x, None, 7)
    back.chunk(0, order.q_x)
    back.chunk(1, order.q_x)
    send_queries((spot.xn, sib_x))
    gather.last()
    y_sum.across_one()
    gather.got(sib_y, None, 8)
    back.chunk(0, order.q_y)
    back.chunk(1, order.q_y)
    send_queries((spot.yn, sib_y))
    gather.got(sib_d, 0, 9)
    gather.got(sib_d, 1, 10)
    back.chunk(0, order.q_d)
    back.chunk(1, order.q_d)
    send_queries((spot.diag, sib_d))
    y_sum.to_mate()
    for copy in gather.started:
        copy.wait_send()
    back.keys(0)
    back.keys(1)

    def others(step):
        other = lax.rem(spot.me + step, everyone)
        return other, (lax.div(other, WIDE), lax.rem(other, WIDE))

    def rows_of(ref, owner):
        return ref.at[pl.ds(pl.multiple_of(owner * 32, 32), 32)]

    def to_owner(step, arriving):
        other, to = others(step)
        place = other if arriving else spot.me
        return remote(rows_of(wg_ref, other), w_recv.at[place], ws.at[other], wr.at[place], to)

    def start_owner(step, carry):
        to_owner(step, False).start()
        return carry

    def start_keys(step, carry):
        to_tokens(lax.rem(spot.w + step, WIDE), spot.w, 128, ks, kr).start()
        return carry

    lax.fori_loop(1, WIDE, start_keys, 0)
    plane_mine = pltpu.make_async_copy(
        dqkv_ref.at[:, pl.ds(pl.multiple_of(spot.w * SPAN, SPAN), SPAN), :],
        dq_full.at[:, :, pl.ds(pl.multiple_of(spot.w * 256, 256), 256)],
        local.at[0],
    )
    plane_mine.start()
    og_ref[...] = osum[...].astype(BF16)

    def wait_lanes(step, carry):
        lanes_to(step, False).wait_send()
        lanes_to(step, True).wait_recv()
        return carry

    lax.fori_loop(1, WIDE, wait_lanes, 0)
    lane_total = small_all[0]
    for device in range(1, WIDE):
        lane_total = lane_total + small_all[device]
    small_sum[...] = lane_total
    odd = 4 * lax.rem(spot.w, 2)

    def first_hop(i, act_local, act_remote):
        to = odd + i
        source = og_ref.at[pl.ds(i * 32, 32)]
        place = lax.div(spot.w, 2)

        @pl.when(to == spot.w)
        def _():
            act_local(pltpu.make_async_copy(source, o_held.at[place], local.at[2]))
            act_local(pltpu.make_async_copy(small_sum, s_held.at[place], local.at[3]))

        @pl.when(to != spot.w)
        def _():
            act_remote(remote(source, o_held.at[place], os.at[i], orv.at[place], spot.wide(to)))
            act_remote(remote(small_sum, s_held.at[place], ss.at[i], sr.at[place], spot.wide(to)))

    def first_arrival(place, act):
        giver = 2 * place + lax.div(spot.w, 4)

        @pl.when(giver != spot.w)
        def _():
            held, small = o_held.at[place], s_held.at[place]
            act(remote(held, held, os.at[0], orv.at[place], spot.wide(giver)))
            act(remote(small, small, ss.at[0], sr.at[place], spot.wide(giver)))

    def second_hop(step, arriving):
        plane = lax.rem(spot.n + step, NARROW)
        place = plane if arriving else spot.n
        to = (plane, spot.w)
        return (
            remote(o_held.at[plane], o_recv.at[place], os.at[4 + step], orv.at[4 + place], to),
            remote(s_held.at[plane], s_recv.at[place], ss.at[4 + step], sr.at[4 + place], to),
        )

    for i in range(4):
        first_hop(i, lambda c: c.start(), lambda c: c.start())

    loads[8].wait()
    wg_ref[...] = (mm(h1[0], dqkv_ref[0], TN) + mm(h1[1], dqkv_ref[1], TN)).astype(BF16)
    lax.fori_loop(1, everyone, start_owner, 0)
    owner_mine = pltpu.make_async_copy(rows_of(wg_ref, spot.me), w_recv.at[spot.me], local.at[1])
    owner_mine.start()
    for i in range(4):
        first_hop(i, lambda c: c.wait(), lambda c: c.wait_send())
    for place in range(NARROW):
        first_arrival(place, lambda c: c.wait_recv())
    for step in range(1, NARROW):
        start_all(second_hop(step, False))

    def wait_plane(step, carry):
        other = lax.rem(spot.w + step, WIDE)
        for first, send, recv in ((0, qs, qr), (128, ks, kr)):
            to_tokens(other, spot.w, first, send, recv).wait_send()
            to_tokens(other, other, first, send, recv).wait_recv()
        return carry

    lax.fori_loop(1, WIDE, wait_plane, 0)
    plane_mine.wait()
    for copy in w_loads:
        copy.wait()
    dh1 = jnp.zeros((TOKENS, WIDTH), F32)
    for who in range(WIDE):
        grads = dq_full[:, :, 256 * who : 256 * who + 256].reshape(TOKENS, 256)
        dh1 = dh1 + mm(grads, w_full[who], NT)
    x = x_ref[...].astype(F32)
    scale = lax.rsqrt(jnp.mean(x * x, axis=1, keepdims=True) + EPSILON)
    weighted = dh1 * gain_ref[0:1, :]
    inner = jnp.mean(weighted * x, axis=1, keepdims=True)
    in_grad[...] = (dmid_ref[...] + weighted * scale - x * (scale * scale * scale) * inner).astype(BF16)
    y_sum.finish()
    block_out[...] = (mid_ref[...] + y_sum.total_ref[...]).astype(BF16)

    def wait_owner(step, carry):
        to_owner(step, False).wait_send()
        to_owner(step, True).wait_recv()
        return carry

    lax.fori_loop(1, everyone, wait_owner, 0)
    owner_mine.wait()
    for step in range(1, NARROW):
        for copy in second_hop(step, False):
            copy.wait_send()
        for copy in second_hop(step, True):
            copy.wait_recv()
    gain_total = jnp.zeros((32, 1), F32)
    for w in range(WIDE):
        total = widen(w_recv[w])
        for plane in range(1, NARROW):
            total = total + widen(w_recv[plane * WIDE + w])
        q_grad[:, 128 * w : 128 * w + 128] = total[:, 0:128]
        k_grad[:, 64 * w : 64 * w + 64] = total[:, 128:192]
        v_grad[:, 64 * w : 64 * w + 64] = total[:, 192:256]
        gain_total += jnp.sum(total * widen(w_own[:, 256 * w : 256 * w + 256]), axis=1, keepdims=True)
    o_recv[spot.n] = o_held[spot.n]
    s_recv[spot.n] = s_held[spot.n]
    total = widen(o_recv[0])
    for plane in range(1, NARROW):
        total = total + widen(o_recv[plane])
    o_grad[...] = total
    total = s_recv[0]
    for plane in range(1, NARROW):
        total = total + s_recv[plane]
    load_out[...] = total[33:34, 0:32].astype(jnp.int32)
    lane = lax.rem(spot.me, 4)
    mine = jnp.zeros((40, 32), F32)
    for part in range(4):
        mine = mine + jnp.where(lane == part, 1.0, 0.0) * total[:, 32 * part : 32 * part + 32]
    square = jnp.concatenate([mine, jnp.zeros((40, 96), F32)], axis=1)
    square = jnp.concatenate([square, jnp.zeros((88, 128), F32)], axis=0)
    router_grad[...] = jnp.transpose(square)[0:32, 0:32]
    column = jnp.concatenate([jnp.broadcast_to(gain_total, (32, 128)), jnp.zeros((96, 128), F32)], axis=0)
    attn_gain_grad = jnp.transpose(column)[0:1, 0:32] / gain_own[...].astype(F32)
    two_gains[...] = jnp.concatenate([attn_gain_grad, mine[32:33]], axis=0)

    for copy in quarter_copies:
        copy.wait_send()
        copy.wait_recv()


def backward_call(*operands):
    dma = pltpu.SemaphoreType.DMA
    vmem = pltpu.VMEM
    everyone = NARROW * WIDE
    copies = PlaneGather.COPIES
    return pl.pallas_call(
        backward_kernel,
        name="backward",
        out_shape=(
            jax.ShapeDtypeStruct((TOKENS, WIDTH), BF16),
            jax.ShapeDtypeStruct((TOKENS, WIDTH), BF16),
            jax.ShapeDtypeStruct((32, WIDTH), F32),
            jax.ShapeDtypeStruct((32, WIDTH // 2), F32),
            jax.ShapeDtypeStruct((32, WIDTH // 2), F32),
            jax.ShapeDtypeStruct((32, WIDTH), F32),
            jax.ShapeDtypeStruct((32, 32), F32),
            jax.ShapeDtypeStruct((2, 32), F32),
            jax.ShapeDtypeStruct((1, 32), jnp.int32),
        )
        + (QUARTER,) * 3,
        in_specs=[IN_HBM] * 16 + [IN_VMEM] * 7,
        out_specs=(IN_VMEM,) * 9 + (IN_HBM,) * 3,
        scratch_shapes=[
            vmem((GROUP, 8, TOKENS), F32),
            vmem((TOKENS, WIDTH), BF16),
            vmem((WIDE, TOKENS, WIDTH), BF16),
            vmem((TOKENS, WIDTH), F32),
            vmem((40, WIDTH), F32),
            vmem((WIDE, 40, 128), F32),
            vmem((40, 128), F32),
            vmem((WIDTH, 128), BF16),
            vmem((128, WIDTH), BF16),
            vmem((WIDE, WIDTH, 256), BF16),
            vmem((2, SEQ, WIDTH), BF16),
            vmem((2, SEQ, 256), BF16),
            vmem((2, SEQ, 128), F32),
            vmem((2, SEQ, 128), BF16),
            vmem((2, SEQ, 256), F32),
            vmem((2, SEQ, 256), BF16),
            vmem((2, SEQ, 128), F32),
            vmem((512, HEAD_DIM), F32),
            vmem((128, WIDTH), F32),
            vmem((128, WIDTH), BF16),
            vmem((WIDTH, 256), BF16),
            vmem((2, SPAN, 2 * WIDTH), BF16),
            vmem((everyone, 32, 256), BF16),
            vmem((NARROW, 32, WIDTH), BF16),
            vmem((NARROW, 40, 128), F32),
            vmem((NARROW, 32, WIDTH), BF16),
            vmem((NARROW, 40, 128), F32),
            dma((GROUP,)),
            dma((GROUP,)),
            dma((copies,)),
            dma((copies,)),
            dma((WIDE,)),
            dma((WIDE,)),
            dma((WIDE,)),
            dma((WIDE,)),
            dma((WIDE,)),
            dma((WIDE,)),
            dma((everyone,)),
            dma((everyone,)),
            dma((8,)),
            dma((8,)),
            dma((8,)),
            dma((8,)),
            dma((3,)),
            dma((3,)),
            dma((18,)),
        ]
        + reduce_scratch()
        + reduce_scratch(),
        compiler_params=pltpu.CompilerParams(collective_id=3, has_side_effects=True, vmem_limit_bytes=VMEM_BYTES),
        cost_estimate=duration(1),
    )(*operands)


def swap(values, distance):
    return lax.ppermute(values, "narrow", [(i, i ^ distance) for i in range(NARROW)])


def position_tables():
    freq = (1.0 / np.float32(THETA) ** (np.arange(32, dtype=np.float32) * np.float32(2.0) / np.float32(HEAD_DIM))).astype(np.float32)
    angle = np.arange(SEQ, dtype=np.float32)[:, None] * freq[None, :]
    cosine = np.tile(np.cos(angle.astype(np.float64)), (1, 4)).astype(np.float32)
    sine = np.tile(np.sin(angle.astype(np.float64)), (1, 4)).astype(np.float32)
    return cosine, sine, np.tile(freq[None, :], (8, 4)).astype(np.float32)


def fast_device(
    hidden_in, out_grad, seg_ids, expert_ids, attn_gain, w_query, w_key, w_value, w_output,
    moe_gain, w_router, w_gate_up, w_down,
):
    n = lax.axis_index("narrow")
    w = lax.axis_index("wide")
    half = n % 2
    me = n * WIDE + w
    cos_table, sin_table, freq = position_tables()

    x_own = hidden_in.reshape(TOKENS, WIDTH)
    dy_own = out_grad.reshape(TOKENS, WIDTH)
    (
        h1, qkv, lse, o_heads, angle, gain_rows, mid, gate, w_out, w_heads, w_own, h2_all, dy_all, table_all,
        mate_0, far_0, far_mate_0, mate_1, far_1, far_mate_early_1,
    ) = forward_call(
        hidden_in, dy_own, seg_ids, w_query, w_key, w_value, w_output, w_router,
        attn_gain.reshape(1, 32), moe_gain.reshape(1, 32), cos_table, sin_table, freq,
        jnp.transpose(expert_ids, (0, 2, 1)), w_gate_up, w_down,
    )
    w_out = w_out.reshape(WIDTH, WIDTH + 128)

    def send_grads(own, mate, far, far_mate):
        return own, swap(mate, 1), swap(far, 2), swap(far_mate, 3)

    gated_0, dx_0, rows_1, grad_rows_1, dgate_0, *grads_0, far_mate_rest_1 = expert_0_call(
        h2_all, dy_all, table_all, w_gate_up, w_down, (mate_0, far_0, far_mate_0)
    )
    dgate_0, w_heads = lax.optimization_barrier((dgate_0, w_heads))
    w_full = lax.all_gather(w_heads.reshape(WIDTH, 256), "wide", axis=0, tiled=False)
    grads_0 = send_grads(*grads_0)
    y_here, y_there, part_here, part_there, dgate, *grads_1 = expert_1_call(
        rows_1, grad_rows_1, gated_0, dx_0, dgate_0, table_all, w_gate_up, w_down, (mate_1, far_1, far_mate_early_1, far_mate_rest_1)
    )
    (
        block_out, in_grad, q_grad, k_grad, v_grad, o_grad, router_grad, two_gains, load, *arrived_1,
    ) = backward_call(
        part_here, part_there, y_here, y_there, dgate, h2_all, w_out, w_full, h1, qkv, lse, o_heads, angle, *grads_1[1:],
        x_own, mid, gate, gain_rows, dy_own, w_own, attn_gain.reshape(1, 32),
    )
    (
        gate_up_sum, down_sum, block_out, in_grad, q_grad, k_grad, v_grad, o_grad,
        router_grad, attn_gain_grad, moe_gain_grad, load,
    ) = results_call(
        grads_0, (grads_1[0], *arrived_1),
        (block_out, in_grad, q_grad, k_grad, v_grad, o_grad), (router_grad, two_gains, load),
    )
    return (
        block_out.reshape(hidden_in.shape),
        in_grad.reshape(hidden_in.shape),
        attn_gain_grad.reshape(32),
        q_grad,
        k_grad,
        v_grad,
        o_grad,
        moe_gain_grad.reshape(32),
        router_grad,
        gate_up_sum,
        down_sum,
        load.reshape(32),
    )


def solution(mesh):
    planned = mesh.shape["narrow"] == NARROW and mesh.shape["wide"] == WIDE
    return jax.shard_map(
        fast_device if planned else general_device,
        mesh=mesh,
        in_specs=(
            P("narrow", "wide", None),
            P("narrow", "wide", None),
            P("narrow", "wide"),
            P("narrow", "wide", None),
            P(("narrow", "wide")),
            P(("narrow", "wide"), None),
            P(("narrow", "wide"), None),
            P(("narrow", "wide"), None),
            P(("narrow", "wide"), None),
            P(("narrow", "wide")),
            P(("narrow", "wide"), None),
            P("wide", "narrow", None),
            P("wide", "narrow", None),
        ),
        out_specs=(
            P("narrow", "wide", None),
            P("narrow", "wide", None),
            P(("narrow", "wide")),
            P(("narrow", "wide"), None),
            P(("narrow", "wide"), None),
            P(("narrow", "wide"), None),
            P(("narrow", "wide"), None),
            P(("narrow", "wide")),
            P(("narrow", "wide"), None),
            P("wide", "narrow", None),
            P("wide", "narrow", None),
            P(),
        ),
        check_vma=False,
    )
```
